32 devices in a mesh: shard: 16 (over z, y, x), rep: 2 (over core).
Axes of the slice: x: 2, y: 2, z: 4, core: 2. Of those that a mesh axis runs over, the one named last changes fastest.
Arguments:
- images: bfloat16 [32, 8, 16, 768], P(('shard', 'rep')), may hold values from -6 to 6
- cotangent: bfloat16 [32, 8, 16, 1536], P(('shard', 'rep')), may hold values from -6 to 6
- depthwise_weight: bfloat16 [768, 49], P('shard'), may hold values from -0.875 to 0.875
- norm_gain: bfloat16 [768], P('shard'), may hold values from 0.5 to 1.5
- norm_bias: bfloat16 [768], P('shard'), may hold values from -3 to 3
- up_weight: bfloat16 [768, 1536], P('shard'), may hold values from -0.21875 to 0.21875
Outputs:
- grad_images: bfloat16 [32, 8, 16, 768], P(('shard', 'rep'))
- grad_up: float32 [768, 1536], P('shard')
- grad_depthwise: float32 [768, 49], P('shard')
- grad_gain: float32 [768], P('shard')
- grad_bias: float32 [768], P('shard')
The draws below stay inside these ranges and needn't reach their ends.
All inputs are finite; a program needn't handle non-finite values.
Results may differ from the reference program's by a relative error of at most 0.0056.
Values may be sent and summed in bfloat16 or wider, within the bound.
No kernel may reach another device: no remote copies, remote signals or barrier semaphores. Data moves between devices by JAX's collectives and lax.ppermute only.
A program may use at most 128 MiB of HBM per device.

```python
import math
import jax
import jax.numpy as jnp
from jax import lax

D = 768
HID = 1536
KS = 7
TH = 8
TW = 16
IMAGES = 32


def spiked(drawn, stream_key, source, target, parts, factor):
    owner, partner = [(jnp.arange(drawn.shape[position]) // (drawn.shape[position] // parts)).reshape([-1 if axis == position else 1 for axis in range(drawn.ndim)]) for position in (source, target)]
    chosen = jax.random.permutation(stream_key, parts)[partner]
    strong = (owner == chosen) | (owner == (partner + parts // 2) % parts)
    return jnp.where(strong, factor * drawn, drawn)


def block_scale(own_key, dims, split, low, largest):
    level, own = 1.0, jax.random.fold_in(own_key, 6)
    for axis_at, shards_of in split:
        heights = jnp.exp(jax.random.uniform(jax.random.fold_in(own, axis_at), (shards_of,), jnp.float32, low / len(split), largest / len(split)))
        level = level * jnp.repeat(heights, dims[axis_at] // shards_of).reshape([-1 if axis == axis_at else 1 for axis in range(len(dims))])
    return level


def noise(rng, dims, width, most, pieces=(), held_as=jnp.bfloat16):
    entries = width * jax.random.normal(rng, dims, jnp.float32)
    if pieces:
        entries = entries * block_scale(rng, dims, pieces, -0.22, 0.18)
    return jnp.clip(entries, -most, most).astype(held_as)


def bell_draw_with(key, shape, scale, reach, cuts, heavy, dtype=jnp.bfloat16):
    entries = scale * jax.random.normal(key, shape, jnp.float32)
    if cuts:
        entries = entries * block_scale(key, shape, cuts, -0.22, 0.18)
    return jnp.clip(spiked(entries, jax.random.fold_in(key, 3), *heavy), -reach, reach).astype(dtype)


def setup_inputs(seed: int = 0) -> dict:
    seeds = jax.random.split(jax.random.key(seed), 7)
    images = bell_draw_with(seeds[0], (IMAGES, TH, TW, D), 1.0, 6.0, ((0, 32),), (0, 3, 32, 2.75))
    cotangent = noise(seeds[1], (IMAGES, TH, TW, HID), 1.0, 6.0, ((0, 32),))
    depthwise_weight = noise(seeds[2], (D, KS * KS), (KS * KS) ** -0.5, 0.875, ((0, 16),))
    norm_gain = jnp.clip(1.0 + 0.1 * jax.random.normal(seeds[3], (D,), jnp.float32), 0.5, 1.5).astype(jnp.bfloat16)
    norm_bias = noise(seeds[4], (D,), 0.5, 3.0, ((0, 16),))
    up_weight = noise(seeds[5], (D, HID), D ** -0.5, 0.21875, ((0, 16),))
    return dict(images=images, cotangent=cotangent, depthwise_weight=depthwise_weight, norm_gain=norm_gain, norm_bias=norm_bias, up_weight=up_weight)


norm_eps = 1e-06

def gelu_slope(inputs):
    cumulative = 0.5 * (1.0 + lax.erf(inputs * 0.7071067811865476))
    return cumulative + inputs * jnp.exp(-0.5 * inputs * inputs) * 0.3989422804014327

def pad_tile(source, margin):
    return jnp.pad(source, ((0, 0), (margin, margin), (margin, margin), (0, 0)))

def depthwise(source, kernel, extent):
    margin = extent // 2
    height, breadth = (source.shape[1], source.shape[2])
    padded = pad_tile(source, margin)
    running = jnp.zeros_like(source)
    for down_step in range(extent):
        for across in range(extent):
            running = running + padded[:, down_step:down_step + height, across:across + breadth, :] * kernel[:, down_step * extent + across]
    return running

def depthwise_back(grad_conv, kernel, extent):
    margin = extent // 2
    height, breadth = (grad_conv.shape[1], grad_conv.shape[2])
    padded = pad_tile(grad_conv, margin)
    running = jnp.zeros_like(grad_conv)
    for down_step in range(extent):
        for across in range(extent):
            top = 2 * margin - down_step
            left = 2 * margin - across
            running = running + padded[:, top:top + height, left:left + breadth, :] * kernel[:, down_step * extent + across]
    return running

def kernel_grad(source, grad_conv, extent):
    margin = extent // 2
    height, breadth = (source.shape[1], source.shape[2])
    padded = pad_tile(source, margin)
    columns = []
    for down_step in range(extent):
        for across in range(extent):
            columns.append(lax.optimization_barrier(jnp.sum(grad_conv * padded[:, down_step:down_step + height, across:across + breadth, :], axis=(0, 1, 2))))
    return jnp.stack(columns, axis=1)

def local_pass(x_tile, cot_tile, dw_weight, gain, bias, weight, extent):
    source = x_tile.astype(jnp.float32)
    kernel = dw_weight.astype(jnp.float32)
    conv_out = depthwise(source, kernel, extent)
    average = lax.optimization_barrier(jnp.mean(conv_out, axis=-1, keepdims=True))
    centered = conv_out - average
    inv_std = lax.rsqrt(lax.optimization_barrier(jnp.mean(centered * centered, axis=-1, keepdims=True)) + norm_eps)
    whitened = centered * inv_std
    gain_f = gain.astype(jnp.float32)
    normed = (whitened * gain_f + bias.astype(jnp.float32)).astype(jnp.bfloat16)
    depth = source.shape[-1]
    hidden = weight.shape[1]
    flattened = normed.reshape(-1, depth)
    pre_act = jnp.dot(flattened, weight, preferred_element_type=jnp.float32)
    grad_pre = (cot_tile.reshape(-1, hidden).astype(jnp.float32) * gelu_slope(pre_act)).astype(jnp.bfloat16)
    grad_normed = lax.dot_general(grad_pre, weight, (((1,), (1,)), ((), ())), preferred_element_type=jnp.float32).reshape(conv_out.shape)
    weight_term = lax.dot_general(flattened, grad_pre, (((0,), (0,)), ((), ())), preferred_element_type=jnp.float32)
    gain_term = lax.optimization_barrier(jnp.sum(grad_normed * whitened, axis=(0, 1, 2)))
    bias_term = lax.optimization_barrier(jnp.sum(grad_normed, axis=(0, 1, 2)))
    grad_white = grad_normed * gain_f
    grad_conv = inv_std * (grad_white - lax.optimization_barrier(jnp.mean(grad_white, axis=-1, keepdims=True)) - whitened * lax.optimization_barrier(jnp.mean(grad_white * whitened, axis=-1, keepdims=True)))
    kernel_term = kernel_grad(source, grad_conv, extent)
    grad_input = depthwise_back(grad_conv, kernel, extent).astype(jnp.bfloat16)
    return (grad_input, weight_term, kernel_term, gain_term, bias_term)

def reference(images, cotangent, depthwise_weight, norm_gain, norm_bias, up_weight):

    def accumulate(totals, slices):
        x_tile, cot_tile = slices
        grad_input, weight_term, kernel_term, gain_term, bias_term = local_pass(x_tile[None], cot_tile[None], depthwise_weight, norm_gain, norm_bias, up_weight, KS)
        return ((totals[0] + weight_term, totals[1] + kernel_term, totals[2] + gain_term, totals[3] + bias_term), grad_input[0])
    start_sums = (jnp.zeros((D, HID), jnp.float32), jnp.zeros((D, KS * KS), jnp.float32), jnp.zeros((D,), jnp.float32), jnp.zeros((D,), jnp.float32))
    summed, grad_images = lax.scan(accumulate, start_sums, (images, cotangent))
    factor = 1.0 / math.sqrt(IMAGES * TH * TW)
    return (grad_images, summed[0] * factor, summed[1] * factor, summed[2] * factor, summed[3] * factor)
```

```python
import functools
import math

import jax
import jax.numpy as jnp
from jax import lax
from jax.experimental import pallas as pl
from jax.experimental.pallas import tpu as pltpu
from jax.sharding import PartitionSpec as P

KS = 7
TAPS = KS * KS
MARGIN = KS // 2
LANES = 128
INNER = 4
NORM_EPS = 1e-06
BF16 = jnp.bfloat16
F32 = jnp.float32
VMEM = pl.BlockSpec(memory_space=pltpu.VMEM)


def params():
    return pltpu.CompilerParams(vmem_limit_bytes=48 * 1024 * 1024)


def gelu_slope(inputs):
    cumulative = 0.5 * (1.0 + lax.erf(inputs * 0.7071067811865476))
    return cumulative + inputs * jnp.exp(-0.5 * inputs * inputs) * 0.3989422804014327


def block_rows(relative, group, line, own, lines):
    if relative:
        place = lax.axis_index("shard") ^ (line * INNER + group)
        return pl.multiple_of(place * own, 16)
    return (group * lines + line) * own


def place_rows(pieces, target, own, relative, cast=None):
    for group, piece in enumerate(pieces):
        lines = piece.shape[0] // own
        if not relative:
            target[group * piece.shape[0] : (group + 1) * piece.shape[0], :] = (
                piece[...] if cast is None else piece[...].astype(cast)
            )
            continue
        for line in range(lines):
            rows = piece[line * own : (line + 1) * own, :]
            start = block_rows(True, group, line, own, lines)
            target[pl.ds(start, own), :] = rows if cast is None else rows.astype(cast)


def split_rows(source, pieces, own, relative):
    for group, piece in enumerate(pieces):
        lines = piece.shape[0] // own
        if not relative:
            piece[...] = source[group * piece.shape[0] : (group + 1) * piece.shape[0], :].astype(
                piece.dtype
            )
            continue
        for line in range(lines):
            start = block_rows(True, group, line, own, lines)
            piece[line * own : (line + 1) * own, :] = source[pl.ds(start, own), :].astype(
                piece.dtype
            )


def correlate(padded, tile, tap_row, height, breadth):
    sums = [None] * height
    for across in range(KS):
        shifted = padded[tile, :, 8 - MARGIN + across : 8 - MARGIN + across + breadth, :]
        for down in range(KS):
            row = tap_row(down, across)
            for line in range(height):
                origin = line + down - MARGIN
                if 0 <= origin < height:
                    term = shifted[origin] * row
                    sums[line] = term if sums[line] is None else sums[line] + term
    return sums


def conv_norm_kernel(relative, own, *refs):
    small = refs[:INNER]
    x_ref, normed_ref, white_ref, inv_ref, taps_ref, gathered, padded, conv = refs[INNER:]
    height, breadth, depth = x_ref.shape[1:]
    tiles = depth // LANES
    pixels = height * breadth
    place_rows(small, gathered, own, relative, F32)
    padded[...] = jnp.zeros_like(padded)
    for tile in range(tiles):
        lanes = slice(tile * LANES, (tile + 1) * LANES)
        taps_ref[tile] = gathered[lanes, :].T
        padded[tile, :, 8 : 8 + breadth, :] = x_ref[0, :, :, lanes].astype(F32)

    def one_tile(tile, carry):
        sums = correlate(
            padded,
            tile,
            lambda down, across: taps_ref[tile, pl.ds(down * KS + across, 1), :],
            height,
            breadth,
        )
        for line in range(height):
            conv[tile, line * breadth : (line + 1) * breadth, :] = sums[line]
        return carry

    lax.fori_loop(0, tiles, one_tile, 0)
    total = conv[0]
    for tile in range(1, tiles):
        total = total + conv[tile]
    average = jnp.sum(total, axis=-1, keepdims=True) / depth
    squares = None
    for tile in range(tiles):
        centered = conv[tile] - average
        squares = centered * centered if squares is None else squares + centered * centered
    variance = jnp.sum(squares, axis=-1, keepdims=True) / depth
    inv_std = lax.rsqrt(variance + NORM_EPS)
    inv_ref[...] = jnp.broadcast_to(inv_std, (pixels, LANES))
    for tile in range(tiles):
        lanes = slice(tile * LANES, (tile + 1) * LANES)
        whitened = (conv[tile] - average) * inv_std
        white_ref[:, lanes] = whitened
        gain = taps_ref[tile, TAPS : TAPS + 1, :]
        bias = taps_ref[tile, TAPS + 1 : TAPS + 2, :]
        normed_ref[:, lanes] = (whitened * gain + bias).astype(BF16)


def project_kernel(relative, own, *refs):
    weights = refs[:INNER]
    n_own, n_other, c_own, c_other = refs[INNER : INNER + 4]
    pieces = refs[INNER + 4 : 2 * INNER + 4]
    gp_ref, weight, normed, grad = refs[2 * INNER + 4 :]
    pixels = n_own.shape[0]
    hidden = weight.shape[1]
    place_rows(weights, weight, own, relative)
    normed[:pixels, :] = n_own[...]
    normed[pixels:, :] = n_other[...]
    step = 256 if hidden % 256 == 0 else hidden
    for start in range(0, hidden, step):
        columns = slice(start, start + step)
        pre_act = jnp.dot(normed[...], weight[:, columns], preferred_element_type=F32)
        slope = gelu_slope(pre_act)
        gp_ref[:pixels, columns] = (c_own[:, columns].astype(F32) * slope[:pixels]).astype(BF16)
        gp_ref[pixels:, columns] = (c_other[:, columns].astype(F32) * slope[pixels:]).astype(BF16)
        grad[:, columns] = lax.dot_general(
            normed[...], gp_ref[:, columns], (((0,), (0,)), ((), ())), preferred_element_type=F32
        )
    split_rows(grad, pieces, own, relative)


def back_project_kernel(relative, own, *refs):
    weights = refs[:INNER]
    gp_ref, own_ref, other_ref, weight = refs[INNER:]
    pixels = own_ref.shape[0]
    place_rows(weights, weight, own, relative)
    grad_normed = lax.dot_general(
        gp_ref[...], weight[...], (((1,), (1,)), ((), ())), preferred_element_type=F32
    )
    own_ref[...] = grad_normed[:pixels]
    other_ref[...] = grad_normed[pixels:]


def norm_back_kernel(relative, own, *refs):
    gn_own, gn_other, white_ref, inv_ref, taps_ref, x_ref = refs[:6]
    pieces = refs[6 : 6 + INNER]
    grad_ref, padded, rows, small = refs[6 + INNER :]
    height, breadth, depth = x_ref.shape[1:]
    tiles = depth // LANES
    pixels = height * breadth
    padded[...] = jnp.zeros_like(padded)
    rows[...] = jnp.zeros_like(rows)
    first = None
    second = None
    for tile in range(tiles):
        lanes = slice(tile * LANES, (tile + 1) * LANES)
        padded[tile, :, 8 : 8 + breadth, :] = x_ref[0, :, :, lanes].astype(F32)
        grad_normed = gn_own[:, lanes] + gn_other[:, lanes]
        whitened = white_ref[:, lanes]
        product = grad_normed * whitened
        gain = taps_ref[tile, TAPS : TAPS + 1, :]
        rows[tile, TAPS : TAPS + 1, :] = jnp.sum(product, axis=0, keepdims=True)
        rows[tile, TAPS + 1 : TAPS + 2, :] = jnp.sum(grad_normed, axis=0, keepdims=True)
        one, two = grad_normed * gain, product * gain
        first = one if first is None else first + one
        second = two if second is None else second + two
    mean_first = jnp.sum(first, axis=-1, keepdims=True) / depth
    mean_second = jnp.sum(second, axis=-1, keepdims=True) / depth
    for tile in range(tiles):
        lanes = slice(tile * LANES, (tile + 1) * LANES)
        gain = taps_ref[tile, TAPS : TAPS + 1, :]
        grad_white = (gn_own[:, lanes] + gn_other[:, lanes]) * gain
        grad_conv = inv_ref[...] * (grad_white - mean_first - white_ref[:, lanes] * mean_second)
        grad_ref[tile] = grad_conv.reshape(height, breadth, LANES)

    def one_tile(tile, carry):
        grads = [grad_ref[tile, line] for line in range(height)]
        for across in range(KS):
            shifted = padded[tile, :, 8 - MARGIN + across : 8 - MARGIN + across + breadth, :]
            for down in range(KS):
                total = None
                for line in range(height):
                    origin = line + down - MARGIN
                    if 0 <= origin < height:
                        term = grads[line] * shifted[origin]
                        total = term if total is None else total + term
                rows[tile, pl.ds(down * KS + across, 1), :] = jnp.sum(total, axis=0, keepdims=True)
        return carry

    lax.fori_loop(0, tiles, one_tile, 0)
    for tile in range(tiles):
        small[tile * LANES : (tile + 1) * LANES, :] = rows[tile].T
    split_rows(small, pieces, own, relative)


def conv_back_kernel(grad_ref, taps_ref, out_ref, padded):
    tiles, height, breadth, _ = grad_ref.shape
    padded[...] = jnp.zeros_like(padded)
    padded[:, :, 8 : 8 + breadth, :] = grad_ref[...]

    def one_tile(tile, carry):
        sums = correlate(
            padded,
            tile,
            lambda down, across: taps_ref[tile, pl.ds(TAPS - 1 - down * KS - across, 1), :],
            height,
            breadth,
        )
        start = pl.multiple_of(tile * LANES, LANES)
        for line in range(height):
            out_ref[0, line, :, pl.ds(start, LANES)] = sums[line].astype(BF16)
        return carry

    lax.fori_loop(0, tiles, one_tile, 0)


def call(kernel, name, outs, scratch, flops, *args):
    moved = sum(math.prod(a.shape) * a.dtype.itemsize for a in args)
    moved += sum(math.prod(o.shape) * o.dtype.itemsize for o in outs)
    return pl.pallas_call(
        kernel,
        out_shape=outs,
        in_specs=[VMEM] * len(args),
        out_specs=[VMEM] * len(outs),
        scratch_shapes=scratch,
        compiler_params=params(),
        cost_estimate=pl.CostEstimate(flops=flops, bytes_accessed=moved, transcendentals=0),
        name=name,
    )(*args)


def body(images, cotangent, depthwise_weight, norm_gain, norm_bias, up_weight):
    shards, reps = lax.axis_size("shard"), lax.axis_size("rep")
    own, hidden = up_weight.shape
    depth = own * shards
    lines = shards // INNER
    half = hidden // 2
    height, breadth = images.shape[1:3]
    pixels = height * breadth
    tiles = depth // LANES
    me = lax.axis_index("shard")
    side = lax.axis_index("rep") % 2
    relative = own % 16 == 0

    def over_shard(array, flip):
        return lax.ppermute(array, "shard", [(i, i ^ flip) for i in range(shards)])

    def over_core(array):
        return lax.ppermute(array, "rep", [(i, i ^ 1) for i in range(reps)])

    def true_order(pieces):
        if relative:
            return pieces
        stacked = jnp.stack(pieces).reshape(shards, own, -1)
        flips = jnp.arange(shards) ^ me
        places = (flips % INNER) * lines + flips // INNER
        return list(jnp.take(stacked, places, axis=0).reshape(INNER, lines * own, -1))

    def relative_order(pieces):
        if relative:
            return pieces
        stacked = jnp.concatenate([p.astype(F32) for p in pieces]).reshape(shards, own, -1)
        flips = (jnp.arange(lines)[None, :] * INNER + jnp.arange(INNER)[:, None]).reshape(-1)
        moved = jnp.take(stacked, flips ^ me, axis=0).reshape(INNER, lines * own, -1)
        return [moved[0]] + [moved[i].astype(BF16) for i in range(1, INNER)]

    columns = lax.dynamic_slice(up_weight, (0, side * half), (own, half))
    extras = jnp.concatenate(
        [
            depthwise_weight,
            norm_gain[:, None],
            norm_bias[:, None],
            jnp.zeros((own, LANES - TAPS - 2), BF16),
        ],
        axis=1,
    )
    packed = jnp.concatenate([columns, extras], axis=1)
    gathered = [packed] + [over_shard(packed, INNER * line) for line in range(1, lines)]
    weight_lines = jnp.concatenate([g[:, :half] for g in gathered])
    extra_lines = jnp.concatenate([g[:, half:] for g in gathered])
    weights = [weight_lines] + [over_shard(weight_lines, flip) for flip in range(1, INNER)]
    extras = [extra_lines] + [over_shard(extra_lines, flip) for flip in range(1, INNER)]
    weights, extras = true_order(weights), true_order(extras)

    cotangent = cotangent.reshape(pixels, hidden)
    cot_own = lax.dynamic_slice(cotangent, (0, side * half), (pixels, half))
    cot_other = over_core(lax.dynamic_slice(cotangent, (0, (1 - side) * half), (pixels, half)))

    shape = jax.ShapeDtypeStruct
    padded = pltpu.VMEM((tiles, height, breadth + 16, LANES), F32)
    conv_flops = 2 * TAPS * pixels * depth
    normed, whitened, inv_std, taps = call(
        functools.partial(conv_norm_kernel, relative, own),
        "conv_norm",
        [
            shape((pixels, depth), BF16),
            shape((pixels, depth), F32),
            shape((pixels, LANES), F32),
            shape((tiles, LANES, LANES), F32),
        ],
        [
            pltpu.VMEM((depth, LANES), F32),
            padded,
            pltpu.VMEM((tiles, pixels, LANES), F32),
        ],
        conv_flops,
        *extras,
        images,
    )
    normed_other = over_core(normed)

    rows = lines * own
    *pieces, grad_pre = call(
        functools.partial(project_kernel, relative, own),
        "project",
        [shape((rows, half), F32)]
        + [shape((rows, half), BF16)] * (INNER - 1)
        + [shape((2 * pixels, half), BF16)],
        [
            pltpu.VMEM((depth, half), BF16),
            pltpu.VMEM((2 * pixels, depth), BF16),
            pltpu.VMEM((depth, half), F32),
        ],
        8 * pixels * depth * half,
        *weights,
        normed,
        normed_other,
        cot_own,
        cot_other,
    )
    pieces = relative_order(pieces)
    arrived = [over_shard(piece, flip) for flip, piece in enumerate(pieces) if flip]

    gn_own, gn_send = call(
        functools.partial(back_project_kernel, relative, own),
        "back_project",
        [shape((pixels, depth), F32)] * 2,
        [pltpu.VMEM((depth, half), BF16)],
        4 * pixels * depth * half,
        *weights,
        grad_pre,
    )
    gn_other = over_core(gn_send)
    *small, grad_conv = call(
        functools.partial(norm_back_kernel, relative, own),
        "norm_back",
        [shape((rows, LANES), F32)]
        + [shape((rows, LANES), BF16)] * (INNER - 1)
        + [shape((tiles, height, breadth, LANES), F32)],
        [
            padded,
            pltpu.VMEM((tiles, LANES, LANES), F32),
            pltpu.VMEM((depth, LANES), F32),
        ],
        conv_flops,
        gn_own,
        gn_other,
        whitened,
        inv_std,
        taps,
        images,
    )
    small = relative_order(small)
    small_arrived = [over_shard(piece, flip) for flip, piece in enumerate(small) if flip]
    (grad_images,) = call(
        conv_back_kernel,
        "conv_back",
        [shape(images.shape, BF16)],
        [padded],
        conv_flops,
        grad_conv,
        taps,
    )

    plane = pieces[0] + sum(piece.astype(F32) for piece in arrived)
    small_plane = small[0] + sum(piece.astype(F32) for piece in small_arrived)
    merged = jnp.concatenate([plane, small_plane], axis=1).reshape(lines, own, half + LANES)
    total = merged[0]
    for line in range(1, lines):
        total = total + over_shard(merged[line].astype(BF16), INNER * line).astype(F32)
    if reps > 2:
        groups = [[i for i in range(reps) if i % 2 == s] for s in range(2)]
        total = lax.psum(total, "rep", axis_index_groups=groups)
    other = over_core(total)
    factor = 1.0 / math.sqrt(images.shape[0] * pixels * shards * reps)
    total, other = total * factor, other * factor
    grad_up = jnp.where(
        side == 0,
        jnp.concatenate([total[:, :half], other[:, :half]], axis=1),
        jnp.concatenate([other[:, :half], total[:, :half]], axis=1),
    )
    sums = total[:, half:] + other[:, half:]
    return (grad_images, grad_up, sums[:, :TAPS], sums[:, TAPS], sums[:, TAPS + 1])


def solution(mesh):
    placed = (
        P(("shard", "rep"), None, None, None),
        P(("shard", "rep"), None, None, None),
        P("shard", None),
        P("shard"),
        P("shard"),
        P("shard", None),
    )
    return jax.shard_map(
        body,
        mesh=mesh,
        in_specs=placed,
        out_specs=(
            P(("shard", "rep"), None, None, None),
            P("shard", None),
            P("shard", None),
            P("shard"),
            P("shard"),
        ),
        check_vma=False,
    )
```

```python
import functools
import math

import jax
import jax.numpy as jnp
from jax import lax
from jax.experimental import pallas as pl
from jax.experimental.pallas import tpu as pltpu
from jax.sharding import PartitionSpec as P

KS = 7
TAPS = KS * KS
MARGIN = KS // 2
LANES = 128
INNER = 4
NORM_EPS = 1e-06
BF16 = jnp.bfloat16
F32 = jnp.float32
VMEM = pl.BlockSpec(memory_space=pltpu.VMEM)


def params():
    return pltpu.CompilerParams(vmem_limit_bytes=48 * 1024 * 1024)


def gelu_slope(inputs):
    cumulative = 0.5 * (1.0 + lax.erf(inputs * 0.7071067811865476))
    return cumulative + inputs * jnp.exp(-0.5 * inputs * inputs) * 0.3989422804014327


def block_rows(relative, group, line, own, lines):
    if relative:
        place = lax.axis_index("shard") ^ (line * INNER + group)
        return pl.multiple_of(place * own, 16)
    return (group * lines + line) * own


def place_rows(pieces, target, own, relative, cast=None):
    for group, piece in enumerate(pieces):
        lines = piece.shape[0] // own
        if not relative:
            target[group * piece.shape[0] : (group + 1) * piece.shape[0], :] = (
                piece[...] if cast is None else piece[...].astype(cast)
            )
            continue
        for line in range(lines):
            rows = piece[line * own : (line + 1) * own, :]
            start = block_rows(True, group, line, own, lines)
            target[pl.ds(start, own), :] = rows if cast is None else rows.astype(cast)


def split_rows(source, pieces, own, relative):
    for group, piece in enumerate(pieces):
        lines = piece.shape[0] // own
        if not relative:
            piece[...] = source[group * piece.shape[0] : (group + 1) * piece.shape[0], :].astype(
                piece.dtype
            )
            continue
        for line in range(lines):
            start = block_rows(True, group, line, own, lines)
            piece[line * own : (line + 1) * own, :] = source[pl.ds(start, own), :].astype(
                piece.dtype
            )


def correlate(padded, tile, tap_row, height, breadth):
    sums = [None] * height
    for across in range(KS):
        shifted = padded[tile, :, 8 - MARGIN + across : 8 - MARGIN + across + breadth, :]
        for down in range(KS):
            row = tap_row(down, across)
            for line in range(height):
                origin = line + down - MARGIN
                if 0 <= origin < height:
                    term = shifted[origin] * row
                    sums[line] = term if sums[line] is None else sums[line] + term
    return sums


def pack_kernel(w_ref, dw_ref, gain_ref, bias_ref, near_ref, far_ref, turned, wide):
    own, hidden = w_ref.shape
    quarter = hidden // 4
    side = lax.axis_index("rep") % 2
    parity = (lax.axis_index("shard") // INNER) % 2
    turned[...] = jnp.zeros_like(turned)
    turned[TAPS : TAPS + 1, :own] = gain_ref[...].astype(F32)
    turned[TAPS + 1 : TAPS + 2, :own] = bias_ref[...].astype(F32)
    wide[...] = jnp.zeros_like(wide)
    wide[:, :TAPS] = dw_ref[...].astype(F32)
    extras = (wide[...] + turned[...].T[:own]).astype(BF16)
    for ref, which in ((near_ref, parity), (far_ref, 1 - parity)):
        start = pl.multiple_of(side * (2 * quarter) + which * quarter, LANES)
        ref[:, :quarter] = w_ref[:, pl.ds(start, quarter)]
        ref[:, quarter:] = extras


def conv_norm_kernel(relative, own, *refs):
    small = refs[:INNER]
    x_ref, other_ref = refs[INNER : INNER + 2]
    normed_ref, white_ref, inv_ref, taps_ref, gathered, padded, conv = refs[INNER + 2 :]
    height, breadth, depth = x_ref.shape[1:]
    tiles = depth // LANES
    pixels = height * breadth
    place_rows(small, gathered, own, relative, F32)
    padded[...] = jnp.zeros_like(padded)
    for tile in range(tiles):
        lanes = slice(tile * LANES, (tile + 1) * LANES)
        taps_ref[tile] = gathered[lanes, :].T

    for image, source in enumerate((x_ref, other_ref)):
        for tile in range(tiles):
            lanes = slice(tile * LANES, (tile + 1) * LANES)
            padded[tile, :, 8 : 8 + breadth, :] = source[0, :, :, lanes].astype(F32)

        def one_tile(tile, carry):
            sums = correlate(
                padded,
                tile,
                lambda down, across: taps_ref[tile, pl.ds(down * KS + across, 1), :],
                height,
                breadth,
            )
            for line in range(height):
                conv[tile, line * breadth : (line + 1) * breadth, :] = sums[line]
            return carry

        lax.fori_loop(0, tiles, one_tile, 0)
        total = conv[0]
        for tile in range(1, tiles):
            total = total + conv[tile]
        average = jnp.sum(total, axis=-1, keepdims=True) / depth
        squares = None
        for tile in range(tiles):
            centered = conv[tile] - average
            squares = centered * centered if squares is None else squares + centered * centered
        variance = jnp.sum(squares, axis=-1, keepdims=True) / depth
        inv_std = lax.rsqrt(variance + NORM_EPS)
        if image == 0:
            inv_ref[...] = jnp.broadcast_to(inv_std, (pixels, LANES))
        for tile in range(tiles):
            lanes = slice(tile * LANES, (tile + 1) * LANES)
            whitened = (conv[tile] - average) * inv_std
            if image == 0:
                white_ref[:, lanes] = whitened
            gain = taps_ref[tile, TAPS : TAPS + 1, :]
            bias = taps_ref[tile, TAPS + 1 : TAPS + 2, :]
            normed_ref[image * pixels : (image + 1) * pixels, lanes] = (
                whitened * gain + bias
            ).astype(BF16)


def cot_pack_kernel(cot_ref, sibling_ref, out_ref):
    pixels, half = sibling_ref.shape
    quarter = half // 2
    side = lax.axis_index("rep") % 2
    parity = (lax.axis_index("shard") // INNER) % 2
    start = pl.multiple_of(side * half + (1 - parity) * quarter, LANES)
    out_ref[:pixels, :] = cot_ref[:, pl.ds(start, quarter)]
    start = pl.multiple_of((1 - parity) * quarter, LANES)
    out_ref[pixels:, :] = sibling_ref[:, pl.ds(start, quarter)]


def project_kernel(relative, own, *refs):
    weights = refs[:INNER]
    n_own, n_sibling, cot_ref, sibling_ref, far_ref = refs[INNER : INNER + 5]
    pieces = refs[INNER + 5 : 2 * INNER + 5]
    gp_ref, weight, normed, cot, grad = refs[2 * INNER + 5 :]
    pixels, half = sibling_ref.shape
    quarter = half // 2
    side = lax.axis_index("rep") % 2
    parity = (lax.axis_index("shard") // INNER) % 2
    place_rows(weights, weight, own, relative)
    normed[: 2 * pixels, :] = n_own[...]
    normed[2 * pixels :, :] = n_sibling[...]
    start = pl.multiple_of(side * half + parity * quarter, LANES)
    cot[:pixels, :] = cot_ref[:, pl.ds(start, quarter)]
    cot[pixels : 2 * pixels, :] = far_ref[:pixels, :]
    start = pl.multiple_of(parity * quarter, LANES)
    cot[2 * pixels : 3 * pixels, :] = sibling_ref[:, pl.ds(start, quarter)]
    cot[3 * pixels :, :] = far_ref[pixels:, :]
    for start in range(0, quarter, LANES):
        columns = slice(start, start + LANES)
        pre_act = jnp.dot(normed[...], weight[:, columns], preferred_element_type=F32)
        gp_ref[:, columns] = (cot[:, columns].astype(F32) * gelu_slope(pre_act)).astype(BF16)
    grad[...] = lax.dot_general(
        normed[...], gp_ref[...], (((0,), (0,)), ((), ())), preferred_element_type=F32
    )
    split_rows(grad, pieces, own, relative)


def back_project_kernel(relative, own, *refs):
    weights = refs[:INNER]
    gp_ref, own_ref, other_ref, weight = refs[INNER:]
    rows = own_ref.shape[0]
    place_rows(weights, weight, own, relative)
    grad_normed = lax.dot_general(
        gp_ref[...], weight[...], (((1,), (1,)), ((), ())), preferred_element_type=F32
    )
    own_ref[...] = grad_normed[:rows]
    other_ref[...] = grad_normed[rows:]


def core_sum_kernel(own_ref, other_ref, kept_ref, sent_ref):
    pixels = kept_ref.shape[0]
    kept_ref[...] = own_ref[:pixels] + other_ref[:pixels]
    sent_ref[...] = (own_ref[pixels:] + other_ref[pixels:]).astype(BF16)


def norm_back_kernel(relative, own, *refs):
    gn_own, gn_other, white_ref, inv_ref, taps_ref, x_ref = refs[:6]
    pieces = refs[6 : 6 + INNER]
    grad_ref, padded, rows, small = refs[6 + INNER :]
    height, breadth, depth = x_ref.shape[1:]
    tiles = depth // LANES
    pixels = height * breadth
    padded[...] = jnp.zeros_like(padded)
    rows[...] = jnp.zeros_like(rows)
    first = None
    second = None
    for tile in range(tiles):
        lanes = slice(tile * LANES, (tile + 1) * LANES)
        padded[tile, :, 8 : 8 + breadth, :] = x_ref[0, :, :, lanes].astype(F32)
        grad_normed = gn_own[:, lanes] + gn_other[:, lanes].astype(F32)
        whitened = white_ref[:, lanes]
        product = grad_normed * whitened
        gain = taps_ref[tile, TAPS : TAPS + 1, :]
        rows[tile, TAPS : TAPS + 1, :] = jnp.sum(product, axis=0, keepdims=True)
        rows[tile, TAPS + 1 : TAPS + 2, :] = jnp.sum(grad_normed, axis=0, keepdims=True)
        one, two = grad_normed * gain, product * gain
        first = one if first is None else first + one
        second = two if second is None else second + two
    mean_first = jnp.sum(first, axis=-1, keepdims=True) / depth
    mean_second = jnp.sum(second, axis=-1, keepdims=True) / depth
    for tile in range(tiles):
        lanes = slice(tile * LANES, (tile + 1) * LANES)
        gain = taps_ref[tile, TAPS : TAPS + 1, :]
        grad_white = (gn_own[:, lanes] + gn_other[:, lanes].astype(F32)) * gain
        grad_conv = inv_ref[...] * (grad_white - mean_first - white_ref[:, lanes] * mean_second)
        grad_ref[tile] = grad_conv.reshape(height, breadth, LANES)

    def one_tile(tile, carry):
        grads = [grad_ref[tile, line] for line in range(height)]
        for across in range(KS):
            shifted = padded[tile, :, 8 - MARGIN + across : 8 - MARGIN + across + breadth, :]
            for down in range(KS):
                total = None
                for line in range(height):
                    origin = line + down - MARGIN
                    if 0 <= origin < height:
                        term = grads[line] * shifted[origin]
                        total = term if total is None else total + term
                rows[tile, pl.ds(down * KS + across, 1), :] = jnp.sum(total, axis=0, keepdims=True)
        return carry

    lax.fori_loop(0, tiles, one_tile, 0)
    for tile in range(tiles):
        small[tile * LANES : (tile + 1) * LANES, :] = rows[tile].T
    split_rows(small, pieces, own, relative)


def conv_back_kernel(grad_ref, taps_ref, out_ref, padded):
    tiles, height, breadth, _ = grad_ref.shape
    padded[...] = jnp.zeros_like(padded)
    padded[:, :, 8 : 8 + breadth, :] = grad_ref[...]

    def one_tile(tile, carry):
        sums = correlate(
            padded,
            tile,
            lambda down, across: taps_ref[tile, pl.ds(TAPS - 1 - down * KS - across, 1), :],
            height,
            breadth,
        )
        start = pl.multiple_of(tile * LANES, LANES)
        for line in range(height):
            out_ref[0, line, :, pl.ds(start, LANES)] = sums[line].astype(BF16)
        return carry

    lax.fori_loop(0, tiles, one_tile, 0)


def call(kernel, name, outs, scratch, flops, *args):
    moved = sum(math.prod(a.shape) * a.dtype.itemsize for a in args)
    moved += sum(math.prod(o.shape) * o.dtype.itemsize for o in outs)
    return pl.pallas_call(
        kernel,
        out_shape=outs,
        in_specs=[VMEM] * len(args),
        out_specs=[VMEM] * len(outs),
        scratch_shapes=scratch,
        compiler_params=params(),
        cost_estimate=pl.CostEstimate(flops=flops, bytes_accessed=moved, transcendentals=0),
        name=name,
    )(*args)


def body(images, cotangent, depthwise_weight, norm_gain, norm_bias, up_weight):
    shards, reps = lax.axis_size("shard"), lax.axis_size("rep")
    own, hidden = up_weight.shape
    depth = own * shards
    lines = shards // INNER
    half, quarter = hidden // 2, hidden // 4
    height, breadth = images.shape[1:3]
    pixels = height * breadth
    tiles = depth // LANES
    me = lax.axis_index("shard")
    side = lax.axis_index("rep") % 2
    parity = (me // INNER) % 2
    relative = own % 16 == 0

    def over_shard(array, flip):
        return lax.ppermute(array, "shard", [(i, i ^ flip) for i in range(shards)])

    def over_core(array):
        return lax.ppermute(array, "rep", [(i, i ^ 1) for i in range(reps)])

    def true_order(pieces):
        if relative:
            return pieces
        stacked = jnp.stack(pieces).reshape(shards, own, -1)
        flips = jnp.arange(shards) ^ me
        places = (flips % INNER) * lines + flips // INNER
        return list(jnp.take(stacked, places, axis=0).reshape(INNER, lines * own, -1))

    def relative_order(pieces):
        if relative:
            return pieces
        stacked = jnp.concatenate([p.astype(F32) for p in pieces]).reshape(shards, own, -1)
        flips = (jnp.arange(lines)[None, :] * INNER + jnp.arange(INNER)[:, None]).reshape(-1)
        moved = jnp.take(stacked, flips ^ me, axis=0).reshape(INNER, lines * own, -1)
        return [moved[0]] + [moved[i].astype(BF16) for i in range(1, INNER)]

    shape = jax.ShapeDtypeStruct
    near, far = call(
        pack_kernel,
        "pack",
        [shape((own, quarter + LANES), BF16)] * 2,
        [pltpu.VMEM((LANES, LANES), F32), pltpu.VMEM((own, LANES), F32)],
        0,
        up_weight,
        depthwise_weight,
        norm_gain[None, :],
        norm_bias[None, :],
    )
    gathered = [near] + [
        over_shard(far if line % 2 else near, INNER * line) for line in range(1, lines)
    ]
    weight_lines = jnp.concatenate([g[:, :quarter] for g in gathered])
    extra_lines = jnp.concatenate([g[:, quarter:] for g in gathered])
    weights = [weight_lines] + [over_shard(weight_lines, flip) for flip in range(1, INNER)]
    extras = [extra_lines] + [over_shard(extra_lines, flip) for flip in range(1, INNER)]
    weights, extras = true_order(weights), true_order(extras)

    images_far = over_shard(images, INNER)
    cotangent = cotangent.reshape(pixels, hidden)
    cot_sibling = over_core(lax.dynamic_slice(cotangent, (0, (1 - side) * half), (pixels, half)))
    (cot_sent,) = call(
        cot_pack_kernel,
        "cot_pack",
        [shape((2 * pixels, quarter), BF16)],
        [],
        0,
        cotangent,
        cot_sibling,
    )
    cot_far = over_shard(cot_sent, INNER)

    padded = pltpu.VMEM((tiles, height, breadth + 16, LANES), F32)
    conv_flops = 2 * TAPS * pixels * depth
    normed, whitened, inv_std, taps = call(
        functools.partial(conv_norm_kernel, relative, own),
        "conv_norm",
        [
            shape((2 * pixels, depth), BF16),
            shape((pixels, depth), F32),
            shape((pixels, LANES), F32),
            shape((tiles, LANES, LANES), F32),
        ],
        [
            pltpu.VMEM((depth, LANES), F32),
            padded,
            pltpu.VMEM((tiles, pixels, LANES), F32),
        ],
        2 * conv_flops,
        *extras,
        images,
        images_far,
    )
    normed_sibling = over_core(normed)

    rows = lines * own
    *pieces, grad_pre = call(
        functools.partial(project_kernel, relative, own),
        "project",
        [shape((rows, quarter), F32)]
        + [shape((rows, quarter), BF16)] * (INNER - 1)
        + [shape((4 * pixels, quarter), BF16)],
        [
            pltpu.VMEM((depth, quarter), BF16),
            pltpu.VMEM((4 * pixels, depth), BF16),
            pltpu.VMEM((4 * pixels, quarter), BF16),
            pltpu.VMEM((depth, quarter), F32),
        ],
        16 * pixels * depth * quarter,
        *weights,
        normed,
        normed_sibling,
        cotangent,
        cot_sibling,
        cot_far,
    )
    pieces = relative_order(pieces)
    arrived = [over_shard(piece, flip) for flip, piece in enumerate(pieces) if flip]

    gn_kept, gn_sent = call(
        functools.partial(back_project_kernel, relative, own),
        "back_project",
        [shape((2 * pixels, depth), F32)] * 2,
        [pltpu.VMEM((depth, quarter), BF16)],
        8 * pixels * depth * quarter,
        *weights,
        grad_pre,
    )
    gn_kept, gn_sent = call(
        core_sum_kernel,
        "core_sum",
        [shape((pixels, depth), F32), shape((pixels, depth), BF16)],
        [],
        2 * pixels * depth,
        gn_kept,
        over_core(gn_sent),
    )
    gn_other = over_shard(gn_sent, INNER)
    *small, grad_conv = call(
        functools.partial(norm_back_kernel, relative, own),
        "norm_back",
        [shape((rows, LANES), F32)]
        + [shape((rows, LANES), BF16)] * (INNER - 1)
        + [shape((tiles, height, breadth, LANES), F32)],
        [
            padded,
            pltpu.VMEM((tiles, LANES, LANES), F32),
            pltpu.VMEM((depth, LANES), F32),
        ],
        conv_flops,
        gn_kept,
        gn_other,
        whitened,
        inv_std,
        taps,
        images,
    )
    small = relative_order(small)
    small_arrived = [over_shard(piece, flip) for flip, piece in enumerate(small) if flip]
    (grad_images,) = call(
        conv_back_kernel,
        "conv_back",
        [shape(images.shape, BF16)],
        [padded],
        conv_flops,
        grad_conv,
        taps,
    )

    plane = pieces[0] + sum(piece.astype(F32) for piece in arrived)
    small_plane = small[0] + sum(piece.astype(F32) for piece in small_arrived)
    merged = jnp.concatenate([plane, small_plane], axis=1).reshape(lines, own, quarter + LANES)
    merged, grad_images = lax.optimization_barrier((merged, grad_images))
    same, cross = merged[0], None
    for line in range(1, lines):
        came = over_shard(merged[line].astype(BF16), INNER * line).astype(F32)
        if line % 2 == 0:
            same = same + came
        else:
            cross = came if cross is None else cross + came
    total = jnp.concatenate(
        [same[:, :quarter], cross[:, :quarter], same[:, quarter:] + cross[:, quarter:]], axis=1
    )
    if reps > 2:
        groups = [[i for i in range(reps) if i % 2 == s] for s in range(2)]
        total = lax.psum(total, "rep", axis_index_groups=groups)
    other = over_core(total)
    factor = 1.0 / math.sqrt(images.shape[0] * pixels * shards * reps)
    total, other = total * factor, other * factor
    first = jnp.where(side == 0, total, other)
    second = jnp.where(side == 0, other, total)
    grad_up = jnp.concatenate(
        [
            jnp.where(parity == 0, part[:, low : low + quarter], part[:, quarter - low : half - low])
            for part in (first, second)
            for low in (0, quarter)
        ],
        axis=1,
    )
    sums = total[:, half:] + other[:, half:]
    return (grad_images, grad_up, sums[:, :TAPS], sums[:, TAPS], sums[:, TAPS + 1])


def solution(mesh):
    placed = (
        P(("shard", "rep"), None, None, None),
        P(("shard", "rep"), None, None, None),
        P("shard", None),
        P("shard"),
        P("shard"),
        P("shard", None),
    )
    return jax.shard_map(
        body,
        mesh=mesh,
        in_specs=placed,
        out_specs=(
            P(("shard", "rep"), None, None, None),
            P("shard", None),
            P("shard", None),
            P("shard"),
            P("shard"),
        ),
        check_vma=False,
    )
```

```python
import functools
import math

import jax
import jax.numpy as jnp
from jax import lax
from jax.experimental import pallas as pl
from jax.experimental.pallas import tpu as pltpu
from jax.sharding import PartitionSpec as P

KS = 7
TAPS = KS * KS
MARGIN = KS // 2
LANES = 128
INNER = 4
NORM_EPS = 1e-06
BF16 = jnp.bfloat16
F32 = jnp.float32
VMEM = pl.BlockSpec(memory_space=pltpu.VMEM)


def params():
    return pltpu.CompilerParams(vmem_limit_bytes=48 * 1024 * 1024)


def gelu_slope(inputs):
    cumulative = 0.5 * (1.0 + lax.erf(inputs * 0.7071067811865476))
    return cumulative + inputs * jnp.exp(-0.5 * inputs * inputs) * 0.3989422804014327


def block_rows(relative, group, line, own, lines):
    if relative:
        place = lax.axis_index("shard") ^ (line * INNER + group)
        return pl.multiple_of(place * own, 16)
    return (group * lines + line) * own


def place_rows(pieces, target, own, relative, cast=None):
    for group, piece in enumerate(pieces):
        lines = piece.shape[0] // own
        if not relative:
            target[group * piece.shape[0] : (group + 1) * piece.shape[0], :] = (
                piece[...] if cast is None else piece[...].astype(cast)
            )
            continue
        for line in range(lines):
            rows = piece[line * own : (line + 1) * own, :]
            start = block_rows(True, group, line, own, lines)
            target[pl.ds(start, own), :] = rows if cast is None else rows.astype(cast)


def split_rows(source, pieces, own, relative):
    for group, piece in enumerate(pieces):
        lines = piece.shape[0] // own
        if not relative:
            piece[...] = source[group * piece.shape[0] : (group + 1) * piece.shape[0], :].astype(
                piece.dtype
            )
            continue
        for line in range(lines):
            start = block_rows(True, group, line, own, lines)
            piece[line * own : (line + 1) * own, :] = source[pl.ds(start, own), :].astype(
                piece.dtype
            )


def correlate(padded, tile, tap_row, height, breadth):
    sums = [None] * height
    for across in range(KS):
        shifted = padded[tile, :, 8 - MARGIN + across : 8 - MARGIN + across + breadth, :]
        for down in range(KS):
            row = tap_row(down, across)
            for line in range(height):
                origin = line + down - MARGIN
                if 0 <= origin < height:
                    term = shifted[origin] * row
                    sums[line] = term if sums[line] is None else sums[line] + term
    return sums


def pack_kernel(w_hbm, dw_hbm, gain_ref, bias_ref, near_ref, far_ref, w_ref, dw_ref, turned, wide, sems):
    own, hidden = w_ref.shape
    quarter = hidden // 4
    side = lax.axis_index("rep") % 2
    parity = (lax.axis_index("shard") // INNER) % 2
    copies = [
        pltpu.make_async_copy(w_hbm, w_ref, sems.at[0]),
        pltpu.make_async_copy(dw_hbm, dw_ref, sems.at[1]),
    ]
    for copy in copies:
        copy.start()
    turned[...] = jnp.zeros_like(turned)
    turned[TAPS : TAPS + 1, :own] = gain_ref[...].astype(F32)
    turned[TAPS + 1 : TAPS + 2, :own] = bias_ref[...].astype(F32)
    wide[...] = jnp.zeros_like(wide)
    for copy in copies:
        copy.wait()
    wide[:, :TAPS] = dw_ref[...].astype(F32)
    extras = (wide[...] + turned[...].T[:own]).astype(BF16)
    for ref, which in ((near_ref, parity), (far_ref, 1 - parity)):
        start = pl.multiple_of(side * (2 * quarter) + which * quarter, LANES)
        ref[:, :quarter] = w_ref[:, pl.ds(start, quarter)]
        ref[:, quarter:] = extras


def assemble_kernel(*refs):
    pieces, (weight_ref, extra_ref) = refs[:-2], refs[-2:]
    own = pieces[0].shape[0]
    quarter = weight_ref.shape[1]
    for line, piece in enumerate(pieces):
        weight_ref[line * own : (line + 1) * own, :] = piece[:, :quarter]
        extra_ref[line * own : (line + 1) * own, :] = piece[:, quarter:]


def finish_kernel(factor, mine_ref, other_ref, up_ref, dw_ref, gain_ref, bias_ref):
    own, half = mine_ref.shape[0], mine_ref.shape[1] - LANES
    quarter = half // 2
    side = lax.axis_index("rep") % 2
    parity = (lax.axis_index("shard") // INNER) % 2
    for ref, place in ((mine_ref, side), (other_ref, 1 - side)):
        for which, low in ((parity, 0), (1 - parity, quarter)):
            start = pl.multiple_of(place * half + which * quarter, LANES)
            up_ref[:, pl.ds(start, quarter)] = ref[:, low : low + quarter] * factor
    sums = (mine_ref[:, half:] + other_ref[:, half:]) * factor
    dw_ref[...] = sums[:, :TAPS]
    turned = sums.T
    gain_ref[...] = turned[TAPS : TAPS + 1, :]
    bias_ref[...] = turned[TAPS + 1 : TAPS + 2, :]


def conv_norm_kernel(relative, own, *refs):
    small = refs[:INNER]
    sources = refs[INNER : INNER + 4]
    x_ref = sources[0]
    normed_ref, white_ref, inv_ref, taps_ref, gathered, padded, conv = refs[INNER + 4 :]
    height, breadth, depth = x_ref.shape[1:]
    tiles = depth // LANES
    pixels = height * breadth
    place_rows(small, gathered, own, relative, F32)
    padded[...] = jnp.zeros_like(padded)
    for tile in range(tiles):
        lanes = slice(tile * LANES, (tile + 1) * LANES)
        taps_ref[tile] = gathered[lanes, :].T

    for image, source in enumerate(sources):
        for tile in range(tiles):
            lanes = slice(tile * LANES, (tile + 1) * LANES)
            padded[tile, :, 8 : 8 + breadth, :] = source[0, :, :, lanes].astype(F32)

        def one_tile(tile, carry):
            sums = correlate(
                padded,
                tile,
                lambda down, across: taps_ref[tile, pl.ds(down * KS + across, 1), :],
                height,
                breadth,
            )
            for line in range(height):
                conv[tile, line * breadth : (line + 1) * breadth, :] = sums[line]
            return carry

        lax.fori_loop(0, tiles, one_tile, 0)
        total = conv[0]
        for tile in range(1, tiles):
            total = total + conv[tile]
        average = jnp.sum(total, axis=-1, keepdims=True) / depth
        squares = None
        for tile in range(tiles):
            centered = conv[tile] - average
            squares = centered * centered if squares is None else squares + centered * centered
        variance = jnp.sum(squares, axis=-1, keepdims=True) / depth
        inv_std = lax.rsqrt(variance + NORM_EPS)
        if image == 0:
            inv_ref[...] = jnp.broadcast_to(inv_std, (pixels, LANES))
        for tile in range(tiles):
            lanes = slice(tile * LANES, (tile + 1) * LANES)
            whitened = (conv[tile] - average) * inv_std
            if image == 0:
                white_ref[:, lanes] = whitened
            gain = taps_ref[tile, TAPS : TAPS + 1, :]
            bias = taps_ref[tile, TAPS + 1 : TAPS + 2, :]
            normed_ref[image * pixels : (image + 1) * pixels, lanes] = (
                whitened * gain + bias
            ).astype(BF16)


def cot_pack_kernel(cot_ref, sibling_ref, out_ref):
    pixels, half = sibling_ref.shape
    quarter = half // 2
    side = lax.axis_index("rep") % 2
    parity = (lax.axis_index("shard") // INNER) % 2
    start = pl.multiple_of(side * half + (1 - parity) * quarter, LANES)
    out_ref[:pixels, :] = cot_ref[:, pl.ds(start, quarter)]
    start = pl.multiple_of((1 - parity) * quarter, LANES)
    out_ref[pixels:, :] = sibling_ref[:, pl.ds(start, quarter)]


def project_kernel(relative, own, *refs):
    weights = refs[:INNER]
    normed, cot_ref, sibling_ref, far_ref = refs[INNER : INNER + 4]
    pieces = refs[INNER + 4 : 2 * INNER + 4]
    gp_ref, weight, cot, grad = refs[2 * INNER + 4 :]
    pixels, half = sibling_ref.shape
    quarter = half // 2
    side = lax.axis_index("rep") % 2
    parity = (lax.axis_index("shard") // INNER) % 2
    place_rows(weights, weight, own, relative)
    start = pl.multiple_of(side * half + parity * quarter, LANES)
    cot[:pixels, :] = cot_ref[:, pl.ds(start, quarter)]
    cot[pixels : 2 * pixels, :] = far_ref[:pixels, :]
    start = pl.multiple_of(parity * quarter, LANES)
    cot[2 * pixels : 3 * pixels, :] = sibling_ref[:, pl.ds(start, quarter)]
    cot[3 * pixels :, :] = far_ref[pixels:, :]
    for start in range(0, quarter, LANES):
        columns = slice(start, start + LANES)
        pre_act = jnp.dot(normed[...], weight[:, columns], preferred_element_type=F32)
        gp_ref[:, columns] = (cot[:, columns].astype(F32) * gelu_slope(pre_act)).astype(BF16)
    grad[...] = lax.dot_general(
        normed[...], gp_ref[...], (((0,), (0,)), ((), ())), preferred_element_type=F32
    )
    split_rows(grad, pieces, own, relative)


def back_project_kernel(relative, own, *refs):
    weights = refs[:INNER]
    gp_ref, own_ref, other_ref, weight = refs[INNER:]
    rows = own_ref.shape[0]
    place_rows(weights, weight, own, relative)
    grad_normed = lax.dot_general(
        gp_ref[...], weight[...], (((1,), (1,)), ((), ())), preferred_element_type=F32
    )
    own_ref[...] = grad_normed[:rows]
    other_ref[...] = grad_normed[rows:]


def core_sum_kernel(own_ref, other_ref, kept_ref, sent_ref):
    pixels = kept_ref.shape[0]
    kept_ref[...] = own_ref[:pixels] + other_ref[:pixels]
    sent_ref[...] = (own_ref[pixels:] + other_ref[pixels:]).astype(BF16)


def norm_back_kernel(relative, own, *refs):
    gn_own, gn_other, white_ref, inv_ref, taps_ref, x_ref = refs[:6]
    pieces = refs[6 : 6 + INNER]
    grad_ref, padded, rows, small = refs[6 + INNER :]
    height, breadth, depth = x_ref.shape[1:]
    tiles = depth // LANES
    pixels = height * breadth
    padded[...] = jnp.zeros_like(padded)
    rows[...] = jnp.zeros_like(rows)
    first = None
    second = None
    for tile in range(tiles):
        lanes = slice(tile * LANES, (tile + 1) * LANES)
        padded[tile, :, 8 : 8 + breadth, :] = x_ref[0, :, :, lanes].astype(F32)
        grad_normed = gn_own[:, lanes] + gn_other[:, lanes].astype(F32)
        whitened = white_ref[:, lanes]
        product = grad_normed * whitened
        gain = taps_ref[tile, TAPS : TAPS + 1, :]
        rows[tile, TAPS : TAPS + 1, :] = jnp.sum(product, axis=0, keepdims=True)
        rows[tile, TAPS + 1 : TAPS + 2, :] = jnp.sum(grad_normed, axis=0, keepdims=True)
        one, two = grad_normed * gain, product * gain
        first = one if first is None else first + one
        second = two if second is None else second + two
    mean_first = jnp.sum(first, axis=-1, keepdims=True) / depth
    mean_second = jnp.sum(second, axis=-1, keepdims=True) / depth
    for tile in range(tiles):
        lanes = slice(tile * LANES, (tile + 1) * LANES)
        gain = taps_ref[tile, TAPS : TAPS + 1, :]
        grad_white = (gn_own[:, lanes] + gn_other[:, lanes].astype(F32)) * gain
        grad_conv = inv_ref[...] * (grad_white - mean_first - white_ref[:, lanes] * mean_second)
        grad_ref[tile] = grad_conv.reshape(height, breadth, LANES)

    def one_tile(tile, carry):
        grads = [grad_ref[tile, line] for line in range(height)]
        for across in range(KS):
            shifted = padded[tile, :, 8 - MARGIN + across : 8 - MARGIN + across + breadth, :]
            for down in range(KS):
                total = None
                for line in range(height):
                    origin = line + down - MARGIN
                    if 0 <= origin < height:
                        term = grads[line] * shifted[origin]
                        total = term if total is None else total + term
                rows[tile, pl.ds(down * KS + across, 1), :] = jnp.sum(total, axis=0, keepdims=True)
        return carry

    lax.fori_loop(0, tiles, one_tile, 0)
    for tile in range(tiles):
        small[tile * LANES : (tile + 1) * LANES, :] = rows[tile].T
    split_rows(small, pieces, own, relative)


def conv_back_kernel(grad_ref, taps_ref, out_ref, padded):
    tiles, height, breadth, _ = grad_ref.shape
    padded[...] = jnp.zeros_like(padded)
    padded[:, :, 8 : 8 + breadth, :] = grad_ref[...]

    def one_tile(tile, carry):
        sums = correlate(
            padded,
            tile,
            lambda down, across: taps_ref[tile, pl.ds(TAPS - 1 - down * KS - across, 1), :],
            height,
            breadth,
        )
        start = pl.multiple_of(tile * LANES, LANES)
        for line in range(height):
            out_ref[0, line, :, pl.ds(start, LANES)] = sums[line].astype(BF16)
        return carry

    lax.fori_loop(0, tiles, one_tile, 0)


def call(kernel, name, outs, scratch, micros, *args, in_specs=None):
    flops = int(micros * 1.1e9)
    moved = sum(math.prod(a.shape) * a.dtype.itemsize for a in args)
    moved += sum(math.prod(o.shape) * o.dtype.itemsize for o in outs)
    return pl.pallas_call(
        kernel,
        out_shape=outs,
        in_specs=in_specs or [VMEM] * len(args),
        out_specs=[VMEM] * len(outs),
        scratch_shapes=scratch,
        compiler_params=params(),
        cost_estimate=pl.CostEstimate(flops=flops, bytes_accessed=moved, transcendentals=0),
        name=name,
    )(*args)


def body(images, cotangent, depthwise_weight, norm_gain, norm_bias, up_weight):
    shards, reps = lax.axis_size("shard"), lax.axis_size("rep")
    own, hidden = up_weight.shape
    depth = own * shards
    lines = shards // INNER
    half, quarter = hidden // 2, hidden // 4
    height, breadth = images.shape[1:3]
    pixels = height * breadth
    tiles = depth // LANES
    me = lax.axis_index("shard")
    side = lax.axis_index("rep") % 2
    parity = (me // INNER) % 2
    relative = own % 16 == 0

    def over_shard(array, flip):
        return lax.ppermute(array, "shard", [(i, i ^ flip) for i in range(shards)])

    def over_core(array):
        return lax.ppermute(array, "rep", [(i, i ^ 1) for i in range(reps)])

    def true_order(pieces):
        if relative:
            return pieces
        stacked = jnp.stack(pieces).reshape(shards, own, -1)
        flips = jnp.arange(shards) ^ me
        places = (flips % INNER) * lines + flips // INNER
        return list(jnp.take(stacked, places, axis=0).reshape(INNER, lines * own, -1))

    def relative_order(pieces):
        if relative:
            return pieces
        stacked = jnp.concatenate([p.astype(F32) for p in pieces]).reshape(shards, own, -1)
        flips = (jnp.arange(lines)[None, :] * INNER + jnp.arange(INNER)[:, None]).reshape(-1)
        moved = jnp.take(stacked, flips ^ me, axis=0).reshape(INNER, lines * own, -1)
        return [moved[0]] + [moved[i].astype(BF16) for i in range(1, INNER)]

    shape = jax.ShapeDtypeStruct
    near, far = call(
        pack_kernel,
        "pack",
        [shape((own, quarter + LANES), BF16)] * 2,
        [
            pltpu.VMEM(up_weight.shape, BF16),
            pltpu.VMEM(depthwise_weight.shape, BF16),
            pltpu.VMEM((LANES, LANES), F32),
            pltpu.VMEM((own, LANES), F32),
            pltpu.SemaphoreType.DMA((2,)),
        ],
        0.5,
        up_weight,
        depthwise_weight,
        norm_gain[None, :],
        norm_bias[None, :],
        in_specs=[pl.BlockSpec(memory_space=pl.ANY)] * 2 + [VMEM] * 2,
    )
    gathered = [near] + [
        over_shard(far if line % 2 else near, INNER * line) for line in range(1, lines)
    ]
    rows = lines * own
    weight_lines, extra_lines = call(
        assemble_kernel,
        "assemble",
        [shape((rows, quarter), BF16), shape((rows, LANES), BF16)],
        [],
        0.3,
        *gathered,
    )
    weights = [weight_lines] + [over_shard(weight_lines, flip) for flip in range(1, INNER)]
    extras = [extra_lines] + [over_shard(extra_lines, flip) for flip in range(1, INNER)]
    weights, extras = true_order(weights), true_order(extras)

    images_far = over_shard(images, INNER)
    images_sibling, images_corner = over_core(images), over_core(images_far)
    cotangent = cotangent.reshape(pixels, hidden)
    cot_sibling = over_core(lax.dynamic_slice(cotangent, (0, (1 - side) * half), (pixels, half)))
    (cot_sent,) = call(
        cot_pack_kernel,
        "cot_pack",
        [shape((2 * pixels, quarter), BF16)],
        [],
        0.5,
        cotangent,
        cot_sibling,
    )
    cot_far = over_shard(cot_sent, INNER)

    padded = pltpu.VMEM((tiles, height, breadth + 16, LANES), F32)
    normed, whitened, inv_std, taps = call(
        functools.partial(conv_norm_kernel, relative, own),
        "conv_norm",
        [
            shape((4 * pixels, depth), BF16),
            shape((pixels, depth), F32),
            shape((pixels, LANES), F32),
            shape((tiles, LANES, LANES), F32),
        ],
        [
            pltpu.VMEM((depth, LANES), F32),
            padded,
            pltpu.VMEM((tiles, pixels, LANES), F32),
        ],
        0.1,
        *extras,
        images,
        images_far,
        images_sibling,
        images_corner,
    )

    *pieces, grad_pre = call(
        functools.partial(project_kernel, relative, own),
        "project",
        [shape((rows, quarter), F32)]
        + [shape((rows, quarter), BF16)] * (INNER - 1)
        + [shape((4 * pixels, quarter), BF16)],
        [
            pltpu.VMEM((depth, quarter), BF16),
            pltpu.VMEM((4 * pixels, quarter), BF16),
            pltpu.VMEM((depth, quarter), F32),
        ],
        1.6,
        *weights,
        normed,
        cotangent,
        cot_sibling,
        cot_far,
    )
    pieces = relative_order(pieces)
    arrived = [over_shard(piece, flip) for flip, piece in enumerate(pieces) if flip]

    gn_kept, gn_sent = call(
        functools.partial(back_project_kernel, relative, own),
        "back_project",
        [shape((2 * pixels, depth), F32)] * 2,
        [pltpu.VMEM((depth, quarter), BF16)],
        0.7,
        *weights,
        grad_pre,
    )
    gn_kept, gn_sent = call(
        core_sum_kernel,
        "core_sum",
        [shape((pixels, depth), F32), shape((pixels, depth), BF16)],
        [],
        0.4,
        gn_kept,
        over_core(gn_sent),
    )
    gn_other = over_shard(gn_sent, INNER)
    *small, grad_conv = call(
        functools.partial(norm_back_kernel, relative, own),
        "norm_back",
        [shape((rows, LANES), F32)]
        + [shape((rows, LANES), BF16)] * (INNER - 1)
        + [shape((tiles, height, breadth, LANES), F32)],
        [
            padded,
            pltpu.VMEM((tiles, LANES, LANES), F32),
            pltpu.VMEM((depth, LANES), F32),
        ],
        1.7,
        gn_kept,
        gn_other,
        whitened,
        inv_std,
        taps,
        images,
    )
    small = relative_order(small)
    small_arrived = [over_shard(piece, flip) for flip, piece in enumerate(small) if flip]
    (grad_images,) = call(
        conv_back_kernel,
        "conv_back",
        [shape(images.shape, BF16)],
        [padded],
        1.9,
        grad_conv,
        taps,
    )

    plane = pieces[0] + sum(piece.astype(F32) for piece in arrived)
    small_plane = small[0] + sum(piece.astype(F32) for piece in small_arrived)
    merged = jnp.concatenate([plane, small_plane], axis=1).reshape(lines, own, quarter + LANES)
    merged, grad_images = lax.optimization_barrier((merged, grad_images))
    same, cross = merged[0], None
    for line in range(1, lines):
        came = over_shard(merged[line].astype(BF16), INNER * line).astype(F32)
        if line % 2 == 0:
            same = same + came
        else:
            cross = came if cross is None else cross + came
    total = jnp.concatenate(
        [same[:, :quarter], cross[:, :quarter], same[:, quarter:] + cross[:, quarter:]], axis=1
    )
    if reps > 2:
        groups = [[i for i in range(reps) if i % 2 == s] for s in range(2)]
        total = lax.psum(total, "rep", axis_index_groups=groups)
    other = over_core(total)
    factor = 1.0 / math.sqrt(images.shape[0] * pixels * shards * reps)
    grad_up, grad_depthwise, grad_gain, grad_bias = call(
        functools.partial(finish_kernel, factor),
        "finish",
        [
            shape((own, hidden), F32),
            shape((own, TAPS), F32),
            shape((1, own), F32),
            shape((1, own), F32),
        ],
        [],
        0.5,
        total,
        other,
    )
    return (grad_images, grad_up, grad_depthwise, grad_gain[0], grad_bias[0])


def solution(mesh):
    placed = (
        P(("shard", "rep"), None, None, None),
        P(("shard", "rep"), None, None, None),
        P("shard", None),
        P("shard"),
        P("shard"),
        P("shard", None),
    )
    return jax.shard_map(
        body,
        mesh=mesh,
        in_specs=placed,
        out_specs=(
            P(("shard", "rep"), None, None, None),
            P("shard", None),
            P("shard", None),
            P("shard"),
            P("shard"),
        ),
        check_vma=False,
    )
```

```python
import functools
import math

import jax
import jax.numpy as jnp
from jax import lax
from jax.experimental import pallas as pl
from jax.experimental.pallas import tpu as pltpu
from jax.sharding import PartitionSpec as P

KS = 7
TAPS = KS * KS
MARGIN = KS // 2
LANES = 128
INNER = 4
NORM_EPS = 1e-06
BF16 = jnp.bfloat16
F32 = jnp.float32
VMEM = pl.BlockSpec(memory_space=pltpu.VMEM)


def params():
    return pltpu.CompilerParams(vmem_limit_bytes=48 * 1024 * 1024)


def gelu_slope(inputs):
    cumulative = 0.5 * (1.0 + lax.erf(inputs * 0.7071067811865476))
    return cumulative + inputs * jnp.exp(-0.5 * inputs * inputs) * 0.3989422804014327


def block_rows(relative, group, line, own, lines):
    if relative:
        place = lax.axis_index("shard") ^ (line * INNER + group)
        return pl.multiple_of(place * own, 16)
    return (group * lines + line) * own


def place_rows(pieces, target, own, relative, cast=None):
    for group, piece in enumerate(pieces):
        lines = piece.shape[0] // own
        if not relative:
            target[group * piece.shape[0] : (group + 1) * piece.shape[0], :] = (
                piece[...] if cast is None else piece[...].astype(cast)
            )
            continue
        for line in range(lines):
            rows = piece[line * own : (line + 1) * own, :]
            start = block_rows(True, group, line, own, lines)
            target[pl.ds(start, own), :] = rows if cast is None else rows.astype(cast)


def split_rows(source, pieces, own, relative):
    for group, piece in enumerate(pieces):
        lines = piece.shape[0] // own
        if not relative:
            piece[...] = source[group * piece.shape[0] : (group + 1) * piece.shape[0], :].astype(
                piece.dtype
            )
            continue
        for line in range(lines):
            start = block_rows(True, group, line, own, lines)
            piece[line * own : (line + 1) * own, :] = source[pl.ds(start, own), :].astype(
                piece.dtype
            )


def correlate(padded, tile, tap_row, height, breadth):
    sums = [None] * height
    for across in range(KS):
        shifted = padded[tile, :, 8 - MARGIN + across : 8 - MARGIN + across + breadth, :]
        for down in range(KS):
            row = tap_row(down, across)
            for line in range(height):
                origin = line + down - MARGIN
                if 0 <= origin < height:
                    term = shifted[origin] * row
                    sums[line] = term if sums[line] is None else sums[line] + term
    return sums


def pack_kernel(w_hbm, dw_hbm, gain_ref, bias_ref, near_ref, far_ref, w_ref, dw_ref, turned, wide, sems):
    own, hidden = w_ref.shape
    quarter = hidden // 4
    side = lax.axis_index("rep") % 2
    parity = (lax.axis_index("shard") // INNER) % 2
    copies = [
        pltpu.make_async_copy(w_hbm, w_ref, sems.at[0]),
        pltpu.make_async_copy(dw_hbm, dw_ref, sems.at[1]),
    ]
    for copy in copies:
        copy.start()
    turned[...] = jnp.zeros_like(turned)
    turned[TAPS : TAPS + 1, :own] = gain_ref[...].astype(F32)
    turned[TAPS + 1 : TAPS + 2, :own] = bias_ref[...].astype(F32)
    wide[...] = jnp.zeros_like(wide)
    for copy in copies:
        copy.wait()
    wide[:, :TAPS] = dw_ref[...].astype(F32)
    extras = (wide[...] + turned[...].T[:own]).astype(BF16)
    for ref, which in ((near_ref, parity), (far_ref, 1 - parity)):
        start = pl.multiple_of(side * (2 * quarter) + which * quarter, LANES)
        ref[:, :quarter] = w_ref[:, pl.ds(start, quarter)]
        ref[:, quarter:] = extras


def assemble_kernel(*refs):
    pieces, (weight_ref, extra_ref) = refs[:-2], refs[-2:]
    own = pieces[0].shape[0]
    quarter = weight_ref.shape[1]
    for line, piece in enumerate(pieces):
        weight_ref[line * own : (line + 1) * own, :] = piece[:, :quarter]
        extra_ref[line * own : (line + 1) * own, :] = piece[:, quarter:]


def line_sum_kernel(*refs):
    pieces, total_ref = refs[:-1], refs[-1]
    quarter = pieces[0].shape[1] - LANES
    same, cross = pieces[0][...], None
    for line, piece in enumerate(pieces):
        if line % 2:
            cross = piece[...].astype(F32) if cross is None else cross + piece[...].astype(F32)
        elif line:
            same = same + piece[...].astype(F32)
    total_ref[:, :quarter] = same[:, :quarter]
    total_ref[:, quarter : 2 * quarter] = cross[:, :quarter]
    total_ref[:, 2 * quarter :] = same[:, quarter:] + cross[:, quarter:]


def finish_kernel(factor, mine_ref, other_ref, up_ref, dw_ref, gain_ref, bias_ref):
    own, half = mine_ref.shape[0], mine_ref.shape[1] - LANES
    quarter = half // 2
    side = lax.axis_index("rep") % 2
    parity = (lax.axis_index("shard") // INNER) % 2
    for ref, place in ((mine_ref, side), (other_ref, 1 - side)):
        for which, low in ((parity, 0), (1 - parity, quarter)):
            start = pl.multiple_of(place * half + which * quarter, LANES)
            up_ref[:, pl.ds(start, quarter)] = ref[:, low : low + quarter] * factor
    sums = (mine_ref[:, half:] + other_ref[:, half:]) * factor
    dw_ref[...] = sums[:, :TAPS]
    turned = sums.T
    gain_ref[...] = turned[TAPS : TAPS + 1, :]
    bias_ref[...] = turned[TAPS + 1 : TAPS + 2, :]


def conv_norm_kernel(relative, own, *refs):
    small = refs[:INNER]
    sources = refs[INNER : INNER + 4]
    x_ref = sources[0]
    normed_ref, white_ref, inv_ref, taps_ref, gathered, padded, conv = refs[INNER + 4 :]
    height, breadth, depth = x_ref.shape[1:]
    tiles = depth // LANES
    pixels = height * breadth
    place_rows(small, gathered, own, relative, F32)
    padded[...] = jnp.zeros_like(padded)
    for tile in range(tiles):
        lanes = slice(tile * LANES, (tile + 1) * LANES)
        taps_ref[tile] = gathered[lanes, :].T

    for image, source in enumerate(sources):
        for tile in range(tiles):
            lanes = slice(tile * LANES, (tile + 1) * LANES)
            padded[tile, :, 8 : 8 + breadth, :] = source[0, :, :, lanes].astype(F32)

        def one_tile(tile, carry):
            sums = correlate(
                padded,
                tile,
                lambda down, across: taps_ref[tile, pl.ds(down * KS + across, 1), :],
                height,
                breadth,
            )
            for line in range(height):
                conv[tile, line * breadth : (line + 1) * breadth, :] = sums[line]
            return carry

        lax.fori_loop(0, tiles, one_tile, 0)
        total = conv[0]
        for tile in range(1, tiles):
            total = total + conv[tile]
        average = jnp.sum(total, axis=-1, keepdims=True) / depth
        squares = None
        for tile in range(tiles):
            centered = conv[tile] - average
            squares = centered * centered if squares is None else squares + centered * centered
        variance = jnp.sum(squares, axis=-1, keepdims=True) / depth
        inv_std = lax.rsqrt(variance + NORM_EPS)
        if image == 0:
            inv_ref[...] = jnp.broadcast_to(inv_std, (pixels, LANES))
        for tile in range(tiles):
            lanes = slice(tile * LANES, (tile + 1) * LANES)
            whitened = (conv[tile] - average) * inv_std
            if image == 0:
                white_ref[:, lanes] = whitened
            gain = taps_ref[tile, TAPS : TAPS + 1, :]
            bias = taps_ref[tile, TAPS + 1 : TAPS + 2, :]
            normed_ref[image * pixels : (image + 1) * pixels, lanes] = (
                whitened * gain + bias
            ).astype(BF16)


def cot_pack_kernel(cot_ref, across_ref, sibling_ref):
    half = sibling_ref.shape[1]
    quarter = half // 2
    side = lax.axis_index("rep") % 2
    parity = (lax.axis_index("shard") // INNER) % 2
    for place in range(2):
        start = pl.multiple_of(place * half + (1 - parity) * quarter, LANES)
        across_ref[:, place * quarter : (place + 1) * quarter] = cot_ref[:, pl.ds(start, quarter)]
    sibling_ref[...] = cot_ref[:, pl.ds(pl.multiple_of((1 - side) * half, LANES), half)]


def project_kernel(relative, own, *refs):
    weights = refs[:INNER]
    normed, cot_ref, sibling_ref, across_ref, corner_ref = refs[INNER : INNER + 5]
    pieces = refs[INNER + 5 : 2 * INNER + 5]
    gp_ref, weight, cot, grad = refs[2 * INNER + 5 :]
    pixels, half = sibling_ref.shape
    quarter = half // 2
    side = lax.axis_index("rep") % 2
    parity = (lax.axis_index("shard") // INNER) % 2
    place_rows(weights, weight, own, relative)
    start = pl.multiple_of(side * half + parity * quarter, LANES)
    cot[:pixels, :] = cot_ref[:, pl.ds(start, quarter)]
    start = pl.multiple_of(side * quarter, LANES)
    cot[pixels : 2 * pixels, :] = across_ref[:, pl.ds(start, quarter)]
    start = pl.multiple_of(parity * quarter, LANES)
    cot[2 * pixels : 3 * pixels, :] = sibling_ref[:, pl.ds(start, quarter)]
    start = pl.multiple_of(side * quarter, LANES)
    cot[3 * pixels :, :] = corner_ref[:, pl.ds(start, quarter)]
    for start in range(0, quarter, LANES):
        columns = slice(start, start + LANES)
        pre_act = jnp.dot(normed[...], weight[:, columns], preferred_element_type=F32)
        gp_ref[:, columns] = (cot[:, columns].astype(F32) * gelu_slope(pre_act)).astype(BF16)
    grad[...] = lax.dot_general(
        normed[...], gp_ref[...], (((0,), (0,)), ((), ())), preferred_element_type=F32
    )
    split_rows(grad, pieces, own, relative)


def back_project_kernel(relative, own, *refs):
    weights = refs[:INNER]
    gp_ref, own_ref, other_ref, weight = refs[INNER:]
    rows = own_ref.shape[0]
    place_rows(weights, weight, own, relative)
    grad_normed = lax.dot_general(
        gp_ref[...], weight[...], (((1,), (1,)), ((), ())), preferred_element_type=F32
    )
    own_ref[...] = grad_normed[:rows]
    other_ref[...] = grad_normed[rows:]


def core_sum_kernel(own_ref, other_ref, kept_ref, sent_ref):
    pixels = kept_ref.shape[0]
    kept_ref[...] = own_ref[:pixels] + other_ref[:pixels]
    sent_ref[...] = (own_ref[pixels:] + other_ref[pixels:]).astype(BF16)


def norm_back_kernel(relative, own, *refs):
    gn_own, gn_other, white_ref, inv_ref, taps_ref, x_ref = refs[:6]
    pieces = refs[6 : 6 + INNER]
    grad_ref, padded, rows, small = refs[6 + INNER :]
    height, breadth, depth = x_ref.shape[1:]
    tiles = depth // LANES
    pixels = height * breadth
    padded[...] = jnp.zeros_like(padded)
    rows[...] = jnp.zeros_like(rows)
    first = None
    second = None
    for tile in range(tiles):
        lanes = slice(tile * LANES, (tile + 1) * LANES)
        padded[tile, :, 8 : 8 + breadth, :] = x_ref[0, :, :, lanes].astype(F32)
        grad_normed = gn_own[:, lanes] + gn_other[:, lanes].astype(F32)
        whitened = white_ref[:, lanes]
        product = grad_normed * whitened
        gain = taps_ref[tile, TAPS : TAPS + 1, :]
        rows[tile, TAPS : TAPS + 1, :] = jnp.sum(product, axis=0, keepdims=True)
        rows[tile, TAPS + 1 : TAPS + 2, :] = jnp.sum(grad_normed, axis=0, keepdims=True)
        one, two = grad_normed * gain, product * gain
        first = one if first is None else first + one
        second = two if second is None else second + two
    mean_first = jnp.sum(first, axis=-1, keepdims=True) / depth
    mean_second = jnp.sum(second, axis=-1, keepdims=True) / depth
    for tile in range(tiles):
        lanes = slice(tile * LANES, (tile + 1) * LANES)
        gain = taps_ref[tile, TAPS : TAPS + 1, :]
        grad_white = (gn_own[:, lanes] + gn_other[:, lanes].astype(F32)) * gain
        grad_conv = inv_ref[...] * (grad_white - mean_first - white_ref[:, lanes] * mean_second)
        grad_ref[tile] = grad_conv.reshape(height, breadth, LANES)

    def one_tile(tile, carry):
        grads = [grad_ref[tile, line] for line in range(height)]
        for across in range(KS):
            shifted = padded[tile, :, 8 - MARGIN + across : 8 - MARGIN + across + breadth, :]
            for down in range(KS):
                total = None
                for line in range(height):
                    origin = line + down - MARGIN
                    if 0 <= origin < height:
                        term = grads[line] * shifted[origin]
                        total = term if total is None else total + term
                rows[tile, pl.ds(down * KS + across, 1), :] = jnp.sum(total, axis=0, keepdims=True)
        return carry

    lax.fori_loop(0, tiles, one_tile, 0)
    for tile in range(tiles):
        small[tile * LANES : (tile + 1) * LANES, :] = rows[tile].T
    split_rows(small, pieces, own, relative)


def conv_back_kernel(grad_ref, taps_ref, out_ref, padded):
    tiles, height, breadth, _ = grad_ref.shape
    padded[...] = jnp.zeros_like(padded)
    padded[:, :, 8 : 8 + breadth, :] = grad_ref[...]

    def one_tile(tile, carry):
        sums = correlate(
            padded,
            tile,
            lambda down, across: taps_ref[tile, pl.ds(TAPS - 1 - down * KS - across, 1), :],
            height,
            breadth,
        )
        start = pl.multiple_of(tile * LANES, LANES)
        for line in range(height):
            out_ref[0, line, :, pl.ds(start, LANES)] = sums[line].astype(BF16)
        return carry

    lax.fori_loop(0, tiles, one_tile, 0)


def call(kernel, name, outs, scratch, micros, *args, in_specs=None):
    flops = int(micros * 1.1e9)
    moved = sum(math.prod(a.shape) * a.dtype.itemsize for a in args)
    moved += sum(math.prod(o.shape) * o.dtype.itemsize for o in outs)
    return pl.pallas_call(
        kernel,
        out_shape=outs,
        in_specs=in_specs or [VMEM] * len(args),
        out_specs=[VMEM] * len(outs),
        scratch_shapes=scratch,
        compiler_params=params(),
        cost_estimate=pl.CostEstimate(flops=flops, bytes_accessed=moved, transcendentals=0),
        name=name,
    )(*args)


def body(images, cotangent, depthwise_weight, norm_gain, norm_bias, up_weight):
    shards, reps = lax.axis_size("shard"), lax.axis_size("rep")
    own, hidden = up_weight.shape
    depth = own * shards
    lines = shards // INNER
    half, quarter = hidden // 2, hidden // 4
    height, breadth = images.shape[1:3]
    pixels = height * breadth
    tiles = depth // LANES
    me = lax.axis_index("shard")
    side = lax.axis_index("rep") % 2
    parity = (me // INNER) % 2
    relative = own % 16 == 0

    def over_shard(array, flip):
        return lax.ppermute(array, "shard", [(i, i ^ flip) for i in range(shards)])

    def over_core(array):
        return lax.ppermute(array, "rep", [(i, i ^ 1) for i in range(reps)])

    def true_order(pieces):
        if relative:
            return pieces
        stacked = jnp.stack(pieces).reshape(shards, own, -1)
        flips = jnp.arange(shards) ^ me
        places = (flips % INNER) * lines + flips // INNER
        return list(jnp.take(stacked, places, axis=0).reshape(INNER, lines * own, -1))

    def relative_order(pieces):
        if relative:
            return pieces
        stacked = jnp.concatenate([p.astype(F32) for p in pieces]).reshape(shards, own, -1)
        flips = (jnp.arange(lines)[None, :] * INNER + jnp.arange(INNER)[:, None]).reshape(-1)
        moved = jnp.take(stacked, flips ^ me, axis=0).reshape(INNER, lines * own, -1)
        return [moved[0]] + [moved[i].astype(BF16) for i in range(1, INNER)]

    shape = jax.ShapeDtypeStruct
    near, far = call(
        pack_kernel,
        "pack",
        [shape((own, quarter + LANES), BF16)] * 2,
        [
            pltpu.VMEM(up_weight.shape, BF16),
            pltpu.VMEM(depthwise_weight.shape, BF16),
            pltpu.VMEM((LANES, LANES), F32),
            pltpu.VMEM((own, LANES), F32),
            pltpu.SemaphoreType.DMA((2,)),
        ],
        0.5,
        up_weight,
        depthwise_weight,
        norm_gain[None, :],
        norm_bias[None, :],
        in_specs=[pl.BlockSpec(memory_space=pl.ANY)] * 2 + [VMEM] * 2,
    )
    near, far, images, cotangent = lax.optimization_barrier((near, far, images, cotangent))
    gathered = [near] + [
        over_shard(far if line % 2 else near, INNER * line) for line in range(1, lines)
    ]
    cotangent = cotangent.reshape(pixels, hidden)
    cot_across, cot_sibling = call(
        cot_pack_kernel,
        "cot_pack",
        [shape((pixels, half), BF16)] * 2,
        [],
        0.4,
        cotangent,
    )
    cot_across, cot_sibling = over_shard(cot_across, INNER), over_core(cot_sibling)
    images_far, images_sibling = over_shard(images, INNER), over_core(images)

    rows = lines * own
    weight_lines, extra_lines = call(
        assemble_kernel,
        "assemble",
        [shape((rows, quarter), BF16), shape((rows, LANES), BF16)],
        [],
        2.0,
        *gathered,
    )
    weights = [weight_lines] + [over_shard(weight_lines, flip) for flip in range(1, INNER)]
    extras = [extra_lines] + [over_shard(extra_lines, flip) for flip in range(1, INNER)]
    *extras, cot_across, images_far = lax.optimization_barrier((*extras, cot_across, images_far))
    cot_corner, images_corner = over_core(cot_across), over_core(images_far)
    weights, extras = true_order(weights), true_order(extras)

    padded = pltpu.VMEM((tiles, height, breadth + 16, LANES), F32)
    normed, whitened, inv_std, taps = call(
        functools.partial(conv_norm_kernel, relative, own),
        "conv_norm",
        [
            shape((4 * pixels, depth), BF16),
            shape((pixels, depth), F32),
            shape((pixels, LANES), F32),
            shape((tiles, LANES, LANES), F32),
        ],
        [
            pltpu.VMEM((depth, LANES), F32),
            padded,
            pltpu.VMEM((tiles, pixels, LANES), F32),
        ],
        0.1,
        *extras,
        images,
        images_far,
        images_sibling,
        images_corner,
    )

    *pieces, grad_pre = call(
        functools.partial(project_kernel, relative, own),
        "project",
        [shape((rows, quarter), F32)]
        + [shape((rows, quarter), BF16)] * (INNER - 1)
        + [shape((4 * pixels, quarter), BF16)],
        [
            pltpu.VMEM((depth, quarter), BF16),
            pltpu.VMEM((4 * pixels, quarter), BF16),
            pltpu.VMEM((depth, quarter), F32),
        ],
        1.6,
        *weights,
        normed,
        cotangent,
        cot_sibling,
        cot_across,
        cot_corner,
    )
    gn_kept, gn_sent = call(
        functools.partial(back_project_kernel, relative, own),
        "back_project",
        [shape((2 * pixels, depth), F32)] * 2,
        [pltpu.VMEM((depth, quarter), BF16)],
        0.7,
        *weights,
        grad_pre,
    )
    gn_kept, gn_sent = call(
        core_sum_kernel,
        "core_sum",
        [shape((pixels, depth), F32), shape((pixels, depth), BF16)],
        [],
        0.4,
        gn_kept,
        over_core(gn_sent),
    )
    gn_sent, *pieces = lax.optimization_barrier((gn_sent, *relative_order(pieces)))
    gn_other = over_shard(gn_sent, INNER)
    arrived = [over_shard(piece, flip) for flip, piece in enumerate(pieces) if flip]
    *small, grad_conv = call(
        functools.partial(norm_back_kernel, relative, own),
        "norm_back",
        [shape((rows, LANES), F32)]
        + [shape((rows, LANES), BF16)] * (INNER - 1)
        + [shape((tiles, height, breadth, LANES), F32)],
        [
            padded,
            pltpu.VMEM((tiles, LANES, LANES), F32),
            pltpu.VMEM((depth, LANES), F32),
        ],
        1.7,
        gn_kept,
        gn_other,
        whitened,
        inv_std,
        taps,
        images,
    )
    small = relative_order(small)
    small_arrived = [over_shard(piece, flip) for flip, piece in enumerate(small) if flip]
    (grad_images,) = call(
        conv_back_kernel,
        "conv_back",
        [shape(images.shape, BF16)],
        [padded],
        1.9,
        grad_conv,
        taps,
    )

    plane = pieces[0] + sum(piece.astype(F32) for piece in arrived)
    small_plane = small[0] + sum(piece.astype(F32) for piece in small_arrived)
    merged = jnp.concatenate([plane, small_plane], axis=1).reshape(lines, own, quarter + LANES)
    merged, grad_images = lax.optimization_barrier((merged, grad_images))
    came = [
        over_shard(merged[line].astype(BF16), INNER * line) for line in range(1, lines)
    ]
    (total,) = call(
        line_sum_kernel,
        "line_sum",
        [shape((own, half + LANES), F32)],
        [],
        0.3,
        merged[0],
        *came,
    )
    if reps > 2:
        groups = [[i for i in range(reps) if i % 2 == s] for s in range(2)]
        total = lax.psum(total, "rep", axis_index_groups=groups)
    other = over_core(total)
    factor = 1.0 / math.sqrt(images.shape[0] * pixels * shards * reps)
    grad_up, grad_depthwise, grad_gain, grad_bias = call(
        functools.partial(finish_kernel, factor),
        "finish",
        [
            shape((own, hidden), F32),
            shape((own, TAPS), F32),
            shape((1, own), F32),
            shape((1, own), F32),
        ],
        [],
        0.5,
        total,
        other,
    )
    return (grad_images, grad_up, grad_depthwise, grad_gain[0], grad_bias[0])


def solution(mesh):
    placed = (
        P(("shard", "rep"), None, None, None),
        P(("shard", "rep"), None, None, None),
        P("shard", None),
        P("shard"),
        P("shard"),
        P("shard", None),
    )
    return jax.shard_map(
        body,
        mesh=mesh,
        in_specs=placed,
        out_specs=(
            P(("shard", "rep"), None, None, None),
            P("shard", None),
            P("shard", None),
            P("shard"),
            P("shard"),
        ),
        check_vma=False,
    )
```

```python
import functools
import math

import jax
import jax.numpy as jnp
from jax import lax
from jax.experimental import pallas as pl
from jax.experimental.pallas import tpu as pltpu
from jax.sharding import PartitionSpec as P

KS = 7
TAPS = KS * KS
MARGIN = KS // 2
LANES = 128
INNER = 4
NORM_EPS = 1e-06
BF16 = jnp.bfloat16
F32 = jnp.float32
VMEM = pl.BlockSpec(memory_space=pltpu.VMEM)


def params():
    return pltpu.CompilerParams(vmem_limit_bytes=48 * 1024 * 1024)


def gelu_slope(inputs):
    cumulative = 0.5 * (1.0 + lax.erf(inputs * 0.7071067811865476))
    return cumulative + inputs * jnp.exp(-0.5 * inputs * inputs) * 0.3989422804014327


def block_rows(relative, group, line, own, lines):
    if relative:
        place = lax.axis_index("shard") ^ (line * INNER + group)
        return pl.multiple_of(place * own, 16)
    return (group * lines + line) * own


def place_rows(pieces, target, own, relative, cast=None):
    for group, piece in enumerate(pieces):
        lines = piece.shape[0] // own
        if not relative:
            target[group * piece.shape[0] : (group + 1) * piece.shape[0], :] = (
                piece[...] if cast is None else piece[...].astype(cast)
            )
            continue
        for line in range(lines):
            rows = piece[line * own : (line + 1) * own, :]
            start = block_rows(True, group, line, own, lines)
            target[pl.ds(start, own), :] = rows if cast is None else rows.astype(cast)


def split_rows(source, pieces, own, relative):
    for group, piece in enumerate(pieces):
        lines = piece.shape[0] // own
        if not relative:
            piece[...] = source[group * piece.shape[0] : (group + 1) * piece.shape[0], :].astype(
                piece.dtype
            )
            continue
        for line in range(lines):
            start = block_rows(True, group, line, own, lines)
            piece[line * own : (line + 1) * own, :] = source[pl.ds(start, own), :].astype(
                piece.dtype
            )


def correlate(padded, tile, tap_row, height, breadth):
    sums = [None] * height
    for across in range(KS):
        shifted = padded[tile, :, 8 - MARGIN + across : 8 - MARGIN + across + breadth, :]
        for down in range(KS):
            row = tap_row(down, across)
            for line in range(height):
                origin = line + down - MARGIN
                if 0 <= origin < height:
                    term = shifted[origin] * row
                    sums[line] = term if sums[line] is None else sums[line] + term
    return sums


def pack_kernel(w_hbm, dw_hbm, gain_ref, bias_ref, near_ref, far_ref, w_ref, dw_ref, turned, wide, sems):
    own, hidden = w_ref.shape
    quarter = hidden // 4
    side = lax.axis_index("rep") % 2
    parity = (lax.axis_index("shard") // INNER) % 2
    copies = [
        pltpu.make_async_copy(w_hbm, w_ref, sems.at[0]),
        pltpu.make_async_copy(dw_hbm, dw_ref, sems.at[1]),
    ]
    for copy in copies:
        copy.start()
    turned[...] = jnp.zeros_like(turned)
    turned[TAPS : TAPS + 1, :own] = gain_ref[...].astype(F32)
    turned[TAPS + 1 : TAPS + 2, :own] = bias_ref[...].astype(F32)
    wide[...] = jnp.zeros_like(wide)
    for copy in copies:
        copy.wait()
    wide[:, :TAPS] = dw_ref[...].astype(F32)
    extras = (wide[...] + turned[...].T[:own]).astype(BF16)
    for ref, which in ((near_ref, parity), (far_ref, 1 - parity)):
        start = pl.multiple_of(side * (2 * quarter) + which * quarter, LANES)
        ref[:, :quarter] = w_ref[:, pl.ds(start, quarter)]
        ref[:, quarter:] = extras


def assemble_kernel(*refs):
    pieces, (weight_ref, extra_ref) = refs[:-2], refs[-2:]
    own = pieces[0].shape[0]
    quarter = weight_ref.shape[1]
    for line, piece in enumerate(pieces):
        weight_ref[line * own : (line + 1) * own, :] = piece[:, :quarter]
        extra_ref[line * own : (line + 1) * own, :] = piece[:, quarter:]


def plane_sum_kernel(lines, *refs):
    pieces, small, outs = refs[:INNER], refs[INNER : 2 * INNER], refs[2 * INNER :]
    own = pieces[0].shape[0] // lines
    quarter = pieces[0].shape[1]
    for line, out in enumerate(outs):
        rows = slice(line * own, (line + 1) * own)
        for parts, columns in ((pieces, slice(0, quarter)), (small, slice(quarter, None))):
            total = parts[0][rows, :]
            for part in parts[1:]:
                total = total + part[rows, :].astype(F32)
            out[:, columns] = total.astype(out.dtype)


def line_sum_kernel(*refs):
    pieces, total_ref = refs[:-1], refs[-1]
    quarter = pieces[0].shape[1] - LANES
    same, cross = pieces[0][...], None
    for line, piece in enumerate(pieces):
        if line % 2:
            cross = piece[...].astype(F32) if cross is None else cross + piece[...].astype(F32)
        elif line:
            same = same + piece[...].astype(F32)
    total_ref[:, :quarter] = same[:, :quarter]
    total_ref[:, quarter : 2 * quarter] = cross[:, :quarter]
    total_ref[:, 2 * quarter :] = same[:, quarter:] + cross[:, quarter:]


def finish_kernel(factor, mine_ref, other_ref, up_ref, dw_ref, gain_ref, bias_ref):
    own, half = mine_ref.shape[0], mine_ref.shape[1] - LANES
    quarter = half // 2
    side = lax.axis_index("rep") % 2
    parity = (lax.axis_index("shard") // INNER) % 2
    for ref, place in ((mine_ref, side), (other_ref, 1 - side)):
        for which, low in ((parity, 0), (1 - parity, quarter)):
            start = pl.multiple_of(place * half + which * quarter, LANES)
            up_ref[:, pl.ds(start, quarter)] = ref[:, low : low + quarter] * factor
    sums = (mine_ref[:, half:] + other_ref[:, half:]) * factor
    dw_ref[...] = sums[:, :TAPS]
    turned = sums.T
    gain_ref[...] = turned[TAPS : TAPS + 1, :]
    bias_ref[...] = turned[TAPS + 1 : TAPS + 2, :]


def conv_norm_kernel(relative, own, *refs):
    small = refs[:INNER]
    sources = refs[INNER : INNER + 2]
    x_ref = sources[0]
    normed_ref, white_ref, inv_ref, taps_ref, gathered, padded, conv = refs[INNER + 2 :]
    height, breadth, depth = x_ref.shape[1:]
    tiles = depth // LANES
    pixels = height * breadth
    place_rows(small, gathered, own, relative, F32)
    padded[...] = jnp.zeros_like(padded)
    for tile in range(tiles):
        lanes = slice(tile * LANES, (tile + 1) * LANES)
        taps_ref[tile] = gathered[lanes, :].T

    for image, source in enumerate(sources):
        for tile in range(tiles):
            lanes = slice(tile * LANES, (tile + 1) * LANES)
            padded[tile, :, 8 : 8 + breadth, :] = source[0, :, :, lanes].astype(F32)

        def one_tile(tile, carry):
            sums = correlate(
                padded,
                tile,
                lambda down, across: taps_ref[tile, pl.ds(down * KS + across, 1), :],
                height,
                breadth,
            )
            for line in range(height):
                conv[tile, line * breadth : (line + 1) * breadth, :] = sums[line]
            return carry

        lax.fori_loop(0, tiles, one_tile, 0)
        total = conv[0]
        for tile in range(1, tiles):
            total = total + conv[tile]
        average = jnp.sum(total, axis=-1, keepdims=True) / depth
        squares = None
        for tile in range(tiles):
            centered = conv[tile] - average
            squares = centered * centered if squares is None else squares + centered * centered
        variance = jnp.sum(squares, axis=-1, keepdims=True) / depth
        inv_std = lax.rsqrt(variance + NORM_EPS)
        if image == 0:
            inv_ref[...] = jnp.broadcast_to(inv_std, (pixels, LANES))
        for tile in range(tiles):
            lanes = slice(tile * LANES, (tile + 1) * LANES)
            whitened = (conv[tile] - average) * inv_std
            if image == 0:
                white_ref[:, lanes] = whitened
            gain = taps_ref[tile, TAPS : TAPS + 1, :]
            bias = taps_ref[tile, TAPS + 1 : TAPS + 2, :]
            normed_ref[image * pixels : (image + 1) * pixels, lanes] = (
                whitened * gain + bias
            ).astype(BF16)


def cot_pack_kernel(cot_ref, across_ref, sibling_ref):
    half = sibling_ref.shape[1]
    quarter = half // 2
    side = lax.axis_index("rep") % 2
    parity = (lax.axis_index("shard") // INNER) % 2
    for place in range(2):
        start = pl.multiple_of(place * half + (1 - parity) * quarter, LANES)
        across_ref[:, place * quarter : (place + 1) * quarter] = cot_ref[:, pl.ds(start, quarter)]
    sibling_ref[...] = cot_ref[:, pl.ds(pl.multiple_of((1 - side) * half, LANES), half)]


def order_kernel(relative, own, *refs):
    place_rows(refs[:INNER], refs[INNER], own, relative)


def project_kernel(relative, own, *refs):
    weight, n_own, n_sibling, cot_ref, sibling_ref, across_ref, corner_ref = refs[:7]
    pieces = refs[7 : 7 + INNER]
    gp_ref, normed, cot, grad = refs[7 + INNER :]
    pixels, half = sibling_ref.shape
    quarter = half // 2
    side = lax.axis_index("rep") % 2
    parity = (lax.axis_index("shard") // INNER) % 2
    normed[: 2 * pixels, :] = n_own[...]
    normed[2 * pixels :, :] = n_sibling[...]
    start = pl.multiple_of(side * half + parity * quarter, LANES)
    cot[:pixels, :] = cot_ref[:, pl.ds(start, quarter)]
    start = pl.multiple_of(side * quarter, LANES)
    cot[pixels : 2 * pixels, :] = across_ref[:, pl.ds(start, quarter)]
    start = pl.multiple_of(parity * quarter, LANES)
    cot[2 * pixels : 3 * pixels, :] = sibling_ref[:, pl.ds(start, quarter)]
    start = pl.multiple_of(side * quarter, LANES)
    cot[3 * pixels :, :] = corner_ref[:, pl.ds(start, quarter)]
    for start in range(0, quarter, LANES):
        columns = slice(start, start + LANES)
        pre_act = jnp.dot(normed[...], weight[:, columns], preferred_element_type=F32)
        gp_ref[:, columns] = (cot[:, columns].astype(F32) * gelu_slope(pre_act)).astype(BF16)
    grad[...] = lax.dot_general(
        normed[...], gp_ref[...], (((0,), (0,)), ((), ())), preferred_element_type=F32
    )
    split_rows(grad, pieces, own, relative)


def back_project_kernel(weight, gp_ref, own_ref, other_ref):
    rows = own_ref.shape[0]
    grad_normed = lax.dot_general(
        gp_ref[...], weight[...], (((1,), (1,)), ((), ())), preferred_element_type=F32
    )
    own_ref[...] = grad_normed[:rows]
    other_ref[...] = grad_normed[rows:]


def core_sum_kernel(own_ref, other_ref, kept_ref, sent_ref):
    pixels = kept_ref.shape[0]
    kept_ref[...] = own_ref[:pixels] + other_ref[:pixels]
    sent_ref[...] = (own_ref[pixels:] + other_ref[pixels:]).astype(BF16)


def norm_back_kernel(relative, own, *refs):
    gn_own, gn_other, white_ref, inv_ref, taps_ref, x_ref = refs[:6]
    pieces = refs[6 : 6 + INNER]
    grad_ref, padded, rows, small = refs[6 + INNER :]
    height, breadth, depth = x_ref.shape[1:]
    tiles = depth // LANES
    pixels = height * breadth
    padded[...] = jnp.zeros_like(padded)
    rows[...] = jnp.zeros_like(rows)
    first = None
    second = None
    for tile in range(tiles):
        lanes = slice(tile * LANES, (tile + 1) * LANES)
        padded[tile, :, 8 : 8 + breadth, :] = x_ref[0, :, :, lanes].astype(F32)
        grad_normed = gn_own[:, lanes] + gn_other[:, lanes].astype(F32)
        whitened = white_ref[:, lanes]
        product = grad_normed * whitened
        gain = taps_ref[tile, TAPS : TAPS + 1, :]
        rows[tile, TAPS : TAPS + 1, :] = jnp.sum(product, axis=0, keepdims=True)
        rows[tile, TAPS + 1 : TAPS + 2, :] = jnp.sum(grad_normed, axis=0, keepdims=True)
        one, two = grad_normed * gain, product * gain
        first = one if first is None else first + one
        second = two if second is None else second + two
    mean_first = jnp.sum(first, axis=-1, keepdims=True) / depth
    mean_second = jnp.sum(second, axis=-1, keepdims=True) / depth
    for tile in range(tiles):
        lanes = slice(tile * LANES, (tile + 1) * LANES)
        gain = taps_ref[tile, TAPS : TAPS + 1, :]
        grad_white = (gn_own[:, lanes] + gn_other[:, lanes].astype(F32)) * gain
        grad_conv = inv_ref[...] * (grad_white - mean_first - white_ref[:, lanes] * mean_second)
        grad_ref[tile] = grad_conv.reshape(height, breadth, LANES)

    def one_tile(tile, carry):
        grads = [grad_ref[tile, line] for line in range(height)]
        for across in range(KS):
            shifted = padded[tile, :, 8 - MARGIN + across : 8 - MARGIN + across + breadth, :]
            for down in range(KS):
                total = None
                for line in range(height):
                    origin = line + down - MARGIN
                    if 0 <= origin < height:
                        term = grads[line] * shifted[origin]
                        total = term if total is None else total + term
                rows[tile, pl.ds(down * KS + across, 1), :] = jnp.sum(total, axis=0, keepdims=True)
        return carry

    lax.fori_loop(0, tiles, one_tile, 0)
    for tile in range(tiles):
        small[tile * LANES : (tile + 1) * LANES, :] = rows[tile].T
    split_rows(small, pieces, own, relative)


def conv_back_kernel(grad_ref, taps_ref, out_ref, padded):
    tiles, height, breadth, _ = grad_ref.shape
    padded[...] = jnp.zeros_like(padded)
    padded[:, :, 8 : 8 + breadth, :] = grad_ref[...]

    def one_tile(tile, carry):
        sums = correlate(
            padded,
            tile,
            lambda down, across: taps_ref[tile, pl.ds(TAPS - 1 - down * KS - across, 1), :],
            height,
            breadth,
        )
        start = pl.multiple_of(tile * LANES, LANES)
        for line in range(height):
            out_ref[0, line, :, pl.ds(start, LANES)] = sums[line].astype(BF16)
        return carry

    lax.fori_loop(0, tiles, one_tile, 0)


def call(kernel, name, outs, scratch, micros, *args, in_specs=None):
    flops = int(micros * 1.1e9)
    moved = sum(math.prod(a.shape) * a.dtype.itemsize for a in args)
    moved += sum(math.prod(o.shape) * o.dtype.itemsize for o in outs)
    return pl.pallas_call(
        kernel,
        out_shape=outs,
        in_specs=in_specs or [VMEM] * len(args),
        out_specs=[VMEM] * len(outs),
        scratch_shapes=scratch,
        compiler_params=params(),
        cost_estimate=pl.CostEstimate(flops=flops, bytes_accessed=moved, transcendentals=0),
        name=name,
    )(*args)


def body(images, cotangent, depthwise_weight, norm_gain, norm_bias, up_weight):
    shards, reps = lax.axis_size("shard"), lax.axis_size("rep")
    own, hidden = up_weight.shape
    depth = own * shards
    lines = shards // INNER
    half, quarter = hidden // 2, hidden // 4
    height, breadth = images.shape[1:3]
    pixels = height * breadth
    tiles = depth // LANES
    me = lax.axis_index("shard")
    side = lax.axis_index("rep") % 2
    parity = (me // INNER) % 2
    relative = own % 16 == 0

    def over_shard(array, flip):
        return lax.ppermute(array, "shard", [(i, i ^ flip) for i in range(shards)])

    def over_core(array):
        return lax.ppermute(array, "rep", [(i, i ^ 1) for i in range(reps)])

    def true_order(pieces):
        if relative:
            return pieces
        stacked = jnp.stack(pieces).reshape(shards, own, -1)
        flips = jnp.arange(shards) ^ me
        places = (flips % INNER) * lines + flips // INNER
        return list(jnp.take(stacked, places, axis=0).reshape(INNER, lines * own, -1))

    def relative_order(pieces):
        if relative:
            return pieces
        stacked = jnp.concatenate([p.astype(F32) for p in pieces]).reshape(shards, own, -1)
        flips = (jnp.arange(lines)[None, :] * INNER + jnp.arange(INNER)[:, None]).reshape(-1)
        moved = jnp.take(stacked, flips ^ me, axis=0).reshape(INNER, lines * own, -1)
        return [moved[0]] + [moved[i].astype(BF16) for i in range(1, INNER)]

    shape = jax.ShapeDtypeStruct
    near, far = call(
        pack_kernel,
        "pack",
        [shape((own, quarter + LANES), BF16)] * 2,
        [
            pltpu.VMEM(up_weight.shape, BF16),
            pltpu.VMEM(depthwise_weight.shape, BF16),
            pltpu.VMEM((LANES, LANES), F32),
            pltpu.VMEM((own, LANES), F32),
            pltpu.SemaphoreType.DMA((2,)),
        ],
        0.5,
        up_weight,
        depthwise_weight,
        norm_gain[None, :],
        norm_bias[None, :],
        in_specs=[pl.BlockSpec(memory_space=pltpu.HBM)] * 2 + [VMEM] * 2,
    )
    near, far, images, cotangent = lax.optimization_barrier((near, far, images, cotangent))
    gathered = [near] + [
        over_shard(far if line % 2 else near, INNER * line) for line in range(1, lines)
    ]
    cotangent = cotangent.reshape(pixels, hidden)
    cot_across, cot_sibling = call(
        cot_pack_kernel,
        "cot_pack",
        [shape((pixels, half), BF16)] * 2,
        [],
        0.4,
        cotangent,
    )
    cot_across, cot_sibling = over_shard(cot_across, INNER), over_core(cot_sibling)
    images_far = over_shard(images, INNER)

    rows = lines * own
    weight_lines, extra_lines = call(
        assemble_kernel,
        "assemble",
        [shape((rows, quarter), BF16), shape((rows, LANES), BF16)],
        [],
        2.0,
        *gathered,
    )
    weights = [weight_lines] + [over_shard(weight_lines, flip) for flip in range(1, INNER)]
    extras = [extra_lines] + [over_shard(extra_lines, flip) for flip in range(1, INNER)]
    *extras, cot_across = lax.optimization_barrier((*extras, cot_across))
    cot_corner = over_core(cot_across)
    weights, extras = true_order(weights), true_order(extras)
    (weight,) = call(
        functools.partial(order_kernel, relative, own),
        "order",
        [shape((depth, quarter), BF16)],
        [],
        3.0,
        *weights,
    )

    padded = pltpu.VMEM((tiles, height, breadth + 16, LANES), F32)
    normed, whitened, inv_std, taps = call(
        functools.partial(conv_norm_kernel, relative, own),
        "conv_norm",
        [
            shape((2 * pixels, depth), BF16),
            shape((pixels, depth), F32),
            shape((pixels, LANES), F32),
            shape((tiles, LANES, LANES), F32),
        ],
        [
            pltpu.VMEM((depth, LANES), F32),
            padded,
            pltpu.VMEM((tiles, pixels, LANES), F32),
        ],
        0.1,
        *extras,
        images,
        images_far,
    )
    normed_sibling = over_core(normed)
    *pieces, grad_pre = call(
        functools.partial(project_kernel, relative, own),
        "project",
        [shape((rows, quarter), F32)]
        + [shape((rows, quarter), BF16)] * (INNER - 1)
        + [shape((4 * pixels, quarter), BF16)],
        [
            pltpu.VMEM((4 * pixels, depth), BF16),
            pltpu.VMEM((4 * pixels, quarter), BF16),
            pltpu.VMEM((depth, quarter), F32),
        ],
        1.6,
        weight,
        normed,
        normed_sibling,
        cotangent,
        cot_sibling,
        cot_across,
        cot_corner,
    )
    gn_kept, gn_sent = call(
        back_project_kernel,
        "back_project",
        [shape((2 * pixels, depth), F32)] * 2,
        [],
        0.7,
        weight,
        grad_pre,
    )
    gn_kept, gn_sent = call(
        core_sum_kernel,
        "core_sum",
        [shape((pixels, depth), F32), shape((pixels, depth), BF16)],
        [],
        0.4,
        gn_kept,
        over_core(gn_sent),
    )
    gn_sent, *pieces = lax.optimization_barrier((gn_sent, *relative_order(pieces)))
    gn_other = over_shard(gn_sent, INNER)
    arrived = [over_shard(piece, flip) for flip, piece in enumerate(pieces) if flip]
    *small, grad_conv = call(
        functools.partial(norm_back_kernel, relative, own),
        "norm_back",
        [shape((rows, LANES), F32)]
        + [shape((rows, LANES), BF16)] * (INNER - 1)
        + [shape((tiles, height, breadth, LANES), F32)],
        [
            padded,
            pltpu.VMEM((tiles, LANES, LANES), F32),
            pltpu.VMEM((depth, LANES), F32),
        ],
        1.7,
        gn_kept,
        gn_other,
        whitened,
        inv_std,
        taps,
        images,
    )
    small = relative_order(small)
    small_arrived = [over_shard(piece, flip) for flip, piece in enumerate(small) if flip]
    (grad_images,) = call(
        conv_back_kernel,
        "conv_back",
        [shape(images.shape, BF16)],
        [padded],
        1.9,
        grad_conv,
        taps,
    )

    home, *sent = call(
        functools.partial(plane_sum_kernel, lines),
        "plane_sum",
        [shape((own, quarter + LANES), F32)] + [shape((own, quarter + LANES), BF16)] * (lines - 1),
        [],
        0.4,
        pieces[0],
        *arrived,
        small[0],
        *small_arrived,
    )
    home, grad_images = lax.optimization_barrier((home, grad_images))
    came = [over_shard(piece, INNER * line) for line, piece in enumerate(sent, 1)]
    (total,) = call(
        line_sum_kernel,
        "line_sum",
        [shape((own, half + LANES), F32)],
        [],
        0.3,
        home,
        *came,
    )
    if reps > 2:
        groups = [[i for i in range(reps) if i % 2 == s] for s in range(2)]
        total = lax.psum(total, "rep", axis_index_groups=groups)
    other = over_core(total)
    factor = 1.0 / math.sqrt(images.shape[0] * pixels * shards * reps)
    grad_up, grad_depthwise, grad_gain, grad_bias = call(
        functools.partial(finish_kernel, factor),
        "finish",
        [
            shape((own, hidden), F32),
            shape((own, TAPS), F32),
            shape((1, own), F32),
            shape((1, own), F32),
        ],
        [],
        0.5,
        total,
        other,
    )
    return (grad_images, grad_up, grad_depthwise, grad_gain[0], grad_bias[0])


def solution(mesh):
    placed = (
        P(("shard", "rep"), None, None, None),
        P(("shard", "rep"), None, None, None),
        P("shard", None),
        P("shard"),
        P("shard"),
        P("shard", None),
    )
    return jax.shard_map(
        body,
        mesh=mesh,
        in_specs=placed,
        out_specs=(
            P(("shard", "rep"), None, None, None),
            P("shard", None),
            P("shard", None),
            P("shard"),
            P("shard"),
        ),
        check_vma=False,
    )
```

```python
import functools
import math

import jax
import jax.numpy as jnp
from jax import lax
from jax.experimental import pallas as pl
from jax.experimental.pallas import tpu as pltpu
from jax.sharding import PartitionSpec as P

KS = 7
TAPS = KS * KS
MARGIN = KS // 2
LANES = 128
INNER = 4
NORM_EPS = 1e-06
BF16 = jnp.bfloat16
F32 = jnp.float32
VMEM = pl.BlockSpec(memory_space=pltpu.VMEM)


def params(mebibytes):
    return pltpu.CompilerParams(vmem_limit_bytes=mebibytes * 1024 * 1024)


def gelu_slope(inputs):
    cumulative = 0.5 * (1.0 + lax.erf(inputs * 0.7071067811865476))
    return cumulative + inputs * jnp.exp(-0.5 * inputs * inputs) * 0.3989422804014327


def block_rows(relative, group, line, own, lines):
    if relative:
        place = lax.axis_index("shard") ^ (line * INNER + group)
        return pl.multiple_of(place * own, 16)
    return (group * lines + line) * own


def place_rows(pieces, target, own, relative, cast=None):
    for group, piece in enumerate(pieces):
        lines = piece.shape[0] // own
        if not relative:
            target[group * piece.shape[0] : (group + 1) * piece.shape[0], :] = (
                piece[...] if cast is None else piece[...].astype(cast)
            )
            continue
        for line in range(lines):
            rows = piece[line * own : (line + 1) * own, :]
            start = block_rows(True, group, line, own, lines)
            target[pl.ds(start, own), :] = rows if cast is None else rows.astype(cast)


def split_rows(source, pieces, own, relative):
    for group, piece in enumerate(pieces):
        lines = piece.shape[0] // own
        if not relative:
            piece[...] = source[group * piece.shape[0] : (group + 1) * piece.shape[0], :].astype(
                piece.dtype
            )
            continue
        for line in range(lines):
            start = block_rows(True, group, line, own, lines)
            piece[line * own : (line + 1) * own, :] = source[pl.ds(start, own), :].astype(
                piece.dtype
            )


def correlate(padded, tile, tap_row, height, breadth):
    sums = [None] * height
    for across in range(KS):
        shifted = padded[tile, :, 8 - MARGIN + across : 8 - MARGIN + across + breadth, :]
        for down in range(KS):
            row = tap_row(down, across)
            for line in range(height):
                origin = line + down - MARGIN
                if 0 <= origin < height:
                    term = shifted[origin] * row
                    sums[line] = term if sums[line] is None else sums[line] + term
    return sums


def pack_kernel(w_hbm, dw_hbm, gain_ref, bias_ref, near_ref, far_ref, w_ref, dw_ref, turned, wide, sems):
    own, hidden = w_ref.shape
    quarter = hidden // 4
    side = lax.axis_index("rep") % 2
    parity = (lax.axis_index("shard") // INNER) % 2
    copies = [
        pltpu.make_async_copy(w_hbm, w_ref, sems.at[0]),
        pltpu.make_async_copy(dw_hbm, dw_ref, sems.at[1]),
    ]
    for copy in copies:
        copy.start()
    turned[...] = jnp.zeros_like(turned)
    turned[TAPS : TAPS + 1, :own] = gain_ref[...].astype(F32)
    turned[TAPS + 1 : TAPS + 2, :own] = bias_ref[...].astype(F32)
    wide[...] = jnp.zeros_like(wide)
    for copy in copies:
        copy.wait()
    wide[:, :TAPS] = dw_ref[...].astype(F32)
    extras = (wide[...] + turned[...].T[:own]).astype(BF16)
    for ref, which in ((near_ref, parity), (far_ref, 1 - parity)):
        start = pl.multiple_of(side * (2 * quarter) + which * quarter, LANES)
        ref[:, :quarter] = w_ref[:, pl.ds(start, quarter)]
        ref[:, quarter:] = extras


def assemble_kernel(*refs):
    pieces, (weight_ref, extra_ref) = refs[:-2], refs[-2:]
    own = pieces[0].shape[0]
    quarter = weight_ref.shape[1]
    for line, piece in enumerate(pieces):
        weight_ref[line * own : (line + 1) * own, :] = piece[:, :quarter]
        extra_ref[line * own : (line + 1) * own, :] = piece[:, quarter:]


def plane_sum_kernel(lines, *refs):
    pieces, small, outs = refs[:INNER], refs[INNER : 2 * INNER], refs[2 * INNER :]
    own = pieces[0].shape[0] // lines
    quarter = pieces[0].shape[1]
    for line, out in enumerate(outs):
        rows = slice(line * own, (line + 1) * own)
        for parts, columns in ((pieces, slice(0, quarter)), (small, slice(quarter, None))):
            total = parts[0][rows, :]
            for part in parts[1:]:
                total = total + part[rows, :].astype(F32)
            out[:, columns] = total.astype(out.dtype)


def line_sum_kernel(*refs):
    pieces, total_ref = refs[:-1], refs[-1]
    quarter = pieces[0].shape[1] - LANES
    same, cross = pieces[0][...], None
    for line, piece in enumerate(pieces):
        if line % 2:
            cross = piece[...].astype(F32) if cross is None else cross + piece[...].astype(F32)
        elif line:
            same = same + piece[...].astype(F32)
    total_ref[:, :quarter] = same[:, :quarter]
    total_ref[:, quarter : 2 * quarter] = cross[:, :quarter]
    total_ref[:, 2 * quarter :] = same[:, quarter:] + cross[:, quarter:]


def finish_kernel(factor, mine_ref, other_ref, up_ref, dw_ref, gain_ref, bias_ref):
    own, half = mine_ref.shape[0], mine_ref.shape[1] - LANES
    quarter = half // 2
    side = lax.axis_index("rep") % 2
    parity = (lax.axis_index("shard") // INNER) % 2
    for ref, place in ((mine_ref, side), (other_ref, 1 - side)):
        for which, low in ((parity, 0), (1 - parity, quarter)):
            start = pl.multiple_of(place * half + which * quarter, LANES)
            up_ref[:, pl.ds(start, quarter)] = ref[:, low : low + quarter] * factor
    sums = (mine_ref[:, half:] + other_ref[:, half:]) * factor
    dw_ref[...] = sums[:, :TAPS]
    turned = sums.T
    gain_ref[...] = turned[TAPS : TAPS + 1, :]
    bias_ref[...] = turned[TAPS + 1 : TAPS + 2, :]


def conv_norm_kernel(relative, own, *refs):
    small = refs[:INNER]
    sources = refs[INNER : INNER + 2]
    x_ref = sources[0]
    normed_ref, white_ref, inv_ref, taps_ref, gathered, padded, conv = refs[INNER + 2 :]
    height, breadth, depth = x_ref.shape[1:]
    tiles = depth // LANES
    pixels = height * breadth
    place_rows(small, gathered, own, relative, F32)
    padded[...] = jnp.zeros_like(padded)
    for tile in range(tiles):
        lanes = slice(tile * LANES, (tile + 1) * LANES)
        taps_ref[tile] = gathered[lanes, :].T

    for image, source in enumerate(sources):
        for tile in range(tiles):
            lanes = slice(tile * LANES, (tile + 1) * LANES)
            padded[tile, :, 8 : 8 + breadth, :] = source[0, :, :, lanes].astype(F32)

        def one_tile(tile, carry):
            sums = correlate(
                padded,
                tile,
                lambda down, across: taps_ref[tile, pl.ds(down * KS + across, 1), :],
                height,
                breadth,
            )
            for line in range(height):
                conv[tile, line * breadth : (line + 1) * breadth, :] = sums[line]
            return carry

        lax.fori_loop(0, tiles, one_tile, 0)
        total = conv[0]
        for tile in range(1, tiles):
            total = total + conv[tile]
        average = jnp.sum(total, axis=-1, keepdims=True) / depth
        squares = None
        for tile in range(tiles):
            centered = conv[tile] - average
            squares = centered * centered if squares is None else squares + centered * centered
        variance = jnp.sum(squares, axis=-1, keepdims=True) / depth
        inv_std = lax.rsqrt(variance + NORM_EPS)
        if image == 0:
            inv_ref[...] = jnp.broadcast_to(inv_std, (pixels, LANES))
        for tile in range(tiles):
            lanes = slice(tile * LANES, (tile + 1) * LANES)
            whitened = (conv[tile] - average) * inv_std
            if image == 0:
                white_ref[:, lanes] = whitened
            gain = taps_ref[tile, TAPS : TAPS + 1, :]
            bias = taps_ref[tile, TAPS + 1 : TAPS + 2, :]
            normed_ref[image * pixels : (image + 1) * pixels, lanes] = (
                whitened * gain + bias
            ).astype(BF16)


def cot_pack_kernel(cot_ref, across_ref, sibling_ref):
    half = sibling_ref.shape[1]
    quarter = half // 2
    side = lax.axis_index("rep") % 2
    parity = (lax.axis_index("shard") // INNER) % 2
    for place in range(2):
        start = pl.multiple_of(place * half + (1 - parity) * quarter, LANES)
        across_ref[:, place * quarter : (place + 1) * quarter] = cot_ref[:, pl.ds(start, quarter)]
    sibling_ref[...] = cot_ref[:, pl.ds(pl.multiple_of((1 - side) * half, LANES), half)]


def order_kernel(relative, own, *refs):
    place_rows(refs[:INNER], refs[INNER], own, relative)


def project_kernel(relative, own, *refs):
    weight, n_own, n_sibling, cot_ref, sibling_ref, across_ref, corner_ref = refs[:7]
    pieces = refs[7 : 7 + INNER]
    gp_ref, normed, cot, grad = refs[7 + INNER :]
    pixels, half = sibling_ref.shape
    quarter = half // 2
    side = lax.axis_index("rep") % 2
    parity = (lax.axis_index("shard") // INNER) % 2
    normed[: 2 * pixels, :] = n_own[...]
    normed[2 * pixels :, :] = n_sibling[...]
    start = pl.multiple_of(side * half + parity * quarter, LANES)
    cot[:pixels, :] = cot_ref[:, pl.ds(start, quarter)]
    start = pl.multiple_of(side * quarter, LANES)
    cot[pixels : 2 * pixels, :] = across_ref[:, pl.ds(start, quarter)]
    start = pl.multiple_of(parity * quarter, LANES)
    cot[2 * pixels : 3 * pixels, :] = sibling_ref[:, pl.ds(start, quarter)]
    start = pl.multiple_of(side * quarter, LANES)
    cot[3 * pixels :, :] = corner_ref[:, pl.ds(start, quarter)]
    for start in range(0, quarter, LANES):
        columns = slice(start, start + LANES)
        pre_act = jnp.dot(normed[...], weight[:, columns], preferred_element_type=F32)
        gp_ref[:, columns] = (cot[:, columns].astype(F32) * gelu_slope(pre_act)).astype(BF16)
    grad[...] = lax.dot_general(
        normed[...], gp_ref[...], (((0,), (0,)), ((), ())), preferred_element_type=F32
    )
    split_rows(grad, pieces, own, relative)


def back_project_kernel(weight, gp_ref, own_ref, other_ref):
    rows = own_ref.shape[0]
    grad_normed = lax.dot_general(
        gp_ref[...], weight[...], (((1,), (1,)), ((), ())), preferred_element_type=F32
    )
    own_ref[...] = grad_normed[:rows]
    other_ref[...] = grad_normed[rows:]


def core_sum_kernel(own_ref, other_ref, kept_ref, sent_ref):
    pixels = kept_ref.shape[0]
    kept_ref[...] = own_ref[:pixels] + other_ref[:pixels]
    sent_ref[...] = (own_ref[pixels:] + other_ref[pixels:]).astype(BF16)


def norm_back_kernel(relative, own, *refs):
    gn_own, gn_other, white_ref, inv_ref, taps_ref, x_ref = refs[:6]
    pieces = refs[6 : 6 + INNER]
    grad_ref, padded, rows, small = refs[6 + INNER :]
    height, breadth, depth = x_ref.shape[1:]
    tiles = depth // LANES
    pixels = height * breadth
    padded[...] = jnp.zeros_like(padded)
    rows[...] = jnp.zeros_like(rows)
    first = None
    second = None
    for tile in range(tiles):
        lanes = slice(tile * LANES, (tile + 1) * LANES)
        padded[tile, :, 8 : 8 + breadth, :] = x_ref[0, :, :, lanes].astype(F32)
        grad_normed = gn_own[:, lanes] + gn_other[:, lanes].astype(F32)
        whitened = white_ref[:, lanes]
        product = grad_normed * whitened
        gain = taps_ref[tile, TAPS : TAPS + 1, :]
        rows[tile, TAPS : TAPS + 1, :] = jnp.sum(product, axis=0, keepdims=True)
        rows[tile, TAPS + 1 : TAPS + 2, :] = jnp.sum(grad_normed, axis=0, keepdims=True)
        one, two = grad_normed * gain, product * gain
        first = one if first is None else first + one
        second = two if second is None else second + two
    mean_first = jnp.sum(first, axis=-1, keepdims=True) / depth
    mean_second = jnp.sum(second, axis=-1, keepdims=True) / depth
    for tile in range(tiles):
        lanes = slice(tile * LANES, (tile + 1) * LANES)
        gain = taps_ref[tile, TAPS : TAPS + 1, :]
        grad_white = (gn_own[:, lanes] + gn_other[:, lanes].astype(F32)) * gain
        grad_conv = inv_ref[...] * (grad_white - mean_first - white_ref[:, lanes] * mean_second)
        grad_ref[tile] = grad_conv.reshape(height, breadth, LANES)

    def one_tile(tile, carry):
        grads = [grad_ref[tile, line] for line in range(height)]
        for across in range(KS):
            shifted = padded[tile, :, 8 - MARGIN + across : 8 - MARGIN + across + breadth, :]
            for down in range(KS):
                total = None
                for line in range(height):
                    origin = line + down - MARGIN
                    if 0 <= origin < height:
                        term = grads[line] * shifted[origin]
                        total = term if total is None else total + term
                rows[tile, pl.ds(down * KS + across, 1), :] = jnp.sum(total, axis=0, keepdims=True)
        return carry

    lax.fori_loop(0, tiles, one_tile, 0)
    for tile in range(tiles):
        small[tile * LANES : (tile + 1) * LANES, :] = rows[tile].T
    split_rows(small, pieces, own, relative)


def conv_back_kernel(grad_ref, taps_ref, out_ref, padded):
    tiles, height, breadth, _ = grad_ref.shape
    padded[...] = jnp.zeros_like(padded)
    padded[:, :, 8 : 8 + breadth, :] = grad_ref[...]

    def one_tile(tile, carry):
        sums = correlate(
            padded,
            tile,
            lambda down, across: taps_ref[tile, pl.ds(TAPS - 1 - down * KS - across, 1), :],
            height,
            breadth,
        )
        start = pl.multiple_of(tile * LANES, LANES)
        for line in range(height):
            out_ref[0, line, :, pl.ds(start, LANES)] = sums[line].astype(BF16)
        return carry

    lax.fori_loop(0, tiles, one_tile, 0)


def call(kernel, name, outs, scratch, micros, *args, in_specs=None, mebibytes=48):
    flops = int(micros * 1.1e9)
    moved = sum(math.prod(a.shape) * a.dtype.itemsize for a in args)
    moved += sum(math.prod(o.shape) * o.dtype.itemsize for o in outs)
    return pl.pallas_call(
        kernel,
        out_shape=outs,
        in_specs=in_specs or [VMEM] * len(args),
        out_specs=[VMEM] * len(outs),
        scratch_shapes=scratch,
        compiler_params=params(mebibytes),
        cost_estimate=pl.CostEstimate(flops=flops, bytes_accessed=moved, transcendentals=0),
        name=name,
    )(*args)


def body(images, cotangent, depthwise_weight, norm_gain, norm_bias, up_weight):
    shards, reps = lax.axis_size("shard"), lax.axis_size("rep")
    own, hidden = up_weight.shape
    depth = own * shards
    lines = shards // INNER
    half, quarter = hidden // 2, hidden // 4
    height, breadth = images.shape[1:3]
    pixels = height * breadth
    tiles = depth // LANES
    me = lax.axis_index("shard")
    side = lax.axis_index("rep") % 2
    parity = (me // INNER) % 2
    relative = own % 16 == 0

    def over_shard(array, flip):
        return lax.ppermute(array, "shard", [(i, i ^ flip) for i in range(shards)])

    def over_core(array):
        return lax.ppermute(array, "rep", [(i, i ^ 1) for i in range(reps)])

    def true_order(pieces):
        if relative:
            return pieces
        stacked = jnp.stack(pieces).reshape(shards, own, -1)
        flips = jnp.arange(shards) ^ me
        places = (flips % INNER) * lines + flips // INNER
        return list(jnp.take(stacked, places, axis=0).reshape(INNER, lines * own, -1))

    def relative_order(pieces):
        if relative:
            return pieces
        stacked = jnp.concatenate([p.astype(F32) for p in pieces]).reshape(shards, own, -1)
        flips = (jnp.arange(lines)[None, :] * INNER + jnp.arange(INNER)[:, None]).reshape(-1)
        moved = jnp.take(stacked, flips ^ me, axis=0).reshape(INNER, lines * own, -1)
        return [moved[0]] + [moved[i].astype(BF16) for i in range(1, INNER)]

    shape = jax.ShapeDtypeStruct
    near, far = call(
        pack_kernel,
        "pack",
        [shape((own, quarter + LANES), BF16)] * 2,
        [
            pltpu.VMEM(up_weight.shape, BF16),
            pltpu.VMEM(depthwise_weight.shape, BF16),
            pltpu.VMEM((LANES, LANES), F32),
            pltpu.VMEM((own, LANES), F32),
            pltpu.SemaphoreType.DMA((2,)),
        ],
        0.5,
        up_weight,
        depthwise_weight,
        norm_gain[None, :],
        norm_bias[None, :],
        in_specs=[pl.BlockSpec(memory_space=pltpu.HBM)] * 2 + [VMEM] * 2,
        mebibytes=63,
    )
    near, far, images, cotangent = lax.optimization_barrier((near, far, images, cotangent))
    gathered = [near] + [
        over_shard(far if line % 2 else near, INNER * line) for line in range(1, lines)
    ]
    cotangent = cotangent.reshape(pixels, hidden)
    cot_across, cot_sibling = call(
        cot_pack_kernel,
        "cot_pack",
        [shape((pixels, half), BF16)] * 2,
        [],
        0.4,
        cotangent,
    )
    cot_across, cot_sibling = over_shard(cot_across, INNER), over_core(cot_sibling)
    images_far = over_shard(images, INNER)

    rows = lines * own
    weight_lines, extra_lines = call(
        assemble_kernel,
        "assemble",
        [shape((rows, quarter), BF16), shape((rows, LANES), BF16)],
        [],
        2.0,
        *gathered,
    )
    weights = [weight_lines] + [over_shard(weight_lines, flip) for flip in range(1, INNER)]
    extras = [extra_lines] + [over_shard(extra_lines, flip) for flip in range(1, INNER)]
    weights, extras = true_order(weights), true_order(extras)
    (weight,) = call(
        functools.partial(order_kernel, relative, own),
        "order",
        [shape((depth, quarter), BF16)],
        [],
        3.0,
        *weights,
    )

    padded = pltpu.VMEM((tiles, height, breadth + 16, LANES), F32)
    normed, whitened, inv_std, taps = call(
        functools.partial(conv_norm_kernel, relative, own),
        "conv_norm",
        [
            shape((2 * pixels, depth), BF16),
            shape((pixels, depth), F32),
            shape((pixels, LANES), F32),
            shape((tiles, LANES, LANES), F32),
        ],
        [
            pltpu.VMEM((depth, LANES), F32),
            padded,
            pltpu.VMEM((tiles, pixels, LANES), F32),
        ],
        0.1,
        *extras,
        images,
        images_far,
    )
    normed, cot_across = lax.optimization_barrier((normed, cot_across))
    normed_sibling, cot_corner = over_core(normed), over_core(cot_across)
    *pieces, grad_pre = call(
        functools.partial(project_kernel, relative, own),
        "project",
        [shape((rows, quarter), F32)]
        + [shape((rows, quarter), BF16)] * (INNER - 1)
        + [shape((4 * pixels, quarter), BF16)],
        [
            pltpu.VMEM((4 * pixels, depth), BF16),
            pltpu.VMEM((4 * pixels, quarter), BF16),
            pltpu.VMEM((depth, quarter), F32),
        ],
        1.6,
        weight,
        normed,
        normed_sibling,
        cotangent,
        cot_sibling,
        cot_across,
        cot_corner,
    )
    gn_kept, gn_sent = call(
        back_project_kernel,
        "back_project",
        [shape((2 * pixels, depth), F32)] * 2,
        [],
        0.7,
        weight,
        grad_pre,
    )
    gn_kept, gn_sent = call(
        core_sum_kernel,
        "core_sum",
        [shape((pixels, depth), F32), shape((pixels, depth), BF16)],
        [],
        0.4,
        gn_kept,
        over_core(gn_sent),
    )
    pieces = relative_order(pieces)
    gn_other = over_shard(gn_sent, INNER)
    arrived = [over_shard(piece, flip) for flip, piece in enumerate(pieces) if flip]
    *small, grad_conv = call(
        functools.partial(norm_back_kernel, relative, own),
        "norm_back",
        [shape((rows, LANES), F32)]
        + [shape((rows, LANES), BF16)] * (INNER - 1)
        + [shape((tiles, height, breadth, LANES), F32)],
        [
            padded,
            pltpu.VMEM((tiles, LANES, LANES), F32),
            pltpu.VMEM((depth, LANES), F32),
        ],
        1.7,
        gn_kept,
        gn_other,
        whitened,
        inv_std,
        taps,
        images,
    )
    small = relative_order(small)
    small_arrived = [over_shard(piece, flip) for flip, piece in enumerate(small) if flip]
    (grad_images,) = call(
        conv_back_kernel,
        "conv_back",
        [shape(images.shape, BF16)],
        [padded],
        0.1,
        grad_conv,
        taps,
    )

    *small_arrived, grad_images = lax.optimization_barrier((*small_arrived, grad_images))
    home, *sent = call(
        functools.partial(plane_sum_kernel, lines),
        "plane_sum",
        [shape((own, quarter + LANES), F32)] + [shape((own, quarter + LANES), BF16)] * (lines - 1),
        [],
        0.4,
        pieces[0],
        *arrived,
        small[0],
        *small_arrived,
    )
    came = [over_shard(piece, INNER * line) for line, piece in enumerate(sent, 1)]
    (total,) = call(
        line_sum_kernel,
        "line_sum",
        [shape((own, half + LANES), F32)],
        [],
        0.3,
        home,
        *came,
    )
    if reps > 2:
        groups = [[i for i in range(reps) if i % 2 == s] for s in range(2)]
        total = lax.psum(total, "rep", axis_index_groups=groups)
    other = over_core(total)
    factor = 1.0 / math.sqrt(images.shape[0] * pixels * shards * reps)
    grad_up, grad_depthwise, grad_gain, grad_bias = call(
        functools.partial(finish_kernel, factor),
        "finish",
        [
            shape((own, hidden), F32),
            shape((own, TAPS), F32),
            shape((1, own), F32),
            shape((1, own), F32),
        ],
        [],
        0.5,
        total,
        other,
    )
    return (grad_images, grad_up, grad_depthwise, grad_gain[0], grad_bias[0])


def solution(mesh):
    placed = (
        P(("shard", "rep"), None, None, None),
        P(("shard", "rep"), None, None, None),
        P("shard", None),
        P("shard"),
        P("shard"),
        P("shard", None),
    )
    return jax.shard_map(
        body,
        mesh=mesh,
        in_specs=placed,
        out_specs=(
            P(("shard", "rep"), None, None, None),
            P("shard", None),
            P("shard", None),
            P("shard"),
            P("shard"),
        ),
        check_vma=False,
    )
```

```python
import functools
import math

import jax
import jax.numpy as jnp
from jax import lax
from jax.experimental import pallas as pl
from jax.experimental.pallas import tpu as pltpu
from jax.sharding import PartitionSpec as P

KS = 7
TAPS = KS * KS
MARGIN = KS // 2
LANES = 128
INNER = 4
NORM_EPS = 1e-06
BF16 = jnp.bfloat16
F32 = jnp.float32
VMEM = pl.BlockSpec(memory_space=pltpu.VMEM)


def params(mebibytes):
    return pltpu.CompilerParams(vmem_limit_bytes=mebibytes * 1024 * 1024)


def gelu_slope(inputs):
    cumulative = 0.5 * (1.0 + lax.erf(inputs * 0.7071067811865476))
    return cumulative + inputs * jnp.exp(-0.5 * inputs * inputs) * 0.3989422804014327


def block_rows(relative, group, line, own, lines):
    if relative:
        place = lax.axis_index("shard") ^ (line * INNER + group)
        return pl.multiple_of(place * own, 16)
    return (group * lines + line) * own


def place_rows(pieces, target, own, relative, cast=None):
    for group, piece in enumerate(pieces):
        lines = piece.shape[0] // own
        if not relative:
            target[group * piece.shape[0] : (group + 1) * piece.shape[0], :] = (
                piece[...] if cast is None else piece[...].astype(cast)
            )
            continue
        for line in range(lines):
            rows = piece[line * own : (line + 1) * own, :]
            start = block_rows(True, group, line, own, lines)
            target[pl.ds(start, own), :] = rows if cast is None else rows.astype(cast)


def split_rows(source, pieces, own, relative):
    for group, piece in enumerate(pieces):
        lines = piece.shape[0] // own
        if not relative:
            piece[...] = source[group * piece.shape[0] : (group + 1) * piece.shape[0], :].astype(
                piece.dtype
            )
            continue
        for line in range(lines):
            start = block_rows(True, group, line, own, lines)
            piece[line * own : (line + 1) * own, :] = source[pl.ds(start, own), :].astype(
                piece.dtype
            )


def correlate(padded, tile, tap_row, height, breadth):
    sums = [None] * height
    for across in range(KS):
        shifted = padded[tile, :, 8 - MARGIN + across : 8 - MARGIN + across + breadth, :]
        for down in range(KS):
            row = tap_row(down, across)
            for line in range(height):
                origin = line + down - MARGIN
                if 0 <= origin < height:
                    term = shifted[origin] * row
                    sums[line] = term if sums[line] is None else sums[line] + term
    return sums


def pack_kernel(w_ref, dw_ref, gain_ref, bias_ref, near_ref, far_ref, turned, wide):
    own, hidden = w_ref.shape
    quarter = hidden // 4
    side = lax.axis_index("rep") % 2
    parity = (lax.axis_index("shard") // INNER) % 2
    turned[...] = jnp.zeros_like(turned)
    turned[TAPS : TAPS + 1, :own] = gain_ref[...].astype(F32)
    turned[TAPS + 1 : TAPS + 2, :own] = bias_ref[...].astype(F32)
    wide[...] = jnp.zeros_like(wide)
    wide[:, :TAPS] = dw_ref[...].astype(F32)
    extras = (wide[...] + turned[...].T[:own]).astype(BF16)
    for ref, which in ((near_ref, parity), (far_ref, 1 - parity)):
        start = pl.multiple_of(side * (2 * quarter) + which * quarter, LANES)
        ref[:, :quarter] = w_ref[:, pl.ds(start, quarter)]
        ref[:, quarter:] = extras


def assemble_kernel(*refs):
    pieces, (weight_ref, extra_ref) = refs[:-2], refs[-2:]
    own = pieces[0].shape[0]
    quarter = weight_ref.shape[1]
    for line, piece in enumerate(pieces):
        weight_ref[line * own : (line + 1) * own, :] = piece[:, :quarter]
        extra_ref[line * own : (line + 1) * own, :] = piece[:, quarter:]


def plane_sum_kernel(lines, *refs):
    pieces, small, outs = refs[:INNER], refs[INNER : 2 * INNER], refs[2 * INNER :]
    own = pieces[0].shape[0] // lines
    quarter = pieces[0].shape[1]
    for line, out in enumerate(outs):
        rows = slice(line * own, (line + 1) * own)
        for parts, columns in ((pieces, slice(0, quarter)), (small, slice(quarter, None))):
            total = parts[0][rows, :]
            for part in parts[1:]:
                total = total + part[rows, :].astype(F32)
            out[:, columns] = total.astype(out.dtype)


def line_sum_kernel(*refs):
    pieces, total_ref = refs[:-1], refs[-1]
    quarter = pieces[0].shape[1] - LANES
    same, cross = pieces[0][...], None
    for line, piece in enumerate(pieces):
        if line % 2:
            cross = piece[...].astype(F32) if cross is None else cross + piece[...].astype(F32)
        elif line:
            same = same + piece[...].astype(F32)
    total_ref[:, :quarter] = same[:, :quarter]
    total_ref[:, quarter : 2 * quarter] = cross[:, :quarter]
    total_ref[:, 2 * quarter :] = same[:, quarter:] + cross[:, quarter:]


def finish_kernel(factor, mine_ref, other_ref, up_ref, dw_ref, gain_ref, bias_ref):
    own, half = mine_ref.shape[0], mine_ref.shape[1] - LANES
    quarter = half // 2
    side = lax.axis_index("rep") % 2
    parity = (lax.axis_index("shard") // INNER) % 2
    for ref, place in ((mine_ref, side), (other_ref, 1 - side)):
        for which, low in ((parity, 0), (1 - parity, quarter)):
            start = pl.multiple_of(place * half + which * quarter, LANES)
            up_ref[:, pl.ds(start, quarter)] = ref[:, low : low + quarter] * factor
    sums = (mine_ref[:, half:] + other_ref[:, half:]) * factor
    dw_ref[...] = sums[:, :TAPS]
    turned = sums.T
    gain_ref[...] = turned[TAPS : TAPS + 1, :]
    bias_ref[...] = turned[TAPS + 1 : TAPS + 2, :]


def conv_norm_kernel(relative, own, *refs):
    small = refs[:INNER]
    sources = refs[INNER : INNER + 2]
    x_ref = sources[0]
    normed_ref, white_ref, inv_ref, taps_ref, gathered, padded, conv = refs[INNER + 2 :]
    height, breadth, depth = x_ref.shape[1:]
    tiles = depth // LANES
    pixels = height * breadth
    place_rows(small, gathered, own, relative, F32)
    padded[...] = jnp.zeros_like(padded)
    for tile in range(tiles):
        lanes = slice(tile * LANES, (tile + 1) * LANES)
        taps_ref[tile] = gathered[lanes, :].T

    for image, source in enumerate(sources):
        for tile in range(tiles):
            lanes = slice(tile * LANES, (tile + 1) * LANES)
            padded[tile, :, 8 : 8 + breadth, :] = source[0, :, :, lanes].astype(F32)

        def one_tile(tile, carry):
            sums = correlate(
                padded,
                tile,
                lambda down, across: taps_ref[tile, pl.ds(down * KS + across, 1), :],
                height,
                breadth,
            )
            for line in range(height):
                conv[tile, line * breadth : (line + 1) * breadth, :] = sums[line]
            return carry

        lax.fori_loop(0, tiles, one_tile, 0)
        total = conv[0]
        for tile in range(1, tiles):
            total = total + conv[tile]
        average = jnp.sum(total, axis=-1, keepdims=True) / depth
        squares = None
        for tile in range(tiles):
            centered = conv[tile] - average
            squares = centered * centered if squares is None else squares + centered * centered
        variance = jnp.sum(squares, axis=-1, keepdims=True) / depth
        inv_std = lax.rsqrt(variance + NORM_EPS)
        rows = slice(image * pixels, (image + 1) * pixels)
        inv_ref[rows, :] = jnp.broadcast_to(inv_std, (pixels, LANES))
        for tile in range(tiles):
            lanes = slice(tile * LANES, (tile + 1) * LANES)
            whitened = (conv[tile] - average) * inv_std
            white_ref[rows, lanes] = whitened
            gain = taps_ref[tile, TAPS : TAPS + 1, :]
            bias = taps_ref[tile, TAPS + 1 : TAPS + 2, :]
            normed_ref[rows, lanes] = (whitened * gain + bias).astype(BF16)


def cot_pack_kernel(cot_ref, across_ref, sibling_ref):
    half = sibling_ref.shape[1]
    quarter = half // 2
    side = lax.axis_index("rep") % 2
    parity = (lax.axis_index("shard") // INNER) % 2
    for place in range(2):
        start = pl.multiple_of(place * half + (1 - parity) * quarter, LANES)
        across_ref[:, place * quarter : (place + 1) * quarter] = cot_ref[:, pl.ds(start, quarter)]
    sibling_ref[...] = cot_ref[:, pl.ds(pl.multiple_of((1 - side) * half, LANES), half)]


def order_kernel(relative, own, *refs):
    place_rows(refs[:INNER], refs[INNER], own, relative)


def project_kernel(relative, own, *refs):
    weight, n_own, n_sibling, cot_ref, sibling_ref, across_ref, corner_ref = refs[:7]
    pieces = refs[7 : 7 + INNER]
    gp_ref, normed, cot, grad = refs[7 + INNER :]
    pixels, half = sibling_ref.shape
    quarter = half // 2
    side = lax.axis_index("rep") % 2
    parity = (lax.axis_index("shard") // INNER) % 2
    normed[: 2 * pixels, :] = n_own[...]
    normed[2 * pixels :, :] = n_sibling[...]
    start = pl.multiple_of(side * half + parity * quarter, LANES)
    cot[:pixels, :] = cot_ref[:, pl.ds(start, quarter)]
    start = pl.multiple_of(side * quarter, LANES)
    cot[pixels : 2 * pixels, :] = across_ref[:, pl.ds(start, quarter)]
    start = pl.multiple_of(parity * quarter, LANES)
    cot[2 * pixels : 3 * pixels, :] = sibling_ref[:, pl.ds(start, quarter)]
    start = pl.multiple_of(side * quarter, LANES)
    cot[3 * pixels :, :] = corner_ref[:, pl.ds(start, quarter)]
    for start in range(0, quarter, LANES):
        columns = slice(start, start + LANES)
        pre_act = jnp.dot(normed[...], weight[:, columns], preferred_element_type=F32)
        gp_ref[:, columns] = (cot[:, columns].astype(F32) * gelu_slope(pre_act)).astype(BF16)
    grad[...] = lax.dot_general(
        normed[...], gp_ref[...], (((0,), (0,)), ((), ())), preferred_element_type=F32
    )
    split_rows(grad, pieces, own, relative)


def back_project_kernel(weight, gp_ref, own_ref, other_ref):
    rows = own_ref.shape[0]
    grad_normed = lax.dot_general(
        gp_ref[...], weight[...], (((1,), (1,)), ((), ())), preferred_element_type=F32
    )
    own_ref[...] = grad_normed[:rows]
    other_ref[...] = grad_normed[rows:]


def norm_back_kernel(relative, own, *refs):
    gn_own, gn_other, white_ref, inv_ref, taps_ref, x_ref, far_ref = refs[:7]
    pieces = refs[7 : 7 + INNER]
    grad_ref, sent_ref, padded, grads_ref, rows, small = refs[7 + INNER :]
    height, breadth, depth = x_ref.shape[1:]
    tiles = depth // LANES
    pixels = height * breadth
    padded[...] = jnp.zeros_like(padded)
    rows[...] = jnp.zeros_like(rows)
    for image, source in enumerate((x_ref, far_ref)):
        span = slice(image * pixels, (image + 1) * pixels)
        first = None
        second = None
        for tile in range(tiles):
            lanes = slice(tile * LANES, (tile + 1) * LANES)
            padded[image, tile, :, 8 : 8 + breadth, :] = source[0, :, :, lanes].astype(F32)
            grad_normed = gn_own[span, lanes] + gn_other[span, lanes]
            whitened = white_ref[span, lanes]
            product = grad_normed * whitened
            gain = taps_ref[tile, TAPS : TAPS + 1, :]
            rows[tile, TAPS : TAPS + 1, :] += jnp.sum(product, axis=0, keepdims=True)
            rows[tile, TAPS + 1 : TAPS + 2, :] += jnp.sum(grad_normed, axis=0, keepdims=True)
            one, two = grad_normed * gain, product * gain
            first = one if first is None else first + one
            second = two if second is None else second + two
        mean_first = jnp.sum(first, axis=-1, keepdims=True) / depth
        mean_second = jnp.sum(second, axis=-1, keepdims=True) / depth
        for tile in range(tiles):
            lanes = slice(tile * LANES, (tile + 1) * LANES)
            gain = taps_ref[tile, TAPS : TAPS + 1, :]
            grad_white = (gn_own[span, lanes] + gn_other[span, lanes]) * gain
            grad_conv = inv_ref[span, :] * (
                grad_white - mean_first - white_ref[span, lanes] * mean_second
            )
            grad_conv = grad_conv.reshape(height, breadth, LANES)
            grads_ref[image, tile] = grad_conv
            if image == 0:
                grad_ref[tile] = grad_conv
            else:
                sent_ref[tile] = grad_conv.astype(BF16)

    def one_tile(tile, carry):
        grads = [[grads_ref[image, tile, line] for line in range(height)] for image in range(2)]
        for across in range(KS):
            columns = slice(8 - MARGIN + across, 8 - MARGIN + across + breadth)
            shifted = [padded[image, tile, :, columns, :] for image in range(2)]
            for down in range(KS):
                total = None
                for image in range(2):
                    for line in range(height):
                        origin = line + down - MARGIN
                        if 0 <= origin < height:
                            term = grads[image][line] * shifted[image][origin]
                            total = term if total is None else total + term
                rows[tile, pl.ds(down * KS + across, 1), :] = jnp.sum(total, axis=0, keepdims=True)
        return carry

    lax.fori_loop(0, tiles, one_tile, 0)
    for tile in range(tiles):
        small[tile * LANES : (tile + 1) * LANES, :] = rows[tile].T
    split_rows(small, pieces, own, relative)


def conv_back_kernel(grad_ref, other_ref, taps_ref, out_ref, padded):
    tiles, height, breadth, _ = grad_ref.shape
    padded[...] = jnp.zeros_like(padded)
    padded[:, :, 8 : 8 + breadth, :] = grad_ref[...] + other_ref[...].astype(F32)

    def one_tile(tile, carry):
        sums = correlate(
            padded,
            tile,
            lambda down, across: taps_ref[tile, pl.ds(TAPS - 1 - down * KS - across, 1), :],
            height,
            breadth,
        )
        start = pl.multiple_of(tile * LANES, LANES)
        for line in range(height):
            out_ref[0, line, :, pl.ds(start, LANES)] = sums[line].astype(BF16)
        return carry

    lax.fori_loop(0, tiles, one_tile, 0)


def call(kernel, name, outs, scratch, micros, *args, mebibytes=48):
    flops = int(micros * 1.1e9)
    moved = sum(math.prod(a.shape) * a.dtype.itemsize for a in args)
    moved += sum(math.prod(o.shape) * o.dtype.itemsize for o in outs)
    return pl.pallas_call(
        kernel,
        out_shape=outs,
        in_specs=[VMEM] * len(args),
        out_specs=[VMEM] * len(outs),
        scratch_shapes=scratch,
        compiler_params=params(mebibytes),
        cost_estimate=pl.CostEstimate(flops=flops, bytes_accessed=moved, transcendentals=0),
        name=name,
    )(*args)


def body(images, cotangent, depthwise_weight, norm_gain, norm_bias, up_weight):
    shards, reps = lax.axis_size("shard"), lax.axis_size("rep")
    own, hidden = up_weight.shape
    depth = own * shards
    lines = shards // INNER
    half, quarter = hidden // 2, hidden // 4
    height, breadth = images.shape[1:3]
    pixels = height * breadth
    tiles = depth // LANES
    me = lax.axis_index("shard")
    side = lax.axis_index("rep") % 2
    parity = (me // INNER) % 2
    relative = own % 16 == 0

    def over_shard(array, flip):
        return lax.ppermute(array, "shard", [(i, i ^ flip) for i in range(shards)])

    def over_core(array):
        return lax.ppermute(array, "rep", [(i, i ^ 1) for i in range(reps)])

    def true_order(pieces):
        if relative:
            return pieces
        stacked = jnp.stack(pieces).reshape(shards, own, -1)
        flips = jnp.arange(shards) ^ me
        places = (flips % INNER) * lines + flips // INNER
        return list(jnp.take(stacked, places, axis=0).reshape(INNER, lines * own, -1))

    def relative_order(pieces):
        if relative:
            return pieces
        stacked = jnp.concatenate([p.astype(F32) for p in pieces]).reshape(shards, own, -1)
        flips = (jnp.arange(lines)[None, :] * INNER + jnp.arange(INNER)[:, None]).reshape(-1)
        moved = jnp.take(stacked, flips ^ me, axis=0).reshape(INNER, lines * own, -1)
        return [moved[0]] + [moved[i].astype(BF16) for i in range(1, INNER)]

    shape = jax.ShapeDtypeStruct
    near, far = call(
        pack_kernel,
        "pack",
        [shape((own, quarter + LANES), BF16)] * 2,
        [
            pltpu.VMEM((LANES, LANES), F32),
            pltpu.VMEM((own, LANES), F32),
        ],
        0.5,
        up_weight,
        depthwise_weight,
        norm_gain[None, :],
        norm_bias[None, :],
        mebibytes=63,
    )
    near, far, images, cotangent = lax.optimization_barrier((near, far, images, cotangent))
    gathered = [near] + [
        over_shard(far if line % 2 else near, INNER * line) for line in range(1, lines)
    ]
    cotangent = cotangent.reshape(pixels, hidden)
    cot_across, cot_sibling = call(
        cot_pack_kernel,
        "cot_pack",
        [shape((pixels, half), BF16)] * 2,
        [],
        0.4,
        cotangent,
    )
    cot_across, cot_sibling = over_shard(cot_across, INNER), over_core(cot_sibling)
    images_far = over_shard(images, INNER)

    rows = lines * own
    weight_lines, extra_lines = call(
        assemble_kernel,
        "assemble",
        [shape((rows, quarter), BF16), shape((rows, LANES), BF16)],
        [],
        2.0,
        *gathered,
    )
    weights = [weight_lines] + [over_shard(weight_lines, flip) for flip in range(1, INNER)]
    extras = [extra_lines] + [over_shard(extra_lines, flip) for flip in range(1, INNER)]
    weights, extras = true_order(weights), true_order(extras)
    (weight,) = call(
        functools.partial(order_kernel, relative, own),
        "order",
        [shape((depth, quarter), BF16)],
        [],
        3.0,
        *weights,
    )

    padded = pltpu.VMEM((tiles, height, breadth + 16, LANES), F32)
    normed, whitened, inv_std, taps = call(
        functools.partial(conv_norm_kernel, relative, own),
        "conv_norm",
        [
            shape((2 * pixels, depth), BF16),
            shape((2 * pixels, depth), F32),
            shape((2 * pixels, LANES), F32),
            shape((tiles, LANES, LANES), F32),
        ],
        [
            pltpu.VMEM((depth, LANES), F32),
            padded,
            pltpu.VMEM((tiles, pixels, LANES), F32),
        ],
        0.1,
        *extras,
        images,
        images_far,
    )
    normed, cot_across = lax.optimization_barrier((normed, cot_across))
    normed_sibling, cot_corner = over_core(normed), over_core(cot_across)
    *pieces, grad_pre = call(
        functools.partial(project_kernel, relative, own),
        "project",
        [shape((rows, quarter), F32)]
        + [shape((rows, quarter), BF16)] * (INNER - 1)
        + [shape((4 * pixels, quarter), BF16)],
        [
            pltpu.VMEM((4 * pixels, depth), BF16),
            pltpu.VMEM((4 * pixels, quarter), BF16),
            pltpu.VMEM((depth, quarter), F32),
        ],
        1.6,
        weight,
        normed,
        normed_sibling,
        cotangent,
        cot_sibling,
        cot_across,
        cot_corner,
    )
    gn_kept, gn_sent = call(
        back_project_kernel,
        "back_project",
        [shape((2 * pixels, depth), F32)] * 2,
        [],
        0.7,
        weight,
        grad_pre,
    )
    pieces = relative_order(pieces)
    arrived = [over_shard(piece, flip) for flip, piece in enumerate(pieces) if flip]
    *small, grad_conv, grad_sent = call(
        functools.partial(norm_back_kernel, relative, own),
        "norm_back",
        [shape((rows, LANES), F32)]
        + [shape((rows, LANES), BF16)] * (INNER - 1)
        + [
            shape((tiles, height, breadth, LANES), F32),
            shape((tiles, height, breadth, LANES), BF16),
        ],
        [
            pltpu.VMEM((2, tiles, height, breadth + 16, LANES), F32),
            pltpu.VMEM((2, tiles, height, breadth, LANES), F32),
            pltpu.VMEM((tiles, LANES, LANES), F32),
            pltpu.VMEM((depth, LANES), F32),
        ],
        0.1,
        gn_kept,
        over_core(gn_sent),
        whitened,
        inv_std,
        taps,
        images,
        images_far,
    )
    small = relative_order(small)
    small_arrived = [over_shard(piece, flip) for flip, piece in enumerate(small) if flip]
    grad_other = over_shard(grad_sent, INNER)
    (grad_images,) = call(
        conv_back_kernel,
        "conv_back",
        [shape(images.shape, BF16)],
        [padded],
        1.9,
        grad_conv,
        grad_other,
        taps,
    )

    home, *sent = call(
        functools.partial(plane_sum_kernel, lines),
        "plane_sum",
        [shape((own, quarter + LANES), F32)] + [shape((own, quarter + LANES), BF16)] * (lines - 1),
        [],
        0.4,
        pieces[0],
        *arrived,
        small[0],
        *small_arrived,
    )
    home, grad_images = lax.optimization_barrier((home, grad_images))
    came = [over_shard(piece, INNER * line) for line, piece in enumerate(sent, 1)]
    (total,) = call(
        line_sum_kernel,
        "line_sum",
        [shape((own, half + LANES), F32)],
        [],
        0.3,
        home,
        *came,
    )
    if reps > 2:
        groups = [[i for i in range(reps) if i % 2 == s] for s in range(2)]
        total = lax.psum(total, "rep", axis_index_groups=groups)
    other = over_core(total)
    factor = 1.0 / math.sqrt(images.shape[0] * pixels * shards * reps)
    grad_up, grad_depthwise, grad_gain, grad_bias = call(
        functools.partial(finish_kernel, factor),
        "finish",
        [
            shape((own, hidden), F32),
            shape((own, TAPS), F32),
            shape((1, own), F32),
            shape((1, own), F32),
        ],
        [],
        0.5,
        total,
        other,
    )
    return (grad_images, grad_up, grad_depthwise, grad_gain[0], grad_bias[0])


def solution(mesh):
    placed = (
        P(("shard", "rep"), None, None, None),
        P(("shard", "rep"), None, None, None),
        P("shard", None),
        P("shard"),
        P("shard"),
        P("shard", None),
    )
    return jax.shard_map(
        body,
        mesh=mesh,
        in_specs=placed,
        out_specs=(
            P(("shard", "rep"), None, None, None),
            P("shard", None),
            P("shard", None),
            P("shard"),
            P("shard"),
        ),
        check_vma=False,
    )
```

```python
import functools
import math

import jax
import jax.numpy as jnp
from jax import lax
from jax.experimental import pallas as pl
from jax.experimental.pallas import tpu as pltpu
from jax.sharding import PartitionSpec as P

KS = 7
TAPS = KS * KS
MARGIN = KS // 2
LANES = 128
INNER = 4
NORM_EPS = 1e-06
BF16 = jnp.bfloat16
F32 = jnp.float32
VMEM = pl.BlockSpec(memory_space=pltpu.VMEM)


def params(mebibytes):
    return pltpu.CompilerParams(vmem_limit_bytes=mebibytes * 1024 * 1024)


def gelu_slope(inputs):
    cumulative = 0.5 * (1.0 + lax.erf(inputs * 0.7071067811865476))
    return cumulative + inputs * jnp.exp(-0.5 * inputs * inputs) * 0.3989422804014327


def block_rows(relative, group, line, own, lines):
    if relative:
        place = lax.axis_index("shard") ^ (line * INNER + group)
        return pl.multiple_of(place * own, 16)
    return (group * lines + line) * own


def place_rows(pieces, target, own, relative, cast=None):
    for group, piece in enumerate(pieces):
        lines = piece.shape[0] // own
        if not relative:
            target[group * piece.shape[0] : (group + 1) * piece.shape[0], :] = (
                piece[...] if cast is None else piece[...].astype(cast)
            )
            continue
        for line in range(lines):
            rows = piece[line * own : (line + 1) * own, :]
            start = block_rows(True, group, line, own, lines)
            target[pl.ds(start, own), :] = rows if cast is None else rows.astype(cast)


def split_rows(source, pieces, own, relative):
    for group, piece in enumerate(pieces):
        lines = piece.shape[0] // own
        if not relative:
            piece[...] = source[group * piece.shape[0] : (group + 1) * piece.shape[0], :].astype(
                piece.dtype
            )
            continue
        for line in range(lines):
            start = block_rows(True, group, line, own, lines)
            piece[line * own : (line + 1) * own, :] = source[pl.ds(start, own), :].astype(
                piece.dtype
            )


def correlate(padded, tile, tap_row, height, breadth):
    sums = [None] * height
    for across in range(KS):
        shifted = padded[tile, :, 8 - MARGIN + across : 8 - MARGIN + across + breadth, :]
        for down in range(KS):
            row = tap_row(down, across)
            for line in range(height):
                origin = line + down - MARGIN
                if 0 <= origin < height:
                    term = shifted[origin] * row
                    sums[line] = term if sums[line] is None else sums[line] + term
    return sums


def pack_kernel(w_ref, dw_ref, gain_ref, bias_ref, near_ref, far_ref, turned, wide):
    own, hidden = w_ref.shape
    quarter = hidden // 4
    side = lax.axis_index("rep") % 2
    parity = (lax.axis_index("shard") // INNER) % 2
    turned[...] = jnp.zeros_like(turned)
    turned[TAPS : TAPS + 1, :own] = gain_ref[...].astype(F32)
    turned[TAPS + 1 : TAPS + 2, :own] = bias_ref[...].astype(F32)
    wide[...] = jnp.zeros_like(wide)
    wide[:, :TAPS] = dw_ref[...].astype(F32)
    extras = (wide[...] + turned[...].T[:own]).astype(BF16)
    for ref, which in ((near_ref, parity), (far_ref, 1 - parity)):
        start = pl.multiple_of(side * (2 * quarter) + which * quarter, LANES)
        ref[:, :quarter] = w_ref[:, pl.ds(start, quarter)]
        ref[:, quarter:] = extras


def assemble_kernel(*refs):
    pieces, (weight_ref, extra_ref) = refs[:-2], refs[-2:]
    own = pieces[0].shape[0]
    quarter = weight_ref.shape[1]
    for line, piece in enumerate(pieces):
        weight_ref[line * own : (line + 1) * own, :] = piece[:, :quarter]
        extra_ref[line * own : (line + 1) * own, :] = piece[:, quarter:]


def plane_sum_kernel(lines, *refs):
    pieces, small, outs = refs[:INNER], refs[INNER : 2 * INNER], refs[2 * INNER :]
    own = pieces[0].shape[0] // lines
    quarter = pieces[0].shape[1]
    for line, out in enumerate(outs):
        rows = slice(line * own, (line + 1) * own)
        for parts, columns in ((pieces, slice(0, quarter)), (small, slice(quarter, None))):
            total = parts[0][rows, :]
            for part in parts[1:]:
                total = total + part[rows, :].astype(F32)
            out[:, columns] = total.astype(out.dtype)


def line_sum_kernel(*refs):
    pieces, total_ref = refs[:-1], refs[-1]
    quarter = pieces[0].shape[1] - LANES
    same, cross = pieces[0][...], None
    for line, piece in enumerate(pieces):
        if line % 2:
            cross = piece[...].astype(F32) if cross is None else cross + piece[...].astype(F32)
        elif line:
            same = same + piece[...].astype(F32)
    total_ref[:, :quarter] = same[:, :quarter]
    total_ref[:, quarter : 2 * quarter] = cross[:, :quarter]
    total_ref[:, 2 * quarter :] = same[:, quarter:] + cross[:, quarter:]


def finish_kernel(factor, mine_ref, other_ref, up_ref, dw_ref, gain_ref, bias_ref):
    own, half = mine_ref.shape[0], mine_ref.shape[1] - LANES
    quarter = half // 2
    side = lax.axis_index("rep") % 2
    parity = (lax.axis_index("shard") // INNER) % 2
    for ref, place in ((mine_ref, side), (other_ref, 1 - side)):
        for which, low in ((parity, 0), (1 - parity, quarter)):
            start = pl.multiple_of(place * half + which * quarter, LANES)
            up_ref[:, pl.ds(start, quarter)] = ref[:, low : low + quarter] * factor
    sums = (mine_ref[:, half:] + other_ref[:, half:]) * factor
    dw_ref[...] = sums[:, :TAPS]
    turned = sums.T
    gain_ref[...] = turned[TAPS : TAPS + 1, :]
    bias_ref[...] = turned[TAPS + 1 : TAPS + 2, :]


def conv_norm_kernel(relative, own, *refs):
    small = refs[:INNER]
    sources = refs[INNER : INNER + 2]
    x_ref = sources[0]
    normed_ref, white_ref, inv_ref, taps_ref, gathered, padded, conv = refs[INNER + 2 :]
    height, breadth, depth = x_ref.shape[1:]
    tiles = depth // LANES
    pixels = height * breadth
    place_rows(small, gathered, own, relative, F32)
    padded[...] = jnp.zeros_like(padded)
    for tile in range(tiles):
        lanes = slice(tile * LANES, (tile + 1) * LANES)
        taps_ref[tile] = gathered[lanes, :].T

    for image, source in enumerate(sources):
        for tile in range(tiles):
            lanes = slice(tile * LANES, (tile + 1) * LANES)
            padded[tile, :, 8 : 8 + breadth, :] = source[0, :, :, lanes].astype(F32)

        def one_tile(tile, carry):
            sums = correlate(
                padded,
                tile,
                lambda down, across: taps_ref[tile, pl.ds(down * KS + across, 1), :],
                height,
                breadth,
            )
            for line in range(height):
                conv[tile, line * breadth : (line + 1) * breadth, :] = sums[line]
            return carry

        lax.fori_loop(0, tiles, one_tile, 0)
        total = conv[0]
        for tile in range(1, tiles):
            total = total + conv[tile]
        average = jnp.sum(total, axis=-1, keepdims=True) / depth
        squares = None
        for tile in range(tiles):
            centered = conv[tile] - average
            squares = centered * centered if squares is None else squares + centered * centered
        variance = jnp.sum(squares, axis=-1, keepdims=True) / depth
        inv_std = lax.rsqrt(variance + NORM_EPS)
        rows = slice(image * pixels, (image + 1) * pixels)
        inv_ref[rows, :] = jnp.broadcast_to(inv_std, (pixels, LANES))
        for tile in range(tiles):
            lanes = slice(tile * LANES, (tile + 1) * LANES)
            whitened = (conv[tile] - average) * inv_std
            white_ref[rows, lanes] = whitened
            gain = taps_ref[tile, TAPS : TAPS + 1, :]
            bias = taps_ref[tile, TAPS + 1 : TAPS + 2, :]
            normed_ref[rows, lanes] = (whitened * gain + bias).astype(BF16)


def cot_pack_kernel(cot_ref, across_ref, sibling_ref):
    half = sibling_ref.shape[1]
    quarter = half // 2
    side = lax.axis_index("rep") % 2
    parity = (lax.axis_index("shard") // INNER) % 2
    for place in range(2):
        start = pl.multiple_of(place * half + (1 - parity) * quarter, LANES)
        across_ref[:, place * quarter : (place + 1) * quarter] = cot_ref[:, pl.ds(start, quarter)]
    sibling_ref[...] = cot_ref[:, pl.ds(pl.multiple_of((1 - side) * half, LANES), half)]


def order_kernel(relative, own, *refs):
    place_rows(refs[:INNER], refs[INNER], own, relative)


def project_kernel(relative, own, *refs):
    weight, n_own, n_sibling, cot_ref, sibling_ref, across_ref, corner_ref = refs[:7]
    pieces = refs[7 : 7 + INNER]
    gp_ref, normed, cot, grad = refs[7 + INNER :]
    pixels, half = sibling_ref.shape
    quarter = half // 2
    side = lax.axis_index("rep") % 2
    parity = (lax.axis_index("shard") // INNER) % 2
    normed[: 2 * pixels, :] = n_own[...]
    normed[2 * pixels :, :] = n_sibling[...]
    start = pl.multiple_of(side * half + parity * quarter, LANES)
    cot[:pixels, :] = cot_ref[:, pl.ds(start, quarter)]
    start = pl.multiple_of(side * quarter, LANES)
    cot[pixels : 2 * pixels, :] = across_ref[:, pl.ds(start, quarter)]
    start = pl.multiple_of(parity * quarter, LANES)
    cot[2 * pixels : 3 * pixels, :] = sibling_ref[:, pl.ds(start, quarter)]
    start = pl.multiple_of(side * quarter, LANES)
    cot[3 * pixels :, :] = corner_ref[:, pl.ds(start, quarter)]
    for start in range(0, quarter, LANES):
        columns = slice(start, start + LANES)
        pre_act = jnp.dot(normed[...], weight[:, columns], preferred_element_type=F32)
        gp_ref[:, columns] = (cot[:, columns].astype(F32) * gelu_slope(pre_act)).astype(BF16)
    grad[...] = lax.dot_general(
        normed[...], gp_ref[...], (((0,), (0,)), ((), ())), preferred_element_type=F32
    )
    split_rows(grad, pieces, own, relative)


def back_project_kernel(weight, gp_ref, own_ref, other_ref):
    rows = own_ref.shape[0]
    grad_normed = lax.dot_general(
        gp_ref[...], weight[...], (((1,), (1,)), ((), ())), preferred_element_type=F32
    )
    own_ref[...] = grad_normed[:rows]
    other_ref[...] = grad_normed[rows:]


def norm_back_kernel(relative, own, *refs):
    gn_own, gn_other, white_ref, inv_ref, taps_ref, x_ref, far_ref = refs[:7]
    pieces = refs[7 : 7 + INNER]
    grad_ref, sent_ref, padded, grads_ref, rows, small = refs[7 + INNER :]
    height, breadth, depth = x_ref.shape[1:]
    tiles = depth // LANES
    pixels = height * breadth
    padded[...] = jnp.zeros_like(padded)
    rows[...] = jnp.zeros_like(rows)
    for image, source in enumerate((x_ref, far_ref)):
        span = slice(image * pixels, (image + 1) * pixels)
        first = None
        second = None
        for tile in range(tiles):
            lanes = slice(tile * LANES, (tile + 1) * LANES)
            padded[image, tile, :, 8 : 8 + breadth, :] = source[0, :, :, lanes].astype(F32)
            grad_normed = gn_own[span, lanes] + gn_other[span, lanes]
            whitened = white_ref[span, lanes]
            product = grad_normed * whitened
            gain = taps_ref[tile, TAPS : TAPS + 1, :]
            rows[tile, TAPS : TAPS + 1, :] += jnp.sum(product, axis=0, keepdims=True)
            rows[tile, TAPS + 1 : TAPS + 2, :] += jnp.sum(grad_normed, axis=0, keepdims=True)
            one, two = grad_normed * gain, product * gain
            first = one if first is None else first + one
            second = two if second is None else second + two
        mean_first = jnp.sum(first, axis=-1, keepdims=True) / depth
        mean_second = jnp.sum(second, axis=-1, keepdims=True) / depth
        for tile in range(tiles):
            lanes = slice(tile * LANES, (tile + 1) * LANES)
            gain = taps_ref[tile, TAPS : TAPS + 1, :]
            grad_white = (gn_own[span, lanes] + gn_other[span, lanes]) * gain
            grad_conv = inv_ref[span, :] * (
                grad_white - mean_first - white_ref[span, lanes] * mean_second
            )
            grad_conv = grad_conv.reshape(height, breadth, LANES)
            grads_ref[image, tile] = grad_conv
            if image == 0:
                grad_ref[tile] = grad_conv
            else:
                sent_ref[tile] = grad_conv.astype(BF16)

    def one_tile(tile, carry):
        grads = [[grads_ref[image, tile, line] for line in range(height)] for image in range(2)]
        for across in range(KS):
            columns = slice(8 - MARGIN + across, 8 - MARGIN + across + breadth)
            shifted = [padded[image, tile, :, columns, :] for image in range(2)]
            for down in range(KS):
                total = None
                for image in range(2):
                    for line in range(height):
                        origin = line + down - MARGIN
                        if 0 <= origin < height:
                            term = grads[image][line] * shifted[image][origin]
                            total = term if total is None else total + term
                rows[tile, pl.ds(down * KS + across, 1), :] = jnp.sum(total, axis=0, keepdims=True)
        return carry

    lax.fori_loop(0, tiles, one_tile, 0)
    for tile in range(tiles):
        small[tile * LANES : (tile + 1) * LANES, :] = rows[tile].T
    split_rows(small, pieces, own, relative)


def conv_back_kernel(grad_ref, other_ref, taps_ref, out_ref, padded):
    tiles, height, breadth, _ = grad_ref.shape
    padded[...] = jnp.zeros_like(padded)
    padded[:, :, 8 : 8 + breadth, :] = grad_ref[...] + other_ref[...].astype(F32)

    def one_tile(tile, carry):
        sums = correlate(
            padded,
            tile,
            lambda down, across: taps_ref[tile, pl.ds(TAPS - 1 - down * KS - across, 1), :],
            height,
            breadth,
        )
        start = pl.multiple_of(tile * LANES, LANES)
        for line in range(height):
            out_ref[0, line, :, pl.ds(start, LANES)] = sums[line].astype(BF16)
        return carry

    lax.fori_loop(0, tiles, one_tile, 0)


def call(kernel, name, outs, scratch, micros, *args, mebibytes=48):
    flops = int(micros * 1.1e9)
    moved = sum(math.prod(a.shape) * a.dtype.itemsize for a in args)
    moved += sum(math.prod(o.shape) * o.dtype.itemsize for o in outs)
    return pl.pallas_call(
        kernel,
        out_shape=outs,
        in_specs=[VMEM] * len(args),
        out_specs=[VMEM] * len(outs),
        scratch_shapes=scratch,
        compiler_params=params(mebibytes),
        cost_estimate=pl.CostEstimate(flops=flops, bytes_accessed=moved, transcendentals=0),
        name=name,
    )(*args)


def body(images, cotangent, depthwise_weight, norm_gain, norm_bias, up_weight):
    shards, reps = lax.axis_size("shard"), lax.axis_size("rep")
    own, hidden = up_weight.shape
    depth = own * shards
    lines = shards // INNER
    half, quarter = hidden // 2, hidden // 4
    height, breadth = images.shape[1:3]
    pixels = height * breadth
    tiles = depth // LANES
    me = lax.axis_index("shard")
    side = lax.axis_index("rep") % 2
    parity = (me // INNER) % 2
    relative = own % 16 == 0

    def over_shard(array, flip):
        return lax.ppermute(array, "shard", [(i, i ^ flip) for i in range(shards)])

    def over_core(array):
        return lax.ppermute(array, "rep", [(i, i ^ 1) for i in range(reps)])

    def true_order(pieces):
        if relative:
            return pieces
        stacked = jnp.stack(pieces).reshape(shards, own, -1)
        flips = jnp.arange(shards) ^ me
        places = (flips % INNER) * lines + flips // INNER
        return list(jnp.take(stacked, places, axis=0).reshape(INNER, lines * own, -1))

    def relative_order(pieces):
        if relative:
            return pieces
        stacked = jnp.concatenate([p.astype(F32) for p in pieces]).reshape(shards, own, -1)
        flips = (jnp.arange(lines)[None, :] * INNER + jnp.arange(INNER)[:, None]).reshape(-1)
        moved = jnp.take(stacked, flips ^ me, axis=0).reshape(INNER, lines * own, -1)
        return [moved[0]] + [moved[i].astype(BF16) for i in range(1, INNER)]

    shape = jax.ShapeDtypeStruct
    near, far = call(
        pack_kernel,
        "pack",
        [shape((own, quarter + LANES), BF16)] * 2,
        [
            pltpu.VMEM((LANES, LANES), F32),
            pltpu.VMEM((own, LANES), F32),
        ],
        0.5,
        up_weight,
        depthwise_weight,
        norm_gain[None, :],
        norm_bias[None, :],
        mebibytes=63,
    )
    near, far, images, cotangent = lax.optimization_barrier((near, far, images, cotangent))
    gathered = [near] + [
        over_shard(far if line % 2 else near, INNER * line) for line in range(1, lines)
    ]
    cotangent = cotangent.reshape(pixels, hidden)
    cot_across, cot_sibling = call(
        cot_pack_kernel,
        "cot_pack",
        [shape((pixels, half), BF16)] * 2,
        [],
        0.4,
        cotangent,
    )
    cot_across, cot_sibling = over_shard(cot_across, INNER), over_core(cot_sibling)
    images_far = over_shard(images, INNER)

    rows = lines * own
    weight_lines, extra_lines = call(
        assemble_kernel,
        "assemble",
        [shape((rows, quarter), BF16), shape((rows, LANES), BF16)],
        [],
        2.0,
        *gathered,
    )
    weights = [weight_lines] + [over_shard(weight_lines, flip) for flip in range(1, INNER)]
    extras = [extra_lines] + [over_shard(extra_lines, flip) for flip in range(1, INNER)]
    weights, extras = true_order(weights), true_order(extras)
    (weight,) = call(
        functools.partial(order_kernel, relative, own),
        "order",
        [shape((depth, quarter), BF16)],
        [],
        3.0,
        *weights,
    )

    padded = pltpu.VMEM((tiles, height, breadth + 16, LANES), F32)
    normed, whitened, inv_std, taps = call(
        functools.partial(conv_norm_kernel, relative, own),
        "conv_norm",
        [
            shape((2 * pixels, depth), BF16),
            shape((2 * pixels, depth), F32),
            shape((2 * pixels, LANES), F32),
            shape((tiles, LANES, LANES), F32),
        ],
        [
            pltpu.VMEM((depth, LANES), F32),
            padded,
            pltpu.VMEM((tiles, pixels, LANES), F32),
        ],
        0.1,
        *extras,
        images,
        images_far,
    )
    normed, cot_across = lax.optimization_barrier((normed, cot_across))
    normed_sibling, cot_corner = over_core(normed), over_core(cot_across)
    *pieces, grad_pre = call(
        functools.partial(project_kernel, relative, own),
        "project",
        [shape((rows, quarter), F32)]
        + [shape((rows, quarter), BF16)] * (INNER - 1)
        + [shape((4 * pixels, quarter), BF16)],
        [
            pltpu.VMEM((4 * pixels, depth), BF16),
            pltpu.VMEM((4 * pixels, quarter), BF16),
            pltpu.VMEM((depth, quarter), F32),
        ],
        1.6,
        weight,
        normed,
        normed_sibling,
        cotangent,
        cot_sibling,
        cot_across,
        cot_corner,
    )
    gn_kept, gn_sent = call(
        back_project_kernel,
        "back_project",
        [shape((2 * pixels, depth), F32)] * 2,
        [],
        0.7,
        weight,
        grad_pre,
    )
    pieces = relative_order(pieces)
    arrived = [over_shard(piece, flip) for flip, piece in enumerate(pieces) if flip]
    *small, grad_conv, grad_sent = call(
        functools.partial(norm_back_kernel, relative, own),
        "norm_back",
        [shape((rows, LANES), F32)]
        + [shape((rows, LANES), BF16)] * (INNER - 1)
        + [
            shape((tiles, height, breadth, LANES), F32),
            shape((tiles, height, breadth, LANES), BF16),
        ],
        [
            pltpu.VMEM((2, tiles, height, breadth + 16, LANES), F32),
            pltpu.VMEM((2, tiles, height, breadth, LANES), F32),
            pltpu.VMEM((tiles, LANES, LANES), F32),
            pltpu.VMEM((depth, LANES), F32),
        ],
        0.1,
        gn_kept,
        over_core(gn_sent),
        whitened,
        inv_std,
        taps,
        images,
        images_far,
    )
    small = relative_order(small)
    small_arrived = [over_shard(piece, flip) for flip, piece in enumerate(small) if flip]
    grad_other = over_shard(grad_sent, INNER)
    (grad_images,) = call(
        conv_back_kernel,
        "conv_back",
        [shape(images.shape, BF16)],
        [padded],
        0.1,
        grad_conv,
        grad_other,
        taps,
    )

    home, *sent = call(
        functools.partial(plane_sum_kernel, lines),
        "plane_sum",
        [shape((own, quarter + LANES), F32)] + [shape((own, quarter + LANES), BF16)] * (lines - 1),
        [],
        2.0,
        pieces[0],
        *arrived,
        small[0],
        *small_arrived,
    )
    home, grad_images = lax.optimization_barrier((home, grad_images))
    came = [over_shard(piece, INNER * line) for line, piece in enumerate(sent, 1)]
    (total,) = call(
        line_sum_kernel,
        "line_sum",
        [shape((own, half + LANES), F32)],
        [],
        0.3,
        home,
        *came,
    )
    if reps > 2:
        groups = [[i for i in range(reps) if i % 2 == s] for s in range(2)]
        total = lax.psum(total, "rep", axis_index_groups=groups)
    other = over_core(total)
    factor = 1.0 / math.sqrt(images.shape[0] * pixels * shards * reps)
    grad_up, grad_depthwise, grad_gain, grad_bias = call(
        functools.partial(finish_kernel, factor),
        "finish",
        [
            shape((own, hidden), F32),
            shape((own, TAPS), F32),
            shape((1, own), F32),
            shape((1, own), F32),
        ],
        [],
        0.5,
        total,
        other,
    )
    return (grad_images, grad_up, grad_depthwise, grad_gain[0], grad_bias[0])


def solution(mesh):
    placed = (
        P(("shard", "rep"), None, None, None),
        P(("shard", "rep"), None, None, None),
        P("shard", None),
        P("shard"),
        P("shard"),
        P("shard", None),
    )
    return jax.shard_map(
        body,
        mesh=mesh,
        in_specs=placed,
        out_specs=(
            P(("shard", "rep"), None, None, None),
            P("shard", None),
            P("shard", None),
            P("shard"),
            P("shard"),
        ),
        check_vma=False,
    )
```

```python
import functools
import math

import jax
import jax.numpy as jnp
from jax import lax
from jax.experimental import pallas as pl
from jax.experimental.pallas import tpu as pltpu
from jax.sharding import PartitionSpec as P

KS = 7
TAPS = KS * KS
MARGIN = KS // 2
LANES = 128
INNER = 4
NORM_EPS = 1e-06
BF16 = jnp.bfloat16
F32 = jnp.float32
VMEM = pl.BlockSpec(memory_space=pltpu.VMEM)


def params(mebibytes):
    return pltpu.CompilerParams(vmem_limit_bytes=mebibytes * 1024 * 1024)


def gelu_slope(inputs):
    cumulative = 0.5 * (1.0 + lax.erf(inputs * 0.7071067811865476))
    return cumulative + inputs * jnp.exp(-0.5 * inputs * inputs) * 0.3989422804014327


def block_rows(relative, group, line, own, lines):
    if relative:
        place = lax.axis_index("shard") ^ (line * INNER + group)
        return pl.multiple_of(place * own, 16)
    return (group * lines + line) * own


def place_rows(pieces, target, own, relative, cast=None):
    for group, piece in enumerate(pieces):
        lines = piece.shape[0] // own
        if not relative:
            target[group * piece.shape[0] : (group + 1) * piece.shape[0], :] = (
                piece[...] if cast is None else piece[...].astype(cast)
            )
            continue
        for line in range(lines):
            rows = piece[line * own : (line + 1) * own, :]
            start = block_rows(True, group, line, own, lines)
            target[pl.ds(start, own), :] = rows if cast is None else rows.astype(cast)


def split_rows(source, pieces, own, relative):
    for group, piece in enumerate(pieces):
        lines = piece.shape[0] // own
        if not relative:
            piece[...] = source[group * piece.shape[0] : (group + 1) * piece.shape[0], :].astype(
                piece.dtype
            )
            continue
        for line in range(lines):
            start = block_rows(True, group, line, own, lines)
            piece[line * own : (line + 1) * own, :] = source[pl.ds(start, own), :].astype(
                piece.dtype
            )


def correlate(padded, tile, tap_row, height, breadth):
    sums = [None] * height
    for across in range(KS):
        shifted = padded[tile, :, 8 - MARGIN + across : 8 - MARGIN + across + breadth, :]
        for down in range(KS):
            row = tap_row(down, across)
            for line in range(height):
                origin = line + down - MARGIN
                if 0 <= origin < height:
                    term = shifted[origin] * row
                    sums[line] = term if sums[line] is None else sums[line] + term
    return sums


def pack_kernel(w_ref, dw_ref, gain_ref, bias_ref, home_ref, near_ref, far_ref, turned, wide):
    own, hidden = w_ref.shape
    quarter = hidden // 4
    side = lax.axis_index("rep") % 2
    parity = (lax.axis_index("shard") // INNER) % 2
    turned[...] = jnp.zeros_like(turned)
    turned[TAPS : TAPS + 1, :own] = gain_ref[...].astype(F32)
    turned[TAPS + 1 : TAPS + 2, :own] = bias_ref[...].astype(F32)
    wide[...] = jnp.zeros_like(wide)
    wide[:, :TAPS] = dw_ref[...].astype(F32)
    extras = (wide[...] + turned[...].T[:own]).astype(BF16)
    kinds = ((home_ref, side, parity), (near_ref, 1 - side, parity), (far_ref, 1 - side, 1 - parity))
    for ref, place, which in kinds:
        start = pl.multiple_of(place * (2 * quarter) + which * quarter, LANES)
        ref[:, :quarter] = w_ref[:, pl.ds(start, quarter)]
        ref[:, quarter:] = extras


def assemble_kernel(*refs):
    pieces, (weight_ref, extra_ref) = refs[:-2], refs[-2:]
    own = pieces[0].shape[0]
    quarter = weight_ref.shape[1]
    for line, piece in enumerate(pieces):
        weight_ref[line * own : (line + 1) * own, :] = piece[:, :quarter]
    extras = jnp.concatenate([piece[:, quarter:].astype(F32) for piece in pieces], axis=0)
    if extra_ref.shape[0] < extras.shape[0]:
        extras = fold(extras)
    extra_ref[...] = extras.astype(BF16)


def plane_sum_kernel(lines, *refs):
    pieces, small, outs = refs[:INNER], refs[INNER : 2 * INNER], refs[2 * INNER :]
    own = pieces[0].shape[0] // lines
    quarter = pieces[0].shape[1]
    extras = small[0][...]
    for part in small[1:]:
        extras = extras + part[...].astype(F32)
    if extras.shape[0] < pieces[0].shape[0]:
        extras = unfold(extras)
    for line, out in enumerate(outs):
        rows = slice(line * own, (line + 1) * own)
        total = pieces[0][rows, :]
        for part in pieces[1:]:
            total = total + part[rows, :].astype(F32)
        out[:, :quarter] = total.astype(out.dtype)
        out[:, quarter:] = extras[rows, :].astype(out.dtype)


def line_sum_kernel(*refs):
    pieces, total_ref = refs[:-1], refs[-1]
    quarter = pieces[0].shape[1] - LANES
    near, far = None, None
    for line, piece in enumerate(pieces[1:], 1):
        came = piece[...].astype(F32)
        if line % 2:
            far = came if far is None else far + came
        else:
            near = came if near is None else near + came
    total_ref[:, :quarter] = pieces[0][:, :quarter]
    total_ref[:, quarter : 2 * quarter] = near[:, :quarter]
    total_ref[:, 2 * quarter : 3 * quarter] = far[:, :quarter]
    total_ref[:, 3 * quarter :] = pieces[0][:, quarter:] + near[:, quarter:] + far[:, quarter:]


def finish_kernel(factor, mine_ref, other_ref, up_ref, dw_ref, gain_ref, bias_ref):
    own, quarter = mine_ref.shape[0], (mine_ref.shape[1] - LANES) // 3
    side = lax.axis_index("rep") % 2
    parity = (lax.axis_index("shard") // INNER) % 2
    for place, home, came in ((side, mine_ref, other_ref), (1 - side, other_ref, mine_ref)):
        start = pl.multiple_of((2 * place + parity) * quarter, LANES)
        total = home[:, :quarter] + came[:, quarter : 2 * quarter]
        up_ref[:, pl.ds(start, quarter)] = total * factor
        start = pl.multiple_of((2 * place + 1 - parity) * quarter, LANES)
        up_ref[:, pl.ds(start, quarter)] = came[:, 2 * quarter : 3 * quarter] * factor
    low = 3 * quarter
    sums = (mine_ref[:, low:] + other_ref[:, low:]) * factor
    dw_ref[...] = sums[:, :TAPS]
    turned = sums.T
    gain_ref[...] = turned[TAPS : TAPS + 1, :]
    bias_ref[...] = turned[TAPS + 1 : TAPS + 2, :]


def fold(rows):
    half = rows.shape[0] // 2
    low = lax.broadcasted_iota(jnp.int32, (half, LANES), 1) < LANES // 2
    return jnp.where(low, rows[:half], pltpu.roll(rows[half:], LANES // 2, 1))


def unfold(rows):
    return jnp.concatenate([rows, pltpu.roll(rows, LANES // 2, 1)], axis=0)


def conv_norm_kernel(relative, own, *refs):
    small = refs[:INNER]
    sources = refs[INNER : INNER + 2]
    x_ref = sources[0]
    normed_ref, white_ref, inv_ref, taps_ref, gathered, unfolded, padded, conv = refs[INNER + 2 :]
    height, breadth, depth = x_ref.shape[1:]
    tiles = depth // LANES
    pixels = height * breadth
    if relative:
        for group, piece in enumerate(small):
            unfolded[group * 2 * piece.shape[0] : (group + 1) * 2 * piece.shape[0], :] = unfold(
                piece[...].astype(F32)
            )
        count = unfolded.shape[0] // INNER
        small = [unfolded.at[pl.ds(group * count, count), :] for group in range(INNER)]
    place_rows(small, gathered, own, relative, F32)
    padded[...] = jnp.zeros_like(padded)
    for tile in range(tiles):
        lanes = slice(tile * LANES, (tile + 1) * LANES)
        taps_ref[tile] = gathered[lanes, :].T

    for image, source in enumerate(sources):
        for tile in range(tiles):
            lanes = slice(tile * LANES, (tile + 1) * LANES)
            padded[tile, :, 8 : 8 + breadth, :] = source[0, :, :, lanes].astype(F32)

        def one_tile(tile, carry):
            sums = correlate(
                padded,
                tile,
                lambda down, across: taps_ref[tile, pl.ds(down * KS + across, 1), :],
                height,
                breadth,
            )
            for line in range(height):
                conv[tile, line * breadth : (line + 1) * breadth, :] = sums[line]
            return carry

        lax.fori_loop(0, tiles, one_tile, 0)
        total = conv[0]
        for tile in range(1, tiles):
            total = total + conv[tile]
        average = jnp.sum(total, axis=-1, keepdims=True) / depth
        squares = None
        for tile in range(tiles):
            centered = conv[tile] - average
            squares = centered * centered if squares is None else squares + centered * centered
        variance = jnp.sum(squares, axis=-1, keepdims=True) / depth
        inv_std = lax.rsqrt(variance + NORM_EPS)
        rows = slice(image * pixels, (image + 1) * pixels)
        inv_ref[rows, :] = jnp.broadcast_to(inv_std, (pixels, LANES))
        for tile in range(tiles):
            lanes = slice(tile * LANES, (tile + 1) * LANES)
            whitened = (conv[tile] - average) * inv_std
            white_ref[rows, lanes] = whitened
            gain = taps_ref[tile, TAPS : TAPS + 1, :]
            bias = taps_ref[tile, TAPS + 1 : TAPS + 2, :]
            normed_ref[rows, lanes] = (whitened * gain + bias).astype(BF16)


def cot_pack_kernel(cot_ref, across_ref, sibling_ref):
    half = sibling_ref.shape[1]
    quarter = half // 2
    side = lax.axis_index("rep") % 2
    parity = (lax.axis_index("shard") // INNER) % 2
    for place in range(2):
        start = pl.multiple_of(place * half + (1 - parity) * quarter, LANES)
        across_ref[:, place * quarter : (place + 1) * quarter] = cot_ref[:, pl.ds(start, quarter)]
    sibling_ref[...] = cot_ref[:, pl.ds(pl.multiple_of((1 - side) * half, LANES), half)]


def order_kernel(relative, own, *refs):
    place_rows(refs[:INNER], refs[INNER], own, relative)


def project_kernel(relative, own, *refs):
    weight, n_own, n_sibling, cot_ref, sibling_ref, across_ref, corner_ref = refs[:7]
    pieces = refs[7 : 7 + INNER]
    gp_ref, normed, cot, grad = refs[7 + INNER :]
    pixels, half = sibling_ref.shape
    quarter = half // 2
    side = lax.axis_index("rep") % 2
    parity = (lax.axis_index("shard") // INNER) % 2
    normed[: 2 * pixels, :] = n_own[...]
    normed[2 * pixels :, :] = n_sibling[...]
    start = pl.multiple_of(side * half + parity * quarter, LANES)
    cot[:pixels, :] = cot_ref[:, pl.ds(start, quarter)]
    start = pl.multiple_of(side * quarter, LANES)
    cot[pixels : 2 * pixels, :] = across_ref[:, pl.ds(start, quarter)]
    start = pl.multiple_of(parity * quarter, LANES)
    cot[2 * pixels : 3 * pixels, :] = sibling_ref[:, pl.ds(start, quarter)]
    start = pl.multiple_of(side * quarter, LANES)
    cot[3 * pixels :, :] = corner_ref[:, pl.ds(start, quarter)]
    for start in range(0, quarter, LANES):
        columns = slice(start, start + LANES)
        pre_act = jnp.dot(normed[...], weight[:, columns], preferred_element_type=F32)
        gp_ref[:, columns] = (cot[:, columns].astype(F32) * gelu_slope(pre_act)).astype(BF16)
    grad[...] = lax.dot_general(
        normed[...], gp_ref[...], (((0,), (0,)), ((), ())), preferred_element_type=F32
    )
    split_rows(grad, pieces, own, relative)


def back_project_kernel(weight, gp_ref, own_ref, other_ref):
    rows = own_ref.shape[0]
    grad_normed = lax.dot_general(
        gp_ref[...], weight[...], (((1,), (1,)), ((), ())), preferred_element_type=F32
    )
    own_ref[...] = grad_normed[:rows]
    other_ref[...] = grad_normed[rows:]


def norm_back_kernel(relative, own, *refs):
    gn_own, gn_other, white_ref, inv_ref, taps_ref, x_ref, far_ref = refs[:7]
    pieces = refs[7 : 7 + INNER]
    grad_ref, sent_ref, padded, grads_ref, rows, small, unfolded = refs[7 + INNER :]
    height, breadth, depth = x_ref.shape[1:]
    tiles = depth // LANES
    pixels = height * breadth
    padded[...] = jnp.zeros_like(padded)
    rows[...] = jnp.zeros_like(rows)
    for image, source in enumerate((x_ref, far_ref)):
        span = slice(image * pixels, (image + 1) * pixels)
        first = None
        second = None
        for tile in range(tiles):
            lanes = slice(tile * LANES, (tile + 1) * LANES)
            padded[image, tile, :, 8 : 8 + breadth, :] = source[0, :, :, lanes].astype(F32)
            grad_normed = gn_own[span, lanes] + gn_other[span, lanes]
            whitened = white_ref[span, lanes]
            product = grad_normed * whitened
            gain = taps_ref[tile, TAPS : TAPS + 1, :]
            rows[tile, TAPS : TAPS + 1, :] += jnp.sum(product, axis=0, keepdims=True)
            rows[tile, TAPS + 1 : TAPS + 2, :] += jnp.sum(grad_normed, axis=0, keepdims=True)
            one, two = grad_normed * gain, product * gain
            first = one if first is None else first + one
            second = two if second is None else second + two
        mean_first = jnp.sum(first, axis=-1, keepdims=True) / depth
        mean_second = jnp.sum(second, axis=-1, keepdims=True) / depth
        for tile in range(tiles):
            lanes = slice(tile * LANES, (tile + 1) * LANES)
            gain = taps_ref[tile, TAPS : TAPS + 1, :]
            grad_white = (gn_own[span, lanes] + gn_other[span, lanes]) * gain
            grad_conv = inv_ref[span, :] * (
                grad_white - mean_first - white_ref[span, lanes] * mean_second
            )
            grad_conv = grad_conv.reshape(height, breadth, LANES)
            grads_ref[image, tile] = grad_conv
            if image == 0:
                grad_ref[tile] = grad_conv
            else:
                sent_ref[tile] = grad_conv.astype(BF16)

    def one_tile(tile, carry):
        grads = [[grads_ref[image, tile, line] for line in range(height)] for image in range(2)]
        for across in range(KS):
            columns = slice(8 - MARGIN + across, 8 - MARGIN + across + breadth)
            shifted = [padded[image, tile, :, columns, :] for image in range(2)]
            for down in range(KS):
                total = None
                for image in range(2):
                    for line in range(height):
                        origin = line + down - MARGIN
                        if 0 <= origin < height:
                            term = grads[image][line] * shifted[image][origin]
                            total = term if total is None else total + term
                rows[tile, pl.ds(down * KS + across, 1), :] = jnp.sum(total, axis=0, keepdims=True)
        return carry

    lax.fori_loop(0, tiles, one_tile, 0)
    for tile in range(tiles):
        small[tile * LANES : (tile + 1) * LANES, :] = rows[tile].T
    if relative:
        whole = [unfolded.at[group] for group in range(INNER)]
        split_rows(small, whole, own, relative)
        for source, piece in zip(whole, pieces):
            piece[...] = fold(source[...]).astype(piece.dtype)
    else:
        split_rows(small, pieces, own, relative)


def conv_back_kernel(grad_ref, other_ref, taps_ref, out_ref, padded):
    tiles, height, breadth, _ = grad_ref.shape
    padded[...] = jnp.zeros_like(padded)
    padded[:, :, 8 : 8 + breadth, :] = grad_ref[...] + other_ref[...].astype(F32)

    def one_tile(tile, carry):
        sums = correlate(
            padded,
            tile,
            lambda down, across: taps_ref[tile, pl.ds(TAPS - 1 - down * KS - across, 1), :],
            height,
            breadth,
        )
        start = pl.multiple_of(tile * LANES, LANES)
        for line in range(height):
            out_ref[0, line, :, pl.ds(start, LANES)] = sums[line].astype(BF16)
        return carry

    lax.fori_loop(0, tiles, one_tile, 0)


def call(kernel, name, outs, scratch, micros, *args, mebibytes=48):
    flops = int(micros * 1.1e9)
    moved = sum(math.prod(a.shape) * a.dtype.itemsize for a in args)
    moved += sum(math.prod(o.shape) * o.dtype.itemsize for o in outs)
    return pl.pallas_call(
        kernel,
        out_shape=outs,
        in_specs=[VMEM] * len(args),
        out_specs=[VMEM] * len(outs),
        scratch_shapes=scratch,
        compiler_params=params(mebibytes),
        cost_estimate=pl.CostEstimate(flops=flops, bytes_accessed=moved, transcendentals=0),
        name=name,
    )(*args)


def body(images, cotangent, depthwise_weight, norm_gain, norm_bias, up_weight):
    shards, reps = lax.axis_size("shard"), lax.axis_size("rep")
    own, hidden = up_weight.shape
    depth = own * shards
    lines = shards // INNER
    half, quarter = hidden // 2, hidden // 4
    height, breadth = images.shape[1:3]
    pixels = height * breadth
    tiles = depth // LANES
    me = lax.axis_index("shard")
    side = lax.axis_index("rep") % 2
    parity = (me // INNER) % 2
    relative = own % 16 == 0

    def over_shard(array, flip):
        return lax.ppermute(array, "shard", [(i, i ^ flip) for i in range(shards)])

    def crossing(array, flip):
        pairs = [
            (i * reps + r, (i ^ flip) * reps + (r ^ 1)) for i in range(shards) for r in range(reps)
        ]
        return lax.ppermute(array, ("shard", "rep"), pairs)

    def over_core(array):
        return lax.ppermute(array, "rep", [(i, i ^ 1) for i in range(reps)])

    def true_order(pieces):
        if relative:
            return pieces
        stacked = jnp.stack(pieces).reshape(shards, own, -1)
        flips = jnp.arange(shards) ^ me
        places = (flips % INNER) * lines + flips // INNER
        return list(jnp.take(stacked, places, axis=0).reshape(INNER, lines * own, -1))

    def relative_order(pieces):
        if relative:
            return pieces
        stacked = jnp.concatenate([p.astype(F32) for p in pieces]).reshape(shards, own, -1)
        flips = (jnp.arange(lines)[None, :] * INNER + jnp.arange(INNER)[:, None]).reshape(-1)
        moved = jnp.take(stacked, flips ^ me, axis=0).reshape(INNER, lines * own, -1)
        return [moved[0]] + [moved[i].astype(BF16) for i in range(1, INNER)]

    shape = jax.ShapeDtypeStruct
    home, near, far = call(
        pack_kernel,
        "pack",
        [shape((own, quarter + LANES), BF16)] * 3,
        [
            pltpu.VMEM((LANES, LANES), F32),
            pltpu.VMEM((own, LANES), F32),
        ],
        0.5,
        up_weight,
        depthwise_weight,
        norm_gain[None, :],
        norm_bias[None, :],
        mebibytes=63,
    )
    home, near, far, images, cotangent = lax.optimization_barrier(
        (home, near, far, images, cotangent)
    )
    gathered = [home] + [
        crossing(far if line % 2 else near, INNER * line) for line in range(1, lines)
    ]
    cotangent = cotangent.reshape(pixels, hidden)
    cot_across, cot_sibling = call(
        cot_pack_kernel,
        "cot_pack",
        [shape((pixels, half), BF16)] * 2,
        [],
        0.4,
        cotangent,
    )
    cot_across, cot_sibling = crossing(cot_across, INNER), over_core(cot_sibling)
    images_far = crossing(images, INNER)

    rows = lines * own
    folded = rows // 2 if relative else rows
    weight_lines, extra_lines = call(
        assemble_kernel,
        "assemble",
        [shape((rows, quarter), BF16), shape((folded, LANES), BF16)],
        [],
        2.0,
        *gathered,
    )
    weights = [weight_lines] + [over_shard(weight_lines, flip) for flip in range(1, INNER)]
    extras = [extra_lines] + [crossing(extra_lines, flip) for flip in range(1, INNER)]
    weights, extras = true_order(weights), true_order(extras)
    (weight,) = call(
        functools.partial(order_kernel, relative, own),
        "order",
        [shape((depth, quarter), BF16)],
        [],
        3.0,
        *weights,
    )

    padded = pltpu.VMEM((tiles, height, breadth + 16, LANES), F32)
    normed, whitened, inv_std, taps = call(
        functools.partial(conv_norm_kernel, relative, own),
        "conv_norm",
        [
            shape((2 * pixels, depth), BF16),
            shape((2 * pixels, depth), F32),
            shape((2 * pixels, LANES), F32),
            shape((tiles, LANES, LANES), F32),
        ],
        [
            pltpu.VMEM((depth, LANES), F32),
            pltpu.VMEM((depth, LANES), F32),
            padded,
            pltpu.VMEM((tiles, pixels, LANES), F32),
        ],
        0.1,
        *extras,
        images,
        images_far,
    )
    normed, cot_across = lax.optimization_barrier((normed, cot_across))
    normed_sibling, cot_corner = over_core(normed), over_core(cot_across)
    *pieces, grad_pre = call(
        functools.partial(project_kernel, relative, own),
        "project",
        [shape((rows, quarter), F32)]
        + [shape((rows, quarter), BF16)] * (INNER - 1)
        + [shape((4 * pixels, quarter), BF16)],
        [
            pltpu.VMEM((4 * pixels, depth), BF16),
            pltpu.VMEM((4 * pixels, quarter), BF16),
            pltpu.VMEM((depth, quarter), F32),
        ],
        1.6,
        weight,
        normed,
        normed_sibling,
        cotangent,
        cot_sibling,
        cot_across,
        cot_corner,
    )
    gn_kept, gn_sent = call(
        back_project_kernel,
        "back_project",
        [shape((2 * pixels, depth), F32)] * 2,
        [],
        0.7,
        weight,
        grad_pre,
    )
    pieces = relative_order(pieces)
    arrived = [over_shard(piece, flip) for flip, piece in enumerate(pieces) if flip]
    *small, grad_conv, grad_sent = call(
        functools.partial(norm_back_kernel, relative, own),
        "norm_back",
        [shape((folded, LANES), F32)]
        + [shape((folded, LANES), BF16)] * (INNER - 1)
        + [
            shape((tiles, height, breadth, LANES), F32),
            shape((tiles, height, breadth, LANES), BF16),
        ],
        [
            pltpu.VMEM((2, tiles, height, breadth + 16, LANES), F32),
            pltpu.VMEM((2, tiles, height, breadth, LANES), F32),
            pltpu.VMEM((tiles, LANES, LANES), F32),
            pltpu.VMEM((depth, LANES), F32),
            pltpu.VMEM((INNER, rows, LANES), F32),
        ],
        0.1,
        gn_kept,
        over_core(gn_sent),
        whitened,
        inv_std,
        taps,
        images,
        images_far,
    )
    small = relative_order(small)
    small_arrived = [crossing(piece, flip) for flip, piece in enumerate(small) if flip]
    grad_other = crossing(grad_sent, INNER)
    (grad_images,) = call(
        conv_back_kernel,
        "conv_back",
        [shape(images.shape, BF16)],
        [padded],
        0.1,
        grad_conv,
        grad_other,
        taps,
    )

    home, *sent = call(
        functools.partial(plane_sum_kernel, lines),
        "plane_sum",
        [shape((own, quarter + LANES), F32)] + [shape((own, quarter + LANES), BF16)] * (lines - 1),
        [],
        2.0,
        pieces[0],
        *arrived,
        small[0],
        *small_arrived,
    )
    home, grad_images = lax.optimization_barrier((home, grad_images))
    came = [crossing(piece, INNER * line) for line, piece in enumerate(sent, 1)]
    (total,) = call(
        line_sum_kernel,
        "line_sum",
        [shape((own, 3 * quarter + LANES), F32)],
        [],
        0.3,
        home,
        *came,
    )
    if reps > 2:
        groups = [[i for i in range(reps) if i % 2 == s] for s in range(2)]
        total = lax.psum(total, "rep", axis_index_groups=groups)
    other = over_core(total)
    factor = 1.0 / math.sqrt(images.shape[0] * pixels * shards * reps)
    grad_up, grad_depthwise, grad_gain, grad_bias = call(
        functools.partial(finish_kernel, factor),
        "finish",
        [
            shape((own, hidden), F32),
            shape((own, TAPS), F32),
            shape((1, own), F32),
            shape((1, own), F32),
        ],
        [],
        0.5,
        total,
        other,
    )
    return (grad_images, grad_up, grad_depthwise, grad_gain[0], grad_bias[0])


def solution(mesh):
    placed = (
        P(("shard", "rep"), None, None, None),
        P(("shard", "rep"), None, None, None),
        P("shard", None),
        P("shard"),
        P("shard"),
        P("shard", None),
    )
    return jax.shard_map(
        body,
        mesh=mesh,
        in_specs=placed,
        out_specs=(
            P(("shard", "rep"), None, None, None),
            P("shard", None),
            P("shard", None),
            P("shard"),
            P("shard"),
        ),
        check_vma=False,
    )
```

```python
import functools
import math

import jax
import jax.numpy as jnp
from jax import lax
from jax.experimental import pallas as pl
from jax.experimental.pallas import tpu as pltpu
from jax.sharding import PartitionSpec as P

KS = 7
TAPS = KS * KS
MARGIN = KS // 2
LANES = 128
INNER = 4
NORM_EPS = 1e-06
BF16 = jnp.bfloat16
F32 = jnp.float32
VMEM = pl.BlockSpec(memory_space=pltpu.VMEM)


def params(mebibytes):
    return pltpu.CompilerParams(vmem_limit_bytes=mebibytes * 1024 * 1024)


def gelu_slope(inputs):
    cumulative = 0.5 * (1.0 + lax.erf(inputs * 0.7071067811865476))
    return cumulative + inputs * jnp.exp(-0.5 * inputs * inputs) * 0.3989422804014327


def block_rows(relative, group, line, own, lines):
    if relative:
        place = lax.axis_index("shard") ^ (line * INNER + group)
        return pl.multiple_of(place * own, 16)
    return (group * lines + line) * own


def place_rows(pieces, target, own, relative, cast=None):
    for group, piece in enumerate(pieces):
        lines = piece.shape[0] // own
        if not relative:
            target[group * piece.shape[0] : (group + 1) * piece.shape[0], :] = (
                piece[...] if cast is None else piece[...].astype(cast)
            )
            continue
        for line in range(lines):
            rows = piece[line * own : (line + 1) * own, :]
            start = block_rows(True, group, line, own, lines)
            target[pl.ds(start, own), :] = rows if cast is None else rows.astype(cast)


def split_rows(source, pieces, own, relative):
    for group, piece in enumerate(pieces):
        lines = piece.shape[0] // own
        if not relative:
            piece[...] = source[group * piece.shape[0] : (group + 1) * piece.shape[0], :].astype(
                piece.dtype
            )
            continue
        for line in range(lines):
            start = block_rows(True, group, line, own, lines)
            piece[line * own : (line + 1) * own, :] = source[pl.ds(start, own), :].astype(
                piece.dtype
            )


def correlate(padded, tile, tap_row, height, breadth):
    sums = [None] * height
    for across in range(KS):
        shifted = padded[tile, :, 8 - MARGIN + across : 8 - MARGIN + across + breadth, :]
        for down in range(KS):
            row = tap_row(down, across)
            for line in range(height):
                origin = line + down - MARGIN
                if 0 <= origin < height:
                    term = shifted[origin] * row
                    sums[line] = term if sums[line] is None else sums[line] + term
    return sums


def pack_kernel(w_ref, dw_ref, gain_ref, bias_ref, home_ref, near_ref, far_ref, turned, wide):
    own, hidden = w_ref.shape
    quarter = hidden // 4
    side = lax.axis_index("rep") % 2
    parity = (lax.axis_index("shard") // INNER) % 2
    turned[...] = jnp.zeros_like(turned)
    turned[TAPS : TAPS + 1, :own] = gain_ref[...].astype(F32)
    turned[TAPS + 1 : TAPS + 2, :own] = bias_ref[...].astype(F32)
    wide[...] = jnp.zeros_like(wide)
    wide[:, :TAPS] = dw_ref[...].astype(F32)
    extras = (wide[...] + turned[...].T[:own]).astype(BF16)
    kinds = ((home_ref, side, parity), (near_ref, 1 - side, parity), (far_ref, 1 - side, 1 - parity))
    for ref, place, which in kinds:
        start = pl.multiple_of(place * (2 * quarter) + which * quarter, LANES)
        ref[:, :quarter] = w_ref[:, pl.ds(start, quarter)]
        ref[:, quarter:] = extras


def assemble_kernel(*refs):
    pieces, out_ref = refs[:-1], refs[-1]
    own = pieces[0].shape[0]
    rows, quarter = own * len(pieces), out_ref.shape[1]
    for line, piece in enumerate(pieces):
        out_ref[line * own : (line + 1) * own, :] = piece[:, :quarter]
    extras = fold(jnp.concatenate([piece[:, quarter:].astype(F32) for piece in pieces], axis=0))
    count = out_ref.shape[0] - rows
    for place in range(quarter // LANES):
        lanes = slice(place * LANES, (place + 1) * LANES)
        out_ref[rows:, lanes] = extras[place * count : (place + 1) * count].astype(BF16)


def small_rows(lower):
    parts = [lower[:, at : at + LANES] for at in range(0, lower.shape[1], LANES)]
    return unfold(jnp.concatenate(parts, axis=0))


def plane_sum_kernel(lines, *refs):
    pieces, small, outs = refs[:INNER], refs[INNER : 2 * INNER], refs[2 * INNER :]
    own = pieces[0].shape[0] // lines
    quarter = pieces[0].shape[1]
    extras = small[0][...]
    for part in small[1:]:
        extras = extras + part[...].astype(F32)
    if extras.shape[0] < pieces[0].shape[0]:
        extras = unfold(extras)
    for line, out in enumerate(outs):
        rows = slice(line * own, (line + 1) * own)
        total = pieces[0][rows, :]
        for part in pieces[1:]:
            total = total + part[rows, :].astype(F32)
        out[:, :quarter] = total.astype(out.dtype)
        out[:, quarter:] = extras[rows, :].astype(out.dtype)


def line_sum_kernel(*refs):
    pieces, total_ref = refs[:-1], refs[-1]
    quarter = pieces[0].shape[1] - LANES
    near, far = None, None
    for line, piece in enumerate(pieces[1:], 1):
        came = piece[...].astype(F32)
        if line % 2:
            far = came if far is None else far + came
        else:
            near = came if near is None else near + came
    total_ref[:, :quarter] = pieces[0][:, :quarter]
    total_ref[:, quarter : 2 * quarter] = near[:, :quarter]
    total_ref[:, 2 * quarter : 3 * quarter] = far[:, :quarter]
    total_ref[:, 3 * quarter :] = pieces[0][:, quarter:] + near[:, quarter:] + far[:, quarter:]


def finish_kernel(factor, mine_ref, other_ref, up_ref, dw_ref, gain_ref, bias_ref):
    own, quarter = mine_ref.shape[0], (mine_ref.shape[1] - LANES) // 3
    side = lax.axis_index("rep") % 2
    parity = (lax.axis_index("shard") // INNER) % 2
    for place, home, came in ((side, mine_ref, other_ref), (1 - side, other_ref, mine_ref)):
        start = pl.multiple_of((2 * place + parity) * quarter, LANES)
        total = home[:, :quarter] + came[:, quarter : 2 * quarter]
        up_ref[:, pl.ds(start, quarter)] = total * factor
        start = pl.multiple_of((2 * place + 1 - parity) * quarter, LANES)
        up_ref[:, pl.ds(start, quarter)] = came[:, 2 * quarter : 3 * quarter] * factor
    low = 3 * quarter
    sums = (mine_ref[:, low:] + other_ref[:, low:]) * factor
    dw_ref[...] = sums[:, :TAPS]
    turned = sums.T
    gain_ref[...] = turned[TAPS : TAPS + 1, :]
    bias_ref[...] = turned[TAPS + 1 : TAPS + 2, :]


def fold(rows):
    half = rows.shape[0] // 2
    low = lax.broadcasted_iota(jnp.int32, (half, LANES), 1) < LANES // 2
    return jnp.where(low, rows[:half], pltpu.roll(rows[half:], LANES // 2, 1))


def unfold(rows):
    return jnp.concatenate([rows, jnp.roll(rows, LANES // 2, 1)], axis=0)


def conv_norm_kernel(relative, own, *refs):
    small = refs[:INNER]
    sources = refs[INNER : INNER + 2]
    x_ref = sources[0]
    normed_ref, white_ref, inv_ref, taps_ref, gathered, unfolded, padded, conv = refs[INNER + 2 :]
    height, breadth, depth = x_ref.shape[1:]
    tiles = depth // LANES
    pixels = height * breadth
    if relative:
        count = unfolded.shape[0] // INNER
        for group, piece in enumerate(small):
            unfolded[group * count : (group + 1) * count, :] = small_rows(
                piece[count:, :].astype(F32)
            )
        small = [unfolded.at[pl.ds(group * count, count), :] for group in range(INNER)]
    place_rows(small, gathered, own, relative, F32)
    padded[...] = jnp.zeros_like(padded)
    for tile in range(tiles):
        lanes = slice(tile * LANES, (tile + 1) * LANES)
        taps_ref[tile] = gathered[lanes, :].T

    for image, source in enumerate(sources):
        for tile in range(tiles):
            lanes = slice(tile * LANES, (tile + 1) * LANES)
            padded[tile, :, 8 : 8 + breadth, :] = source[0, :, :, lanes].astype(F32)

        def one_tile(tile, carry):
            sums = correlate(
                padded,
                tile,
                lambda down, across: taps_ref[tile, pl.ds(down * KS + across, 1), :],
                height,
                breadth,
            )
            for line in range(height):
                conv[tile, line * breadth : (line + 1) * breadth, :] = sums[line]
            return carry

        lax.fori_loop(0, tiles, one_tile, 0)
        total = conv[0]
        for tile in range(1, tiles):
            total = total + conv[tile]
        average = jnp.sum(total, axis=-1, keepdims=True) / depth
        squares = None
        for tile in range(tiles):
            centered = conv[tile] - average
            squares = centered * centered if squares is None else squares + centered * centered
        variance = jnp.sum(squares, axis=-1, keepdims=True) / depth
        inv_std = lax.rsqrt(variance + NORM_EPS)
        rows = slice(image * pixels, (image + 1) * pixels)
        inv_ref[rows, :] = jnp.broadcast_to(inv_std, (pixels, LANES))
        for tile in range(tiles):
            lanes = slice(tile * LANES, (tile + 1) * LANES)
            whitened = (conv[tile] - average) * inv_std
            white_ref[rows, lanes] = whitened
            gain = taps_ref[tile, TAPS : TAPS + 1, :]
            bias = taps_ref[tile, TAPS + 1 : TAPS + 2, :]
            normed_ref[rows, lanes] = (whitened * gain + bias).astype(BF16)


def cot_pack_kernel(cot_ref, across_ref, sibling_ref):
    half = sibling_ref.shape[1]
    quarter = half // 2
    side = lax.axis_index("rep") % 2
    parity = (lax.axis_index("shard") // INNER) % 2
    for place in range(2):
        start = pl.multiple_of(place * half + (1 - parity) * quarter, LANES)
        across_ref[:, place * quarter : (place + 1) * quarter] = cot_ref[:, pl.ds(start, quarter)]
    sibling_ref[...] = cot_ref[:, pl.ds(pl.multiple_of((1 - side) * half, LANES), half)]


def order_kernel(relative, own, *refs):
    rows = refs[INNER].shape[0] // INNER
    place_rows([ref.at[pl.ds(0, rows), :] for ref in refs[:INNER]], refs[INNER], own, relative)


def project_kernel(relative, own, *refs):
    weight, n_own, n_sibling, cot_ref, sibling_ref, across_ref, corner_ref = refs[:7]
    pieces = refs[7 : 7 + INNER]
    gp_ref, normed, cot, grad = refs[7 + INNER :]
    pixels, half = sibling_ref.shape
    quarter = half // 2
    side = lax.axis_index("rep") % 2
    parity = (lax.axis_index("shard") // INNER) % 2
    normed[: 2 * pixels, :] = n_own[...]
    normed[2 * pixels :, :] = n_sibling[...]
    start = pl.multiple_of(side * half + parity * quarter, LANES)
    cot[:pixels, :] = cot_ref[:, pl.ds(start, quarter)]
    start = pl.multiple_of(side * quarter, LANES)
    cot[pixels : 2 * pixels, :] = across_ref[:, pl.ds(start, quarter)]
    start = pl.multiple_of(parity * quarter, LANES)
    cot[2 * pixels : 3 * pixels, :] = sibling_ref[:, pl.ds(start, quarter)]
    start = pl.multiple_of(side * quarter, LANES)
    cot[3 * pixels :, :] = corner_ref[:, pl.ds(start, quarter)]
    for start in range(0, quarter, LANES):
        columns = slice(start, start + LANES)
        pre_act = jnp.dot(normed[...], weight[:, columns], preferred_element_type=F32)
        gp_ref[:, columns] = (cot[:, columns].astype(F32) * gelu_slope(pre_act)).astype(BF16)
    grad[...] = lax.dot_general(
        normed[...], gp_ref[...], (((0,), (0,)), ((), ())), preferred_element_type=F32
    )
    split_rows(grad, pieces, own, relative)


def back_project_kernel(weight, gp_ref, own_ref, other_ref):
    rows = own_ref.shape[0]
    grad_normed = lax.dot_general(
        gp_ref[...], weight[...], (((1,), (1,)), ((), ())), preferred_element_type=F32
    )
    own_ref[...] = grad_normed[:rows]
    other_ref[...] = grad_normed[rows:]


def norm_back_kernel(relative, own, *refs):
    gn_own, gn_other, white_ref, inv_ref, taps_ref, x_ref, far_ref = refs[:7]
    pieces = refs[7 : 7 + INNER]
    grad_ref, sent_ref, padded, grads_ref, rows, small, unfolded = refs[7 + INNER :]
    height, breadth, depth = x_ref.shape[1:]
    tiles = depth // LANES
    pixels = height * breadth
    padded[...] = jnp.zeros_like(padded)
    rows[...] = jnp.zeros_like(rows)
    for image, source in enumerate((x_ref, far_ref)):
        span = slice(image * pixels, (image + 1) * pixels)
        first = None
        second = None
        for tile in range(tiles):
            lanes = slice(tile * LANES, (tile + 1) * LANES)
            padded[image, tile, :, 8 : 8 + breadth, :] = source[0, :, :, lanes].astype(F32)
            grad_normed = gn_own[span, lanes] + gn_other[span, lanes]
            whitened = white_ref[span, lanes]
            product = grad_normed * whitened
            gain = taps_ref[tile, TAPS : TAPS + 1, :]
            rows[tile, TAPS : TAPS + 1, :] += jnp.sum(product, axis=0, keepdims=True)
            rows[tile, TAPS + 1 : TAPS + 2, :] += jnp.sum(grad_normed, axis=0, keepdims=True)
            one, two = grad_normed * gain, product * gain
            first = one if first is None else first + one
            second = two if second is None else second + two
        mean_first = jnp.sum(first, axis=-1, keepdims=True) / depth
        mean_second = jnp.sum(second, axis=-1, keepdims=True) / depth
        for tile in range(tiles):
            lanes = slice(tile * LANES, (tile + 1) * LANES)
            gain = taps_ref[tile, TAPS : TAPS + 1, :]
            grad_white = (gn_own[span, lanes] + gn_other[span, lanes]) * gain
            grad_conv = inv_ref[span, :] * (
                grad_white - mean_first - white_ref[span, lanes] * mean_second
            )
            grad_conv = grad_conv.reshape(height, breadth, LANES)
            grads_ref[image, tile] = grad_conv
            if image == 0:
                grad_ref[tile] = grad_conv
            else:
                sent_ref[tile] = grad_conv.astype(BF16)

    def one_tile(tile, carry):
        grads = [[grads_ref[image, tile, line] for line in range(height)] for image in range(2)]
        for across in range(KS):
            columns = slice(8 - MARGIN + across, 8 - MARGIN + across + breadth)
            shifted = [padded[image, tile, :, columns, :] for image in range(2)]
            for down in range(KS):
                total = None
                for image in range(2):
                    for line in range(height):
                        origin = line + down - MARGIN
                        if 0 <= origin < height:
                            term = grads[image][line] * shifted[image][origin]
                            total = term if total is None else total + term
                rows[tile, pl.ds(down * KS + across, 1), :] = jnp.sum(total, axis=0, keepdims=True)
        return carry

    lax.fori_loop(0, tiles, one_tile, 0)
    for tile in range(tiles):
        small[tile * LANES : (tile + 1) * LANES, :] = rows[tile].T
    if relative:
        whole = [unfolded.at[group] for group in range(INNER)]
        split_rows(small, whole, own, relative)
        for source, piece in zip(whole, pieces):
            piece[...] = fold(source[...]).astype(piece.dtype)
    else:
        split_rows(small, pieces, own, relative)


def conv_back_kernel(grad_ref, other_ref, taps_ref, out_ref, padded):
    tiles, height, breadth, _ = grad_ref.shape
    padded[...] = jnp.zeros_like(padded)
    padded[:, :, 8 : 8 + breadth, :] = grad_ref[...] + other_ref[...].astype(F32)

    def one_tile(tile, carry):
        sums = correlate(
            padded,
            tile,
            lambda down, across: taps_ref[tile, pl.ds(TAPS - 1 - down * KS - across, 1), :],
            height,
            breadth,
        )
        start = pl.multiple_of(tile * LANES, LANES)
        for line in range(height):
            out_ref[0, line, :, pl.ds(start, LANES)] = sums[line].astype(BF16)
        return carry

    lax.fori_loop(0, tiles, one_tile, 0)


def call(kernel, name, outs, scratch, micros, *args, mebibytes=48):
    flops = int(micros * 1.1e9)
    moved = sum(math.prod(a.shape) * a.dtype.itemsize for a in args)
    moved += sum(math.prod(o.shape) * o.dtype.itemsize for o in outs)
    return pl.pallas_call(
        kernel,
        out_shape=outs,
        in_specs=[VMEM] * len(args),
        out_specs=[VMEM] * len(outs),
        scratch_shapes=scratch,
        compiler_params=params(mebibytes),
        cost_estimate=pl.CostEstimate(flops=flops, bytes_accessed=moved, transcendentals=0),
        name=name,
    )(*args)


def body(images, cotangent, depthwise_weight, norm_gain, norm_bias, up_weight):
    shards, reps = lax.axis_size("shard"), lax.axis_size("rep")
    own, hidden = up_weight.shape
    depth = own * shards
    lines = shards // INNER
    half, quarter = hidden // 2, hidden // 4
    height, breadth = images.shape[1:3]
    pixels = height * breadth
    tiles = depth // LANES
    me = lax.axis_index("shard")
    side = lax.axis_index("rep") % 2
    parity = (me // INNER) % 2
    relative = own % 16 == 0

    def over_shard(array, flip):
        return lax.ppermute(array, "shard", [(i, i ^ flip) for i in range(shards)])

    def crossing(array, flip):
        pairs = [
            (i * reps + r, (i ^ flip) * reps + (r ^ 1)) for i in range(shards) for r in range(reps)
        ]
        return lax.ppermute(array, ("shard", "rep"), pairs)

    def over_core(array):
        return lax.ppermute(array, "rep", [(i, i ^ 1) for i in range(reps)])

    def true_order(pieces):
        if relative:
            return pieces
        stacked = jnp.stack(pieces).reshape(shards, own, -1)
        flips = jnp.arange(shards) ^ me
        places = (flips % INNER) * lines + flips // INNER
        return list(jnp.take(stacked, places, axis=0).reshape(INNER, lines * own, -1))

    def relative_order(pieces):
        if relative:
            return pieces
        stacked = jnp.concatenate([p.astype(F32) for p in pieces]).reshape(shards, own, -1)
        flips = (jnp.arange(lines)[None, :] * INNER + jnp.arange(INNER)[:, None]).reshape(-1)
        moved = jnp.take(stacked, flips ^ me, axis=0).reshape(INNER, lines * own, -1)
        return [moved[0]] + [moved[i].astype(BF16) for i in range(1, INNER)]

    shape = jax.ShapeDtypeStruct
    home, near, far = call(
        pack_kernel,
        "pack",
        [shape((own, quarter + LANES), BF16)] * 3,
        [
            pltpu.VMEM((LANES, LANES), F32),
            pltpu.VMEM((own, LANES), F32),
        ],
        0.5,
        up_weight,
        depthwise_weight,
        norm_gain[None, :],
        norm_bias[None, :],
        mebibytes=63,
    )
    home, near, far, images, cotangent = lax.optimization_barrier(
        (home, near, far, images, cotangent)
    )
    gathered = [home] + [
        crossing(far if line % 2 else near, INNER * line) for line in range(1, lines)
    ]
    cotangent = cotangent.reshape(pixels, hidden)
    cot_across, cot_sibling = call(
        cot_pack_kernel,
        "cot_pack",
        [shape((pixels, half), BF16)] * 2,
        [],
        0.4,
        cotangent,
    )
    cot_across, cot_sibling = crossing(cot_across, INNER), over_core(cot_sibling)
    images_far = crossing(images, INNER)

    rows = lines * own
    folded = rows // 2 if relative else rows
    held = rows // 2 * LANES // quarter
    (mixed,) = call(
        assemble_kernel,
        "assemble",
        [shape((rows + held, quarter), BF16)],
        [],
        2.0,
        *gathered,
    )
    weights = [mixed] + [over_shard(mixed, flip) for flip in range(1, INNER)]
    extras = weights
    if not relative:
        extras = true_order([small_rows(piece[rows:]) for piece in weights])
        weights = true_order([piece[:rows] for piece in weights])
    (weight,) = call(
        functools.partial(order_kernel, relative, own),
        "order",
        [shape((depth, quarter), BF16)],
        [],
        3.0,
        *weights,
    )

    padded = pltpu.VMEM((tiles, height, breadth + 16, LANES), F32)
    normed, whitened, inv_std, taps = call(
        functools.partial(conv_norm_kernel, relative, own),
        "conv_norm",
        [
            shape((2 * pixels, depth), BF16),
            shape((2 * pixels, depth), F32),
            shape((2 * pixels, LANES), F32),
            shape((tiles, LANES, LANES), F32),
        ],
        [
            pltpu.VMEM((depth, LANES), F32),
            pltpu.VMEM((depth, LANES), F32),
            padded,
            pltpu.VMEM((tiles, pixels, LANES), F32),
        ],
        0.1,
        *extras,
        images,
        images_far,
    )
    normed, cot_across = lax.optimization_barrier((normed, cot_across))
    normed_sibling, cot_corner = over_core(normed), over_core(cot_across)
    *pieces, grad_pre = call(
        functools.partial(project_kernel, relative, own),
        "project",
        [shape((rows, quarter), F32)]
        + [shape((rows, quarter), BF16)] * (INNER - 1)
        + [shape((4 * pixels, quarter), BF16)],
        [
            pltpu.VMEM((4 * pixels, depth), BF16),
            pltpu.VMEM((4 * pixels, quarter), BF16),
            pltpu.VMEM((depth, quarter), F32),
        ],
        1.6,
        weight,
        normed,
        normed_sibling,
        cotangent,
        cot_sibling,
        cot_across,
        cot_corner,
    )
    gn_kept, gn_sent = call(
        back_project_kernel,
        "back_project",
        [shape((2 * pixels, depth), F32)] * 2,
        [],
        0.7,
        weight,
        grad_pre,
    )
    pieces = relative_order(pieces)
    arrived = [over_shard(piece, flip) for flip, piece in enumerate(pieces) if flip]
    *small, grad_conv, grad_sent = call(
        functools.partial(norm_back_kernel, relative, own),
        "norm_back",
        [shape((folded, LANES), F32)]
        + [shape((folded, LANES), BF16)] * (INNER - 1)
        + [
            shape((tiles, height, breadth, LANES), F32),
            shape((tiles, height, breadth, LANES), BF16),
        ],
        [
            pltpu.VMEM((2, tiles, height, breadth + 16, LANES), F32),
            pltpu.VMEM((2, tiles, height, breadth, LANES), F32),
            pltpu.VMEM((tiles, LANES, LANES), F32),
            pltpu.VMEM((depth, LANES), F32),
            pltpu.VMEM((INNER, rows, LANES), F32),
        ],
        0.1,
        gn_kept,
        over_core(gn_sent),
        whitened,
        inv_std,
        taps,
        images,
        images_far,
    )
    small = relative_order(small)
    small_arrived = [crossing(piece, flip) for flip, piece in enumerate(small) if flip]
    grad_other = crossing(grad_sent, INNER)
    (grad_images,) = call(
        conv_back_kernel,
        "conv_back",
        [shape(images.shape, BF16)],
        [padded],
        0.1,
        grad_conv,
        grad_other,
        taps,
    )

    home, *sent = call(
        functools.partial(plane_sum_kernel, lines),
        "plane_sum",
        [shape((own, quarter + LANES), F32)] + [shape((own, quarter + LANES), BF16)] * (lines - 1),
        [],
        2.0,
        pieces[0],
        *arrived,
        small[0],
        *small_arrived,
    )
    home, grad_images = lax.optimization_barrier((home, grad_images))
    came = [crossing(piece, INNER * line) for line, piece in enumerate(sent, 1)]
    (total,) = call(
        line_sum_kernel,
        "line_sum",
        [shape((own, 3 * quarter + LANES), F32)],
        [],
        0.3,
        home,
        *came,
    )
    if reps > 2:
        groups = [[i for i in range(reps) if i % 2 == s] for s in range(2)]
        total = lax.psum(total, "rep", axis_index_groups=groups)
    other = over_core(total)
    factor = 1.0 / math.sqrt(images.shape[0] * pixels * shards * reps)
    grad_up, grad_depthwise, grad_gain, grad_bias = call(
        functools.partial(finish_kernel, factor),
        "finish",
        [
            shape((own, hidden), F32),
            shape((own, TAPS), F32),
            shape((1, own), F32),
            shape((1, own), F32),
        ],
        [],
        0.5,
        total,
        other,
    )
    return (grad_images, grad_up, grad_depthwise, grad_gain[0], grad_bias[0])


def solution(mesh):
    placed = (
        P(("shard", "rep"), None, None, None),
        P(("shard", "rep"), None, None, None),
        P("shard", None),
        P("shard"),
        P("shard"),
        P("shard", None),
    )
    return jax.shard_map(
        body,
        mesh=mesh,
        in_specs=placed,
        out_specs=(
            P(("shard", "rep"), None, None, None),
            P("shard", None),
            P("shard", None),
            P("shard"),
            P("shard"),
        ),
        check_vma=False,
    )
```

```python
import functools
import math

import jax
import jax.numpy as jnp
from jax import lax
from jax.experimental import pallas as pl
from jax.experimental.pallas import tpu as pltpu
from jax.sharding import PartitionSpec as P

KS = 7
TAPS = KS * KS
MARGIN = KS // 2
LANES = 128
INNER = 4
NORM_EPS = 1e-06
BF16 = jnp.bfloat16
F32 = jnp.float32
VMEM = pl.BlockSpec(memory_space=pltpu.VMEM)


def params(mebibytes):
    return pltpu.CompilerParams(vmem_limit_bytes=mebibytes * 1024 * 1024)


def gelu_slope(inputs):
    cumulative = 0.5 * (1.0 + lax.erf(inputs * 0.7071067811865476))
    return cumulative + inputs * jnp.exp(-0.5 * inputs * inputs) * 0.3989422804014327


def block_rows(relative, group, line, own, lines):
    if relative:
        place = lax.axis_index("shard") ^ (line * INNER + group)
        return pl.multiple_of(place * own, 16)
    return (group * lines + line) * own


def place_rows(pieces, target, own, relative, cast=None):
    for group, piece in enumerate(pieces):
        lines = piece.shape[0] // own
        if not relative:
            target[group * piece.shape[0] : (group + 1) * piece.shape[0], :] = (
                piece[...] if cast is None else piece[...].astype(cast)
            )
            continue
        for line in range(lines):
            rows = piece[line * own : (line + 1) * own, :]
            start = block_rows(True, group, line, own, lines)
            target[pl.ds(start, own), :] = rows if cast is None else rows.astype(cast)


def split_rows(source, pieces, own, relative):
    for group, piece in enumerate(pieces):
        lines = piece.shape[0] // own
        if not relative:
            piece[...] = source[group * piece.shape[0] : (group + 1) * piece.shape[0], :].astype(
                piece.dtype
            )
            continue
        for line in range(lines):
            start = block_rows(True, group, line, own, lines)
            piece[line * own : (line + 1) * own, :] = source[pl.ds(start, own), :].astype(
                piece.dtype
            )


def correlate(padded, tile, tap_row, height, breadth):
    sums = [None] * height
    for across in range(KS):
        shifted = padded[tile, :, 8 - MARGIN + across : 8 - MARGIN + across + breadth, :]
        for down in range(KS):
            row = tap_row(down, across)
            for line in range(height):
                origin = line + down - MARGIN
                if 0 <= origin < height:
                    term = shifted[origin] * row
                    sums[line] = term if sums[line] is None else sums[line] + term
    return sums


def pack_kernel(w_ref, dw_ref, gain_ref, bias_ref, home_ref, near_ref, far_ref, turned, wide):
    own, hidden = w_ref.shape
    quarter = hidden // 4
    side = lax.axis_index("rep") % 2
    parity = (lax.axis_index("shard") // INNER) % 2
    turned[...] = jnp.zeros_like(turned)
    turned[TAPS : TAPS + 1, :own] = gain_ref[...].astype(F32)
    turned[TAPS + 1 : TAPS + 2, :own] = bias_ref[...].astype(F32)
    wide[...] = jnp.zeros_like(wide)
    wide[:, :TAPS] = dw_ref[...].astype(F32)
    extras = (wide[...] + turned[...].T[:own]).astype(BF16)
    kinds = ((home_ref, side, parity), (near_ref, 1 - side, parity), (far_ref, 1 - side, 1 - parity))
    for ref, place, which in kinds:
        start = pl.multiple_of(place * (2 * quarter) + which * quarter, LANES)
        ref[:, :quarter] = w_ref[:, pl.ds(start, quarter)]
        ref[:, quarter:] = extras


def assemble_kernel(*refs):
    pieces, (weight_ref, extra_ref) = refs[:-2], refs[-2:]
    own = pieces[0].shape[0]
    quarter = weight_ref.shape[1]
    for line, piece in enumerate(pieces):
        weight_ref[line * own : (line + 1) * own, :] = piece[:, :quarter]
    extras = jnp.concatenate([piece[:, quarter:].astype(F32) for piece in pieces], axis=0)
    if extra_ref.shape[0] < extras.shape[0]:
        extras = fold(extras)
    extra_ref[...] = extras.astype(BF16)


def plane_sum_kernel(lines, *refs):
    pieces, small, outs = refs[:INNER], refs[INNER : 2 * INNER], refs[2 * INNER :]
    own = pieces[0].shape[0] // lines
    quarter = pieces[0].shape[1]
    extras = small[0][...]
    for part in small[1:]:
        extras = extras + part[...].astype(F32)
    if extras.shape[0] < pieces[0].shape[0]:
        extras = unfold(extras)
    for line, out in enumerate(outs):
        rows = slice(line * own, (line + 1) * own)
        total = pieces[0][rows, :]
        for part in pieces[1:]:
            total = total + part[rows, :].astype(F32)
        out[:, :quarter] = total.astype(out.dtype)
        out[:, quarter:] = extras[rows, :].astype(out.dtype)


def line_sum_kernel(*refs):
    pieces, total_ref = refs[:-1], refs[-1]
    quarter = pieces[0].shape[1] - LANES
    near, far = None, None
    for line, piece in enumerate(pieces[1:], 1):
        came = piece[...].astype(F32)
        if line % 2:
            far = came if far is None else far + came
        else:
            near = came if near is None else near + came
    total_ref[:, :quarter] = pieces[0][:, :quarter]
    total_ref[:, quarter : 2 * quarter] = near[:, :quarter]
    total_ref[:, 2 * quarter : 3 * quarter] = far[:, :quarter]
    total_ref[:, 3 * quarter :] = pieces[0][:, quarter:] + near[:, quarter:] + far[:, quarter:]


def finish_kernel(factor, mine_ref, other_ref, up_ref, dw_ref, gain_ref, bias_ref):
    own, quarter = mine_ref.shape[0], (mine_ref.shape[1] - LANES) // 3
    side = lax.axis_index("rep") % 2
    parity = (lax.axis_index("shard") // INNER) % 2
    for place, home, came in ((side, mine_ref, other_ref), (1 - side, other_ref, mine_ref)):
        start = pl.multiple_of((2 * place + parity) * quarter, LANES)
        total = home[:, :quarter] + came[:, quarter : 2 * quarter]
        up_ref[:, pl.ds(start, quarter)] = total * factor
        start = pl.multiple_of((2 * place + 1 - parity) * quarter, LANES)
        up_ref[:, pl.ds(start, quarter)] = came[:, 2 * quarter : 3 * quarter] * factor
    low = 3 * quarter
    sums = (mine_ref[:, low:] + other_ref[:, low:]) * factor
    dw_ref[...] = sums[:, :TAPS]
    turned = sums.T
    gain_ref[...] = turned[TAPS : TAPS + 1, :]
    bias_ref[...] = turned[TAPS + 1 : TAPS + 2, :]


def fold(rows):
    half = rows.shape[0] // 2
    low = lax.broadcasted_iota(jnp.int32, (half, LANES), 1) < LANES // 2
    return jnp.where(low, rows[:half], pltpu.roll(rows[half:], LANES // 2, 1))


def unfold(rows):
    return jnp.concatenate([rows, pltpu.roll(rows, LANES // 2, 1)], axis=0)


def conv_norm_kernel(relative, own, height, breadth, *refs):
    small = refs[:INNER]
    sources = refs[INNER : INNER + 2]
    x_ref = sources[0]
    normed_ref, white_ref, inv_ref, taps_ref, gathered, unfolded, padded, conv = refs[INNER + 2 :]
    pixels, depth = x_ref.shape
    tiles = depth // LANES
    if relative:
        for group, piece in enumerate(small):
            unfolded[group * 2 * piece.shape[0] : (group + 1) * 2 * piece.shape[0], :] = unfold(
                piece[...].astype(F32)
            )
        count = unfolded.shape[0] // INNER
        small = [unfolded.at[pl.ds(group * count, count), :] for group in range(INNER)]
    place_rows(small, gathered, own, relative, F32)
    padded[...] = jnp.zeros_like(padded)
    for tile in range(tiles):
        lanes = slice(tile * LANES, (tile + 1) * LANES)
        taps_ref[tile] = gathered[lanes, :].T

    for image, source in enumerate(sources):
        for tile in range(tiles):
            lanes = slice(tile * LANES, (tile + 1) * LANES)
            part = source[:pixels, lanes].astype(F32)
            padded[tile, :, 8 : 8 + breadth, :] = part.reshape(height, breadth, LANES)

        def one_tile(tile, carry):
            sums = correlate(
                padded,
                tile,
                lambda down, across: taps_ref[tile, pl.ds(down * KS + across, 1), :],
                height,
                breadth,
            )
            for line in range(height):
                conv[tile, line * breadth : (line + 1) * breadth, :] = sums[line]
            return carry

        lax.fori_loop(0, tiles, one_tile, 0)
        total = conv[0]
        for tile in range(1, tiles):
            total = total + conv[tile]
        average = jnp.sum(total, axis=-1, keepdims=True) / depth
        squares = None
        for tile in range(tiles):
            centered = conv[tile] - average
            squares = centered * centered if squares is None else squares + centered * centered
        variance = jnp.sum(squares, axis=-1, keepdims=True) / depth
        inv_std = lax.rsqrt(variance + NORM_EPS)
        rows = slice(image * pixels, (image + 1) * pixels)
        inv_ref[rows, :] = jnp.broadcast_to(inv_std, (pixels, LANES))
        for tile in range(tiles):
            lanes = slice(tile * LANES, (tile + 1) * LANES)
            whitened = (conv[tile] - average) * inv_std
            white_ref[rows, lanes] = whitened
            gain = taps_ref[tile, TAPS : TAPS + 1, :]
            bias = taps_ref[tile, TAPS + 1 : TAPS + 2, :]
            normed_ref[rows, lanes] = (whitened * gain + bias).astype(BF16)


def cot_pack_kernel(image_ref, cot_ref, across_ref, sibling_ref):
    pixels, half = sibling_ref.shape
    quarter = half // 2
    side = lax.axis_index("rep") % 2
    parity = (lax.axis_index("shard") // INNER) % 2
    for place in range(2):
        start = pl.multiple_of(place * half + (1 - parity) * quarter, LANES)
        lanes = slice(place * quarter, (place + 1) * quarter)
        across_ref[pixels:, lanes] = cot_ref[:, pl.ds(start, quarter)]
    across_ref[:pixels, :] = image_ref[...]
    sibling_ref[...] = cot_ref[:, pl.ds(pl.multiple_of((1 - side) * half, LANES), half)]


def order_kernel(relative, own, *refs):
    place_rows(refs[:INNER], refs[INNER], own, relative)


def project_kernel(relative, own, *refs):
    weight, n_own, n_sibling, cot_ref, sibling_ref, across_ref, corner_ref = refs[:7]
    pieces = refs[7 : 7 + INNER]
    gp_ref, normed, cot, grad = refs[7 + INNER :]
    pixels, half = sibling_ref.shape
    quarter = half // 2
    side = lax.axis_index("rep") % 2
    parity = (lax.axis_index("shard") // INNER) % 2
    normed[: 2 * pixels, :] = n_own[...]
    normed[2 * pixels :, :] = n_sibling[...]
    start = pl.multiple_of(side * half + parity * quarter, LANES)
    cot[:pixels, :] = cot_ref[:, pl.ds(start, quarter)]
    start = pl.multiple_of(side * quarter, LANES)
    cot[pixels : 2 * pixels, :] = across_ref[pixels:, pl.ds(start, quarter)]
    start = pl.multiple_of(parity * quarter, LANES)
    cot[2 * pixels : 3 * pixels, :] = sibling_ref[:, pl.ds(start, quarter)]
    start = pl.multiple_of(side * quarter, LANES)
    cot[3 * pixels :, :] = corner_ref[pixels:, pl.ds(start, quarter)]
    for start in range(0, quarter, LANES):
        columns = slice(start, start + LANES)
        pre_act = jnp.dot(normed[...], weight[:, columns], preferred_element_type=F32)
        gp_ref[:, columns] = (cot[:, columns].astype(F32) * gelu_slope(pre_act)).astype(BF16)
    grad[...] = lax.dot_general(
        normed[...], gp_ref[...], (((0,), (0,)), ((), ())), preferred_element_type=F32
    )
    split_rows(grad, pieces, own, relative)


def back_project_kernel(weight, gp_ref, own_ref, other_ref):
    rows = own_ref.shape[0]
    grad_normed = lax.dot_general(
        gp_ref[...], weight[...], (((1,), (1,)), ((), ())), preferred_element_type=F32
    )
    own_ref[...] = grad_normed[:rows]
    other_ref[...] = grad_normed[rows:]


def norm_back_kernel(relative, own, height, breadth, *refs):
    gn_own, gn_other, white_ref, inv_ref, taps_ref, x_ref, far_ref = refs[:7]
    pieces = refs[7 : 7 + INNER]
    grad_ref, sent_ref, padded, grads_ref, rows, small, unfolded = refs[7 + INNER :]
    pixels, depth = x_ref.shape
    tiles = depth // LANES
    padded[...] = jnp.zeros_like(padded)
    rows[...] = jnp.zeros_like(rows)
    for image, source in enumerate((x_ref, far_ref)):
        span = slice(image * pixels, (image + 1) * pixels)
        first = None
        second = None
        for tile in range(tiles):
            lanes = slice(tile * LANES, (tile + 1) * LANES)
            part = source[:pixels, lanes].astype(F32)
            padded[image, tile, :, 8 : 8 + breadth, :] = part.reshape(height, breadth, LANES)
            grad_normed = gn_own[span, lanes] + gn_other[span, lanes]
            whitened = white_ref[span, lanes]
            product = grad_normed * whitened
            gain = taps_ref[tile, TAPS : TAPS + 1, :]
            rows[tile, TAPS : TAPS + 1, :] += jnp.sum(product, axis=0, keepdims=True)
            rows[tile, TAPS + 1 : TAPS + 2, :] += jnp.sum(grad_normed, axis=0, keepdims=True)
            one, two = grad_normed * gain, product * gain
            first = one if first is None else first + one
            second = two if second is None else second + two
        mean_first = jnp.sum(first, axis=-1, keepdims=True) / depth
        mean_second = jnp.sum(second, axis=-1, keepdims=True) / depth
        for tile in range(tiles):
            lanes = slice(tile * LANES, (tile + 1) * LANES)
            gain = taps_ref[tile, TAPS : TAPS + 1, :]
            grad_white = (gn_own[span, lanes] + gn_other[span, lanes]) * gain
            grad_conv = inv_ref[span, :] * (
                grad_white - mean_first - white_ref[span, lanes] * mean_second
            )
            grad_conv = grad_conv.reshape(height, breadth, LANES)
            grads_ref[image, tile] = grad_conv
            if image == 0:
                grad_ref[tile] = grad_conv
            else:
                sent_ref[tile] = grad_conv.astype(BF16)

    def one_tile(tile, carry):
        grads = [[grads_ref[image, tile, line] for line in range(height)] for image in range(2)]
        for across in range(KS):
            columns = slice(8 - MARGIN + across, 8 - MARGIN + across + breadth)
            shifted = [padded[image, tile, :, columns, :] for image in range(2)]
            for down in range(KS):
                total = None
                for image in range(2):
                    for line in range(height):
                        origin = line + down - MARGIN
                        if 0 <= origin < height:
                            term = grads[image][line] * shifted[image][origin]
                            total = term if total is None else total + term
                rows[tile, pl.ds(down * KS + across, 1), :] = jnp.sum(total, axis=0, keepdims=True)
        return carry

    lax.fori_loop(0, tiles, one_tile, 0)
    for tile in range(tiles):
        small[tile * LANES : (tile + 1) * LANES, :] = rows[tile].T
    if relative:
        whole = [unfolded.at[group] for group in range(INNER)]
        split_rows(small, whole, own, relative)
        for source, piece in zip(whole, pieces):
            piece[...] = fold(source[...]).astype(piece.dtype)
    else:
        split_rows(small, pieces, own, relative)


def conv_back_kernel(grad_ref, other_ref, taps_ref, out_ref, padded):
    tiles, height, breadth, _ = grad_ref.shape
    padded[...] = jnp.zeros_like(padded)
    padded[:, :, 8 : 8 + breadth, :] = grad_ref[...] + other_ref[...].astype(F32)

    def one_tile(tile, carry):
        sums = correlate(
            padded,
            tile,
            lambda down, across: taps_ref[tile, pl.ds(TAPS - 1 - down * KS - across, 1), :],
            height,
            breadth,
        )
        start = pl.multiple_of(tile * LANES, LANES)
        for line in range(height):
            out_ref[0, line, :, pl.ds(start, LANES)] = sums[line].astype(BF16)
        return carry

    lax.fori_loop(0, tiles, one_tile, 0)


def call(kernel, name, outs, scratch, micros, *args, mebibytes=48):
    flops = int(micros * 1.1e9)
    moved = sum(math.prod(a.shape) * a.dtype.itemsize for a in args)
    moved += sum(math.prod(o.shape) * o.dtype.itemsize for o in outs)
    return pl.pallas_call(
        kernel,
        out_shape=outs,
        in_specs=[VMEM] * len(args),
        out_specs=[VMEM] * len(outs),
        scratch_shapes=scratch,
        compiler_params=params(mebibytes),
        cost_estimate=pl.CostEstimate(flops=flops, bytes_accessed=moved, transcendentals=0),
        name=name,
    )(*args)


def body(images, cotangent, depthwise_weight, norm_gain, norm_bias, up_weight):
    shards, reps = lax.axis_size("shard"), lax.axis_size("rep")
    own, hidden = up_weight.shape
    depth = own * shards
    lines = shards // INNER
    half, quarter = hidden // 2, hidden // 4
    height, breadth = images.shape[1:3]
    pixels = height * breadth
    tiles = depth // LANES
    me = lax.axis_index("shard")
    side = lax.axis_index("rep") % 2
    parity = (me // INNER) % 2
    relative = own % 16 == 0

    def over_shard(array, flip):
        return lax.ppermute(array, "shard", [(i, i ^ flip) for i in range(shards)])

    def crossing(array, flip):
        pairs = [
            (i * reps + r, (i ^ flip) * reps + (r ^ 1)) for i in range(shards) for r in range(reps)
        ]
        return lax.ppermute(array, ("shard", "rep"), pairs)

    def over_core(array):
        return lax.ppermute(array, "rep", [(i, i ^ 1) for i in range(reps)])

    def true_order(pieces):
        if relative:
            return pieces
        stacked = jnp.stack(pieces).reshape(shards, own, -1)
        flips = jnp.arange(shards) ^ me
        places = (flips % INNER) * lines + flips // INNER
        return list(jnp.take(stacked, places, axis=0).reshape(INNER, lines * own, -1))

    def relative_order(pieces):
        if relative:
            return pieces
        stacked = jnp.concatenate([p.astype(F32) for p in pieces]).reshape(shards, own, -1)
        flips = (jnp.arange(lines)[None, :] * INNER + jnp.arange(INNER)[:, None]).reshape(-1)
        moved = jnp.take(stacked, flips ^ me, axis=0).reshape(INNER, lines * own, -1)
        return [moved[0]] + [moved[i].astype(BF16) for i in range(1, INNER)]

    shape = jax.ShapeDtypeStruct
    home, near, far = call(
        pack_kernel,
        "pack",
        [shape((own, quarter + LANES), BF16)] * 3,
        [
            pltpu.VMEM((LANES, LANES), F32),
            pltpu.VMEM((own, LANES), F32),
        ],
        0.5,
        up_weight,
        depthwise_weight,
        norm_gain[None, :],
        norm_bias[None, :],
        mebibytes=63,
    )
    image, cotangent = images.reshape(pixels, depth), cotangent.reshape(pixels, hidden)
    home, near, far, image, cotangent = lax.optimization_barrier(
        (home, near, far, image, cotangent)
    )
    gathered = [home] + [
        crossing(far if line % 2 else near, INNER * line) for line in range(1, lines)
    ]
    across, cot_sibling = call(
        cot_pack_kernel,
        "cot_pack",
        [shape((2 * pixels, half), BF16), shape((pixels, half), BF16)],
        [],
        0.4,
        image,
        cotangent,
    )
    across, cot_sibling = crossing(across, INNER), over_core(cot_sibling)

    rows = lines * own
    folded = rows // 2 if relative else rows
    weight_lines, extra_lines = call(
        assemble_kernel,
        "assemble",
        [shape((rows, quarter), BF16), shape((folded, LANES), BF16)],
        [],
        4.0,
        *gathered,
    )
    weights = [weight_lines] + [over_shard(weight_lines, flip) for flip in range(1, INNER)]
    extras = [extra_lines] + [crossing(extra_lines, flip) for flip in range(1, INNER)]
    weights, extras = true_order(weights), true_order(extras)
    (weight,) = call(
        functools.partial(order_kernel, relative, own),
        "order",
        [shape((depth, quarter), BF16)],
        [],
        2.6,
        *weights,
    )

    padded = pltpu.VMEM((tiles, height, breadth + 16, LANES), F32)
    normed, whitened, inv_std, taps = call(
        functools.partial(conv_norm_kernel, relative, own, height, breadth),
        "conv_norm",
        [
            shape((2 * pixels, depth), BF16),
            shape((2 * pixels, depth), F32),
            shape((2 * pixels, LANES), F32),
            shape((tiles, LANES, LANES), F32),
        ],
        [
            pltpu.VMEM((depth, LANES), F32),
            pltpu.VMEM((depth, LANES), F32),
            padded,
            pltpu.VMEM((tiles, pixels, LANES), F32),
        ],
        0.1,
        *extras,
        image,
        across,
    )
    normed, across = lax.optimization_barrier((normed, across))
    normed_sibling, corner = over_core(normed), over_core(across)
    *pieces, grad_pre = call(
        functools.partial(project_kernel, relative, own),
        "project",
        [shape((rows, quarter), F32)]
        + [shape((rows, quarter), BF16)] * (INNER - 1)
        + [shape((4 * pixels, quarter), BF16)],
        [
            pltpu.VMEM((4 * pixels, depth), BF16),
            pltpu.VMEM((4 * pixels, quarter), BF16),
            pltpu.VMEM((depth, quarter), F32),
        ],
        1.6,
        weight,
        normed,
        normed_sibling,
        cotangent,
        cot_sibling,
        across,
        corner,
    )
    gn_kept, gn_sent = call(
        back_project_kernel,
        "back_project",
        [shape((2 * pixels, depth), F32)] * 2,
        [],
        0.7,
        weight,
        grad_pre,
    )
    pieces = relative_order(pieces)
    arrived = [over_shard(piece, flip) for flip, piece in enumerate(pieces) if flip]
    *small, grad_conv, grad_sent = call(
        functools.partial(norm_back_kernel, relative, own, height, breadth),
        "norm_back",
        [shape((folded, LANES), F32)]
        + [shape((folded, LANES), BF16)] * (INNER - 1)
        + [
            shape((tiles, height, breadth, LANES), F32),
            shape((tiles, height, breadth, LANES), BF16),
        ],
        [
            pltpu.VMEM((2, tiles, height, breadth + 16, LANES), F32),
            pltpu.VMEM((2, tiles, height, breadth, LANES), F32),
            pltpu.VMEM((tiles, LANES, LANES), F32),
            pltpu.VMEM((depth, LANES), F32),
            pltpu.VMEM((INNER, rows, LANES), F32),
        ],
        0.1,
        gn_kept,
        over_core(gn_sent),
        whitened,
        inv_std,
        taps,
        image,
        across,
    )
    small = relative_order(small)
    small_arrived = [crossing(piece, flip) for flip, piece in enumerate(small) if flip]
    grad_other = crossing(grad_sent, INNER)
    (grad_images,) = call(
        conv_back_kernel,
        "conv_back",
        [shape(images.shape, BF16)],
        [padded],
        0.1,
        grad_conv,
        grad_other,
        taps,
    )

    home, *sent = call(
        functools.partial(plane_sum_kernel, lines),
        "plane_sum",
        [shape((own, quarter + LANES), F32)] + [shape((own, quarter + LANES), BF16)] * (lines - 1),
        [],
        2.0,
        pieces[0],
        *arrived,
        small[0],
        *small_arrived,
    )
    home, grad_images = lax.optimization_barrier((home, grad_images))
    came = [crossing(piece, INNER * line) for line, piece in enumerate(sent, 1)]
    (total,) = call(
        line_sum_kernel,
        "line_sum",
        [shape((own, 3 * quarter + LANES), F32)],
        [],
        0.3,
        home,
        *came,
    )
    if reps > 2:
        groups = [[i for i in range(reps) if i % 2 == s] for s in range(2)]
        total = lax.psum(total, "rep", axis_index_groups=groups)
    other = over_core(total)
    factor = 1.0 / math.sqrt(images.shape[0] * pixels * shards * reps)
    grad_up, grad_depthwise, grad_gain, grad_bias = call(
        functools.partial(finish_kernel, factor),
        "finish",
        [
            shape((own, hidden), F32),
            shape((own, TAPS), F32),
            shape((1, own), F32),
            shape((1, own), F32),
        ],
        [],
        0.5,
        total,
        other,
    )
    return (grad_images, grad_up, grad_depthwise, grad_gain[0], grad_bias[0])


def solution(mesh):
    placed = (
        P(("shard", "rep"), None, None, None),
        P(("shard", "rep"), None, None, None),
        P("shard", None),
        P("shard"),
        P("shard"),
        P("shard", None),
    )
    return jax.shard_map(
        body,
        mesh=mesh,
        in_specs=placed,
        out_specs=(
            P(("shard", "rep"), None, None, None),
            P("shard", None),
            P("shard", None),
            P("shard"),
            P("shard"),
        ),
        check_vma=False,
    )
```

```python
import functools
import math

import jax
import jax.numpy as jnp
from jax import lax
from jax.experimental import pallas as pl
from jax.experimental.pallas import tpu as pltpu
from jax.sharding import PartitionSpec as P

KS = 7
TAPS = KS * KS
MARGIN = KS // 2
LANES = 128
INNER = 4
NORM_EPS = 1e-06
BF16 = jnp.bfloat16
F32 = jnp.float32
VMEM = pl.BlockSpec(memory_space=pltpu.VMEM)


def params(mebibytes):
    return pltpu.CompilerParams(vmem_limit_bytes=mebibytes * 1024 * 1024)


def gelu_slope(inputs):
    cumulative = 0.5 * (1.0 + lax.erf(inputs * 0.7071067811865476))
    return cumulative + inputs * jnp.exp(-0.5 * inputs * inputs) * 0.3989422804014327


def block_rows(relative, group, line, own, lines):
    if relative:
        place = lax.axis_index("shard") ^ (line * INNER + group)
        return pl.multiple_of(place * own, 16)
    return (group * lines + line) * own


def place_rows(pieces, target, own, relative, cast=None):
    for group, piece in enumerate(pieces):
        lines = piece.shape[0] // own
        if not relative:
            target[group * piece.shape[0] : (group + 1) * piece.shape[0], :] = (
                piece[...] if cast is None else piece[...].astype(cast)
            )
            continue
        for line in range(lines):
            rows = piece[line * own : (line + 1) * own, :]
            start = block_rows(True, group, line, own, lines)
            target[pl.ds(start, own), :] = rows if cast is None else rows.astype(cast)


def split_rows(source, pieces, own, relative):
    for group, piece in enumerate(pieces):
        lines = piece.shape[0] // own
        if not relative:
            piece[...] = source[group * piece.shape[0] : (group + 1) * piece.shape[0], :].astype(
                piece.dtype
            )
            continue
        for line in range(lines):
            start = block_rows(True, group, line, own, lines)
            piece[line * own : (line + 1) * own, :] = source[pl.ds(start, own), :].astype(
                piece.dtype
            )


def correlate(padded, tile, tap_row, height, breadth):
    sums = [None] * height
    for across in range(KS):
        shifted = padded[tile, :, 8 - MARGIN + across : 8 - MARGIN + across + breadth, :]
        for down in range(KS):
            row = tap_row(down, across)
            for line in range(height):
                origin = line + down - MARGIN
                if 0 <= origin < height:
                    term = shifted[origin] * row
                    sums[line] = term if sums[line] is None else sums[line] + term
    return sums


def pack_kernel(w_ref, dw_ref, gain_ref, bias_ref, home_ref, near_ref, far_ref, turned, wide):
    own, hidden = w_ref.shape
    quarter = hidden // 4
    side = lax.axis_index("rep") % 2
    parity = (lax.axis_index("shard") // INNER) % 2
    turned[...] = jnp.zeros_like(turned)
    turned[TAPS : TAPS + 1, :own] = gain_ref[...].astype(F32)
    turned[TAPS + 1 : TAPS + 2, :own] = bias_ref[...].astype(F32)
    wide[...] = jnp.zeros_like(wide)
    wide[:, :TAPS] = dw_ref[...].astype(F32)
    extras = (wide[...] + turned[...].T[:own]).astype(BF16)
    kinds = ((home_ref, side, parity), (near_ref, 1 - side, parity), (far_ref, 1 - side, 1 - parity))
    for ref, place, which in kinds:
        start = pl.multiple_of(place * (2 * quarter) + which * quarter, LANES)
        ref[:, :quarter] = w_ref[:, pl.ds(start, quarter)]
        ref[:, quarter:] = extras


def assemble_kernel(*refs):
    pieces, (weight_ref, extra_ref) = refs[:-2], refs[-2:]
    own = pieces[0].shape[0]
    quarter = weight_ref.shape[1]
    for line, piece in enumerate(pieces):
        weight_ref[line * own : (line + 1) * own, :] = piece[:, :quarter]
    extras = jnp.concatenate([piece[:, quarter:].astype(F32) for piece in pieces], axis=0)
    if extra_ref.shape[0] < extras.shape[0]:
        extras = fold(extras)
    extra_ref[...] = extras.astype(BF16)


def plane_sum_kernel(lines, *refs):
    pieces, small, outs = refs[:INNER], refs[INNER : 2 * INNER], refs[2 * INNER :]
    own = pieces[0].shape[0] // lines
    quarter = pieces[0].shape[1]
    extras = small[0][...]
    for part in small[1:]:
        extras = extras + part[...].astype(F32)
    if extras.shape[0] < pieces[0].shape[0]:
        extras = unfold(extras)
    for line, out in enumerate(outs):
        rows = slice(line * own, (line + 1) * own)
        total = pieces[0][rows, :]
        for part in pieces[1:]:
            total = total + part[rows, :].astype(F32)
        out[:, :quarter] = total.astype(out.dtype)
        out[:, quarter:] = extras[rows, :].astype(out.dtype)


def line_sum_kernel(*refs):
    pieces, total_ref = refs[:-1], refs[-1]
    quarter = pieces[0].shape[1] - LANES
    near, far = None, None
    for line, piece in enumerate(pieces[1:], 1):
        came = piece[...].astype(F32)
        if line % 2:
            far = came if far is None else far + came
        else:
            near = came if near is None else near + came
    total_ref[:, :quarter] = pieces[0][:, :quarter]
    total_ref[:, quarter : 2 * quarter] = near[:, :quarter]
    total_ref[:, 2 * quarter : 3 * quarter] = far[:, :quarter]
    total_ref[:, 3 * quarter :] = pieces[0][:, quarter:] + near[:, quarter:] + far[:, quarter:]


def finish_kernel(factor, mine_ref, other_ref, up_ref, dw_ref, gain_ref, bias_ref):
    own, quarter = mine_ref.shape[0], (mine_ref.shape[1] - LANES) // 3
    side = lax.axis_index("rep") % 2
    parity = (lax.axis_index("shard") // INNER) % 2
    for place, home, came in ((side, mine_ref, other_ref), (1 - side, other_ref, mine_ref)):
        start = pl.multiple_of((2 * place + parity) * quarter, LANES)
        total = home[:, :quarter] + came[:, quarter : 2 * quarter]
        up_ref[:, pl.ds(start, quarter)] = total * factor
        start = pl.multiple_of((2 * place + 1 - parity) * quarter, LANES)
        up_ref[:, pl.ds(start, quarter)] = came[:, 2 * quarter : 3 * quarter] * factor
    low = 3 * quarter
    sums = (mine_ref[:, low:] + other_ref[:, low:]) * factor
    dw_ref[...] = sums[:, :TAPS]
    turned = sums.T
    gain_ref[...] = turned[TAPS : TAPS + 1, :]
    bias_ref[...] = turned[TAPS + 1 : TAPS + 2, :]


def fold(rows):
    half = rows.shape[0] // 2
    low = lax.broadcasted_iota(jnp.int32, (half, LANES), 1) < LANES // 2
    return jnp.where(low, rows[:half], pltpu.roll(rows[half:], LANES // 2, 1))


def unfold(rows):
    return jnp.concatenate([rows, pltpu.roll(rows, LANES // 2, 1)], axis=0)


def conv_norm_kernel(relative, own, height, breadth, *refs):
    small = refs[:INNER]
    sources = refs[INNER : INNER + 2]
    x_ref = sources[0]
    normed_ref, white_ref, inv_ref, taps_ref, gathered, unfolded, padded, conv = refs[INNER + 2 :]
    pixels, depth = x_ref.shape
    tiles = depth // LANES
    if relative:
        for group, piece in enumerate(small):
            unfolded[group * 2 * piece.shape[0] : (group + 1) * 2 * piece.shape[0], :] = unfold(
                piece[...].astype(F32)
            )
        count = unfolded.shape[0] // INNER
        small = [unfolded.at[pl.ds(group * count, count), :] for group in range(INNER)]
    place_rows(small, gathered, own, relative, F32)
    padded[...] = jnp.zeros_like(padded)
    for tile in range(tiles):
        lanes = slice(tile * LANES, (tile + 1) * LANES)
        taps_ref[tile] = gathered[lanes, :].T

    for image, source in enumerate(sources):
        for tile in range(tiles):
            lanes = slice(tile * LANES, (tile + 1) * LANES)
            part = source[:pixels, lanes].astype(F32)
            padded[tile, :, 8 : 8 + breadth, :] = part.reshape(height, breadth, LANES)

        def one_tile(tile, carry):
            sums = correlate(
                padded,
                tile,
                lambda down, across: taps_ref[tile, pl.ds(down * KS + across, 1), :],
                height,
                breadth,
            )
            for line in range(height):
                conv[tile, line * breadth : (line + 1) * breadth, :] = sums[line]
            return carry

        lax.fori_loop(0, tiles, one_tile, 0)
        total = conv[0]
        for tile in range(1, tiles):
            total = total + conv[tile]
        average = jnp.sum(total, axis=-1, keepdims=True) / depth
        squares = None
        for tile in range(tiles):
            centered = conv[tile] - average
            squares = centered * centered if squares is None else squares + centered * centered
        variance = jnp.sum(squares, axis=-1, keepdims=True) / depth
        inv_std = lax.rsqrt(variance + NORM_EPS)
        rows = slice(image * pixels, (image + 1) * pixels)
        inv_ref[rows, :] = jnp.broadcast_to(inv_std, (pixels, LANES))
        for tile in range(tiles):
            lanes = slice(tile * LANES, (tile + 1) * LANES)
            whitened = (conv[tile] - average) * inv_std
            white_ref[rows, lanes] = whitened
            gain = taps_ref[tile, TAPS : TAPS + 1, :]
            bias = taps_ref[tile, TAPS + 1 : TAPS + 2, :]
            normed_ref[rows, lanes] = (whitened * gain + bias).astype(BF16)


def cot_pack_kernel(image_ref, cot_ref, across_ref, sibling_ref):
    pixels, half = sibling_ref.shape
    quarter = half // 2
    side = lax.axis_index("rep") % 2
    parity = (lax.axis_index("shard") // INNER) % 2
    for place in range(2):
        start = pl.multiple_of(place * half + (1 - parity) * quarter, LANES)
        lanes = slice(place * quarter, (place + 1) * quarter)
        across_ref[pixels:, lanes] = cot_ref[:, pl.ds(start, quarter)]
    across_ref[:pixels, :] = image_ref[...]
    sibling_ref[...] = cot_ref[:, pl.ds(pl.multiple_of((1 - side) * half, LANES), half)]


def order_kernel(relative, own, *refs):
    place_rows(refs[:INNER], refs[INNER], own, relative)


def project_kernel(relative, own, *refs):
    weight, n_own, n_sibling, cot_ref, sibling_ref, across_ref, corner_ref = refs[:7]
    pieces = refs[7 : 7 + INNER]
    gp_ref, normed, cot, grad = refs[7 + INNER :]
    pixels, half = sibling_ref.shape
    quarter = half // 2
    side = lax.axis_index("rep") % 2
    parity = (lax.axis_index("shard") // INNER) % 2
    normed[: 2 * pixels, :] = n_own[...]
    normed[2 * pixels :, :] = n_sibling[...]
    start = pl.multiple_of(side * half + parity * quarter, LANES)
    cot[:pixels, :] = cot_ref[:, pl.ds(start, quarter)]
    start = pl.multiple_of(side * quarter, LANES)
    cot[pixels : 2 * pixels, :] = across_ref[pixels:, pl.ds(start, quarter)]
    start = pl.multiple_of(parity * quarter, LANES)
    cot[2 * pixels : 3 * pixels, :] = sibling_ref[:, pl.ds(start, quarter)]
    start = pl.multiple_of(side * quarter, LANES)
    cot[3 * pixels :, :] = corner_ref[pixels:, pl.ds(start, quarter)]
    for start in range(0, quarter, LANES):
        columns = slice(start, start + LANES)
        pre_act = jnp.dot(normed[...], weight[:, columns], preferred_element_type=F32)
        gp_ref[:, columns] = (cot[:, columns].astype(F32) * gelu_slope(pre_act)).astype(BF16)
    grad[...] = lax.dot_general(
        normed[...], gp_ref[...], (((0,), (0,)), ((), ())), preferred_element_type=F32
    )
    split_rows(grad, pieces, own, relative)


def back_project_kernel(weight, gp_ref, own_ref, other_ref):
    rows = own_ref.shape[0]
    grad_normed = lax.dot_general(
        gp_ref[...], weight[...], (((1,), (1,)), ((), ())), preferred_element_type=F32
    )
    own_ref[...] = grad_normed[:rows]
    other_ref[...] = grad_normed[rows:]


def norm_back_kernel(relative, own, height, breadth, *refs):
    gn_own, gn_other, white_ref, inv_ref, taps_ref, x_ref, far_ref = refs[:7]
    pieces = refs[7 : 7 + INNER]
    grad_ref, sent_ref, padded, grads_ref, rows, small, unfolded = refs[7 + INNER :]
    pixels, depth = x_ref.shape
    tiles = depth // LANES
    padded[...] = jnp.zeros_like(padded)
    rows[...] = jnp.zeros_like(rows)
    for image, source in enumerate((x_ref, far_ref)):
        span = slice(image * pixels, (image + 1) * pixels)
        first = None
        second = None
        for tile in range(tiles):
            lanes = slice(tile * LANES, (tile + 1) * LANES)
            part = source[:pixels, lanes].astype(F32)
            padded[image, tile, :, 8 : 8 + breadth, :] = part.reshape(height, breadth, LANES)
            grad_normed = gn_own[span, lanes] + gn_other[span, lanes]
            whitened = white_ref[span, lanes]
            product = grad_normed * whitened
            gain = taps_ref[tile, TAPS : TAPS + 1, :]
            rows[tile, TAPS : TAPS + 1, :] += jnp.sum(product, axis=0, keepdims=True)
            rows[tile, TAPS + 1 : TAPS + 2, :] += jnp.sum(grad_normed, axis=0, keepdims=True)
            one, two = grad_normed * gain, product * gain
            first = one if first is None else first + one
            second = two if second is None else second + two
        mean_first = jnp.sum(first, axis=-1, keepdims=True) / depth
        mean_second = jnp.sum(second, axis=-1, keepdims=True) / depth
        for tile in range(tiles):
            lanes = slice(tile * LANES, (tile + 1) * LANES)
            gain = taps_ref[tile, TAPS : TAPS + 1, :]
            grad_white = (gn_own[span, lanes] + gn_other[span, lanes]) * gain
            grad_conv = inv_ref[span, :] * (
                grad_white - mean_first - white_ref[span, lanes] * mean_second
            )
            grad_conv = grad_conv.reshape(height, breadth, LANES)
            grads_ref[image, tile] = grad_conv
            if image == 0:
                grad_ref[tile] = grad_conv
            else:
                sent_ref[tile] = grad_conv.astype(BF16)

    def one_tile(tile, carry):
        grads = [[grads_ref[image, tile, line] for line in range(height)] for image in range(2)]
        for across in range(KS):
            columns = slice(8 - MARGIN + across, 8 - MARGIN + across + breadth)
            shifted = [padded[image, tile, :, columns, :] for image in range(2)]
            for down in range(KS):
                total = None
                for image in range(2):
                    for line in range(height):
                        origin = line + down - MARGIN
                        if 0 <= origin < height:
                            term = grads[image][line] * shifted[image][origin]
                            total = term if total is None else total + term
                rows[tile, pl.ds(down * KS + across, 1), :] = jnp.sum(total, axis=0, keepdims=True)
        return carry

    lax.fori_loop(0, tiles, one_tile, 0)
    for tile in range(tiles):
        small[tile * LANES : (tile + 1) * LANES, :] = rows[tile].T
    if relative:
        whole = [unfolded.at[group] for group in range(INNER)]
        split_rows(small, whole, own, relative)
        for source, piece in zip(whole, pieces):
            piece[...] = fold(source[...]).astype(piece.dtype)
    else:
        split_rows(small, pieces, own, relative)


def conv_back_kernel(grad_ref, other_ref, taps_ref, out_ref, padded):
    tiles, height, breadth, _ = grad_ref.shape
    padded[...] = jnp.zeros_like(padded)
    padded[:, :, 8 : 8 + breadth, :] = grad_ref[...] + other_ref[...].astype(F32)

    def one_tile(tile, carry):
        sums = correlate(
            padded,
            tile,
            lambda down, across: taps_ref[tile, pl.ds(TAPS - 1 - down * KS - across, 1), :],
            height,
            breadth,
        )
        start = pl.multiple_of(tile * LANES, LANES)
        for line in range(height):
            out_ref[0, line, :, pl.ds(start, LANES)] = sums[line].astype(BF16)
        return carry

    lax.fori_loop(0, tiles, one_tile, 0)


def call(kernel, name, outs, scratch, micros, *args, mebibytes=48):
    flops = int(micros * 1.1e9)
    moved = sum(math.prod(a.shape) * a.dtype.itemsize for a in args)
    moved += sum(math.prod(o.shape) * o.dtype.itemsize for o in outs)
    return pl.pallas_call(
        kernel,
        out_shape=outs,
        in_specs=[VMEM] * len(args),
        out_specs=[VMEM] * len(outs),
        scratch_shapes=scratch,
        compiler_params=params(mebibytes),
        cost_estimate=pl.CostEstimate(flops=flops, bytes_accessed=moved, transcendentals=0),
        name=name,
    )(*args)


def body(images, cotangent, depthwise_weight, norm_gain, norm_bias, up_weight):
    shards, reps = lax.axis_size("shard"), lax.axis_size("rep")
    own, hidden = up_weight.shape
    depth = own * shards
    lines = shards // INNER
    half, quarter = hidden // 2, hidden // 4
    height, breadth = images.shape[1:3]
    pixels = height * breadth
    tiles = depth // LANES
    me = lax.axis_index("shard")
    side = lax.axis_index("rep") % 2
    parity = (me // INNER) % 2
    relative = own % 16 == 0

    def over_shard(array, flip):
        return lax.ppermute(array, "shard", [(i, i ^ flip) for i in range(shards)])

    def crossing(array, flip):
        pairs = [
            (i * reps + r, (i ^ flip) * reps + (r ^ 1)) for i in range(shards) for r in range(reps)
        ]
        return lax.ppermute(array, ("shard", "rep"), pairs)

    def over_core(array):
        return lax.ppermute(array, "rep", [(i, i ^ 1) for i in range(reps)])

    def true_order(pieces):
        if relative:
            return pieces
        stacked = jnp.stack(pieces).reshape(shards, own, -1)
        flips = jnp.arange(shards) ^ me
        places = (flips % INNER) * lines + flips // INNER
        return list(jnp.take(stacked, places, axis=0).reshape(INNER, lines * own, -1))

    def relative_order(pieces):
        if relative:
            return pieces
        stacked = jnp.concatenate([p.astype(F32) for p in pieces]).reshape(shards, own, -1)
        flips = (jnp.arange(lines)[None, :] * INNER + jnp.arange(INNER)[:, None]).reshape(-1)
        moved = jnp.take(stacked, flips ^ me, axis=0).reshape(INNER, lines * own, -1)
        return [moved[0]] + [moved[i].astype(BF16) for i in range(1, INNER)]

    shape = jax.ShapeDtypeStruct
    home, near, far = call(
        pack_kernel,
        "pack",
        [shape((own, quarter + LANES), BF16)] * 3,
        [
            pltpu.VMEM((LANES, LANES), F32),
            pltpu.VMEM((own, LANES), F32),
        ],
        0.5,
        up_weight,
        depthwise_weight,
        norm_gain[None, :],
        norm_bias[None, :],
        mebibytes=63,
    )
    image, cotangent = images.reshape(pixels, depth), cotangent.reshape(pixels, hidden)
    home, near, far, image, cotangent = lax.optimization_barrier(
        (home, near, far, image, cotangent)
    )
    gathered = [home] + [
        crossing(far if line % 2 else near, INNER * line) for line in range(1, lines)
    ]
    across, cot_sibling = call(
        cot_pack_kernel,
        "cot_pack",
        [shape((2 * pixels, half), BF16), shape((pixels, half), BF16)],
        [],
        0.4,
        image,
        cotangent,
    )
    across, cot_sibling = crossing(across, INNER), over_core(cot_sibling)

    rows = lines * own
    folded = rows // 2 if relative else rows
    weight_lines, extra_lines = call(
        assemble_kernel,
        "assemble",
        [shape((rows, quarter), BF16), shape((folded, LANES), BF16)],
        [],
        4.0,
        *gathered,
    )
    weights = [weight_lines] + [over_shard(weight_lines, flip) for flip in range(1, INNER)]
    extras = [extra_lines] + [crossing(extra_lines, flip) for flip in range(1, INNER)]
    weights, extras = true_order(weights), true_order(extras)
    (weight,) = call(
        functools.partial(order_kernel, relative, own),
        "order",
        [shape((depth, quarter), BF16)],
        [],
        3.0,
        *weights,
    )

    padded = pltpu.VMEM((tiles, height, breadth + 16, LANES), F32)
    normed, whitened, inv_std, taps = call(
        functools.partial(conv_norm_kernel, relative, own, height, breadth),
        "conv_norm",
        [
            shape((2 * pixels, depth), BF16),
            shape((2 * pixels, depth), F32),
            shape((2 * pixels, LANES), F32),
            shape((tiles, LANES, LANES), F32),
        ],
        [
            pltpu.VMEM((depth, LANES), F32),
            pltpu.VMEM((depth, LANES), F32),
            padded,
            pltpu.VMEM((tiles, pixels, LANES), F32),
        ],
        0.1,
        *extras,
        image,
        across,
    )
    normed, across = lax.optimization_barrier((normed, across))
    normed_sibling, corner = over_core(normed), over_core(across)
    *pieces, grad_pre = call(
        functools.partial(project_kernel, relative, own),
        "project",
        [shape((rows, quarter), F32)]
        + [shape((rows, quarter), BF16)] * (INNER - 1)
        + [shape((4 * pixels, quarter), BF16)],
        [
            pltpu.VMEM((4 * pixels, depth), BF16),
            pltpu.VMEM((4 * pixels, quarter), BF16),
            pltpu.VMEM((depth, quarter), F32),
        ],
        1.6,
        weight,
        normed,
        normed_sibling,
        cotangent,
        cot_sibling,
        across,
        corner,
    )
    gn_kept, gn_sent = call(
        back_project_kernel,
        "back_project",
        [shape((2 * pixels, depth), F32)] * 2,
        [],
        0.7,
        weight,
        grad_pre,
    )
    pieces = relative_order(pieces)
    arrived = [over_shard(piece, flip) for flip, piece in enumerate(pieces) if flip]
    *small, grad_conv, grad_sent = call(
        functools.partial(norm_back_kernel, relative, own, height, breadth),
        "norm_back",
        [shape((folded, LANES), F32)]
        + [shape((folded, LANES), BF16)] * (INNER - 1)
        + [
            shape((tiles, height, breadth, LANES), F32),
            shape((tiles, height, breadth, LANES), BF16),
        ],
        [
            pltpu.VMEM((2, tiles, height, breadth + 16, LANES), F32),
            pltpu.VMEM((2, tiles, height, breadth, LANES), F32),
            pltpu.VMEM((tiles, LANES, LANES), F32),
            pltpu.VMEM((depth, LANES), F32),
            pltpu.VMEM((INNER, rows, LANES), F32),
        ],
        0.1,
        gn_kept,
        over_core(gn_sent),
        whitened,
        inv_std,
        taps,
        image,
        across,
    )
    small = relative_order(small)
    small_arrived = [crossing(piece, flip) for flip, piece in enumerate(small) if flip]
    grad_other = crossing(grad_sent, INNER)
    (grad_images,) = call(
        conv_back_kernel,
        "conv_back",
        [shape(images.shape, BF16)],
        [padded],
        0.1,
        grad_conv,
        grad_other,
        taps,
    )

    home, *sent = call(
        functools.partial(plane_sum_kernel, lines),
        "plane_sum",
        [shape((own, quarter + LANES), F32)] + [shape((own, quarter + LANES), BF16)] * (lines - 1),
        [],
        2.0,
        pieces[0],
        *arrived,
        small[0],
        *small_arrived,
    )
    home, grad_images = lax.optimization_barrier((home, grad_images))
    came = [crossing(piece, INNER * line) for line, piece in enumerate(sent, 1)]
    (total,) = call(
        line_sum_kernel,
        "line_sum",
        [shape((own, 3 * quarter + LANES), F32)],
        [],
        0.3,
        home,
        *came,
    )
    if reps > 2:
        groups = [[i for i in range(reps) if i % 2 == s] for s in range(2)]
        total = lax.psum(total, "rep", axis_index_groups=groups)
    other = over_core(total)
    factor = 1.0 / math.sqrt(images.shape[0] * pixels * shards * reps)
    grad_up, grad_depthwise, grad_gain, grad_bias = call(
        functools.partial(finish_kernel, factor),
        "finish",
        [
            shape((own, hidden), F32),
            shape((own, TAPS), F32),
            shape((1, own), F32),
            shape((1, own), F32),
        ],
        [],
        0.5,
        total,
        other,
    )
    return (grad_images, grad_up, grad_depthwise, grad_gain[0], grad_bias[0])


def solution(mesh):
    placed = (
        P(("shard", "rep"), None, None, None),
        P(("shard", "rep"), None, None, None),
        P("shard", None),
        P("shard"),
        P("shard"),
        P("shard", None),
    )
    return jax.shard_map(
        body,
        mesh=mesh,
        in_specs=placed,
        out_specs=(
            P(("shard", "rep"), None, None, None),
            P("shard", None),
            P("shard", None),
            P("shard"),
            P("shard"),
        ),
        check_vma=False,
    )
```

```python
import functools
import math

import jax
import jax.numpy as jnp
from jax import lax
from jax.experimental import pallas as pl
from jax.experimental.pallas import tpu as pltpu
from jax.sharding import PartitionSpec as P

KS = 7
TAPS = KS * KS
MARGIN = KS // 2
LANES = 128
INNER = 4
NORM_EPS = 1e-06
BF16 = jnp.bfloat16
F32 = jnp.float32
VMEM = pl.BlockSpec(memory_space=pltpu.VMEM)


def params(mebibytes):
    return pltpu.CompilerParams(vmem_limit_bytes=mebibytes * 1024 * 1024)


def gelu_slope(inputs):
    cumulative = 0.5 * (1.0 + lax.erf(inputs * 0.7071067811865476))
    return cumulative + inputs * jnp.exp(-0.5 * inputs * inputs) * 0.3989422804014327


def block_rows(relative, group, line, own, lines):
    if relative:
        place = lax.axis_index("shard") ^ (line * INNER + group)
        return pl.multiple_of(place * own, 16)
    return (group * lines + line) * own


def place_rows(pieces, target, own, relative, cast=None):
    for group, piece in enumerate(pieces):
        lines = piece.shape[0] // own
        if not relative:
            target[group * piece.shape[0] : (group + 1) * piece.shape[0], :] = (
                piece[...] if cast is None else piece[...].astype(cast)
            )
            continue
        for line in range(lines):
            rows = piece[line * own : (line + 1) * own, :]
            start = block_rows(True, group, line, own, lines)
            target[pl.ds(start, own), :] = rows if cast is None else rows.astype(cast)


def split_rows(source, pieces, own, relative):
    for group, piece in enumerate(pieces):
        lines = piece.shape[0] // own
        if not relative:
            piece[...] = source[group * piece.shape[0] : (group + 1) * piece.shape[0], :].astype(
                piece.dtype
            )
            continue
        for line in range(lines):
            start = block_rows(True, group, line, own, lines)
            piece[line * own : (line + 1) * own, :] = source[pl.ds(start, own), :].astype(
                piece.dtype
            )


def correlate(padded, tile, tap_row, height, breadth):
    sums = [None] * height
    for across in range(KS):
        shifted = padded[tile, :, 8 - MARGIN + across : 8 - MARGIN + across + breadth, :]
        for down in range(KS):
            row = tap_row(down, across)
            for line in range(height):
                origin = line + down - MARGIN
                if 0 <= origin < height:
                    term = shifted[origin] * row
                    sums[line] = term if sums[line] is None else sums[line] + term
    return sums


def pack_kernel(w_ref, dw_ref, gain_ref, bias_ref, home_ref, near_ref, far_ref, turned, wide):
    own, hidden = w_ref.shape
    quarter = hidden // 4
    side = lax.axis_index("rep") % 2
    parity = (lax.axis_index("shard") // INNER) % 2
    turned[...] = jnp.zeros_like(turned)
    turned[TAPS : TAPS + 1, :own] = gain_ref[...].astype(F32)
    turned[TAPS + 1 : TAPS + 2, :own] = bias_ref[...].astype(F32)
    wide[...] = jnp.zeros_like(wide)
    wide[:, :TAPS] = dw_ref[...].astype(F32)
    extras = (wide[...] + turned[...].T[:own]).astype(BF16)
    kinds = ((home_ref, side, parity), (near_ref, 1 - side, parity), (far_ref, 1 - side, 1 - parity))
    for ref, place, which in kinds:
        start = pl.multiple_of(place * (2 * quarter) + which * quarter, LANES)
        ref[:, :quarter] = w_ref[:, pl.ds(start, quarter)]
        ref[:, quarter:] = extras


def assemble_kernel(*refs):
    pieces, (weight_ref, extra_ref) = refs[:-2], refs[-2:]
    own = pieces[0].shape[0]
    quarter = weight_ref.shape[1]
    for line, piece in enumerate(pieces):
        weight_ref[line * own : (line + 1) * own, :] = piece[:, :quarter]
    extras = jnp.concatenate([piece[:, quarter:].astype(F32) for piece in pieces], axis=0)
    if extra_ref.shape[0] < extras.shape[0]:
        extras = fold(extras)
    extra_ref[...] = extras.astype(BF16)


def plane_sum_kernel(lines, *refs):
    home, first, second = refs[:3]
    small, outs = refs[3 : 3 + INNER], refs[3 + INNER :]
    own = home.shape[0] // lines
    quarter = home.shape[1]
    extras = small[0][...]
    for part in small[1:]:
        extras = extras + part[...].astype(F32)
    if extras.shape[0] < home.shape[0]:
        extras = unfold(extras)
    for line, out in enumerate(outs):
        rows = slice(line * own, (line + 1) * own)
        total = home[rows, :] + first[rows, :].astype(F32) + second[rows, :].astype(F32)
        out[:, :quarter] = total.astype(out.dtype)
        out[:, quarter:] = extras[rows, :].astype(out.dtype)


def line_sum_kernel(*refs):
    pieces, total_ref = refs[:-1], refs[-1]
    quarter = pieces[0].shape[1] - LANES
    near, far = None, None
    for line, piece in enumerate(pieces[1:], 1):
        came = piece[...].astype(F32)
        if line % 2:
            far = came if far is None else far + came
        else:
            near = came if near is None else near + came
    total_ref[:, :quarter] = pieces[0][:, :quarter]
    total_ref[:, quarter : 2 * quarter] = near[:, :quarter]
    total_ref[:, 2 * quarter : 3 * quarter] = far[:, :quarter]
    total_ref[:, 3 * quarter :] = pieces[0][:, quarter:] + near[:, quarter:] + far[:, quarter:]


def finish_kernel(factor, mine_ref, other_ref, up_ref, dw_ref, gain_ref, bias_ref):
    own, quarter = mine_ref.shape[0], (mine_ref.shape[1] - LANES) // 3
    side = lax.axis_index("rep") % 2
    parity = (lax.axis_index("shard") // INNER) % 2
    for place, home, came in ((side, mine_ref, other_ref), (1 - side, other_ref, mine_ref)):
        start = pl.multiple_of((2 * place + parity) * quarter, LANES)
        total = home[:, :quarter] + came[:, quarter : 2 * quarter]
        up_ref[:, pl.ds(start, quarter)] = total * factor
        start = pl.multiple_of((2 * place + 1 - parity) * quarter, LANES)
        up_ref[:, pl.ds(start, quarter)] = came[:, 2 * quarter : 3 * quarter] * factor
    low = 3 * quarter
    sums = (mine_ref[:, low:] + other_ref[:, low:]) * factor
    dw_ref[...] = sums[:, :TAPS]
    turned = sums.T
    gain_ref[...] = turned[TAPS : TAPS + 1, :]
    bias_ref[...] = turned[TAPS + 1 : TAPS + 2, :]


def fold(rows):
    half = rows.shape[0] // 2
    low = lax.broadcasted_iota(jnp.int32, (half, LANES), 1) < LANES // 2
    return jnp.where(low, rows[:half], pltpu.roll(rows[half:], LANES // 2, 1))


def unfold(rows):
    return jnp.concatenate([rows, pltpu.roll(rows, LANES // 2, 1)], axis=0)


def conv_norm_kernel(relative, own, height, breadth, *refs):
    small = refs[:INNER]
    sources = refs[INNER : INNER + 2]
    x_ref = sources[0]
    normed_ref, white_ref, inv_ref, taps_ref, gathered, unfolded, padded, conv = refs[INNER + 2 :]
    pixels, depth = x_ref.shape
    tiles = depth // LANES
    if relative:
        for group, piece in enumerate(small):
            unfolded[group * 2 * piece.shape[0] : (group + 1) * 2 * piece.shape[0], :] = unfold(
                piece[...].astype(F32)
            )
        count = unfolded.shape[0] // INNER
        small = [unfolded.at[pl.ds(group * count, count), :] for group in range(INNER)]
    place_rows(small, gathered, own, relative, F32)
    padded[...] = jnp.zeros_like(padded)
    for tile in range(tiles):
        lanes = slice(tile * LANES, (tile + 1) * LANES)
        taps_ref[tile] = gathered[lanes, :].T

    for image, source in enumerate(sources):
        for tile in range(tiles):
            lanes = slice(tile * LANES, (tile + 1) * LANES)
            part = source[:pixels, lanes].astype(F32)
            padded[tile, :, 8 : 8 + breadth, :] = part.reshape(height, breadth, LANES)

        def one_tile(tile, carry):
            sums = correlate(
                padded,
                tile,
                lambda down, across: taps_ref[tile, pl.ds(down * KS + across, 1), :],
                height,
                breadth,
            )
            for line in range(height):
                conv[tile, line * breadth : (line + 1) * breadth, :] = sums[line]
            return carry

        lax.fori_loop(0, tiles, one_tile, 0)
        total = conv[0]
        for tile in range(1, tiles):
            total = total + conv[tile]
        average = jnp.sum(total, axis=-1, keepdims=True) / depth
        squares = None
        for tile in range(tiles):
            centered = conv[tile] - average
            squares = centered * centered if squares is None else squares + centered * centered
        variance = jnp.sum(squares, axis=-1, keepdims=True) / depth
        inv_std = lax.rsqrt(variance + NORM_EPS)
        rows = slice(image * pixels, (image + 1) * pixels)
        inv_ref[rows, :] = jnp.broadcast_to(inv_std, (pixels, LANES))
        for tile in range(tiles):
            lanes = slice(tile * LANES, (tile + 1) * LANES)
            whitened = (conv[tile] - average) * inv_std
            white_ref[rows, lanes] = whitened
            gain = taps_ref[tile, TAPS : TAPS + 1, :]
            bias = taps_ref[tile, TAPS + 1 : TAPS + 2, :]
            normed_ref[rows, lanes] = (whitened * gain + bias).astype(BF16)


def cot_pack_kernel(image_ref, cot_ref, across_ref, sibling_ref):
    pixels, half = sibling_ref.shape
    quarter = half // 2
    side = lax.axis_index("rep") % 2
    parity = (lax.axis_index("shard") // INNER) % 2
    for place in range(2):
        start = pl.multiple_of(place * half + (1 - parity) * quarter, LANES)
        lanes = slice(place * quarter, (place + 1) * quarter)
        across_ref[pixels:, lanes] = cot_ref[:, pl.ds(start, quarter)]
    across_ref[:pixels, :] = image_ref[...]
    sibling_ref[...] = cot_ref[:, pl.ds(pl.multiple_of((1 - side) * half, LANES), half)]


def order_kernel(relative, own, *refs):
    place_rows(refs[:INNER], refs[INNER], own, relative)


def project_kernel(relative, own, *refs):
    weight, n_own, n_sibling, cot_ref, sibling_ref, across_ref, corner_ref = refs[:7]
    *pieces, gp_ref, normed, cot, grad = refs[7:]
    pixels, half = sibling_ref.shape
    quarter = half // 2
    side = lax.axis_index("rep") % 2
    parity = (lax.axis_index("shard") // INNER) % 2
    normed[: 2 * pixels, :] = n_own[...]
    normed[2 * pixels :, :] = n_sibling[...]
    start = pl.multiple_of(side * half + parity * quarter, LANES)
    cot[:pixels, :] = cot_ref[:, pl.ds(start, quarter)]
    start = pl.multiple_of(side * quarter, LANES)
    cot[pixels : 2 * pixels, :] = across_ref[pixels:, pl.ds(start, quarter)]
    start = pl.multiple_of(parity * quarter, LANES)
    cot[2 * pixels : 3 * pixels, :] = sibling_ref[:, pl.ds(start, quarter)]
    start = pl.multiple_of(side * quarter, LANES)
    cot[3 * pixels :, :] = corner_ref[pixels:, pl.ds(start, quarter)]
    for start in range(0, quarter, LANES):
        columns = slice(start, start + LANES)
        pre_act = jnp.dot(normed[...], weight[:, columns], preferred_element_type=F32)
        gp_ref[:, columns] = (cot[:, columns].astype(F32) * gelu_slope(pre_act)).astype(BF16)
    grad[...] = lax.dot_general(
        normed[...], gp_ref[...], (((0,), (0,)), ((), ())), preferred_element_type=F32
    )
    if not relative:
        pieces[0][...] = grad[...]
        return
    home, second, sent = pieces
    lines = home.shape[0] // own
    for line in range(lines):
        rows = slice(line * own, (line + 1) * own)
        below = slice((lines + line) * own, (lines + line + 1) * own)
        for ref, span, group in (
            (home, rows, 0),
            (second, rows, 2 - side),
            (sent, rows, 1 + side),
            (sent, below, INNER - 1),
        ):
            start = block_rows(True, group, line, own, lines)
            ref[span, :] = grad[pl.ds(start, own), :].astype(ref.dtype)


def relay_kernel(second_ref, came_ref, out_ref):
    rows = out_ref.shape[0]
    out_ref[...] = (second_ref[...] + came_ref[rows:, :].astype(F32)).astype(BF16)


def back_project_kernel(weight, gp_ref, own_ref, other_ref):
    rows = own_ref.shape[0]
    grad_normed = lax.dot_general(
        gp_ref[...], weight[...], (((1,), (1,)), ((), ())), preferred_element_type=F32
    )
    own_ref[...] = grad_normed[:rows]
    other_ref[...] = grad_normed[rows:]


def norm_back_kernel(relative, own, height, breadth, *refs):
    gn_own, gn_other, white_ref, inv_ref, taps_ref, x_ref, far_ref = refs[:7]
    pieces = refs[7 : 7 + INNER]
    grad_ref, sent_ref, padded, grads_ref, rows, small, unfolded = refs[7 + INNER :]
    pixels, depth = x_ref.shape
    tiles = depth // LANES
    padded[...] = jnp.zeros_like(padded)
    rows[...] = jnp.zeros_like(rows)
    for image, source in enumerate((x_ref, far_ref)):
        span = slice(image * pixels, (image + 1) * pixels)
        first = None
        second = None
        for tile in range(tiles):
            lanes = slice(tile * LANES, (tile + 1) * LANES)
            part = source[:pixels, lanes].astype(F32)
            padded[image, tile, :, 8 : 8 + breadth, :] = part.reshape(height, breadth, LANES)
            grad_normed = gn_own[span, lanes] + gn_other[span, lanes]
            whitened = white_ref[span, lanes]
            product = grad_normed * whitened
            gain = taps_ref[tile, TAPS : TAPS + 1, :]
            rows[tile, TAPS : TAPS + 1, :] += jnp.sum(product, axis=0, keepdims=True)
            rows[tile, TAPS + 1 : TAPS + 2, :] += jnp.sum(grad_normed, axis=0, keepdims=True)
            one, two = grad_normed * gain, product * gain
            first = one if first is None else first + one
            second = two if second is None else second + two
        mean_first = jnp.sum(first, axis=-1, keepdims=True) / depth
        mean_second = jnp.sum(second, axis=-1, keepdims=True) / depth
        for tile in range(tiles):
            lanes = slice(tile * LANES, (tile + 1) * LANES)
            gain = taps_ref[tile, TAPS : TAPS + 1, :]
            grad_white = (gn_own[span, lanes] + gn_other[span, lanes]) * gain
            grad_conv = inv_ref[span, :] * (
                grad_white - mean_first - white_ref[span, lanes] * mean_second
            )
            grad_conv = grad_conv.reshape(height, breadth, LANES)
            grads_ref[image, tile] = grad_conv
            if image == 0:
                grad_ref[tile] = grad_conv
            else:
                sent_ref[tile] = grad_conv.astype(BF16)

    def one_tile(tile, carry):
        grads = [[grads_ref[image, tile, line] for line in range(height)] for image in range(2)]
        for across in range(KS):
            columns = slice(8 - MARGIN + across, 8 - MARGIN + across + breadth)
            shifted = [padded[image, tile, :, columns, :] for image in range(2)]
            for down in range(KS):
                total = None
                for image in range(2):
                    for line in range(height):
                        origin = line + down - MARGIN
                        if 0 <= origin < height:
                            term = grads[image][line] * shifted[image][origin]
                            total = term if total is None else total + term
                rows[tile, pl.ds(down * KS + across, 1), :] = jnp.sum(total, axis=0, keepdims=True)
        return carry

    lax.fori_loop(0, tiles, one_tile, 0)
    for tile in range(tiles):
        small[tile * LANES : (tile + 1) * LANES, :] = rows[tile].T
    if relative:
        whole = [unfolded.at[group] for group in range(INNER)]
        split_rows(small, whole, own, relative)
        for source, piece in zip(whole, pieces):
            piece[...] = fold(source[...]).astype(piece.dtype)
    else:
        split_rows(small, pieces, own, relative)


def conv_back_kernel(grad_ref, other_ref, taps_ref, out_ref, padded):
    tiles, height, breadth, _ = grad_ref.shape
    padded[...] = jnp.zeros_like(padded)
    padded[:, :, 8 : 8 + breadth, :] = grad_ref[...] + other_ref[...].astype(F32)

    def one_tile(tile, carry):
        sums = correlate(
            padded,
            tile,
            lambda down, across: taps_ref[tile, pl.ds(TAPS - 1 - down * KS - across, 1), :],
            height,
            breadth,
        )
        start = pl.multiple_of(tile * LANES, LANES)
        for line in range(height):
            out_ref[0, line, :, pl.ds(start, LANES)] = sums[line].astype(BF16)
        return carry

    lax.fori_loop(0, tiles, one_tile, 0)


def call(kernel, name, outs, scratch, micros, *args, mebibytes=48):
    flops = int(micros * 1.1e9)
    moved = sum(math.prod(a.shape) * a.dtype.itemsize for a in args)
    moved += sum(math.prod(o.shape) * o.dtype.itemsize for o in outs)
    return pl.pallas_call(
        kernel,
        out_shape=outs,
        in_specs=[VMEM] * len(args),
        out_specs=[VMEM] * len(outs),
        scratch_shapes=scratch,
        compiler_params=params(mebibytes),
        cost_estimate=pl.CostEstimate(flops=flops, bytes_accessed=moved, transcendentals=0),
        name=name,
    )(*args)


def body(images, cotangent, depthwise_weight, norm_gain, norm_bias, up_weight):
    shards, reps = lax.axis_size("shard"), lax.axis_size("rep")
    own, hidden = up_weight.shape
    depth = own * shards
    lines = shards // INNER
    half, quarter = hidden // 2, hidden // 4
    height, breadth = images.shape[1:3]
    pixels = height * breadth
    tiles = depth // LANES
    me = lax.axis_index("shard")
    side = lax.axis_index("rep") % 2
    parity = (me // INNER) % 2
    relative = own % 16 == 0

    def over_shard(array, flip):
        return lax.ppermute(array, "shard", [(i, i ^ flip) for i in range(shards)])

    def crossing(array, flip):
        pairs = [
            (i * reps + r, (i ^ flip) * reps + (r ^ 1)) for i in range(shards) for r in range(reps)
        ]
        return lax.ppermute(array, ("shard", "rep"), pairs)

    def hop(array, place):
        flips = [(1, 2), (2, 1)]
        pairs = [
            (i * reps + r, (i ^ flips[r % 2][place]) * reps + r)
            for i in range(shards)
            for r in range(reps)
        ]
        return lax.ppermute(array, ("shard", "rep"), pairs)

    def over_core(array):
        return lax.ppermute(array, "rep", [(i, i ^ 1) for i in range(reps)])

    def true_order(pieces):
        if relative:
            return pieces
        stacked = jnp.stack(pieces).reshape(shards, own, -1)
        flips = jnp.arange(shards) ^ me
        places = (flips % INNER) * lines + flips // INNER
        return list(jnp.take(stacked, places, axis=0).reshape(INNER, lines * own, -1))

    def relative_order(pieces):
        if relative:
            return pieces
        stacked = jnp.concatenate([p.astype(F32) for p in pieces]).reshape(shards, own, -1)
        flips = (jnp.arange(lines)[None, :] * INNER + jnp.arange(INNER)[:, None]).reshape(-1)
        moved = jnp.take(stacked, flips ^ me, axis=0).reshape(INNER, lines * own, -1)
        return [moved[0]] + [moved[i].astype(BF16) for i in range(1, INNER)]

    shape = jax.ShapeDtypeStruct
    home, near, far = call(
        pack_kernel,
        "pack",
        [shape((own, quarter + LANES), BF16)] * 3,
        [
            pltpu.VMEM((LANES, LANES), F32),
            pltpu.VMEM((own, LANES), F32),
        ],
        0.5,
        up_weight,
        depthwise_weight,
        norm_gain[None, :],
        norm_bias[None, :],
        mebibytes=63,
    )
    image, cotangent = images.reshape(pixels, depth), cotangent.reshape(pixels, hidden)
    home, near, far, image, cotangent = lax.optimization_barrier(
        (home, near, far, image, cotangent)
    )
    gathered = [home] + [
        crossing(far if line % 2 else near, INNER * line) for line in range(1, lines)
    ]
    across, cot_sibling = call(
        cot_pack_kernel,
        "cot_pack",
        [shape((2 * pixels, half), BF16), shape((pixels, half), BF16)],
        [],
        0.4,
        image,
        cotangent,
    )
    across, cot_sibling = crossing(across, INNER), over_core(cot_sibling)

    rows = lines * own
    folded = rows // 2 if relative else rows
    weight_lines, extra_lines = call(
        assemble_kernel,
        "assemble",
        [shape((rows, quarter), BF16), shape((folded, LANES), BF16)],
        [],
        4.0,
        *gathered,
    )
    weights = [weight_lines] + [over_shard(weight_lines, flip) for flip in range(1, INNER)]
    extras = [extra_lines] + [crossing(extra_lines, flip) for flip in range(1, INNER)]
    weights, extras = true_order(weights), true_order(extras)
    (weight,) = call(
        functools.partial(order_kernel, relative, own),
        "order",
        [shape((depth, quarter), BF16)],
        [],
        2.6,
        *weights,
    )

    padded = pltpu.VMEM((tiles, height, breadth + 16, LANES), F32)
    normed, whitened, inv_std, taps = call(
        functools.partial(conv_norm_kernel, relative, own, height, breadth),
        "conv_norm",
        [
            shape((2 * pixels, depth), BF16),
            shape((2 * pixels, depth), F32),
            shape((2 * pixels, LANES), F32),
            shape((tiles, LANES, LANES), F32),
        ],
        [
            pltpu.VMEM((depth, LANES), F32),
            pltpu.VMEM((depth, LANES), F32),
            padded,
            pltpu.VMEM((tiles, pixels, LANES), F32),
        ],
        0.1,
        *extras,
        image,
        across,
    )
    normed, across = lax.optimization_barrier((normed, across))
    normed_sibling, corner = over_core(normed), over_core(across)
    *pieces, grad_pre = call(
        functools.partial(project_kernel, relative, own),
        "project",
        (
            [shape((rows, quarter), F32)] * 2 + [shape((2 * rows, quarter), BF16)]
            if relative
            else [shape((depth, quarter), F32)]
        )
        + [shape((4 * pixels, quarter), BF16)],
        [
            pltpu.VMEM((4 * pixels, depth), BF16),
            pltpu.VMEM((4 * pixels, quarter), BF16),
            pltpu.VMEM((depth, quarter), F32),
        ],
        1.6,
        weight,
        normed,
        normed_sibling,
        cotangent,
        cot_sibling,
        across,
        corner,
    )
    gn_kept, gn_sent = call(
        back_project_kernel,
        "back_project",
        [shape((2 * pixels, depth), F32)] * 2,
        [],
        0.7,
        weight,
        grad_pre,
    )
    if not relative:
        first, second, corner = relative_order(list(pieces[0].reshape(INNER, rows, quarter)))[1:]
        home = relative_order(list(pieces[0].reshape(INNER, rows, quarter)))[0]
        first, second = jnp.where(side == 0, first, second), jnp.where(side == 0, second, first)
        pieces = [home, second.astype(F32), jnp.concatenate([first, corner])]
    home_piece, second_piece, sent_piece = pieces
    first_came = hop(sent_piece, 0)
    *small, grad_conv, grad_sent = call(
        functools.partial(norm_back_kernel, relative, own, height, breadth),
        "norm_back",
        [shape((folded, LANES), F32)]
        + [shape((folded, LANES), BF16)] * (INNER - 1)
        + [
            shape((tiles, height, breadth, LANES), F32),
            shape((tiles, height, breadth, LANES), BF16),
        ],
        [
            pltpu.VMEM((2, tiles, height, breadth + 16, LANES), F32),
            pltpu.VMEM((2, tiles, height, breadth, LANES), F32),
            pltpu.VMEM((tiles, LANES, LANES), F32),
            pltpu.VMEM((depth, LANES), F32),
            pltpu.VMEM((INNER, rows, LANES), F32),
        ],
        0.1,
        gn_kept,
        over_core(gn_sent),
        whitened,
        inv_std,
        taps,
        image,
        across,
    )
    first_came, grad_conv = lax.optimization_barrier((first_came, grad_conv))
    (relayed,) = call(
        relay_kernel,
        "relay",
        [shape((rows, quarter), BF16)],
        [],
        0.3,
        second_piece,
        first_came,
    )
    second_came = hop(relayed, 1)
    small = relative_order(small)
    small_arrived = [crossing(piece, flip) for flip, piece in enumerate(small) if flip]
    grad_other = crossing(grad_sent, INNER)
    (grad_images,) = call(
        conv_back_kernel,
        "conv_back",
        [shape(images.shape, BF16)],
        [padded],
        0.1,
        grad_conv,
        grad_other,
        taps,
    )

    home, *sent = call(
        functools.partial(plane_sum_kernel, lines),
        "plane_sum",
        [shape((own, quarter + LANES), F32)] + [shape((own, quarter + LANES), BF16)] * (lines - 1),
        [],
        0.8,
        home_piece,
        first_came,
        second_came,
        small[0],
        *small_arrived,
    )
    home, grad_images = lax.optimization_barrier((home, grad_images))
    came = [crossing(piece, INNER * line) for line, piece in enumerate(sent, 1)]
    (total,) = call(
        line_sum_kernel,
        "line_sum",
        [shape((own, 3 * quarter + LANES), F32)],
        [],
        0.3,
        home,
        *came,
    )
    if reps > 2:
        groups = [[i for i in range(reps) if i % 2 == s] for s in range(2)]
        total = lax.psum(total, "rep", axis_index_groups=groups)
    other = over_core(total)
    factor = 1.0 / math.sqrt(images.shape[0] * pixels * shards * reps)
    grad_up, grad_depthwise, grad_gain, grad_bias = call(
        functools.partial(finish_kernel, factor),
        "finish",
        [
            shape((own, hidden), F32),
            shape((own, TAPS), F32),
            shape((1, own), F32),
            shape((1, own), F32),
        ],
        [],
        0.5,
        total,
        other,
    )
    return (grad_images, grad_up, grad_depthwise, grad_gain[0], grad_bias[0])


def solution(mesh):
    placed = (
        P(("shard", "rep"), None, None, None),
        P(("shard", "rep"), None, None, None),
        P("shard", None),
        P("shard"),
        P("shard"),
        P("shard", None),
    )
    return jax.shard_map(
        body,
        mesh=mesh,
        in_specs=placed,
        out_specs=(
            P(("shard", "rep"), None, None, None),
            P("shard", None),
            P("shard", None),
            P("shard"),
            P("shard"),
        ),
        check_vma=False,
    )
```

```python
import functools
import math

import jax
import jax.numpy as jnp
from jax import lax
from jax.experimental import pallas as pl
from jax.experimental.pallas import tpu as pltpu
from jax.sharding import PartitionSpec as P

KS = 7
TAPS = KS * KS
MARGIN = KS // 2
LANES = 128
INNER = 4
NORM_EPS = 1e-06
BF16 = jnp.bfloat16
F32 = jnp.float32
VMEM = pl.BlockSpec(memory_space=pltpu.VMEM)


def params(mebibytes):
    return pltpu.CompilerParams(vmem_limit_bytes=mebibytes * 1024 * 1024)


def gelu_slope(inputs):
    cumulative = 0.5 * (1.0 + lax.erf(inputs * 0.7071067811865476))
    return cumulative + inputs * jnp.exp(-0.5 * inputs * inputs) * 0.3989422804014327


def block_rows(relative, group, line, own, lines):
    if relative:
        place = lax.axis_index("shard") ^ (line * INNER + group)
        return pl.multiple_of(place * own, 16)
    return (group * lines + line) * own


def place_rows(pieces, target, own, relative, cast=None):
    for group, piece in enumerate(pieces):
        lines = piece.shape[0] // own
        if not relative:
            target[group * piece.shape[0] : (group + 1) * piece.shape[0], :] = (
                piece[...] if cast is None else piece[...].astype(cast)
            )
            continue
        for line in range(lines):
            rows = piece[line * own : (line + 1) * own, :]
            start = block_rows(True, group, line, own, lines)
            target[pl.ds(start, own), :] = rows if cast is None else rows.astype(cast)


def split_rows(source, pieces, own, relative):
    for group, piece in enumerate(pieces):
        lines = piece.shape[0] // own
        if not relative:
            piece[...] = source[group * piece.shape[0] : (group + 1) * piece.shape[0], :].astype(
                piece.dtype
            )
            continue
        for line in range(lines):
            start = block_rows(True, group, line, own, lines)
            piece[line * own : (line + 1) * own, :] = source[pl.ds(start, own), :].astype(
                piece.dtype
            )


def correlate(padded, tile, tap_row, height, breadth):
    sums = [None] * height
    for across in range(KS):
        shifted = padded[tile, :, 8 - MARGIN + across : 8 - MARGIN + across + breadth, :]
        for down in range(KS):
            row = tap_row(down, across)
            for line in range(height):
                origin = line + down - MARGIN
                if 0 <= origin < height:
                    term = shifted[origin] * row
                    sums[line] = term if sums[line] is None else sums[line] + term
    return sums


def pack_kernel(w_ref, dw_ref, gain_ref, bias_ref, home_ref, near_ref, far_ref, turned, wide):
    own, hidden = w_ref.shape
    quarter = hidden // 4
    side = lax.axis_index("rep") % 2
    parity = (lax.axis_index("shard") // INNER) % 2
    turned[...] = jnp.zeros_like(turned)
    turned[TAPS : TAPS + 1, :own] = gain_ref[...].astype(F32)
    turned[TAPS + 1 : TAPS + 2, :own] = bias_ref[...].astype(F32)
    wide[...] = jnp.zeros_like(wide)
    wide[:, :TAPS] = dw_ref[...].astype(F32)
    extras = (wide[...] + turned[...].T[:own]).astype(BF16)
    kinds = ((home_ref, side, parity), (near_ref, 1 - side, parity), (far_ref, 1 - side, 1 - parity))
    for ref, place, which in kinds:
        start = pl.multiple_of(place * (2 * quarter) + which * quarter, LANES)
        ref[:, :quarter] = w_ref[:, pl.ds(start, quarter)]
        ref[:, quarter:] = extras


def assemble_kernel(*refs):
    pieces, (weight_ref, extra_ref) = refs[:-2], refs[-2:]
    own = pieces[0].shape[0]
    quarter = weight_ref.shape[1]
    for line, piece in enumerate(pieces):
        weight_ref[line * own : (line + 1) * own, :] = piece[:, :quarter]
    extras = jnp.concatenate([piece[:, quarter:].astype(F32) for piece in pieces], axis=0)
    if extra_ref.shape[0] < extras.shape[0]:
        extras = fold(extras)
    extra_ref[...] = extras.astype(BF16)


def plane_sum_kernel(lines, *refs):
    pieces, small, outs = refs[:INNER], refs[INNER : 2 * INNER], refs[2 * INNER :]
    own = pieces[0].shape[0] // lines
    quarter = pieces[0].shape[1]
    extras = small[0][...]
    for part in small[1:]:
        extras = extras + part[...].astype(F32)
    if extras.shape[0] < pieces[0].shape[0]:
        extras = unfold(extras)
    for line, out in enumerate(outs):
        rows = slice(line * own, (line + 1) * own)
        total = pieces[0][rows, :]
        for part in pieces[1:]:
            total = total + part[rows, :].astype(F32)
        out[:, :quarter] = total.astype(out.dtype)
        out[:, quarter:] = extras[rows, :].astype(out.dtype)


def line_sum_kernel(*refs):
    pieces, total_ref = refs[:-1], refs[-1]
    quarter = pieces[0].shape[1] - LANES
    near, far = None, None
    for line, piece in enumerate(pieces[1:], 1):
        came = piece[...].astype(F32)
        if line % 2:
            far = came if far is None else far + came
        else:
            near = came if near is None else near + came
    total_ref[:, :quarter] = pieces[0][:, :quarter]
    total_ref[:, quarter : 2 * quarter] = near[:, :quarter]
    total_ref[:, 2 * quarter : 3 * quarter] = far[:, :quarter]
    total_ref[:, 3 * quarter :] = pieces[0][:, quarter:] + near[:, quarter:] + far[:, quarter:]


def finish_kernel(factor, mine_ref, other_ref, up_ref, dw_ref, gain_ref, bias_ref):
    own, quarter = mine_ref.shape[0], (mine_ref.shape[1] - LANES) // 3
    side = lax.axis_index("rep") % 2
    parity = (lax.axis_index("shard") // INNER) % 2
    for place, home, came in ((side, mine_ref, other_ref), (1 - side, other_ref, mine_ref)):
        start = pl.multiple_of((2 * place + parity) * quarter, LANES)
        total = home[:, :quarter] + came[:, quarter : 2 * quarter]
        up_ref[:, pl.ds(start, quarter)] = total * factor
        start = pl.multiple_of((2 * place + 1 - parity) * quarter, LANES)
        up_ref[:, pl.ds(start, quarter)] = came[:, 2 * quarter : 3 * quarter] * factor
    low = 3 * quarter
    sums = (mine_ref[:, low:] + other_ref[:, low:]) * factor
    dw_ref[...] = sums[:, :TAPS]
    turned = sums.T
    gain_ref[...] = turned[TAPS : TAPS + 1, :]
    bias_ref[...] = turned[TAPS + 1 : TAPS + 2, :]


def fold(rows):
    half = rows.shape[0] // 2
    low = lax.broadcasted_iota(jnp.int32, (half, LANES), 1) < LANES // 2
    return jnp.where(low, rows[:half], pltpu.roll(rows[half:], LANES // 2, 1))


def unfold(rows):
    return jnp.concatenate([rows, pltpu.roll(rows, LANES // 2, 1)], axis=0)


def conv_norm_kernel(relative, own, height, breadth, *refs):
    small = refs[:INNER]
    sources = refs[INNER : INNER + 2]
    x_ref = sources[0]
    normed_ref, white_ref, inv_ref, taps_ref, gathered, unfolded, padded, conv = refs[INNER + 2 :]
    pixels, depth = x_ref.shape
    tiles = depth // LANES
    if relative:
        for group, piece in enumerate(small):
            unfolded[group * 2 * piece.shape[0] : (group + 1) * 2 * piece.shape[0], :] = unfold(
                piece[...].astype(F32)
            )
        count = unfolded.shape[0] // INNER
        small = [unfolded.at[pl.ds(group * count, count), :] for group in range(INNER)]
    place_rows(small, gathered, own, relative, F32)
    padded[...] = jnp.zeros_like(padded)
    for tile in range(tiles):
        lanes = slice(tile * LANES, (tile + 1) * LANES)
        taps_ref[tile] = gathered[lanes, :].T

    for image, source in enumerate(sources):
        for tile in range(tiles):
            lanes = slice(tile * LANES, (tile + 1) * LANES)
            part = source[:pixels, lanes].astype(F32)
            padded[tile, :, 8 : 8 + breadth, :] = part.reshape(height, breadth, LANES)

        def one_tile(tile, carry):
            sums = correlate(
                padded,
                tile,
                lambda down, across: taps_ref[tile, pl.ds(down * KS + across, 1), :],
                height,
                breadth,
            )
            for line in range(height):
                conv[tile, line * breadth : (line + 1) * breadth, :] = sums[line]
            return carry

        lax.fori_loop(0, tiles, one_tile, 0)
        total = conv[0]
        for tile in range(1, tiles):
            total = total + conv[tile]
        average = jnp.sum(total, axis=-1, keepdims=True) / depth
        squares = None
        for tile in range(tiles):
            centered = conv[tile] - average
            squares = centered * centered if squares is None else squares + centered * centered
        variance = jnp.sum(squares, axis=-1, keepdims=True) / depth
        inv_std = lax.rsqrt(variance + NORM_EPS)
        rows = slice(image * pixels, (image + 1) * pixels)
        inv_ref[rows, :] = jnp.broadcast_to(inv_std, (pixels, LANES))
        for tile in range(tiles):
            lanes = slice(tile * LANES, (tile + 1) * LANES)
            whitened = (conv[tile] - average) * inv_std
            white_ref[rows, lanes] = whitened
            gain = taps_ref[tile, TAPS : TAPS + 1, :]
            bias = taps_ref[tile, TAPS + 1 : TAPS + 2, :]
            normed_ref[rows, lanes] = (whitened * gain + bias).astype(BF16)


def cot_pack_kernel(image_ref, cot_ref, across_ref, sibling_ref):
    pixels, half = sibling_ref.shape
    quarter = half // 2
    side = lax.axis_index("rep") % 2
    parity = (lax.axis_index("shard") // INNER) % 2
    for place in range(2):
        start = pl.multiple_of(place * half + (1 - parity) * quarter, LANES)
        lanes = slice(place * quarter, (place + 1) * quarter)
        across_ref[pixels:, lanes] = cot_ref[:, pl.ds(start, quarter)]
    across_ref[:pixels, :] = image_ref[...]
    sibling_ref[...] = cot_ref[:, pl.ds(pl.multiple_of((1 - side) * half, LANES), half)]


def join_kernel(own_ref, came_ref, out_ref):
    rows = own_ref.shape[0]
    out_ref[:rows, :] = own_ref[...]
    out_ref[rows:, :] = came_ref[...]


def order_kernel(relative, own, *refs):
    if not relative:
        place_rows(refs[:INNER], refs[INNER], own, relative)
        return
    home, first, second, out_ref = refs
    side = lax.axis_index("rep") % 2
    lines = home.shape[0] // own
    for line in range(lines):
        rows = slice(line * own, (line + 1) * own)
        below = slice((lines + line) * own, (lines + line + 1) * own)
        for ref, span, group in (
            (home, rows, 0),
            (first, rows, 1 + side),
            (second, rows, 2 - side),
            (second, below, INNER - 1),
        ):
            start = block_rows(True, group, line, own, lines)
            out_ref[pl.ds(start, own), :] = ref[span, :]


def project_kernel(relative, own, *refs):
    weight, n_own, n_sibling, cot_ref, sibling_ref, across_ref, corner_ref = refs[:7]
    pieces = refs[7 : 7 + INNER]
    gp_ref, normed, cot, grad = refs[7 + INNER :]
    pixels, half = sibling_ref.shape
    quarter = half // 2
    side = lax.axis_index("rep") % 2
    parity = (lax.axis_index("shard") // INNER) % 2
    normed[: 2 * pixels, :] = n_own[...]
    normed[2 * pixels :, :] = n_sibling[...]
    start = pl.multiple_of(side * half + parity * quarter, LANES)
    cot[:pixels, :] = cot_ref[:, pl.ds(start, quarter)]
    start = pl.multiple_of(side * quarter, LANES)
    cot[pixels : 2 * pixels, :] = across_ref[pixels:, pl.ds(start, quarter)]
    start = pl.multiple_of(parity * quarter, LANES)
    cot[2 * pixels : 3 * pixels, :] = sibling_ref[:, pl.ds(start, quarter)]
    start = pl.multiple_of(side * quarter, LANES)
    cot[3 * pixels :, :] = corner_ref[pixels:, pl.ds(start, quarter)]
    for start in range(0, quarter, LANES):
        columns = slice(start, start + LANES)
        pre_act = jnp.dot(normed[...], weight[:, columns], preferred_element_type=F32)
        gp_ref[:, columns] = (cot[:, columns].astype(F32) * gelu_slope(pre_act)).astype(BF16)
    grad[...] = lax.dot_general(
        normed[...], gp_ref[...], (((0,), (0,)), ((), ())), preferred_element_type=F32
    )
    split_rows(grad, pieces, own, relative)


def back_project_kernel(weight, gp_ref, own_ref, other_ref):
    rows = own_ref.shape[0]
    grad_normed = lax.dot_general(
        gp_ref[...], weight[...], (((1,), (1,)), ((), ())), preferred_element_type=F32
    )
    own_ref[...] = grad_normed[:rows]
    other_ref[...] = grad_normed[rows:]


def norm_back_kernel(relative, own, height, breadth, *refs):
    gn_own, gn_other, white_ref, inv_ref, taps_ref, x_ref, far_ref = refs[:7]
    pieces = refs[7 : 7 + INNER]
    grad_ref, sent_ref, padded, grads_ref, rows, small, unfolded = refs[7 + INNER :]
    pixels, depth = x_ref.shape
    tiles = depth // LANES
    padded[...] = jnp.zeros_like(padded)
    rows[...] = jnp.zeros_like(rows)
    for image, source in enumerate((x_ref, far_ref)):
        span = slice(image * pixels, (image + 1) * pixels)
        first = None
        second = None
        for tile in range(tiles):
            lanes = slice(tile * LANES, (tile + 1) * LANES)
            part = source[:pixels, lanes].astype(F32)
            padded[image, tile, :, 8 : 8 + breadth, :] = part.reshape(height, breadth, LANES)
            grad_normed = gn_own[span, lanes] + gn_other[span, lanes]
            whitened = white_ref[span, lanes]
            product = grad_normed * whitened
            gain = taps_ref[tile, TAPS : TAPS + 1, :]
            rows[tile, TAPS : TAPS + 1, :] += jnp.sum(product, axis=0, keepdims=True)
            rows[tile, TAPS + 1 : TAPS + 2, :] += jnp.sum(grad_normed, axis=0, keepdims=True)
            one, two = grad_normed * gain, product * gain
            first = one if first is None else first + one
            second = two if second is None else second + two
        mean_first = jnp.sum(first, axis=-1, keepdims=True) / depth
        mean_second = jnp.sum(second, axis=-1, keepdims=True) / depth
        for tile in range(tiles):
            lanes = slice(tile * LANES, (tile + 1) * LANES)
            gain = taps_ref[tile, TAPS : TAPS + 1, :]
            grad_white = (gn_own[span, lanes] + gn_other[span, lanes]) * gain
            grad_conv = inv_ref[span, :] * (
                grad_white - mean_first - white_ref[span, lanes] * mean_second
            )
            grad_conv = grad_conv.reshape(height, breadth, LANES)
            grads_ref[image, tile] = grad_conv
            if image == 0:
                grad_ref[tile] = grad_conv
            else:
                sent_ref[tile] = grad_conv.astype(BF16)

    def one_tile(tile, carry):
        grads = [[grads_ref[image, tile, line] for line in range(height)] for image in range(2)]
        for across in range(KS):
            columns = slice(8 - MARGIN + across, 8 - MARGIN + across + breadth)
            shifted = [padded[image, tile, :, columns, :] for image in range(2)]
            for down in range(KS):
                total = None
                for image in range(2):
                    for line in range(height):
                        origin = line + down - MARGIN
                        if 0 <= origin < height:
                            term = grads[image][line] * shifted[image][origin]
                            total = term if total is None else total + term
                rows[tile, pl.ds(down * KS + across, 1), :] = jnp.sum(total, axis=0, keepdims=True)
        return carry

    lax.fori_loop(0, tiles, one_tile, 0)
    for tile in range(tiles):
        small[tile * LANES : (tile + 1) * LANES, :] = rows[tile].T
    if relative:
        whole = [unfolded.at[group] for group in range(INNER)]
        split_rows(small, whole, own, relative)
        for source, piece in zip(whole, pieces):
            piece[...] = fold(source[...]).astype(piece.dtype)
    else:
        split_rows(small, pieces, own, relative)


def conv_back_kernel(grad_ref, other_ref, taps_ref, out_ref, padded):
    tiles, height, breadth, _ = grad_ref.shape
    padded[...] = jnp.zeros_like(padded)
    padded[:, :, 8 : 8 + breadth, :] = grad_ref[...] + other_ref[...].astype(F32)

    def one_tile(tile, carry):
        sums = correlate(
            padded,
            tile,
            lambda down, across: taps_ref[tile, pl.ds(TAPS - 1 - down * KS - across, 1), :],
            height,
            breadth,
        )
        start = pl.multiple_of(tile * LANES, LANES)
        for line in range(height):
            out_ref[0, line, :, pl.ds(start, LANES)] = sums[line].astype(BF16)
        return carry

    lax.fori_loop(0, tiles, one_tile, 0)


def call(kernel, name, outs, scratch, micros, *args, mebibytes=48):
    flops = int(micros * 1.1e9)
    moved = sum(math.prod(a.shape) * a.dtype.itemsize for a in args)
    moved += sum(math.prod(o.shape) * o.dtype.itemsize for o in outs)
    return pl.pallas_call(
        kernel,
        out_shape=outs,
        in_specs=[VMEM] * len(args),
        out_specs=[VMEM] * len(outs),
        scratch_shapes=scratch,
        compiler_params=params(mebibytes),
        cost_estimate=pl.CostEstimate(flops=flops, bytes_accessed=moved, transcendentals=0),
        name=name,
    )(*args)


def body(images, cotangent, depthwise_weight, norm_gain, norm_bias, up_weight):
    shards, reps = lax.axis_size("shard"), lax.axis_size("rep")
    own, hidden = up_weight.shape
    depth = own * shards
    lines = shards // INNER
    half, quarter = hidden // 2, hidden // 4
    height, breadth = images.shape[1:3]
    pixels = height * breadth
    tiles = depth // LANES
    me = lax.axis_index("shard")
    side = lax.axis_index("rep") % 2
    parity = (me // INNER) % 2
    relative = own % 16 == 0

    def over_shard(array, flip):
        return lax.ppermute(array, "shard", [(i, i ^ flip) for i in range(shards)])

    def crossing(array, flip):
        pairs = [
            (i * reps + r, (i ^ flip) * reps + (r ^ 1)) for i in range(shards) for r in range(reps)
        ]
        return lax.ppermute(array, ("shard", "rep"), pairs)

    def hop(array, place):
        flips = [(1, 2), (2, 1)]
        pairs = [
            (i * reps + r, (i ^ flips[r % 2][place]) * reps + r)
            for i in range(shards)
            for r in range(reps)
        ]
        return lax.ppermute(array, ("shard", "rep"), pairs)

    def over_core(array):
        return lax.ppermute(array, "rep", [(i, i ^ 1) for i in range(reps)])

    def true_order(pieces):
        if relative:
            return pieces
        stacked = jnp.stack(pieces).reshape(shards, own, -1)
        flips = jnp.arange(shards) ^ me
        places = (flips % INNER) * lines + flips // INNER
        return list(jnp.take(stacked, places, axis=0).reshape(INNER, lines * own, -1))

    def relative_order(pieces):
        if relative:
            return pieces
        stacked = jnp.concatenate([p.astype(F32) for p in pieces]).reshape(shards, own, -1)
        flips = (jnp.arange(lines)[None, :] * INNER + jnp.arange(INNER)[:, None]).reshape(-1)
        moved = jnp.take(stacked, flips ^ me, axis=0).reshape(INNER, lines * own, -1)
        return [moved[0]] + [moved[i].astype(BF16) for i in range(1, INNER)]

    shape = jax.ShapeDtypeStruct
    home, near, far = call(
        pack_kernel,
        "pack",
        [shape((own, quarter + LANES), BF16)] * 3,
        [
            pltpu.VMEM((LANES, LANES), F32),
            pltpu.VMEM((own, LANES), F32),
        ],
        0.5,
        up_weight,
        depthwise_weight,
        norm_gain[None, :],
        norm_bias[None, :],
        mebibytes=63,
    )
    image, cotangent = images.reshape(pixels, depth), cotangent.reshape(pixels, hidden)
    home, near, far, image, cotangent = lax.optimization_barrier(
        (home, near, far, image, cotangent)
    )
    gathered = [home] + [
        crossing(far if line % 2 else near, INNER * line) for line in range(1, lines)
    ]
    across, cot_sibling = call(
        cot_pack_kernel,
        "cot_pack",
        [shape((2 * pixels, half), BF16), shape((pixels, half), BF16)],
        [],
        0.4,
        image,
        cotangent,
    )
    across, cot_sibling = crossing(across, INNER), over_core(cot_sibling)

    rows = lines * own
    folded = rows // 2 if relative else rows
    weight_lines, extra_lines = call(
        assemble_kernel,
        "assemble",
        [shape((rows, quarter), BF16), shape((folded, LANES), BF16)],
        [],
        4.0,
        *gathered,
    )
    first_lines = hop(weight_lines, 0)
    (joined,) = call(
        join_kernel,
        "join",
        [shape((2 * rows, quarter), BF16)],
        [],
        0.3,
        weight_lines,
        first_lines,
    )
    second_lines = hop(joined, 1)
    weights = [weight_lines, first_lines, second_lines]
    extras = [extra_lines] + [crossing(extra_lines, flip) for flip in range(1, INNER)]
    if not relative:
        extras = true_order(extras)
        x_lines = jnp.where(side == 0, first_lines, second_lines[:rows])
        y_lines = jnp.where(side == 0, second_lines[:rows], first_lines)
        weights = true_order([weight_lines, x_lines, y_lines, second_lines[rows:]])
    (weight,) = call(
        functools.partial(order_kernel, relative, own),
        "order",
        [shape((depth, quarter), BF16)],
        [],
        1.0,
        *weights,
    )

    padded = pltpu.VMEM((tiles, height, breadth + 16, LANES), F32)
    normed, whitened, inv_std, taps = call(
        functools.partial(conv_norm_kernel, relative, own, height, breadth),
        "conv_norm",
        [
            shape((2 * pixels, depth), BF16),
            shape((2 * pixels, depth), F32),
            shape((2 * pixels, LANES), F32),
            shape((tiles, LANES, LANES), F32),
        ],
        [
            pltpu.VMEM((depth, LANES), F32),
            pltpu.VMEM((depth, LANES), F32),
            padded,
            pltpu.VMEM((tiles, pixels, LANES), F32),
        ],
        0.1,
        *extras,
        image,
        across,
    )
    normed, across = lax.optimization_barrier((normed, across))
    normed_sibling, corner = over_core(normed), over_core(across)
    *pieces, grad_pre = call(
        functools.partial(project_kernel, relative, own),
        "project",
        [shape((rows, quarter), F32)]
        + [shape((rows, quarter), BF16)] * (INNER - 1)
        + [shape((4 * pixels, quarter), BF16)],
        [
            pltpu.VMEM((4 * pixels, depth), BF16),
            pltpu.VMEM((4 * pixels, quarter), BF16),
            pltpu.VMEM((depth, quarter), F32),
        ],
        1.6,
        weight,
        normed,
        normed_sibling,
        cotangent,
        cot_sibling,
        across,
        corner,
    )
    gn_kept, gn_sent = call(
        back_project_kernel,
        "back_project",
        [shape((2 * pixels, depth), F32)] * 2,
        [],
        0.7,
        weight,
        grad_pre,
    )
    pieces = relative_order(pieces)
    arrived = [over_shard(piece, flip) for flip, piece in enumerate(pieces) if flip]
    *small, grad_conv, grad_sent = call(
        functools.partial(norm_back_kernel, relative, own, height, breadth),
        "norm_back",
        [shape((folded, LANES), F32)]
        + [shape((folded, LANES), BF16)] * (INNER - 1)
        + [
            shape((tiles, height, breadth, LANES), F32),
            shape((tiles, height, breadth, LANES), BF16),
        ],
        [
            pltpu.VMEM((2, tiles, height, breadth + 16, LANES), F32),
            pltpu.VMEM((2, tiles, height, breadth, LANES), F32),
            pltpu.VMEM((tiles, LANES, LANES), F32),
            pltpu.VMEM((depth, LANES), F32),
            pltpu.VMEM((INNER, rows, LANES), F32),
        ],
        0.1,
        gn_kept,
        over_core(gn_sent),
        whitened,
        inv_std,
        taps,
        image,
        across,
    )
    small = relative_order(small)
    small_arrived = [crossing(piece, flip) for flip, piece in enumerate(small) if flip]
    grad_other = crossing(grad_sent, INNER)
    (grad_images,) = call(
        conv_back_kernel,
        "conv_back",
        [shape(images.shape, BF16)],
        [padded],
        0.1,
        grad_conv,
        grad_other,
        taps,
    )

    home, *sent = call(
        functools.partial(plane_sum_kernel, lines),
        "plane_sum",
        [shape((own, quarter + LANES), F32)] + [shape((own, quarter + LANES), BF16)] * (lines - 1),
        [],
        2.0,
        pieces[0],
        *arrived,
        small[0],
        *small_arrived,
    )
    home, grad_images = lax.optimization_barrier((home, grad_images))
    came = [crossing(piece, INNER * line) for line, piece in enumerate(sent, 1)]
    (total,) = call(
        line_sum_kernel,
        "line_sum",
        [shape((own, 3 * quarter + LANES), F32)],
        [],
        0.3,
        home,
        *came,
    )
    if reps > 2:
        groups = [[i for i in range(reps) if i % 2 == s] for s in range(2)]
        total = lax.psum(total, "rep", axis_index_groups=groups)
    other = over_core(total)
    factor = 1.0 / math.sqrt(images.shape[0] * pixels * shards * reps)
    grad_up, grad_depthwise, grad_gain, grad_bias = call(
        functools.partial(finish_kernel, factor),
        "finish",
        [
            shape((own, hidden), F32),
            shape((own, TAPS), F32),
            shape((1, own), F32),
            shape((1, own), F32),
        ],
        [],
        0.5,
        total,
        other,
    )
    return (grad_images, grad_up, grad_depthwise, grad_gain[0], grad_bias[0])


def solution(mesh):
    placed = (
        P(("shard", "rep"), None, None, None),
        P(("shard", "rep"), None, None, None),
        P("shard", None),
        P("shard"),
        P("shard"),
        P("shard", None),
    )
    return jax.shard_map(
        body,
        mesh=mesh,
        in_specs=placed,
        out_specs=(
            P(("shard", "rep"), None, None, None),
            P("shard", None),
            P("shard", None),
            P("shard"),
            P("shard"),
        ),
        check_vma=False,
    )
```

```python
import functools
import math

import jax
import jax.numpy as jnp
from jax import lax
from jax.experimental import pallas as pl
from jax.experimental.pallas import tpu as pltpu
from jax.sharding import PartitionSpec as P

KS = 7
TAPS = KS * KS
MARGIN = KS // 2
LANES = 128
INNER = 4
NORM_EPS = 1e-06
BF16 = jnp.bfloat16
F32 = jnp.float32
VMEM = pl.BlockSpec(memory_space=pltpu.VMEM)


def params(mebibytes):
    return pltpu.CompilerParams(vmem_limit_bytes=mebibytes * 1024 * 1024)


def gelu_slope(inputs):
    cumulative = 0.5 * (1.0 + lax.erf(inputs * 0.7071067811865476))
    return cumulative + inputs * jnp.exp(-0.5 * inputs * inputs) * 0.3989422804014327


def block_rows(relative, group, line, own, lines):
    if relative:
        place = lax.axis_index("shard") ^ (line * INNER + group)
        return pl.multiple_of(place * own, 16)
    return (group * lines + line) * own


def place_rows(pieces, target, own, relative, cast=None):
    for group, piece in enumerate(pieces):
        lines = piece.shape[0] // own
        if not relative:
            target[group * piece.shape[0] : (group + 1) * piece.shape[0], :] = (
                piece[...] if cast is None else piece[...].astype(cast)
            )
            continue
        for line in range(lines):
            rows = piece[line * own : (line + 1) * own, :]
            start = block_rows(True, group, line, own, lines)
            target[pl.ds(start, own), :] = rows if cast is None else rows.astype(cast)


def split_rows(source, pieces, own, relative):
    for group, piece in enumerate(pieces):
        lines = piece.shape[0] // own
        if not relative:
            piece[...] = source[group * piece.shape[0] : (group + 1) * piece.shape[0], :].astype(
                piece.dtype
            )
            continue
        for line in range(lines):
            start = block_rows(True, group, line, own, lines)
            piece[line * own : (line + 1) * own, :] = source[pl.ds(start, own), :].astype(
                piece.dtype
            )


def correlate(padded, tile, tap_row, height, breadth):
    sums = [None] * height
    for across in range(KS):
        shifted = padded[tile, :, 8 - MARGIN + across : 8 - MARGIN + across + breadth, :]
        for down in range(KS):
            row = tap_row(down, across)
            for line in range(height):
                origin = line + down - MARGIN
                if 0 <= origin < height:
                    term = shifted[origin] * row
                    sums[line] = term if sums[line] is None else sums[line] + term
    return sums


def pack_kernel(w_ref, dw_ref, gain_ref, bias_ref, home_ref, near_ref, far_ref, turned, wide):
    own, hidden = w_ref.shape
    quarter = hidden // 4
    side = lax.axis_index("rep") % 2
    parity = (lax.axis_index("shard") // INNER) % 2
    turned[...] = jnp.zeros_like(turned)
    turned[TAPS : TAPS + 1, :own] = gain_ref[...].astype(F32)
    turned[TAPS + 1 : TAPS + 2, :own] = bias_ref[...].astype(F32)
    wide[...] = jnp.zeros_like(wide)
    wide[:, :TAPS] = dw_ref[...].astype(F32)
    extras = (wide[...] + turned[...].T[:own]).astype(BF16)
    kinds = ((home_ref, side, parity), (near_ref, 1 - side, parity), (far_ref, 1 - side, 1 - parity))
    for ref, place, which in kinds:
        start = pl.multiple_of(place * (2 * quarter) + which * quarter, LANES)
        ref[:, :quarter] = w_ref[:, pl.ds(start, quarter)]
        ref[:, quarter:] = extras


def assemble_kernel(*refs):
    pieces, (weight_ref, extra_ref) = refs[:-2], refs[-2:]
    own = pieces[0].shape[0]
    quarter = weight_ref.shape[1]
    for line, piece in enumerate(pieces):
        weight_ref[line * own : (line + 1) * own, :] = piece[:, :quarter]
    extras = jnp.concatenate([piece[:, quarter:].astype(F32) for piece in pieces], axis=0)
    if extra_ref.shape[0] < extras.shape[0]:
        extras = fold(extras)
    extra_ref[...] = extras.astype(BF16)


def plane_sum_kernel(lines, *refs):
    pieces, small, outs = refs[:INNER], refs[INNER : 2 * INNER], refs[2 * INNER :]
    own = pieces[0].shape[0] // lines
    quarter = pieces[0].shape[1]
    extras = small[0][...]
    for part in small[1:]:
        extras = extras + part[...].astype(F32)
    if extras.shape[0] < pieces[0].shape[0]:
        extras = unfold(extras)
    for line, out in enumerate(outs):
        rows = slice(line * own, (line + 1) * own)
        total = pieces[0][rows, :]
        for part in pieces[1:]:
            total = total + part[rows, :].astype(F32)
        out[:, :quarter] = total.astype(out.dtype)
        out[:, quarter:] = extras[rows, :].astype(out.dtype)


def line_sum_kernel(*refs):
    pieces, total_ref = refs[:-1], refs[-1]
    quarter = pieces[0].shape[1] - LANES
    near, far = None, None
    for line, piece in enumerate(pieces[1:], 1):
        came = piece[...].astype(F32)
        if line % 2:
            far = came if far is None else far + came
        else:
            near = came if near is None else near + came
    total_ref[:, :quarter] = pieces[0][:, :quarter]
    total_ref[:, quarter : 2 * quarter] = near[:, :quarter]
    total_ref[:, 2 * quarter : 3 * quarter] = far[:, :quarter]
    total_ref[:, 3 * quarter :] = pieces[0][:, quarter:] + near[:, quarter:] + far[:, quarter:]


def finish_kernel(factor, mine_ref, other_ref, up_ref, dw_ref, gain_ref, bias_ref):
    own, quarter = mine_ref.shape[0], (mine_ref.shape[1] - LANES) // 3
    side = lax.axis_index("rep") % 2
    parity = (lax.axis_index("shard") // INNER) % 2
    for place, home, came in ((side, mine_ref, other_ref), (1 - side, other_ref, mine_ref)):
        start = pl.multiple_of((2 * place + parity) * quarter, LANES)
        total = home[:, :quarter] + came[:, quarter : 2 * quarter]
        up_ref[:, pl.ds(start, quarter)] = total * factor
        start = pl.multiple_of((2 * place + 1 - parity) * quarter, LANES)
        up_ref[:, pl.ds(start, quarter)] = came[:, 2 * quarter : 3 * quarter] * factor
    low = 3 * quarter
    sums = (mine_ref[:, low:] + other_ref[:, low:]) * factor
    dw_ref[...] = sums[:, :TAPS]
    turned = sums.T
    gain_ref[...] = turned[TAPS : TAPS + 1, :]
    bias_ref[...] = turned[TAPS + 1 : TAPS + 2, :]


def fold(rows):
    half = rows.shape[0] // 2
    low = lax.broadcasted_iota(jnp.int32, (half, LANES), 1) < LANES // 2
    return jnp.where(low, rows[:half], pltpu.roll(rows[half:], LANES // 2, 1))


def unfold(rows):
    return jnp.concatenate([rows, pltpu.roll(rows, LANES // 2, 1)], axis=0)


def conv_norm_kernel(relative, own, height, breadth, *refs):
    small = refs[:INNER]
    sources = refs[INNER : INNER + 2]
    x_ref = sources[0]
    normed_ref, white_ref, inv_ref, taps_ref, corner_ref, *scratch = refs[INNER + 2 :]
    gathered, unfolded, padded, conv = scratch
    pixels, depth = x_ref.shape
    tiles = depth // LANES
    quarter = corner_ref.shape[1]
    start = pl.multiple_of((1 - lax.axis_index("rep") % 2) * quarter, LANES)
    corner_ref[...] = sources[1][pixels:, pl.ds(start, quarter)]
    if relative:
        for group, piece in enumerate(small):
            unfolded[group * 2 * piece.shape[0] : (group + 1) * 2 * piece.shape[0], :] = unfold(
                piece[...].astype(F32)
            )
        count = unfolded.shape[0] // INNER
        small = [unfolded.at[pl.ds(group * count, count), :] for group in range(INNER)]
    place_rows(small, gathered, own, relative, F32)
    padded[...] = jnp.zeros_like(padded)
    for tile in range(tiles):
        lanes = slice(tile * LANES, (tile + 1) * LANES)
        taps_ref[tile] = gathered[lanes, :].T

    for image, source in enumerate(sources):
        for tile in range(tiles):
            lanes = slice(tile * LANES, (tile + 1) * LANES)
            part = source[:pixels, lanes].astype(F32)
            padded[tile, :, 8 : 8 + breadth, :] = part.reshape(height, breadth, LANES)

        def one_tile(tile, carry):
            sums = correlate(
                padded,
                tile,
                lambda down, across: taps_ref[tile, pl.ds(down * KS + across, 1), :],
                height,
                breadth,
            )
            for line in range(height):
                conv[tile, line * breadth : (line + 1) * breadth, :] = sums[line]
            return carry

        lax.fori_loop(0, tiles, one_tile, 0)
        total = conv[0]
        for tile in range(1, tiles):
            total = total + conv[tile]
        average = jnp.sum(total, axis=-1, keepdims=True) / depth
        squares = None
        for tile in range(tiles):
            centered = conv[tile] - average
            squares = centered * centered if squares is None else squares + centered * centered
        variance = jnp.sum(squares, axis=-1, keepdims=True) / depth
        inv_std = lax.rsqrt(variance + NORM_EPS)
        rows = slice(image * pixels, (image + 1) * pixels)
        inv_ref[rows, :] = jnp.broadcast_to(inv_std, (pixels, LANES))
        for tile in range(tiles):
            lanes = slice(tile * LANES, (tile + 1) * LANES)
            whitened = (conv[tile] - average) * inv_std
            white_ref[rows, lanes] = whitened
            gain = taps_ref[tile, TAPS : TAPS + 1, :]
            bias = taps_ref[tile, TAPS + 1 : TAPS + 2, :]
            normed_ref[rows, lanes] = (whitened * gain + bias).astype(BF16)


def cot_pack_kernel(image_ref, cot_ref, across_ref, sibling_ref):
    pixels, half = sibling_ref.shape
    quarter = half // 2
    side = lax.axis_index("rep") % 2
    parity = (lax.axis_index("shard") // INNER) % 2
    for place in range(2):
        start = pl.multiple_of(place * half + (1 - parity) * quarter, LANES)
        lanes = slice(place * quarter, (place + 1) * quarter)
        across_ref[pixels:, lanes] = cot_ref[:, pl.ds(start, quarter)]
    across_ref[:pixels, :] = image_ref[...]
    sibling_ref[...] = cot_ref[:, pl.ds(pl.multiple_of((1 - side) * half, LANES), half)]


def join_kernel(own_ref, came_ref, out_ref):
    rows = own_ref.shape[0]
    out_ref[:rows, :] = own_ref[...]
    out_ref[rows:, :] = came_ref[...]


def order_kernel(relative, own, *refs):
    if not relative:
        place_rows(refs[:INNER], refs[INNER], own, relative)
        return
    home, first, second, out_ref = refs
    side = lax.axis_index("rep") % 2
    lines = home.shape[0] // own
    for line in range(lines):
        rows = slice(line * own, (line + 1) * own)
        below = slice((lines + line) * own, (lines + line + 1) * own)
        for ref, span, group in (
            (home, rows, 0),
            (first, rows, 1 + side),
            (second, rows, 2 - side),
            (second, below, INNER - 1),
        ):
            start = block_rows(True, group, line, own, lines)
            out_ref[pl.ds(start, own), :] = ref[span, :]


def project_kernel(relative, own, *refs):
    weight, n_own, n_sibling, cot_ref, sibling_ref, across_ref, corner_ref = refs[:7]
    pieces = refs[7 : 7 + INNER]
    gp_ref, normed, cot, grad = refs[7 + INNER :]
    pixels, half = sibling_ref.shape
    quarter = half // 2
    side = lax.axis_index("rep") % 2
    parity = (lax.axis_index("shard") // INNER) % 2
    normed[: 2 * pixels, :] = n_own[...]
    normed[2 * pixels :, :] = n_sibling[...]
    start = pl.multiple_of(side * half + parity * quarter, LANES)
    cot[:pixels, :] = cot_ref[:, pl.ds(start, quarter)]
    start = pl.multiple_of(side * quarter, LANES)
    cot[pixels : 2 * pixels, :] = across_ref[pixels:, pl.ds(start, quarter)]
    start = pl.multiple_of(parity * quarter, LANES)
    cot[2 * pixels : 3 * pixels, :] = sibling_ref[:, pl.ds(start, quarter)]
    cot[3 * pixels :, :] = corner_ref[...]
    for start in range(0, quarter, LANES):
        columns = slice(start, start + LANES)
        pre_act = jnp.dot(normed[...], weight[:, columns], preferred_element_type=F32)
        gp_ref[:, columns] = (cot[:, columns].astype(F32) * gelu_slope(pre_act)).astype(BF16)
    grad[...] = lax.dot_general(
        normed[...], gp_ref[...], (((0,), (0,)), ((), ())), preferred_element_type=F32
    )
    split_rows(grad, pieces, own, relative)


def back_project_kernel(weight, gp_ref, own_ref, other_ref):
    rows = own_ref.shape[0]
    grad_normed = lax.dot_general(
        gp_ref[...], weight[...], (((1,), (1,)), ((), ())), preferred_element_type=F32
    )
    own_ref[...] = grad_normed[:rows]
    other_ref[...] = grad_normed[rows:]


def norm_back_kernel(relative, own, height, breadth, *refs):
    gn_own, gn_other, white_ref, inv_ref, taps_ref, x_ref, far_ref = refs[:7]
    pieces = refs[7 : 7 + INNER]
    grad_ref, sent_ref, padded, grads_ref, rows, small, unfolded = refs[7 + INNER :]
    pixels, depth = x_ref.shape
    tiles = depth // LANES
    padded[...] = jnp.zeros_like(padded)
    rows[...] = jnp.zeros_like(rows)
    for image, source in enumerate((x_ref, far_ref)):
        span = slice(image * pixels, (image + 1) * pixels)
        first = None
        second = None
        for tile in range(tiles):
            lanes = slice(tile * LANES, (tile + 1) * LANES)
            part = source[:pixels, lanes].astype(F32)
            padded[image, tile, :, 8 : 8 + breadth, :] = part.reshape(height, breadth, LANES)
            grad_normed = gn_own[span, lanes] + gn_other[span, lanes]
            whitened = white_ref[span, lanes]
            product = grad_normed * whitened
            gain = taps_ref[tile, TAPS : TAPS + 1, :]
            rows[tile, TAPS : TAPS + 1, :] += jnp.sum(product, axis=0, keepdims=True)
            rows[tile, TAPS + 1 : TAPS + 2, :] += jnp.sum(grad_normed, axis=0, keepdims=True)
            one, two = grad_normed * gain, product * gain
            first = one if first is None else first + one
            second = two if second is None else second + two
        mean_first = jnp.sum(first, axis=-1, keepdims=True) / depth
        mean_second = jnp.sum(second, axis=-1, keepdims=True) / depth
        for tile in range(tiles):
            lanes = slice(tile * LANES, (tile + 1) * LANES)
            gain = taps_ref[tile, TAPS : TAPS + 1, :]
            grad_white = (gn_own[span, lanes] + gn_other[span, lanes]) * gain
            grad_conv = inv_ref[span, :] * (
                grad_white - mean_first - white_ref[span, lanes] * mean_second
            )
            grad_conv = grad_conv.reshape(height, breadth, LANES)
            grads_ref[image, tile] = grad_conv
            if image == 0:
                grad_ref[tile] = grad_conv
            else:
                sent_ref[tile] = grad_conv.astype(BF16)

    def one_tile(tile, carry):
        grads = [[grads_ref[image, tile, line] for line in range(height)] for image in range(2)]
        for across in range(KS):
            columns = slice(8 - MARGIN + across, 8 - MARGIN + across + breadth)
            shifted = [padded[image, tile, :, columns, :] for image in range(2)]
            for down in range(KS):
                total = None
                for image in range(2):
                    for line in range(height):
                        origin = line + down - MARGIN
                        if 0 <= origin < height:
                            term = grads[image][line] * shifted[image][origin]
                            total = term if total is None else total + term
                rows[tile, pl.ds(down * KS + across, 1), :] = jnp.sum(total, axis=0, keepdims=True)
        return carry

    lax.fori_loop(0, tiles, one_tile, 0)
    for tile in range(tiles):
        small[tile * LANES : (tile + 1) * LANES, :] = rows[tile].T
    if relative:
        whole = [unfolded.at[group] for group in range(INNER)]
        split_rows(small, whole, own, relative)
        for source, piece in zip(whole, pieces):
            piece[...] = fold(source[...]).astype(piece.dtype)
    else:
        split_rows(small, pieces, own, relative)


def conv_back_kernel(grad_ref, other_ref, taps_ref, out_ref, padded):
    tiles, height, breadth, _ = grad_ref.shape
    padded[...] = jnp.zeros_like(padded)
    padded[:, :, 8 : 8 + breadth, :] = grad_ref[...] + other_ref[...].astype(F32)

    def one_tile(tile, carry):
        sums = correlate(
            padded,
            tile,
            lambda down, across: taps_ref[tile, pl.ds(TAPS - 1 - down * KS - across, 1), :],
            height,
            breadth,
        )
        start = pl.multiple_of(tile * LANES, LANES)
        for line in range(height):
            out_ref[0, line, :, pl.ds(start, LANES)] = sums[line].astype(BF16)
        return carry

    lax.fori_loop(0, tiles, one_tile, 0)


def call(kernel, name, outs, scratch, micros, *args, mebibytes=48):
    flops = int(micros * 1.1e9)
    moved = sum(math.prod(a.shape) * a.dtype.itemsize for a in args)
    moved += sum(math.prod(o.shape) * o.dtype.itemsize for o in outs)
    return pl.pallas_call(
        kernel,
        out_shape=outs,
        in_specs=[VMEM] * len(args),
        out_specs=[VMEM] * len(outs),
        scratch_shapes=scratch,
        compiler_params=params(mebibytes),
        cost_estimate=pl.CostEstimate(flops=flops, bytes_accessed=moved, transcendentals=0),
        name=name,
    )(*args)


def body(images, cotangent, depthwise_weight, norm_gain, norm_bias, up_weight):
    shards, reps = lax.axis_size("shard"), lax.axis_size("rep")
    own, hidden = up_weight.shape
    depth = own * shards
    lines = shards // INNER
    half, quarter = hidden // 2, hidden // 4
    height, breadth = images.shape[1:3]
    pixels = height * breadth
    tiles = depth // LANES
    me = lax.axis_index("shard")
    side = lax.axis_index("rep") % 2
    parity = (me // INNER) % 2
    relative = own % 16 == 0

    def over_shard(array, flip):
        return lax.ppermute(array, "shard", [(i, i ^ flip) for i in range(shards)])

    def crossing(array, flip):
        pairs = [
            (i * reps + r, (i ^ flip) * reps + (r ^ 1)) for i in range(shards) for r in range(reps)
        ]
        return lax.ppermute(array, ("shard", "rep"), pairs)

    def hop(array, place):
        flips = [(1, 2), (2, 1)]
        pairs = [
            (i * reps + r, (i ^ flips[r % 2][place]) * reps + r)
            for i in range(shards)
            for r in range(reps)
        ]
        return lax.ppermute(array, ("shard", "rep"), pairs)

    def over_core(array):
        return lax.ppermute(array, "rep", [(i, i ^ 1) for i in range(reps)])

    def true_order(pieces):
        if relative:
            return pieces
        stacked = jnp.stack(pieces).reshape(shards, own, -1)
        flips = jnp.arange(shards) ^ me
        places = (flips % INNER) * lines + flips // INNER
        return list(jnp.take(stacked, places, axis=0).reshape(INNER, lines * own, -1))

    def relative_order(pieces):
        if relative:
            return pieces
        stacked = jnp.concatenate([p.astype(F32) for p in pieces]).reshape(shards, own, -1)
        flips = (jnp.arange(lines)[None, :] * INNER + jnp.arange(INNER)[:, None]).reshape(-1)
        moved = jnp.take(stacked, flips ^ me, axis=0).reshape(INNER, lines * own, -1)
        return [moved[0]] + [moved[i].astype(BF16) for i in range(1, INNER)]

    shape = jax.ShapeDtypeStruct
    home, near, far = call(
        pack_kernel,
        "pack",
        [shape((own, quarter + LANES), BF16)] * 3,
        [
            pltpu.VMEM((LANES, LANES), F32),
            pltpu.VMEM((own, LANES), F32),
        ],
        0.5,
        up_weight,
        depthwise_weight,
        norm_gain[None, :],
        norm_bias[None, :],
        mebibytes=63,
    )
    image, cotangent = images.reshape(pixels, depth), cotangent.reshape(pixels, hidden)
    home, near, far, image, cotangent = lax.optimization_barrier(
        (home, near, far, image, cotangent)
    )
    gathered = [home] + [
        crossing(far if line % 2 else near, INNER * line) for line in range(1, lines)
    ]
    across, cot_sibling = call(
        cot_pack_kernel,
        "cot_pack",
        [shape((2 * pixels, half), BF16), shape((pixels, half), BF16)],
        [],
        0.4,
        image,
        cotangent,
    )
    across, cot_sibling = crossing(across, INNER), over_core(cot_sibling)

    rows = lines * own
    folded = rows // 2 if relative else rows
    weight_lines, extra_lines = call(
        assemble_kernel,
        "assemble",
        [shape((rows, quarter), BF16), shape((folded, LANES), BF16)],
        [],
        4.0,
        *gathered,
    )
    first_lines = hop(weight_lines, 0)
    (joined,) = call(
        join_kernel,
        "join",
        [shape((2 * rows, quarter), BF16)],
        [],
        0.3,
        weight_lines,
        first_lines,
    )
    second_lines = hop(joined, 1)
    weights = [weight_lines, first_lines, second_lines]
    extras = [extra_lines] + [crossing(extra_lines, flip) for flip in range(1, INNER)]
    if not relative:
        extras = true_order(extras)
        x_lines = jnp.where(side == 0, first_lines, second_lines[:rows])
        y_lines = jnp.where(side == 0, second_lines[:rows], first_lines)
        weights = true_order([weight_lines, x_lines, y_lines, second_lines[rows:]])
    (weight,) = call(
        functools.partial(order_kernel, relative, own),
        "order",
        [shape((depth, quarter), BF16)],
        [],
        1.0,
        *weights,
    )

    padded = pltpu.VMEM((tiles, height, breadth + 16, LANES), F32)
    normed, whitened, inv_std, taps, corner = call(
        functools.partial(conv_norm_kernel, relative, own, height, breadth),
        "conv_norm",
        [
            shape((2 * pixels, depth), BF16),
            shape((2 * pixels, depth), F32),
            shape((2 * pixels, LANES), F32),
            shape((tiles, LANES, LANES), F32),
            shape((pixels, quarter), BF16),
        ],
        [
            pltpu.VMEM((depth, LANES), F32),
            pltpu.VMEM((depth, LANES), F32),
            padded,
            pltpu.VMEM((tiles, pixels, LANES), F32),
        ],
        0.1,
        *extras,
        image,
        across,
    )
    normed, cot_sibling = lax.optimization_barrier((normed, cot_sibling))
    normed_sibling, corner = over_core(normed), over_core(corner)
    *pieces, grad_pre = call(
        functools.partial(project_kernel, relative, own),
        "project",
        [shape((rows, quarter), F32)]
        + [shape((rows, quarter), BF16)] * (INNER - 1)
        + [shape((4 * pixels, quarter), BF16)],
        [
            pltpu.VMEM((4 * pixels, depth), BF16),
            pltpu.VMEM((4 * pixels, quarter), BF16),
            pltpu.VMEM((depth, quarter), F32),
        ],
        1.6,
        weight,
        normed,
        normed_sibling,
        cotangent,
        cot_sibling,
        across,
        corner,
    )
    gn_kept, gn_sent = call(
        back_project_kernel,
        "back_project",
        [shape((2 * pixels, depth), F32)] * 2,
        [],
        0.7,
        weight,
        grad_pre,
    )
    pieces = relative_order(pieces)
    arrived = [over_shard(piece, flip) for flip, piece in enumerate(pieces) if flip]
    *small, grad_conv, grad_sent = call(
        functools.partial(norm_back_kernel, relative, own, height, breadth),
        "norm_back",
        [shape((folded, LANES), F32)]
        + [shape((folded, LANES), BF16)] * (INNER - 1)
        + [
            shape((tiles, height, breadth, LANES), F32),
            shape((tiles, height, breadth, LANES), BF16),
        ],
        [
            pltpu.VMEM((2, tiles, height, breadth + 16, LANES), F32),
            pltpu.VMEM((2, tiles, height, breadth, LANES), F32),
            pltpu.VMEM((tiles, LANES, LANES), F32),
            pltpu.VMEM((depth, LANES), F32),
            pltpu.VMEM((INNER, rows, LANES), F32),
        ],
        0.1,
        gn_kept,
        over_core(gn_sent),
        whitened,
        inv_std,
        taps,
        image,
        across,
    )
    small = relative_order(small)
    small_arrived = [crossing(piece, flip) for flip, piece in enumerate(small) if flip]
    grad_other = crossing(grad_sent, INNER)
    (grad_images,) = call(
        conv_back_kernel,
        "conv_back",
        [shape(images.shape, BF16)],
        [padded],
        0.1,
        grad_conv,
        grad_other,
        taps,
    )

    home, *sent = call(
        functools.partial(plane_sum_kernel, lines),
        "plane_sum",
        [shape((own, quarter + LANES), F32)] + [shape((own, quarter + LANES), BF16)] * (lines - 1),
        [],
        0.8,
        pieces[0],
        *arrived,
        small[0],
        *small_arrived,
    )
    home, grad_images = lax.optimization_barrier((home, grad_images))
    came = [crossing(piece, INNER * line) for line, piece in enumerate(sent, 1)]
    (total,) = call(
        line_sum_kernel,
        "line_sum",
        [shape((own, 3 * quarter + LANES), F32)],
        [],
        0.3,
        home,
        *came,
    )
    if reps > 2:
        groups = [[i for i in range(reps) if i % 2 == s] for s in range(2)]
        total = lax.psum(total, "rep", axis_index_groups=groups)
    other = over_core(total)
    factor = 1.0 / math.sqrt(images.shape[0] * pixels * shards * reps)
    grad_up, grad_depthwise, grad_gain, grad_bias = call(
        functools.partial(finish_kernel, factor),
        "finish",
        [
            shape((own, hidden), F32),
            shape((own, TAPS), F32),
            shape((1, own), F32),
            shape((1, own), F32),
        ],
        [],
        0.5,
        total,
        other,
    )
    return (grad_images, grad_up, grad_depthwise, grad_gain[0], grad_bias[0])


def solution(mesh):
    placed = (
        P(("shard", "rep"), None, None, None),
        P(("shard", "rep"), None, None, None),
        P("shard", None),
        P("shard"),
        P("shard"),
        P("shard", None),
    )
    return jax.shard_map(
        body,
        mesh=mesh,
        in_specs=placed,
        out_specs=(
            P(("shard", "rep"), None, None, None),
            P("shard", None),
            P("shard", None),
            P("shard"),
            P("shard"),
        ),
        check_vma=False,
    )
```

```python
import functools
import math

import jax
import jax.numpy as jnp
from jax import lax
from jax.experimental import pallas as pl
from jax.experimental.pallas import tpu as pltpu
from jax.sharding import PartitionSpec as P

KS = 7
TAPS = KS * KS
MARGIN = KS // 2
LANES = 128
INNER = 4
NORM_EPS = 1e-06
BF16 = jnp.bfloat16
F32 = jnp.float32
VMEM = pl.BlockSpec(memory_space=pltpu.VMEM)


def params(mebibytes):
    return pltpu.CompilerParams(vmem_limit_bytes=mebibytes * 1024 * 1024)


def gelu_slope(inputs):
    cumulative = 0.5 * (1.0 + lax.erf(inputs * 0.7071067811865476))
    return cumulative + inputs * jnp.exp(-0.5 * inputs * inputs) * 0.3989422804014327


def block_rows(relative, group, line, own, lines):
    if relative:
        place = lax.axis_index("shard") ^ (line * INNER + group)
        return pl.multiple_of(place * own, 16)
    return (group * lines + line) * own


def place_rows(pieces, target, own, relative, cast=None):
    for group, piece in enumerate(pieces):
        lines = piece.shape[0] // own
        if not relative:
            target[group * piece.shape[0] : (group + 1) * piece.shape[0], :] = (
                piece[...] if cast is None else piece[...].astype(cast)
            )
            continue
        for line in range(lines):
            rows = piece[line * own : (line + 1) * own, :]
            start = block_rows(True, group, line, own, lines)
            target[pl.ds(start, own), :] = rows if cast is None else rows.astype(cast)


def split_rows(source, pieces, own, relative):
    for group, piece in enumerate(pieces):
        lines = piece.shape[0] // own
        if not relative:
            piece[...] = source[group * piece.shape[0] : (group + 1) * piece.shape[0], :].astype(
                piece.dtype
            )
            continue
        for line in range(lines):
            start = block_rows(True, group, line, own, lines)
            piece[line * own : (line + 1) * own, :] = source[pl.ds(start, own), :].astype(
                piece.dtype
            )


def correlate(padded, tile, tap_row, height, breadth):
    sums = [None] * height
    for across in range(KS):
        shifted = padded[tile, :, 8 - MARGIN + across : 8 - MARGIN + across + breadth, :]
        for down in range(KS):
            row = tap_row(down, across)
            for line in range(height):
                origin = line + down - MARGIN
                if 0 <= origin < height:
                    term = shifted[origin] * row
                    sums[line] = term if sums[line] is None else sums[line] + term
    return sums


def pack_kernel(w_ref, dw_ref, gain_ref, bias_ref, home_ref, near_ref, far_ref, turned, wide):
    own, hidden = w_ref.shape
    quarter = hidden // 4
    side = lax.axis_index("rep") % 2
    parity = (lax.axis_index("shard") // INNER) % 2
    turned[...] = jnp.zeros_like(turned)
    turned[TAPS : TAPS + 1, :own] = gain_ref[...].astype(F32)
    turned[TAPS + 1 : TAPS + 2, :own] = bias_ref[...].astype(F32)
    wide[...] = jnp.zeros_like(wide)
    wide[:, :TAPS] = dw_ref[...].astype(F32)
    extras = (wide[...] + turned[...].T[:own]).astype(BF16)
    kinds = ((home_ref, side, parity), (near_ref, 1 - side, parity), (far_ref, 1 - side, 1 - parity))
    for ref, place, which in kinds:
        start = pl.multiple_of(place * (2 * quarter) + which * quarter, LANES)
        ref[:, :quarter] = w_ref[:, pl.ds(start, quarter)]
        ref[:, quarter:] = extras


def assemble_kernel(*refs):
    pieces, (weight_ref, extra_ref) = refs[:-2], refs[-2:]
    own = pieces[0].shape[0]
    quarter = weight_ref.shape[1]
    for line, piece in enumerate(pieces):
        weight_ref[line * own : (line + 1) * own, :] = piece[:, :quarter]
    extras = jnp.concatenate([piece[:, quarter:].astype(F32) for piece in pieces], axis=0)
    if extra_ref.shape[0] < extras.shape[0]:
        extras = fold(extras)
    extra_ref[...] = extras.astype(BF16)


def plane_sum_kernel(lines, *refs):
    pieces, small, outs = refs[:INNER], refs[INNER : 2 * INNER], refs[2 * INNER :]
    own = pieces[0].shape[0] // lines
    quarter = pieces[0].shape[1]
    extras = small[0][...]
    for part in small[1:]:
        extras = extras + part[...].astype(F32)
    if extras.shape[0] < pieces[0].shape[0]:
        extras = unfold(extras)
    for line, out in enumerate(outs):
        rows = slice(line * own, (line + 1) * own)
        total = pieces[0][rows, :]
        for part in pieces[1:]:
            total = total + part[rows, :].astype(F32)
        out[:, :quarter] = total.astype(out.dtype)
        out[:, quarter:] = extras[rows, :].astype(out.dtype)


def line_sum_kernel(*refs):
    pieces, total_ref = refs[:-1], refs[-1]
    quarter = pieces[0].shape[1] - LANES
    near, far = None, None
    for line, piece in enumerate(pieces[1:], 1):
        came = piece[...].astype(F32)
        if line % 2:
            far = came if far is None else far + came
        else:
            near = came if near is None else near + came
    total_ref[:, :quarter] = pieces[0][:, :quarter]
    total_ref[:, quarter : 2 * quarter] = near[:, :quarter]
    total_ref[:, 2 * quarter : 3 * quarter] = far[:, :quarter]
    total_ref[:, 3 * quarter :] = pieces[0][:, quarter:] + near[:, quarter:] + far[:, quarter:]


def finish_kernel(factor, mine_ref, other_ref, up_ref, dw_ref, gain_ref, bias_ref):
    own, quarter = mine_ref.shape[0], (mine_ref.shape[1] - LANES) // 3
    side = lax.axis_index("rep") % 2
    parity = (lax.axis_index("shard") // INNER) % 2
    for place, home, came in ((side, mine_ref, other_ref), (1 - side, other_ref, mine_ref)):
        start = pl.multiple_of((2 * place + parity) * quarter, LANES)
        total = home[:, :quarter] + came[:, quarter : 2 * quarter]
        up_ref[:, pl.ds(start, quarter)] = total * factor
        start = pl.multiple_of((2 * place + 1 - parity) * quarter, LANES)
        up_ref[:, pl.ds(start, quarter)] = came[:, 2 * quarter : 3 * quarter] * factor
    low = 3 * quarter
    sums = (mine_ref[:, low:] + other_ref[:, low:]) * factor
    dw_ref[...] = sums[:, :TAPS]
    turned = sums.T
    gain_ref[...] = turned[TAPS : TAPS + 1, :]
    bias_ref[...] = turned[TAPS + 1 : TAPS + 2, :]


def fold(rows):
    half = rows.shape[0] // 2
    low = lax.broadcasted_iota(jnp.int32, (half, LANES), 1) < LANES // 2
    return jnp.where(low, rows[:half], pltpu.roll(rows[half:], LANES // 2, 1))


def unfold(rows):
    return jnp.concatenate([rows, pltpu.roll(rows, LANES // 2, 1)], axis=0)


def clear_borders(padded, breadth):
    shape = padded.shape[:-2] + (8, LANES)
    padded[..., :8, :] = jnp.zeros(shape, F32)
    padded[..., 8 + breadth :, :] = jnp.zeros(shape, F32)


def conv_norm_kernel(relative, own, height, breadth, *refs):
    small = refs[:INNER]
    sources = refs[INNER : INNER + 2]
    x_ref = sources[0]
    normed_ref, white_ref, inv_ref, taps_ref, corner_ref, *scratch = refs[INNER + 2 :]
    gathered, unfolded, padded, conv = scratch
    pixels, depth = x_ref.shape
    tiles = depth // LANES
    quarter = corner_ref.shape[1]
    start = pl.multiple_of((1 - lax.axis_index("rep") % 2) * quarter, LANES)
    corner_ref[...] = sources[1][pixels:, pl.ds(start, quarter)]
    if relative:
        for group, piece in enumerate(small):
            unfolded[group * 2 * piece.shape[0] : (group + 1) * 2 * piece.shape[0], :] = unfold(
                piece[...].astype(F32)
            )
        count = unfolded.shape[0] // INNER
        small = [unfolded.at[pl.ds(group * count, count), :] for group in range(INNER)]
    place_rows(small, gathered, own, relative, F32)
    clear_borders(padded, breadth)
    for tile in range(tiles):
        lanes = slice(tile * LANES, (tile + 1) * LANES)
        taps_ref[tile] = gathered[lanes, :].T

    for image, source in enumerate(sources):
        for tile in range(tiles):
            lanes = slice(tile * LANES, (tile + 1) * LANES)
            part = source[:pixels, lanes].astype(F32)
            padded[tile, :, 8 : 8 + breadth, :] = part.reshape(height, breadth, LANES)

        def one_tile(tile, carry):
            sums = correlate(
                padded,
                tile,
                lambda down, across: taps_ref[tile, pl.ds(down * KS + across, 1), :],
                height,
                breadth,
            )
            for line in range(height):
                conv[tile, line * breadth : (line + 1) * breadth, :] = sums[line]
            return carry

        lax.fori_loop(0, tiles, one_tile, 0)
        total = conv[0]
        for tile in range(1, tiles):
            total = total + conv[tile]
        average = jnp.sum(total, axis=-1, keepdims=True) / depth
        squares = None
        for tile in range(tiles):
            centered = conv[tile] - average
            squares = centered * centered if squares is None else squares + centered * centered
        variance = jnp.sum(squares, axis=-1, keepdims=True) / depth
        inv_std = lax.rsqrt(variance + NORM_EPS)
        rows = slice(image * pixels, (image + 1) * pixels)
        inv_ref[rows, :] = jnp.broadcast_to(inv_std, (pixels, LANES))
        for tile in range(tiles):
            lanes = slice(tile * LANES, (tile + 1) * LANES)
            whitened = (conv[tile] - average) * inv_std
            white_ref[rows, lanes] = whitened
            gain = taps_ref[tile, TAPS : TAPS + 1, :]
            bias = taps_ref[tile, TAPS + 1 : TAPS + 2, :]
            normed_ref[rows, lanes] = (whitened * gain + bias).astype(BF16)


def cot_pack_kernel(image_ref, cot_ref, across_ref, sibling_ref):
    pixels, half = sibling_ref.shape
    quarter = half // 2
    side = lax.axis_index("rep") % 2
    parity = (lax.axis_index("shard") // INNER) % 2
    for place in range(2):
        start = pl.multiple_of(place * half + (1 - parity) * quarter, LANES)
        lanes = slice(place * quarter, (place + 1) * quarter)
        across_ref[pixels:, lanes] = cot_ref[:, pl.ds(start, quarter)]
    across_ref[:pixels, :] = image_ref[...]
    sibling_ref[...] = cot_ref[:, pl.ds(pl.multiple_of((1 - side) * half, LANES), half)]


def join_kernel(own_ref, came_ref, out_ref):
    rows = own_ref.shape[0]
    out_ref[:rows, :] = own_ref[...]
    out_ref[rows:, :] = came_ref[...]


def order_kernel(relative, own, *refs):
    if not relative:
        place_rows(refs[:INNER], refs[INNER], own, relative)
        return
    home, first, second, out_ref = refs
    side = lax.axis_index("rep") % 2
    lines = home.shape[0] // own
    for line in range(lines):
        rows = slice(line * own, (line + 1) * own)
        below = slice((lines + line) * own, (lines + line + 1) * own)
        for ref, span, group in (
            (home, rows, 0),
            (first, rows, 1 + side),
            (second, rows, 2 - side),
            (second, below, INNER - 1),
        ):
            start = block_rows(True, group, line, own, lines)
            out_ref[pl.ds(start, own), :] = ref[span, :]


def project_kernel(relative, own, *refs):
    weight, n_own, n_sibling, cot_ref, sibling_ref, across_ref, corner_ref = refs[:7]
    pieces = refs[7 : 7 + INNER]
    gp_ref, normed, cot, grad = refs[7 + INNER :]
    pixels, half = sibling_ref.shape
    quarter = half // 2
    side = lax.axis_index("rep") % 2
    parity = (lax.axis_index("shard") // INNER) % 2
    normed[: 2 * pixels, :] = n_own[...]
    normed[2 * pixels :, :] = n_sibling[...]
    start = pl.multiple_of(side * half + parity * quarter, LANES)
    cot[:pixels, :] = cot_ref[:, pl.ds(start, quarter)]
    start = pl.multiple_of(side * quarter, LANES)
    cot[pixels : 2 * pixels, :] = across_ref[pixels:, pl.ds(start, quarter)]
    start = pl.multiple_of(parity * quarter, LANES)
    cot[2 * pixels : 3 * pixels, :] = sibling_ref[:, pl.ds(start, quarter)]
    cot[3 * pixels :, :] = corner_ref[...]
    for start in range(0, quarter, LANES):
        columns = slice(start, start + LANES)
        pre_act = jnp.dot(normed[...], weight[:, columns], preferred_element_type=F32)
        gp_ref[:, columns] = (cot[:, columns].astype(F32) * gelu_slope(pre_act)).astype(BF16)
    grad[...] = lax.dot_general(
        normed[...], gp_ref[...], (((0,), (0,)), ((), ())), preferred_element_type=F32
    )
    split_rows(grad, pieces, own, relative)


def back_project_kernel(weight, gp_ref, own_ref, other_ref):
    rows = own_ref.shape[0]
    grad_normed = lax.dot_general(
        gp_ref[...], weight[...], (((1,), (1,)), ((), ())), preferred_element_type=F32
    )
    own_ref[...] = grad_normed[:rows]
    other_ref[...] = grad_normed[rows:]


def norm_back_kernel(relative, own, height, breadth, *refs):
    gn_own, gn_other, white_ref, inv_ref, taps_ref, x_ref, far_ref = refs[:7]
    pieces = refs[7 : 7 + INNER]
    grad_ref, sent_ref, padded, grads_ref, rows, small, unfolded = refs[7 + INNER :]
    pixels, depth = x_ref.shape
    tiles = depth // LANES
    clear_borders(padded, breadth)
    rows[...] = jnp.zeros_like(rows)
    for image, source in enumerate((x_ref, far_ref)):
        span = slice(image * pixels, (image + 1) * pixels)
        first = None
        second = None
        for tile in range(tiles):
            lanes = slice(tile * LANES, (tile + 1) * LANES)
            part = source[:pixels, lanes].astype(F32)
            padded[image, tile, :, 8 : 8 + breadth, :] = part.reshape(height, breadth, LANES)
            grad_normed = gn_own[span, lanes] + gn_other[span, lanes]
            whitened = white_ref[span, lanes]
            product = grad_normed * whitened
            gain = taps_ref[tile, TAPS : TAPS + 1, :]
            rows[tile, TAPS : TAPS + 1, :] += jnp.sum(product, axis=0, keepdims=True)
            rows[tile, TAPS + 1 : TAPS + 2, :] += jnp.sum(grad_normed, axis=0, keepdims=True)
            one, two = grad_normed * gain, product * gain
            first = one if first is None else first + one
            second = two if second is None else second + two
        mean_first = jnp.sum(first, axis=-1, keepdims=True) / depth
        mean_second = jnp.sum(second, axis=-1, keepdims=True) / depth
        for tile in range(tiles):
            lanes = slice(tile * LANES, (tile + 1) * LANES)
            gain = taps_ref[tile, TAPS : TAPS + 1, :]
            grad_white = (gn_own[span, lanes] + gn_other[span, lanes]) * gain
            grad_conv = inv_ref[span, :] * (
                grad_white - mean_first - white_ref[span, lanes] * mean_second
            )
            grad_conv = grad_conv.reshape(height, breadth, LANES)
            grads_ref[image, tile] = grad_conv
            if image == 0:
                grad_ref[tile] = grad_conv
            else:
                sent_ref[tile] = grad_conv.astype(BF16)

    def one_tile(tile, carry):
        grads = [[grads_ref[image, tile, line] for line in range(height)] for image in range(2)]
        for across in range(KS):
            columns = slice(8 - MARGIN + across, 8 - MARGIN + across + breadth)
            shifted = [padded[image, tile, :, columns, :] for image in range(2)]
            for down in range(KS):
                total = None
                for image in range(2):
                    for line in range(height):
                        origin = line + down - MARGIN
                        if 0 <= origin < height:
                            term = grads[image][line] * shifted[image][origin]
                            total = term if total is None else total + term
                rows[tile, pl.ds(down * KS + across, 1), :] = jnp.sum(total, axis=0, keepdims=True)
        return carry

    lax.fori_loop(0, tiles, one_tile, 0)
    for tile in range(tiles):
        small[tile * LANES : (tile + 1) * LANES, :] = rows[tile].T
    if relative:
        whole = [unfolded.at[group] for group in range(INNER)]
        split_rows(small, whole, own, relative)
        for source, piece in zip(whole, pieces):
            piece[...] = fold(source[...]).astype(piece.dtype)
    else:
        split_rows(small, pieces, own, relative)


def conv_back_kernel(grad_ref, other_ref, taps_ref, out_ref, padded):
    tiles, height, breadth, _ = grad_ref.shape
    clear_borders(padded, breadth)
    padded[:, :, 8 : 8 + breadth, :] = grad_ref[...] + other_ref[...].astype(F32)

    def one_tile(tile, carry):
        sums = correlate(
            padded,
            tile,
            lambda down, across: taps_ref[tile, pl.ds(TAPS - 1 - down * KS - across, 1), :],
            height,
            breadth,
        )
        start = pl.multiple_of(tile * LANES, LANES)
        for line in range(height):
            out_ref[0, line, :, pl.ds(start, LANES)] = sums[line].astype(BF16)
        return carry

    lax.fori_loop(0, tiles, one_tile, 0)


def call(kernel, name, outs, scratch, micros, *args, mebibytes=48):
    flops = int(micros * 1.1e9)
    moved = sum(math.prod(a.shape) * a.dtype.itemsize for a in args)
    moved += sum(math.prod(o.shape) * o.dtype.itemsize for o in outs)
    return pl.pallas_call(
        kernel,
        out_shape=outs,
        in_specs=[VMEM] * len(args),
        out_specs=[VMEM] * len(outs),
        scratch_shapes=scratch,
        compiler_params=params(mebibytes),
        cost_estimate=pl.CostEstimate(flops=flops, bytes_accessed=moved, transcendentals=0),
        name=name,
    )(*args)


def body(images, cotangent, depthwise_weight, norm_gain, norm_bias, up_weight):
    shards, reps = lax.axis_size("shard"), lax.axis_size("rep")
    own, hidden = up_weight.shape
    depth = own * shards
    lines = shards // INNER
    half, quarter = hidden // 2, hidden // 4
    height, breadth = images.shape[1:3]
    pixels = height * breadth
    tiles = depth // LANES
    me = lax.axis_index("shard")
    side = lax.axis_index("rep") % 2
    parity = (me // INNER) % 2
    relative = own % 16 == 0

    def over_shard(array, flip):
        return lax.ppermute(array, "shard", [(i, i ^ flip) for i in range(shards)])

    def crossing(array, flip):
        pairs = [
            (i * reps + r, (i ^ flip) * reps + (r ^ 1)) for i in range(shards) for r in range(reps)
        ]
        return lax.ppermute(array, ("shard", "rep"), pairs)

    def hop(array, place):
        flips = [(1, 2), (2, 1)]
        pairs = [
            (i * reps + r, (i ^ flips[r % 2][place]) * reps + r)
            for i in range(shards)
            for r in range(reps)
        ]
        return lax.ppermute(array, ("shard", "rep"), pairs)

    def over_core(array):
        return lax.ppermute(array, "rep", [(i, i ^ 1) for i in range(reps)])

    def true_order(pieces):
        if relative:
            return pieces
        stacked = jnp.stack(pieces).reshape(shards, own, -1)
        flips = jnp.arange(shards) ^ me
        places = (flips % INNER) * lines + flips // INNER
        return list(jnp.take(stacked, places, axis=0).reshape(INNER, lines * own, -1))

    def relative_order(pieces):
        if relative:
            return pieces
        stacked = jnp.concatenate([p.astype(F32) for p in pieces]).reshape(shards, own, -1)
        flips = (jnp.arange(lines)[None, :] * INNER + jnp.arange(INNER)[:, None]).reshape(-1)
        moved = jnp.take(stacked, flips ^ me, axis=0).reshape(INNER, lines * own, -1)
        return [moved[0]] + [moved[i].astype(BF16) for i in range(1, INNER)]

    shape = jax.ShapeDtypeStruct
    home, near, far = call(
        pack_kernel,
        "pack",
        [shape((own, quarter + LANES), BF16)] * 3,
        [
            pltpu.VMEM((LANES, LANES), F32),
            pltpu.VMEM((own, LANES), F32),
        ],
        0.5,
        up_weight,
        depthwise_weight,
        norm_gain[None, :],
        norm_bias[None, :],
        mebibytes=63,
    )
    image, cotangent = images.reshape(pixels, depth), cotangent.reshape(pixels, hidden)
    home, near, far, image, cotangent = lax.optimization_barrier(
        (home, near, far, image, cotangent)
    )
    gathered = [home] + [
        crossing(far if line % 2 else near, INNER * line) for line in range(1, lines)
    ]
    across, cot_sibling = call(
        cot_pack_kernel,
        "cot_pack",
        [shape((2 * pixels, half), BF16), shape((pixels, half), BF16)],
        [],
        0.4,
        image,
        cotangent,
    )
    across, cot_sibling = crossing(across, INNER), over_core(cot_sibling)

    rows = lines * own
    folded = rows // 2 if relative else rows
    weight_lines, extra_lines = call(
        assemble_kernel,
        "assemble",
        [shape((rows, quarter), BF16), shape((folded, LANES), BF16)],
        [],
        4.0,
        *gathered,
    )
    weight_lines, cot_sibling = lax.optimization_barrier((weight_lines, cot_sibling))
    first_lines = hop(weight_lines, 0)
    (joined,) = call(
        join_kernel,
        "join",
        [shape((2 * rows, quarter), BF16)],
        [],
        0.3,
        weight_lines,
        first_lines,
    )
    second_lines = hop(joined, 1)
    weights = [weight_lines, first_lines, second_lines]
    extras = [extra_lines] + [crossing(extra_lines, flip) for flip in range(1, INNER)]
    if not relative:
        extras = true_order(extras)
        x_lines = jnp.where(side == 0, first_lines, second_lines[:rows])
        y_lines = jnp.where(side == 0, second_lines[:rows], first_lines)
        weights = true_order([weight_lines, x_lines, y_lines, second_lines[rows:]])
    (weight,) = call(
        functools.partial(order_kernel, relative, own),
        "order",
        [shape((depth, quarter), BF16)],
        [],
        1.0,
        *weights,
    )

    padded = pltpu.VMEM((tiles, height, breadth + 16, LANES), F32)
    normed, whitened, inv_std, taps, corner = call(
        functools.partial(conv_norm_kernel, relative, own, height, breadth),
        "conv_norm",
        [
            shape((2 * pixels, depth), BF16),
            shape((2 * pixels, depth), F32),
            shape((2 * pixels, LANES), F32),
            shape((tiles, LANES, LANES), F32),
            shape((pixels, quarter), BF16),
        ],
        [
            pltpu.VMEM((depth, LANES), F32),
            pltpu.VMEM((depth, LANES), F32),
            padded,
            pltpu.VMEM((tiles, pixels, LANES), F32),
        ],
        0.1,
        *extras,
        image,
        across,
    )
    normed_sibling, corner = over_core(normed), over_core(corner)
    *pieces, grad_pre = call(
        functools.partial(project_kernel, relative, own),
        "project",
        [shape((rows, quarter), F32)]
        + [shape((rows, quarter), BF16)] * (INNER - 1)
        + [shape((4 * pixels, quarter), BF16)],
        [
            pltpu.VMEM((4 * pixels, depth), BF16),
            pltpu.VMEM((4 * pixels, quarter), BF16),
            pltpu.VMEM((depth, quarter), F32),
        ],
        1.6,
        weight,
        normed,
        normed_sibling,
        cotangent,
        cot_sibling,
        across,
        corner,
    )
    gn_kept, gn_sent = call(
        back_project_kernel,
        "back_project",
        [shape((2 * pixels, depth), F32)] * 2,
        [],
        0.7,
        weight,
        grad_pre,
    )
    pieces = relative_order(pieces)
    arrived = [over_shard(piece, flip) for flip, piece in enumerate(pieces) if flip]
    *small, grad_conv, grad_sent = call(
        functools.partial(norm_back_kernel, relative, own, height, breadth),
        "norm_back",
        [shape((folded, LANES), F32)]
        + [shape((folded, LANES), BF16)] * (INNER - 1)
        + [
            shape((tiles, height, breadth, LANES), F32),
            shape((tiles, height, breadth, LANES), BF16),
        ],
        [
            pltpu.VMEM((2, tiles, height, breadth + 16, LANES), F32),
            pltpu.VMEM((2, tiles, height, breadth, LANES), F32),
            pltpu.VMEM((tiles, LANES, LANES), F32),
            pltpu.VMEM((depth, LANES), F32),
            pltpu.VMEM((INNER, rows, LANES), F32),
        ],
        0.1,
        gn_kept,
        over_core(gn_sent),
        whitened,
        inv_std,
        taps,
        image,
        across,
    )
    small = relative_order(small)
    small_arrived = [crossing(piece, flip) for flip, piece in enumerate(small) if flip]
    grad_other = crossing(grad_sent, INNER)
    (grad_images,) = call(
        conv_back_kernel,
        "conv_back",
        [shape(images.shape, BF16)],
        [padded],
        0.1,
        grad_conv,
        grad_other,
        taps,
    )

    home, *sent = call(
        functools.partial(plane_sum_kernel, lines),
        "plane_sum",
        [shape((own, quarter + LANES), F32)] + [shape((own, quarter + LANES), BF16)] * (lines - 1),
        [],
        2.0,
        pieces[0],
        *arrived,
        small[0],
        *small_arrived,
    )
    home, grad_images = lax.optimization_barrier((home, grad_images))
    came = [crossing(piece, INNER * line) for line, piece in enumerate(sent, 1)]
    (total,) = call(
        line_sum_kernel,
        "line_sum",
        [shape((own, 3 * quarter + LANES), F32)],
        [],
        0.3,
        home,
        *came,
    )
    if reps > 2:
        groups = [[i for i in range(reps) if i % 2 == s] for s in range(2)]
        total = lax.psum(total, "rep", axis_index_groups=groups)
    other = over_core(total)
    factor = 1.0 / math.sqrt(images.shape[0] * pixels * shards * reps)
    grad_up, grad_depthwise, grad_gain, grad_bias = call(
        functools.partial(finish_kernel, factor),
        "finish",
        [
            shape((own, hidden), F32),
            shape((own, TAPS), F32),
            shape((1, own), F32),
            shape((1, own), F32),
        ],
        [],
        0.5,
        total,
        other,
    )
    return (grad_images, grad_up, grad_depthwise, grad_gain[0], grad_bias[0])


def solution(mesh):
    placed = (
        P(("shard", "rep"), None, None, None),
        P(("shard", "rep"), None, None, None),
        P("shard", None),
        P("shard"),
        P("shard"),
        P("shard", None),
    )
    return jax.shard_map(
        body,
        mesh=mesh,
        in_specs=placed,
        out_specs=(
            P(("shard", "rep"), None, None, None),
            P("shard", None),
            P("shard", None),
            P("shard"),
            P("shard"),
        ),
        check_vma=False,
    )
```

```python
import functools
import math

import jax
import jax.numpy as jnp
from jax import lax
from jax.experimental import pallas as pl
from jax.experimental.pallas import tpu as pltpu
from jax.sharding import PartitionSpec as P

KS = 7
TAPS = KS * KS
MARGIN = KS // 2
LANES = 128
INNER = 4
NORM_EPS = 1e-06
BF16 = jnp.bfloat16
F32 = jnp.float32
VMEM = pl.BlockSpec(memory_space=pltpu.VMEM)


def params(mebibytes):
    return pltpu.CompilerParams(vmem_limit_bytes=mebibytes * 1024 * 1024)


def gelu_slope(inputs):
    cumulative = 0.5 * (1.0 + lax.erf(inputs * 0.7071067811865476))
    return cumulative + inputs * jnp.exp(-0.5 * inputs * inputs) * 0.3989422804014327


def block_rows(relative, group, line, own, lines):
    if relative:
        place = lax.axis_index("shard") ^ (line * INNER + group)
        return pl.multiple_of(place * own, 16)
    return (group * lines + line) * own


def place_rows(pieces, target, own, relative, cast=None):
    for group, piece in enumerate(pieces):
        lines = piece.shape[0] // own
        if not relative:
            target[group * piece.shape[0] : (group + 1) * piece.shape[0], :] = (
                piece[...] if cast is None else piece[...].astype(cast)
            )
            continue
        for line in range(lines):
            rows = piece[line * own : (line + 1) * own, :]
            start = block_rows(True, group, line, own, lines)
            target[pl.ds(start, own), :] = rows if cast is None else rows.astype(cast)


def split_rows(source, pieces, own, relative):
    for group, piece in enumerate(pieces):
        lines = piece.shape[0] // own
        if not relative:
            piece[...] = source[group * piece.shape[0] : (group + 1) * piece.shape[0], :].astype(
                piece.dtype
            )
            continue
        for line in range(lines):
            start = block_rows(True, group, line, own, lines)
            piece[line * own : (line + 1) * own, :] = source[pl.ds(start, own), :].astype(
                piece.dtype
            )


def correlate(padded, tile, tap_row, height, breadth):
    sums = [None] * height
    for across in range(KS):
        shifted = padded[tile, :, 8 - MARGIN + across : 8 - MARGIN + across + breadth, :]
        for down in range(KS):
            row = tap_row(down, across)
            for line in range(height):
                origin = line + down - MARGIN
                if 0 <= origin < height:
                    term = shifted[origin] * row
                    sums[line] = term if sums[line] is None else sums[line] + term
    return sums


def tight(own, quarter):
    return own % (16 * (quarter // LANES)) == 0


def with_small(weights, extras):
    own, quarter = weights.shape
    if not tight(own, quarter):
        return jnp.concatenate([weights, extras], axis=1)
    folded = fold(extras)
    count = folded.shape[0] * LANES // quarter
    parts = [folded[at : at + count] for at in range(0, folded.shape[0], count)]
    return jnp.concatenate([weights, jnp.concatenate(parts, axis=1)], axis=0)


def without_small(mixed, own, quarter):
    if not tight(own, quarter):
        return mixed[:, :quarter], mixed[:, quarter:]
    parts = [mixed[own:, at : at + LANES] for at in range(0, quarter, LANES)]
    return mixed[:own], unfold(jnp.concatenate(parts, axis=0))


def mixed_shape(own, quarter):
    if not tight(own, quarter):
        return (own, quarter + LANES)
    return (own + own // 2 * LANES // quarter, quarter)


def pack_kernel(w_ref, dw_ref, gain_ref, bias_ref, home_ref, near_ref, far_ref, turned, wide):
    own, hidden = w_ref.shape
    quarter = hidden // 4
    side = lax.axis_index("rep") % 2
    parity = (lax.axis_index("shard") // INNER) % 2
    turned[...] = jnp.zeros_like(turned)
    turned[TAPS : TAPS + 1, :own] = gain_ref[...].astype(F32)
    turned[TAPS + 1 : TAPS + 2, :own] = bias_ref[...].astype(F32)
    wide[...] = jnp.zeros_like(wide)
    wide[:, :TAPS] = dw_ref[...].astype(F32)
    extras = wide[...] + turned[...].T[:own]
    kinds = ((home_ref, side, parity), (near_ref, 1 - side, parity), (far_ref, 1 - side, 1 - parity))
    for ref, place, which in kinds:
        start = pl.multiple_of(place * (2 * quarter) + which * quarter, LANES)
        weights = w_ref[:, pl.ds(start, quarter)].astype(F32)
        ref[...] = with_small(weights, extras).astype(BF16)


def assemble_kernel(own, *refs):
    pieces, (weight_ref, extra_ref) = refs[:-2], refs[-2:]
    quarter = weight_ref.shape[1]
    parts = [without_small(piece[...].astype(F32), own, quarter) for piece in pieces]
    for line, (weights, _) in enumerate(parts):
        weight_ref[line * own : (line + 1) * own, :] = weights.astype(BF16)
    extras = jnp.concatenate([extra for _, extra in parts], axis=0)
    if extra_ref.shape[0] < extras.shape[0]:
        extras = fold(extras)
    extra_ref[...] = extras.astype(BF16)


def plane_sum_kernel(lines, *refs):
    pieces, small, outs = refs[:INNER], refs[INNER : 2 * INNER], refs[2 * INNER :]
    own = pieces[0].shape[0] // lines
    quarter = pieces[0].shape[1]
    extras = small[0][...]
    for part in small[1:]:
        extras = extras + part[...].astype(F32)
    if extras.shape[0] < pieces[0].shape[0]:
        extras = unfold(extras)
    for line, out in enumerate(outs):
        rows = slice(line * own, (line + 1) * own)
        total = pieces[0][rows, :]
        for part in pieces[1:]:
            total = total + part[rows, :].astype(F32)
        out[...] = with_small(total, extras[rows, :]).astype(out.dtype)


def line_sum_kernel(own, *refs):
    pieces, total_ref = refs[:-1], refs[-1]
    quarter = (total_ref.shape[1] - LANES) // 3
    near, far = None, None
    for line, piece in enumerate(pieces[1:], 1):
        came = piece[...].astype(F32)
        if line % 2:
            far = came if far is None else far + came
        else:
            near = came if near is None else near + came
    home, extras = without_small(pieces[0][...], own, quarter)
    total_ref[:, :quarter] = home
    for place, part in ((1, near), (2, far)):
        weights, more = without_small(part, own, quarter)
        total_ref[:, place * quarter : (place + 1) * quarter] = weights
        extras = extras + more
    total_ref[:, 3 * quarter :] = extras


def finish_kernel(factor, mine_ref, other_ref, up_ref, dw_ref, gain_ref, bias_ref):
    own, quarter = mine_ref.shape[0], (mine_ref.shape[1] - LANES) // 3
    side = lax.axis_index("rep") % 2
    parity = (lax.axis_index("shard") // INNER) % 2
    for place, home, came in ((side, mine_ref, other_ref), (1 - side, other_ref, mine_ref)):
        start = pl.multiple_of((2 * place + parity) * quarter, LANES)
        total = home[:, :quarter] + came[:, quarter : 2 * quarter]
        up_ref[:, pl.ds(start, quarter)] = total * factor
        start = pl.multiple_of((2 * place + 1 - parity) * quarter, LANES)
        up_ref[:, pl.ds(start, quarter)] = came[:, 2 * quarter : 3 * quarter] * factor
    low = 3 * quarter
    sums = (mine_ref[:, low:] + other_ref[:, low:]) * factor
    dw_ref[...] = sums[:, :TAPS]
    turned = sums.T
    gain_ref[...] = turned[TAPS : TAPS + 1, :]
    bias_ref[...] = turned[TAPS + 1 : TAPS + 2, :]


def fold(rows):
    half = rows.shape[0] // 2
    low = lax.broadcasted_iota(jnp.int32, (half, LANES), 1) < LANES // 2
    return jnp.where(low, rows[:half], pltpu.roll(rows[half:], LANES // 2, 1))


def unfold(rows):
    return jnp.concatenate([rows, pltpu.roll(rows, LANES // 2, 1)], axis=0)


def clear_borders(padded, breadth):
    shape = padded.shape[:-2] + (8, LANES)
    padded[..., :8, :] = jnp.zeros(shape, F32)
    padded[..., 8 + breadth :, :] = jnp.zeros(shape, F32)


def conv_norm_kernel(relative, own, height, breadth, *refs):
    small = refs[:INNER]
    sources = refs[INNER : INNER + 2]
    x_ref = sources[0]
    normed_ref, white_ref, inv_ref, taps_ref, corner_ref, *scratch = refs[INNER + 2 :]
    gathered, unfolded, padded, conv = scratch
    pixels, depth = x_ref.shape
    tiles = depth // LANES
    quarter = corner_ref.shape[1]
    start = pl.multiple_of((1 - lax.axis_index("rep") % 2) * quarter, LANES)
    corner_ref[...] = sources[1][pixels:, pl.ds(start, quarter)]
    if relative:
        for group, piece in enumerate(small):
            unfolded[group * 2 * piece.shape[0] : (group + 1) * 2 * piece.shape[0], :] = unfold(
                piece[...].astype(F32)
            )
        count = unfolded.shape[0] // INNER
        small = [unfolded.at[pl.ds(group * count, count), :] for group in range(INNER)]
    place_rows(small, gathered, own, relative, F32)
    clear_borders(padded, breadth)
    for tile in range(tiles):
        lanes = slice(tile * LANES, (tile + 1) * LANES)
        taps_ref[tile] = gathered[lanes, :].T

    for image, source in enumerate(sources):
        for tile in range(tiles):
            lanes = slice(tile * LANES, (tile + 1) * LANES)
            part = source[:pixels, lanes].astype(F32)
            padded[tile, :, 8 : 8 + breadth, :] = part.reshape(height, breadth, LANES)

        def one_tile(tile, carry):
            sums = correlate(
                padded,
                tile,
                lambda down, across: taps_ref[tile, pl.ds(down * KS + across, 1), :],
                height,
                breadth,
            )
            for line in range(height):
                conv[tile, line * breadth : (line + 1) * breadth, :] = sums[line]
            return carry

        lax.fori_loop(0, tiles, one_tile, 0)
        total = conv[0]
        for tile in range(1, tiles):
            total = total + conv[tile]
        average = jnp.sum(total, axis=-1, keepdims=True) / depth
        squares = None
        for tile in range(tiles):
            centered = conv[tile] - average
            squares = centered * centered if squares is None else squares + centered * centered
        variance = jnp.sum(squares, axis=-1, keepdims=True) / depth
        inv_std = lax.rsqrt(variance + NORM_EPS)
        rows = slice(image * pixels, (image + 1) * pixels)
        inv_ref[rows, :] = jnp.broadcast_to(inv_std, (pixels, LANES))
        for tile in range(tiles):
            lanes = slice(tile * LANES, (tile + 1) * LANES)
            whitened = (conv[tile] - average) * inv_std
            white_ref[rows, lanes] = whitened
            gain = taps_ref[tile, TAPS : TAPS + 1, :]
            bias = taps_ref[tile, TAPS + 1 : TAPS + 2, :]
            normed_ref[rows, lanes] = (whitened * gain + bias).astype(BF16)


def cot_pack_kernel(image_ref, cot_ref, across_ref, sibling_ref):
    pixels, half = sibling_ref.shape
    quarter = half // 2
    side = lax.axis_index("rep") % 2
    parity = (lax.axis_index("shard") // INNER) % 2
    for place in range(2):
        start = pl.multiple_of(place * half + (1 - parity) * quarter, LANES)
        lanes = slice(place * quarter, (place + 1) * quarter)
        across_ref[pixels:, lanes] = cot_ref[:, pl.ds(start, quarter)]
    across_ref[:pixels, :] = image_ref[...]
    sibling_ref[...] = cot_ref[:, pl.ds(pl.multiple_of((1 - side) * half, LANES), half)]


def join_kernel(own_ref, came_ref, out_ref):
    rows = own_ref.shape[0]
    out_ref[:rows, :] = own_ref[...]
    out_ref[rows:, :] = came_ref[...]


def order_kernel(relative, own, *refs):
    if not relative:
        place_rows(refs[:INNER], refs[INNER], own, relative)
        return
    home, first, second, out_ref = refs
    side = lax.axis_index("rep") % 2
    lines = home.shape[0] // own
    for line in range(lines):
        rows = slice(line * own, (line + 1) * own)
        below = slice((lines + line) * own, (lines + line + 1) * own)
        for ref, span, group in (
            (home, rows, 0),
            (first, rows, 1 + side),
            (second, rows, 2 - side),
            (second, below, INNER - 1),
        ):
            start = block_rows(True, group, line, own, lines)
            out_ref[pl.ds(start, own), :] = ref[span, :]


def project_kernel(relative, own, *refs):
    weight, n_own, n_sibling, cot_ref, sibling_ref, across_ref, corner_ref = refs[:7]
    pieces = refs[7 : 7 + INNER]
    gp_ref, normed, cot, grad = refs[7 + INNER :]
    pixels, half = sibling_ref.shape
    quarter = half // 2
    side = lax.axis_index("rep") % 2
    parity = (lax.axis_index("shard") // INNER) % 2
    normed[: 2 * pixels, :] = n_own[...]
    normed[2 * pixels :, :] = n_sibling[...]
    start = pl.multiple_of(side * half + parity * quarter, LANES)
    cot[:pixels, :] = cot_ref[:, pl.ds(start, quarter)]
    start = pl.multiple_of(side * quarter, LANES)
    cot[pixels : 2 * pixels, :] = across_ref[pixels:, pl.ds(start, quarter)]
    start = pl.multiple_of(parity * quarter, LANES)
    cot[2 * pixels : 3 * pixels, :] = sibling_ref[:, pl.ds(start, quarter)]
    cot[3 * pixels :, :] = corner_ref[...]
    for start in range(0, quarter, LANES):
        columns = slice(start, start + LANES)
        pre_act = jnp.dot(normed[...], weight[:, columns], preferred_element_type=F32)
        gp_ref[:, columns] = (cot[:, columns].astype(F32) * gelu_slope(pre_act)).astype(BF16)
    grad[...] = lax.dot_general(
        normed[...], gp_ref[...], (((0,), (0,)), ((), ())), preferred_element_type=F32
    )
    split_rows(grad, pieces, own, relative)


def back_project_kernel(weight, gp_ref, own_ref, other_ref):
    rows = own_ref.shape[0]
    grad_normed = lax.dot_general(
        gp_ref[...], weight[...], (((1,), (1,)), ((), ())), preferred_element_type=F32
    )
    own_ref[...] = grad_normed[:rows]
    other_ref[...] = grad_normed[rows:]


def norm_back_kernel(relative, own, height, breadth, *refs):
    gn_own, gn_other, white_ref, inv_ref, taps_ref, x_ref, far_ref = refs[:7]
    pieces = refs[7 : 7 + INNER]
    grad_ref, sent_ref, padded, grads_ref, rows, small, unfolded = refs[7 + INNER :]
    pixels, depth = x_ref.shape
    tiles = depth // LANES
    clear_borders(padded, breadth)
    rows[...] = jnp.zeros_like(rows)
    for image, source in enumerate((x_ref, far_ref)):
        span = slice(image * pixels, (image + 1) * pixels)
        first = None
        second = None
        for tile in range(tiles):
            lanes = slice(tile * LANES, (tile + 1) * LANES)
            part = source[:pixels, lanes].astype(F32)
            padded[image, tile, :, 8 : 8 + breadth, :] = part.reshape(height, breadth, LANES)
            grad_normed = gn_own[span, lanes] + gn_other[span, lanes]
            whitened = white_ref[span, lanes]
            product = grad_normed * whitened
            gain = taps_ref[tile, TAPS : TAPS + 1, :]
            rows[tile, TAPS : TAPS + 1, :] += jnp.sum(product, axis=0, keepdims=True)
            rows[tile, TAPS + 1 : TAPS + 2, :] += jnp.sum(grad_normed, axis=0, keepdims=True)
            one, two = grad_normed * gain, product * gain
            first = one if first is None else first + one
            second = two if second is None else second + two
        mean_first = jnp.sum(first, axis=-1, keepdims=True) / depth
        mean_second = jnp.sum(second, axis=-1, keepdims=True) / depth
        for tile in range(tiles):
            lanes = slice(tile * LANES, (tile + 1) * LANES)
            gain = taps_ref[tile, TAPS : TAPS + 1, :]
            grad_white = (gn_own[span, lanes] + gn_other[span, lanes]) * gain
            grad_conv = inv_ref[span, :] * (
                grad_white - mean_first - white_ref[span, lanes] * mean_second
            )
            grad_conv = grad_conv.reshape(height, breadth, LANES)
            grads_ref[image, tile] = grad_conv
            if image == 0:
                grad_ref[tile] = grad_conv
            else:
                sent_ref[tile] = grad_conv.astype(BF16)

    def one_tile(tile, carry):
        grads = [[grads_ref[image, tile, line] for line in range(height)] for image in range(2)]
        for across in range(KS):
            columns = slice(8 - MARGIN + across, 8 - MARGIN + across + breadth)
            shifted = [padded[image, tile, :, columns, :] for image in range(2)]
            for down in range(KS):
                total = None
                for image in range(2):
                    for line in range(height):
                        origin = line + down - MARGIN
                        if 0 <= origin < height:
                            term = grads[image][line] * shifted[image][origin]
                            total = term if total is None else total + term
                rows[tile, pl.ds(down * KS + across, 1), :] = jnp.sum(total, axis=0, keepdims=True)
        return carry

    lax.fori_loop(0, tiles, one_tile, 0)
    for tile in range(tiles):
        small[tile * LANES : (tile + 1) * LANES, :] = rows[tile].T
    if relative:
        whole = [unfolded.at[group] for group in range(INNER)]
        split_rows(small, whole, own, relative)
        for source, piece in zip(whole, pieces):
            piece[...] = fold(source[...]).astype(piece.dtype)
    else:
        split_rows(small, pieces, own, relative)


def conv_back_kernel(grad_ref, other_ref, taps_ref, out_ref, padded):
    tiles, height, breadth, _ = grad_ref.shape
    clear_borders(padded, breadth)
    padded[:, :, 8 : 8 + breadth, :] = grad_ref[...] + other_ref[...].astype(F32)

    def one_tile(tile, carry):
        sums = correlate(
            padded,
            tile,
            lambda down, across: taps_ref[tile, pl.ds(TAPS - 1 - down * KS - across, 1), :],
            height,
            breadth,
        )
        start = pl.multiple_of(tile * LANES, LANES)
        for line in range(height):
            out_ref[0, line, :, pl.ds(start, LANES)] = sums[line].astype(BF16)
        return carry

    lax.fori_loop(0, tiles, one_tile, 0)


def call(kernel, name, outs, scratch, micros, *args, mebibytes=48):
    flops = int(micros * 1.1e9)
    moved = sum(math.prod(a.shape) * a.dtype.itemsize for a in args)
    moved += sum(math.prod(o.shape) * o.dtype.itemsize for o in outs)
    return pl.pallas_call(
        kernel,
        out_shape=outs,
        in_specs=[VMEM] * len(args),
        out_specs=[VMEM] * len(outs),
        scratch_shapes=scratch,
        compiler_params=params(mebibytes),
        cost_estimate=pl.CostEstimate(flops=flops, bytes_accessed=moved, transcendentals=0),
        name=name,
    )(*args)


def body(images, cotangent, depthwise_weight, norm_gain, norm_bias, up_weight):
    shards, reps = lax.axis_size("shard"), lax.axis_size("rep")
    own, hidden = up_weight.shape
    depth = own * shards
    lines = shards // INNER
    half, quarter = hidden // 2, hidden // 4
    height, breadth = images.shape[1:3]
    pixels = height * breadth
    tiles = depth // LANES
    me = lax.axis_index("shard")
    side = lax.axis_index("rep") % 2
    parity = (me // INNER) % 2
    relative = own % 16 == 0

    def over_shard(array, flip):
        return lax.ppermute(array, "shard", [(i, i ^ flip) for i in range(shards)])

    def crossing(array, flip):
        pairs = [
            (i * reps + r, (i ^ flip) * reps + (r ^ 1)) for i in range(shards) for r in range(reps)
        ]
        return lax.ppermute(array, ("shard", "rep"), pairs)

    def hop(array, place):
        flips = [(1, 2), (2, 1)]
        pairs = [
            (i * reps + r, (i ^ flips[r % 2][place]) * reps + r)
            for i in range(shards)
            for r in range(reps)
        ]
        return lax.ppermute(array, ("shard", "rep"), pairs)

    def over_core(array):
        return lax.ppermute(array, "rep", [(i, i ^ 1) for i in range(reps)])

    def true_order(pieces):
        if relative:
            return pieces
        stacked = jnp.stack(pieces).reshape(shards, own, -1)
        flips = jnp.arange(shards) ^ me
        places = (flips % INNER) * lines + flips // INNER
        return list(jnp.take(stacked, places, axis=0).reshape(INNER, lines * own, -1))

    def relative_order(pieces):
        if relative:
            return pieces
        stacked = jnp.concatenate([p.astype(F32) for p in pieces]).reshape(shards, own, -1)
        flips = (jnp.arange(lines)[None, :] * INNER + jnp.arange(INNER)[:, None]).reshape(-1)
        moved = jnp.take(stacked, flips ^ me, axis=0).reshape(INNER, lines * own, -1)
        return [moved[0]] + [moved[i].astype(BF16) for i in range(1, INNER)]

    shape = jax.ShapeDtypeStruct
    home, near, far = call(
        pack_kernel,
        "pack",
        [shape(mixed_shape(own, quarter), BF16)] * 3,
        [
            pltpu.VMEM((LANES, LANES), F32),
            pltpu.VMEM((own, LANES), F32),
        ],
        0.5,
        up_weight,
        depthwise_weight,
        norm_gain[None, :],
        norm_bias[None, :],
        mebibytes=63,
    )
    image, cotangent = images.reshape(pixels, depth), cotangent.reshape(pixels, hidden)
    home, near, far, image, cotangent = lax.optimization_barrier(
        (home, near, far, image, cotangent)
    )
    gathered = [home] + [
        crossing(far if line % 2 else near, INNER * line) for line in range(1, lines)
    ]
    across, cot_sibling = call(
        cot_pack_kernel,
        "cot_pack",
        [shape((2 * pixels, half), BF16), shape((pixels, half), BF16)],
        [],
        0.4,
        image,
        cotangent,
    )
    across, cot_sibling = crossing(across, INNER), over_core(cot_sibling)

    rows = lines * own
    folded = rows // 2 if relative else rows
    weight_lines, extra_lines = call(
        functools.partial(assemble_kernel, own),
        "assemble",
        [shape((rows, quarter), BF16), shape((folded, LANES), BF16)],
        [],
        4.0,
        *gathered,
    )
    weight_lines, cot_sibling = lax.optimization_barrier((weight_lines, cot_sibling))
    first_lines = hop(weight_lines, 0)
    (joined,) = call(
        join_kernel,
        "join",
        [shape((2 * rows, quarter), BF16)],
        [],
        0.3,
        weight_lines,
        first_lines,
    )
    second_lines = hop(joined, 1)
    weights = [weight_lines, first_lines, second_lines]
    extras = [extra_lines] + [crossing(extra_lines, flip) for flip in range(1, INNER)]
    if not relative:
        extras = true_order(extras)
        x_lines = jnp.where(side == 0, first_lines, second_lines[:rows])
        y_lines = jnp.where(side == 0, second_lines[:rows], first_lines)
        weights = true_order([weight_lines, x_lines, y_lines, second_lines[rows:]])
    (weight,) = call(
        functools.partial(order_kernel, relative, own),
        "order",
        [shape((depth, quarter), BF16)],
        [],
        1.0,
        *weights,
    )

    padded = pltpu.VMEM((tiles, height, breadth + 16, LANES), F32)
    normed, whitened, inv_std, taps, corner = call(
        functools.partial(conv_norm_kernel, relative, own, height, breadth),
        "conv_norm",
        [
            shape((2 * pixels, depth), BF16),
            shape((2 * pixels, depth), F32),
            shape((2 * pixels, LANES), F32),
            shape((tiles, LANES, LANES), F32),
            shape((pixels, quarter), BF16),
        ],
        [
            pltpu.VMEM((depth, LANES), F32),
            pltpu.VMEM((depth, LANES), F32),
            padded,
            pltpu.VMEM((tiles, pixels, LANES), F32),
        ],
        0.1,
        *extras,
        image,
        across,
    )
    normed_sibling, corner = over_core(normed), over_core(corner)
    *pieces, grad_pre = call(
        functools.partial(project_kernel, relative, own),
        "project",
        [shape((rows, quarter), F32)]
        + [shape((rows, quarter), BF16)] * (INNER - 1)
        + [shape((4 * pixels, quarter), BF16)],
        [
            pltpu.VMEM((4 * pixels, depth), BF16),
            pltpu.VMEM((4 * pixels, quarter), BF16),
            pltpu.VMEM((depth, quarter), F32),
        ],
        1.6,
        weight,
        normed,
        normed_sibling,
        cotangent,
        cot_sibling,
        across,
        corner,
    )
    gn_kept, gn_sent = call(
        back_project_kernel,
        "back_project",
        [shape((2 * pixels, depth), F32)] * 2,
        [],
        0.7,
        weight,
        grad_pre,
    )
    pieces = relative_order(pieces)
    arrived = [over_shard(piece, flip) for flip, piece in enumerate(pieces) if flip]
    *small, grad_conv, grad_sent = call(
        functools.partial(norm_back_kernel, relative, own, height, breadth),
        "norm_back",
        [shape((folded, LANES), F32)]
        + [shape((folded, LANES), BF16)] * (INNER - 1)
        + [
            shape((tiles, height, breadth, LANES), F32),
            shape((tiles, height, breadth, LANES), BF16),
        ],
        [
            pltpu.VMEM((2, tiles, height, breadth + 16, LANES), F32),
            pltpu.VMEM((2, tiles, height, breadth, LANES), F32),
            pltpu.VMEM((tiles, LANES, LANES), F32),
            pltpu.VMEM((depth, LANES), F32),
            pltpu.VMEM((INNER, rows, LANES), F32),
        ],
        0.1,
        gn_kept,
        over_core(gn_sent),
        whitened,
        inv_std,
        taps,
        image,
        across,
    )
    small = relative_order(small)
    small_arrived = [crossing(piece, flip) for flip, piece in enumerate(small) if flip]
    grad_other = crossing(grad_sent, INNER)
    (grad_images,) = call(
        conv_back_kernel,
        "conv_back",
        [shape(images.shape, BF16)],
        [padded],
        0.1,
        grad_conv,
        grad_other,
        taps,
    )

    home, *sent = call(
        functools.partial(plane_sum_kernel, lines),
        "plane_sum",
        [shape(mixed_shape(own, quarter), F32)]
        + [shape(mixed_shape(own, quarter), BF16)] * (lines - 1),
        [],
        2.0,
        pieces[0],
        *arrived,
        small[0],
        *small_arrived,
    )
    home, grad_images = lax.optimization_barrier((home, grad_images))
    came = [crossing(piece, INNER * line) for line, piece in enumerate(sent, 1)]
    (total,) = call(
        functools.partial(line_sum_kernel, own),
        "line_sum",
        [shape((own, 3 * quarter + LANES), F32)],
        [],
        0.3,
        home,
        *came,
    )
    if reps > 2:
        groups = [[i for i in range(reps) if i % 2 == s] for s in range(2)]
        total = lax.psum(total, "rep", axis_index_groups=groups)
    other = over_core(total)
    factor = 1.0 / math.sqrt(images.shape[0] * pixels * shards * reps)
    grad_up, grad_depthwise, grad_gain, grad_bias = call(
        functools.partial(finish_kernel, factor),
        "finish",
        [
            shape((own, hidden), F32),
            shape((own, TAPS), F32),
            shape((1, own), F32),
            shape((1, own), F32),
        ],
        [],
        0.5,
        total,
        other,
    )
    return (grad_images, grad_up, grad_depthwise, grad_gain[0], grad_bias[0])


def solution(mesh):
    placed = (
        P(("shard", "rep"), None, None, None),
        P(("shard", "rep"), None, None, None),
        P("shard", None),
        P("shard"),
        P("shard"),
        P("shard", None),
    )
    return jax.shard_map(
        body,
        mesh=mesh,
        in_specs=placed,
        out_specs=(
            P(("shard", "rep"), None, None, None),
            P("shard", None),
            P("shard", None),
            P("shard"),
            P("shard"),
        ),
        check_vma=False,
    )
```

```python
import functools
import math

import jax
import jax.numpy as jnp
from jax import lax
from jax.experimental import pallas as pl
from jax.experimental.pallas import tpu as pltpu
from jax.sharding import PartitionSpec as P

KS = 7
TAPS = KS * KS
MARGIN = KS // 2
LANES = 128
INNER = 4
NORM_EPS = 1e-06
BF16 = jnp.bfloat16
F32 = jnp.float32
VMEM = pl.BlockSpec(memory_space=pltpu.VMEM)


def params(mebibytes):
    return pltpu.CompilerParams(vmem_limit_bytes=mebibytes * 1024 * 1024)


def gelu_slope(inputs):
    cumulative = 0.5 * (1.0 + lax.erf(inputs * 0.7071067811865476))
    return cumulative + inputs * jnp.exp(-0.5 * inputs * inputs) * 0.3989422804014327


def block_rows(relative, group, line, own, lines):
    if relative:
        place = lax.axis_index("shard") ^ (line * INNER + group)
        return pl.multiple_of(place * own, 16)
    return (group * lines + line) * own


def place_rows(pieces, target, own, relative, cast=None):
    for group, piece in enumerate(pieces):
        lines = piece.shape[0] // own
        if not relative:
            target[group * piece.shape[0] : (group + 1) * piece.shape[0], :] = (
                piece[...] if cast is None else piece[...].astype(cast)
            )
            continue
        for line in range(lines):
            rows = piece[line * own : (line + 1) * own, :]
            start = block_rows(True, group, line, own, lines)
            target[pl.ds(start, own), :] = rows if cast is None else rows.astype(cast)


def split_rows(source, pieces, own, relative):
    for group, piece in enumerate(pieces):
        lines = piece.shape[0] // own
        if not relative:
            piece[...] = source[group * piece.shape[0] : (group + 1) * piece.shape[0], :].astype(
                piece.dtype
            )
            continue
        for line in range(lines):
            start = block_rows(True, group, line, own, lines)
            piece[line * own : (line + 1) * own, :] = source[pl.ds(start, own), :].astype(
                piece.dtype
            )


def correlate(padded, tile, tap_row, height, breadth):
    sums = [None] * height
    for across in range(KS):
        shifted = padded[tile, :, 8 - MARGIN + across : 8 - MARGIN + across + breadth, :]
        for down in range(KS):
            row = tap_row(down, across)
            for line in range(height):
                origin = line + down - MARGIN
                if 0 <= origin < height:
                    term = shifted[origin] * row
                    sums[line] = term if sums[line] is None else sums[line] + term
    return sums


def tight(own, quarter):
    return own % (16 * (quarter // LANES)) == 0


def with_small(weights, extras):
    own, quarter = weights.shape
    if not tight(own, quarter):
        return jnp.concatenate([weights, extras], axis=1)
    folded = fold(extras)
    count = folded.shape[0] * LANES // quarter
    parts = [folded[at : at + count] for at in range(0, folded.shape[0], count)]
    return jnp.concatenate([weights, jnp.concatenate(parts, axis=1)], axis=0)


def without_small(mixed, own, quarter):
    if not tight(own, quarter):
        return mixed[:, :quarter], mixed[:, quarter:]
    parts = [mixed[own:, at : at + LANES] for at in range(0, quarter, LANES)]
    return mixed[:own], unfold(jnp.concatenate(parts, axis=0))


def mixed_shape(own, quarter):
    if not tight(own, quarter):
        return (own, quarter + LANES)
    return (own + own // 2 * LANES // quarter, quarter)


def pack_kernel(w_ref, dw_ref, gain_ref, bias_ref, home_ref, near_ref, far_ref, turned, wide):
    own, hidden = w_ref.shape
    quarter = hidden // 4
    side = lax.axis_index("rep") % 2
    parity = (lax.axis_index("shard") // INNER) % 2
    turned[...] = jnp.zeros_like(turned)
    turned[TAPS : TAPS + 1, :own] = gain_ref[...].astype(F32)
    turned[TAPS + 1 : TAPS + 2, :own] = bias_ref[...].astype(F32)
    wide[...] = jnp.zeros_like(wide)
    wide[:, :TAPS] = dw_ref[...].astype(F32)
    extras = wide[...] + turned[...].T[:own]
    kinds = ((home_ref, side, parity), (near_ref, 1 - side, parity), (far_ref, 1 - side, 1 - parity))
    for ref, place, which in kinds:
        start = pl.multiple_of(place * (2 * quarter) + which * quarter, LANES)
        weights = w_ref[:, pl.ds(start, quarter)].astype(F32)
        ref[...] = with_small(weights, extras).astype(BF16)


def assemble_kernel(own, *refs):
    pieces, (weight_ref, extra_ref) = refs[:-2], refs[-2:]
    quarter = weight_ref.shape[1]
    parts = [without_small(piece[...].astype(F32), own, quarter) for piece in pieces]
    for line, (weights, _) in enumerate(parts):
        weight_ref[line * own : (line + 1) * own, :] = weights.astype(BF16)
    extras = jnp.concatenate([extra for _, extra in parts], axis=0)
    if extra_ref.shape[0] < extras.shape[0]:
        extras = fold(extras)
    extra_ref[...] = extras.astype(BF16)


def plane_sum_kernel(lines, *refs):
    pieces, small, outs = refs[:INNER], refs[INNER : 2 * INNER], refs[2 * INNER :]
    own = pieces[0].shape[0] // lines
    quarter = pieces[0].shape[1]
    extras = small[0][...]
    for part in small[1:]:
        extras = extras + part[...].astype(F32)
    if extras.shape[0] < pieces[0].shape[0]:
        extras = unfold(extras)
    for line, out in enumerate(outs):
        rows = slice(line * own, (line + 1) * own)
        total = pieces[0][rows, :]
        for part in pieces[1:]:
            total = total + part[rows, :].astype(F32)
        out[...] = with_small(total, extras[rows, :]).astype(out.dtype)


def line_sum_kernel(own, *refs):
    pieces, total_ref = refs[:-1], refs[-1]
    quarter = (total_ref.shape[1] - LANES) // 3
    near, far = None, None
    for line, piece in enumerate(pieces[1:], 1):
        came = piece[...].astype(F32)
        if line % 2:
            far = came if far is None else far + came
        else:
            near = came if near is None else near + came
    home, extras = without_small(pieces[0][...], own, quarter)
    total_ref[:, :quarter] = home
    for place, part in ((1, near), (2, far)):
        weights, more = without_small(part, own, quarter)
        total_ref[:, place * quarter : (place + 1) * quarter] = weights
        extras = extras + more
    total_ref[:, 3 * quarter :] = extras


def finish_kernel(factor, mine_ref, other_ref, up_ref, dw_ref, gain_ref, bias_ref):
    own, quarter = mine_ref.shape[0], (mine_ref.shape[1] - LANES) // 3
    side = lax.axis_index("rep") % 2
    parity = (lax.axis_index("shard") // INNER) % 2
    for place, home, came in ((side, mine_ref, other_ref), (1 - side, other_ref, mine_ref)):
        start = pl.multiple_of((2 * place + parity) * quarter, LANES)
        total = home[:, :quarter] + came[:, quarter : 2 * quarter]
        up_ref[:, pl.ds(start, quarter)] = total * factor
        start = pl.multiple_of((2 * place + 1 - parity) * quarter, LANES)
        up_ref[:, pl.ds(start, quarter)] = came[:, 2 * quarter : 3 * quarter] * factor
    low = 3 * quarter
    sums = (mine_ref[:, low:] + other_ref[:, low:]) * factor
    dw_ref[...] = sums[:, :TAPS]
    turned = sums.T
    gain_ref[...] = turned[TAPS : TAPS + 1, :]
    bias_ref[...] = turned[TAPS + 1 : TAPS + 2, :]


def fold(rows):
    half = rows.shape[0] // 2
    low = lax.broadcasted_iota(jnp.int32, (half, LANES), 1) < LANES // 2
    return jnp.where(low, rows[:half], pltpu.roll(rows[half:], LANES // 2, 1))


def unfold(rows):
    return jnp.concatenate([rows, pltpu.roll(rows, LANES // 2, 1)], axis=0)


def clear_borders(padded, breadth):
    shape = padded.shape[:-2] + (8, LANES)
    padded[..., :8, :] = jnp.zeros(shape, F32)
    padded[..., 8 + breadth :, :] = jnp.zeros(shape, F32)


def conv_norm_image(source, taps_ref, outs, padded, conv, height, breadth):
    normed_ref, white_ref, inv_ref = outs
    pixels, depth = normed_ref.shape
    tiles = depth // LANES
    clear_borders(padded, breadth)
    for tile in range(tiles):
        lanes = slice(tile * LANES, (tile + 1) * LANES)
        part = source[:pixels, lanes].astype(F32)
        padded[tile, :, 8 : 8 + breadth, :] = part.reshape(height, breadth, LANES)

    def one_tile(tile, carry):
        sums = correlate(
            padded,
            tile,
            lambda down, across: taps_ref[tile, pl.ds(down * KS + across, 1), :],
            height,
            breadth,
        )
        for line in range(height):
            conv[tile, line * breadth : (line + 1) * breadth, :] = sums[line]
        return carry

    lax.fori_loop(0, tiles, one_tile, 0)
    total = conv[0]
    for tile in range(1, tiles):
        total = total + conv[tile]
    average = jnp.sum(total, axis=-1, keepdims=True) / depth
    squares = None
    for tile in range(tiles):
        centered = conv[tile] - average
        squares = centered * centered if squares is None else squares + centered * centered
    variance = jnp.sum(squares, axis=-1, keepdims=True) / depth
    inv_std = lax.rsqrt(variance + NORM_EPS)
    inv_ref[...] = jnp.broadcast_to(inv_std, (pixels, LANES))
    for tile in range(tiles):
        lanes = slice(tile * LANES, (tile + 1) * LANES)
        whitened = (conv[tile] - average) * inv_std
        white_ref[:, lanes] = whitened
        gain = taps_ref[tile, TAPS : TAPS + 1, :]
        bias = taps_ref[tile, TAPS + 1 : TAPS + 2, :]
        normed_ref[:, lanes] = (whitened * gain + bias).astype(BF16)


def conv_norm_kernel(relative, own, height, breadth, *refs):
    small, x_ref = refs[:INNER], refs[INNER]
    *outs, taps_ref, gathered, unfolded, padded, conv = refs[INNER + 1 :]
    if relative:
        for group, piece in enumerate(small):
            unfolded[group * 2 * piece.shape[0] : (group + 1) * 2 * piece.shape[0], :] = unfold(
                piece[...].astype(F32)
            )
        count = unfolded.shape[0] // INNER
        small = [unfolded.at[pl.ds(group * count, count), :] for group in range(INNER)]
    place_rows(small, gathered, own, relative, F32)
    for tile in range(taps_ref.shape[0]):
        taps_ref[tile] = gathered[tile * LANES : (tile + 1) * LANES, :].T
    conv_norm_image(x_ref, taps_ref, outs, padded, conv, height, breadth)


def far_norm_kernel(height, breadth, taps_ref, far_ref, *refs):
    *outs, corner_ref, padded, conv = refs
    pixels, quarter = corner_ref.shape
    start = pl.multiple_of((1 - lax.axis_index("rep") % 2) * quarter, LANES)
    corner_ref[...] = far_ref[pixels:, pl.ds(start, quarter)]
    conv_norm_image(far_ref, taps_ref, outs, padded, conv, height, breadth)


def cot_pack_kernel(image_ref, cot_ref, across_ref, sibling_ref):
    pixels, half = sibling_ref.shape
    quarter = half // 2
    side = lax.axis_index("rep") % 2
    parity = (lax.axis_index("shard") // INNER) % 2
    for place in range(2):
        start = pl.multiple_of(place * half + (1 - parity) * quarter, LANES)
        lanes = slice(place * quarter, (place + 1) * quarter)
        across_ref[pixels:, lanes] = cot_ref[:, pl.ds(start, quarter)]
    across_ref[:pixels, :] = image_ref[...]
    sibling_ref[...] = cot_ref[:, pl.ds(pl.multiple_of((1 - side) * half, LANES), half)]


def join_kernel(own_ref, came_ref, out_ref):
    rows = own_ref.shape[0]
    out_ref[:rows, :] = own_ref[...]
    out_ref[rows:, :] = came_ref[...]


def order_kernel(relative, own, *refs):
    if not relative:
        place_rows(refs[:INNER], refs[INNER], own, relative)
        return
    home, first, second, out_ref = refs
    side = lax.axis_index("rep") % 2
    lines = home.shape[0] // own
    for line in range(lines):
        rows = slice(line * own, (line + 1) * own)
        below = slice((lines + line) * own, (lines + line + 1) * own)
        for ref, span, group in (
            (home, rows, 0),
            (first, rows, 1 + side),
            (second, rows, 2 - side),
            (second, below, INNER - 1),
        ):
            start = block_rows(True, group, line, own, lines)
            out_ref[pl.ds(start, own), :] = ref[span, :]


def project_kernel(relative, own, *refs):
    weight, *parts = refs[:5]
    cot_ref, sibling_ref, across_ref, corner_ref = refs[5:9]
    pieces = refs[9 : 9 + INNER]
    gp_ref, normed, cot, grad = refs[9 + INNER :]
    pixels, half = sibling_ref.shape
    quarter = half // 2
    side = lax.axis_index("rep") % 2
    parity = (lax.axis_index("shard") // INNER) % 2
    for place, part in enumerate(parts):
        normed[place * pixels : (place + 1) * pixels, :] = part[...]
    start = pl.multiple_of(side * half + parity * quarter, LANES)
    cot[:pixels, :] = cot_ref[:, pl.ds(start, quarter)]
    start = pl.multiple_of(side * quarter, LANES)
    cot[pixels : 2 * pixels, :] = across_ref[pixels:, pl.ds(start, quarter)]
    start = pl.multiple_of(parity * quarter, LANES)
    cot[2 * pixels : 3 * pixels, :] = sibling_ref[:, pl.ds(start, quarter)]
    cot[3 * pixels :, :] = corner_ref[...]
    for start in range(0, quarter, LANES):
        columns = slice(start, start + LANES)
        pre_act = jnp.dot(normed[...], weight[:, columns], preferred_element_type=F32)
        gp_ref[:, columns] = (cot[:, columns].astype(F32) * gelu_slope(pre_act)).astype(BF16)
    grad[...] = lax.dot_general(
        normed[...], gp_ref[...], (((0,), (0,)), ((), ())), preferred_element_type=F32
    )
    split_rows(grad, pieces, own, relative)


def back_project_kernel(weight, gp_ref, own_ref, other_ref):
    rows = own_ref.shape[0]
    grad_normed = lax.dot_general(
        gp_ref[...], weight[...], (((1,), (1,)), ((), ())), preferred_element_type=F32
    )
    own_ref[...] = grad_normed[:rows]
    other_ref[...] = grad_normed[rows:]


def norm_back_kernel(relative, own, height, breadth, *refs):
    gn_own, gn_other, *norms = refs[:6]
    taps_ref, x_ref, far_ref = refs[6:9]
    pieces = refs[9 : 9 + INNER]
    grad_ref, sent_ref, padded, grads_ref, rows, small, unfolded = refs[9 + INNER :]
    pixels, depth = x_ref.shape
    tiles = depth // LANES
    clear_borders(padded, breadth)
    rows[...] = jnp.zeros_like(rows)
    for image, source in enumerate((x_ref, far_ref)):
        span = slice(image * pixels, (image + 1) * pixels)
        white_ref, inv_ref = norms[2 * image : 2 * image + 2]
        first = None
        second = None
        for tile in range(tiles):
            lanes = slice(tile * LANES, (tile + 1) * LANES)
            part = source[:pixels, lanes].astype(F32)
            padded[image, tile, :, 8 : 8 + breadth, :] = part.reshape(height, breadth, LANES)
            grad_normed = gn_own[span, lanes] + gn_other[span, lanes]
            whitened = white_ref[:, lanes]
            product = grad_normed * whitened
            gain = taps_ref[tile, TAPS : TAPS + 1, :]
            rows[tile, TAPS : TAPS + 1, :] += jnp.sum(product, axis=0, keepdims=True)
            rows[tile, TAPS + 1 : TAPS + 2, :] += jnp.sum(grad_normed, axis=0, keepdims=True)
            one, two = grad_normed * gain, product * gain
            first = one if first is None else first + one
            second = two if second is None else second + two
        mean_first = jnp.sum(first, axis=-1, keepdims=True) / depth
        mean_second = jnp.sum(second, axis=-1, keepdims=True) / depth
        for tile in range(tiles):
            lanes = slice(tile * LANES, (tile + 1) * LANES)
            gain = taps_ref[tile, TAPS : TAPS + 1, :]
            grad_white = (gn_own[span, lanes] + gn_other[span, lanes]) * gain
            grad_conv = inv_ref[...] * (
                grad_white - mean_first - white_ref[:, lanes] * mean_second
            )
            grad_conv = grad_conv.reshape(height, breadth, LANES)
            grads_ref[image, tile] = grad_conv
            if image == 0:
                grad_ref[tile] = grad_conv
            else:
                sent_ref[tile] = grad_conv.astype(BF16)

    def one_tile(tile, carry):
        grads = [[grads_ref[image, tile, line] for line in range(height)] for image in range(2)]
        for across in range(KS):
            columns = slice(8 - MARGIN + across, 8 - MARGIN + across + breadth)
            shifted = [padded[image, tile, :, columns, :] for image in range(2)]
            for down in range(KS):
                total = None
                for image in range(2):
                    for line in range(height):
                        origin = line + down - MARGIN
                        if 0 <= origin < height:
                            term = grads[image][line] * shifted[image][origin]
                            total = term if total is None else total + term
                rows[tile, pl.ds(down * KS + across, 1), :] = jnp.sum(total, axis=0, keepdims=True)
        return carry

    lax.fori_loop(0, tiles, one_tile, 0)
    for tile in range(tiles):
        small[tile * LANES : (tile + 1) * LANES, :] = rows[tile].T
    if relative:
        whole = [unfolded.at[group] for group in range(INNER)]
        split_rows(small, whole, own, relative)
        for source, piece in zip(whole, pieces):
            piece[...] = fold(source[...]).astype(piece.dtype)
    else:
        split_rows(small, pieces, own, relative)


def conv_back_kernel(grad_ref, other_ref, taps_ref, out_ref, padded):
    tiles, height, breadth, _ = grad_ref.shape
    clear_borders(padded, breadth)
    padded[:, :, 8 : 8 + breadth, :] = grad_ref[...] + other_ref[...].astype(F32)

    def one_tile(tile, carry):
        sums = correlate(
            padded,
            tile,
            lambda down, across: taps_ref[tile, pl.ds(TAPS - 1 - down * KS - across, 1), :],
            height,
            breadth,
        )
        start = pl.multiple_of(tile * LANES, LANES)
        for line in range(height):
            out_ref[0, line, :, pl.ds(start, LANES)] = sums[line].astype(BF16)
        return carry

    lax.fori_loop(0, tiles, one_tile, 0)


def call(kernel, name, outs, scratch, micros, *args, mebibytes=48):
    flops = int(micros * 1.1e9)
    moved = sum(math.prod(a.shape) * a.dtype.itemsize for a in args)
    moved += sum(math.prod(o.shape) * o.dtype.itemsize for o in outs)
    return pl.pallas_call(
        kernel,
        out_shape=outs,
        in_specs=[VMEM] * len(args),
        out_specs=[VMEM] * len(outs),
        scratch_shapes=scratch,
        compiler_params=params(mebibytes),
        cost_estimate=pl.CostEstimate(flops=flops, bytes_accessed=moved, transcendentals=0),
        name=name,
    )(*args)


def body(images, cotangent, depthwise_weight, norm_gain, norm_bias, up_weight):
    shards, reps = lax.axis_size("shard"), lax.axis_size("rep")
    own, hidden = up_weight.shape
    depth = own * shards
    lines = shards // INNER
    half, quarter = hidden // 2, hidden // 4
    height, breadth = images.shape[1:3]
    pixels = height * breadth
    tiles = depth // LANES
    me = lax.axis_index("shard")
    side = lax.axis_index("rep") % 2
    parity = (me // INNER) % 2
    relative = own % 16 == 0

    def over_shard(array, flip):
        return lax.ppermute(array, "shard", [(i, i ^ flip) for i in range(shards)])

    def crossing(array, flip):
        pairs = [
            (i * reps + r, (i ^ flip) * reps + (r ^ 1)) for i in range(shards) for r in range(reps)
        ]
        return lax.ppermute(array, ("shard", "rep"), pairs)

    def hop(array, place):
        flips = [(1, 2), (2, 1)]
        pairs = [
            (i * reps + r, (i ^ flips[r % 2][place]) * reps + r)
            for i in range(shards)
            for r in range(reps)
        ]
        return lax.ppermute(array, ("shard", "rep"), pairs)

    def over_core(array):
        return lax.ppermute(array, "rep", [(i, i ^ 1) for i in range(reps)])

    def true_order(pieces):
        if relative:
            return pieces
        stacked = jnp.stack(pieces).reshape(shards, own, -1)
        flips = jnp.arange(shards) ^ me
        places = (flips % INNER) * lines + flips // INNER
        return list(jnp.take(stacked, places, axis=0).reshape(INNER, lines * own, -1))

    def relative_order(pieces):
        if relative:
            return pieces
        stacked = jnp.concatenate([p.astype(F32) for p in pieces]).reshape(shards, own, -1)
        flips = (jnp.arange(lines)[None, :] * INNER + jnp.arange(INNER)[:, None]).reshape(-1)
        moved = jnp.take(stacked, flips ^ me, axis=0).reshape(INNER, lines * own, -1)
        return [moved[0]] + [moved[i].astype(BF16) for i in range(1, INNER)]

    shape = jax.ShapeDtypeStruct
    home, near, far = call(
        pack_kernel,
        "pack",
        [shape(mixed_shape(own, quarter), BF16)] * 3,
        [
            pltpu.VMEM((LANES, LANES), F32),
            pltpu.VMEM((own, LANES), F32),
        ],
        0.5,
        up_weight,
        depthwise_weight,
        norm_gain[None, :],
        norm_bias[None, :],
        mebibytes=63,
    )
    image, cotangent = images.reshape(pixels, depth), cotangent.reshape(pixels, hidden)
    home, near, far, image, cotangent = lax.optimization_barrier(
        (home, near, far, image, cotangent)
    )
    gathered = [home] + [
        crossing(far if line % 2 else near, INNER * line) for line in range(1, lines)
    ]
    across, cot_sibling = call(
        cot_pack_kernel,
        "cot_pack",
        [shape((2 * pixels, half), BF16), shape((pixels, half), BF16)],
        [],
        0.4,
        image,
        cotangent,
    )
    across, cot_sibling = crossing(across, INNER), over_core(cot_sibling)

    rows = lines * own
    folded = rows // 2 if relative else rows
    weight_lines, extra_lines = call(
        functools.partial(assemble_kernel, own),
        "assemble",
        [shape((rows, quarter), BF16), shape((folded, LANES), BF16)],
        [],
        4.0,
        *gathered,
    )
    weight_lines, cot_sibling = lax.optimization_barrier((weight_lines, cot_sibling))
    first_lines = hop(weight_lines, 0)
    (joined,) = call(
        join_kernel,
        "join",
        [shape((2 * rows, quarter), BF16)],
        [],
        0.3,
        weight_lines,
        first_lines,
    )
    second_lines = hop(joined, 1)
    weights = [weight_lines, first_lines, second_lines]
    extras = [extra_lines] + [crossing(extra_lines, flip) for flip in range(1, INNER)]
    if not relative:
        extras = true_order(extras)
        x_lines = jnp.where(side == 0, first_lines, second_lines[:rows])
        y_lines = jnp.where(side == 0, second_lines[:rows], first_lines)
        weights = true_order([weight_lines, x_lines, y_lines, second_lines[rows:]])
    (weight,) = call(
        functools.partial(order_kernel, relative, own),
        "order",
        [shape((depth, quarter), BF16)],
        [],
        0.3,
        *weights,
    )

    padded = pltpu.VMEM((tiles, height, breadth + 16, LANES), F32)
    norm_shapes = [
        shape((pixels, depth), BF16),
        shape((pixels, depth), F32),
        shape((pixels, LANES), F32),
    ]
    conv = pltpu.VMEM((tiles, pixels, LANES), F32)
    normed, whitened, inv_std, taps = call(
        functools.partial(conv_norm_kernel, relative, own, height, breadth),
        "conv_norm",
        norm_shapes + [shape((tiles, LANES, LANES), F32)],
        [pltpu.VMEM((depth, LANES), F32), pltpu.VMEM((depth, LANES), F32), padded, conv],
        0.1,
        *extras,
        image,
    )
    normed_sibling = over_core(normed)
    far_normed, far_whitened, far_inv_std, corner = call(
        functools.partial(far_norm_kernel, height, breadth),
        "far_norm",
        norm_shapes + [shape((pixels, quarter), BF16)],
        [padded, conv],
        1.0,
        taps,
        across,
    )
    corner_normed, corner = over_core(far_normed), over_core(corner)

    *pieces, grad_pre = call(
        functools.partial(project_kernel, relative, own),
        "project",
        [shape((rows, quarter), F32)]
        + [shape((rows, quarter), BF16)] * (INNER - 1)
        + [shape((4 * pixels, quarter), BF16)],
        [
            pltpu.VMEM((4 * pixels, depth), BF16),
            pltpu.VMEM((4 * pixels, quarter), BF16),
            pltpu.VMEM((depth, quarter), F32),
        ],
        1.6,
        weight,
        normed,
        far_normed,
        normed_sibling,
        corner_normed,
        cotangent,
        cot_sibling,
        across,
        corner,
    )
    gn_kept, gn_sent = call(
        back_project_kernel,
        "back_project",
        [shape((2 * pixels, depth), F32)] * 2,
        [],
        0.7,
        weight,
        grad_pre,
    )
    pieces = relative_order(pieces)
    arrived = [over_shard(piece, flip) for flip, piece in enumerate(pieces) if flip]
    *small, grad_conv, grad_sent = call(
        functools.partial(norm_back_kernel, relative, own, height, breadth),
        "norm_back",
        [shape((folded, LANES), F32)]
        + [shape((folded, LANES), BF16)] * (INNER - 1)
        + [
            shape((tiles, height, breadth, LANES), F32),
            shape((tiles, height, breadth, LANES), BF16),
        ],
        [
            pltpu.VMEM((2, tiles, height, breadth + 16, LANES), F32),
            pltpu.VMEM((2, tiles, height, breadth, LANES), F32),
            pltpu.VMEM((tiles, LANES, LANES), F32),
            pltpu.VMEM((depth, LANES), F32),
            pltpu.VMEM((INNER, rows, LANES), F32),
        ],
        0.1,
        gn_kept,
        over_core(gn_sent),
        whitened,
        inv_std,
        far_whitened,
        far_inv_std,
        taps,
        image,
        across,
    )
    small = relative_order(small)
    small_arrived = [crossing(piece, flip) for flip, piece in enumerate(small) if flip]
    grad_other = crossing(grad_sent, INNER)
    (grad_images,) = call(
        conv_back_kernel,
        "conv_back",
        [shape(images.shape, BF16)],
        [padded],
        0.1,
        grad_conv,
        grad_other,
        taps,
    )

    home, *sent = call(
        functools.partial(plane_sum_kernel, lines),
        "plane_sum",
        [shape(mixed_shape(own, quarter), F32)]
        + [shape(mixed_shape(own, quarter), BF16)] * (lines - 1),
        [],
        2.0,
        pieces[0],
        *arrived,
        small[0],
        *small_arrived,
    )
    home, grad_images = lax.optimization_barrier((home, grad_images))
    came = [crossing(piece, INNER * line) for line, piece in enumerate(sent, 1)]
    (total,) = call(
        functools.partial(line_sum_kernel, own),
        "line_sum",
        [shape((own, 3 * quarter + LANES), F32)],
        [],
        0.3,
        home,
        *came,
    )
    if reps > 2:
        groups = [[i for i in range(reps) if i % 2 == s] for s in range(2)]
        total = lax.psum(total, "rep", axis_index_groups=groups)
    other = over_core(total)
    factor = 1.0 / math.sqrt(images.shape[0] * pixels * shards * reps)
    grad_up, grad_depthwise, grad_gain, grad_bias = call(
        functools.partial(finish_kernel, factor),
        "finish",
        [
            shape((own, hidden), F32),
            shape((own, TAPS), F32),
            shape((1, own), F32),
            shape((1, own), F32),
        ],
        [],
        0.5,
        total,
        other,
    )
    return (grad_images, grad_up, grad_depthwise, grad_gain[0], grad_bias[0])


def solution(mesh):
    placed = (
        P(("shard", "rep"), None, None, None),
        P(("shard", "rep"), None, None, None),
        P("shard", None),
        P("shard"),
        P("shard"),
        P("shard", None),
    )
    return jax.shard_map(
        body,
        mesh=mesh,
        in_specs=placed,
        out_specs=(
            P(("shard", "rep"), None, None, None),
            P("shard", None),
            P("shard", None),
            P("shard"),
            P("shard"),
        ),
        check_vma=False,
    )
```

```python
import functools
import math

import jax
import jax.numpy as jnp
from jax import lax
from jax.experimental import pallas as pl
from jax.experimental.pallas import tpu as pltpu
from jax.sharding import PartitionSpec as P

KS = 7
TAPS = KS * KS
MARGIN = KS // 2
LANES = 128
INNER = 4
NORM_EPS = 1e-06
BF16 = jnp.bfloat16
F32 = jnp.float32
VMEM = pl.BlockSpec(memory_space=pltpu.VMEM)


def params(mebibytes):
    return pltpu.CompilerParams(vmem_limit_bytes=mebibytes * 1024 * 1024)


def gelu_slope(inputs):
    cumulative = 0.5 * (1.0 + lax.erf(inputs * 0.7071067811865476))
    return cumulative + inputs * jnp.exp(-0.5 * inputs * inputs) * 0.3989422804014327


def block_rows(relative, group, line, own, lines):
    if relative:
        place = lax.axis_index("shard") ^ (line * INNER + group)
        return pl.multiple_of(place * own, 16)
    return (group * lines + line) * own


def place_rows(pieces, target, own, relative, cast=None):
    for group, piece in enumerate(pieces):
        lines = piece.shape[0] // own
        if not relative:
            target[group * piece.shape[0] : (group + 1) * piece.shape[0], :] = (
                piece[...] if cast is None else piece[...].astype(cast)
            )
            continue
        for line in range(lines):
            rows = piece[line * own : (line + 1) * own, :]
            start = block_rows(True, group, line, own, lines)
            target[pl.ds(start, own), :] = rows if cast is None else rows.astype(cast)


def split_rows(source, pieces, own, relative):
    for group, piece in enumerate(pieces):
        lines = piece.shape[0] // own
        if not relative:
            piece[...] = source[group * piece.shape[0] : (group + 1) * piece.shape[0], :].astype(
                piece.dtype
            )
            continue
        for line in range(lines):
            start = block_rows(True, group, line, own, lines)
            piece[line * own : (line + 1) * own, :] = source[pl.ds(start, own), :].astype(
                piece.dtype
            )


def correlate(padded, tile, tap_row, height, breadth):
    sums = [None] * height
    for across in range(KS):
        shifted = padded[tile, :, 8 - MARGIN + across : 8 - MARGIN + across + breadth, :]
        for down in range(KS):
            row = tap_row(down, across)
            for line in range(height):
                origin = line + down - MARGIN
                if 0 <= origin < height:
                    term = shifted[origin] * row
                    sums[line] = term if sums[line] is None else sums[line] + term
    return sums


def tight(own, quarter):
    return own % (16 * (quarter // LANES)) == 0


def with_small(weights, extras):
    own, quarter = weights.shape
    if not tight(own, quarter):
        return jnp.concatenate([weights, extras], axis=1)
    folded = fold(extras)
    count = folded.shape[0] * LANES // quarter
    parts = [folded[at : at + count] for at in range(0, folded.shape[0], count)]
    return jnp.concatenate([weights, jnp.concatenate(parts, axis=1)], axis=0)


def without_small(mixed, own, quarter):
    if not tight(own, quarter):
        return mixed[:, :quarter], mixed[:, quarter:]
    parts = [mixed[own:, at : at + LANES] for at in range(0, quarter, LANES)]
    return mixed[:own], unfold(jnp.concatenate(parts, axis=0))


def mixed_shape(own, quarter):
    if not tight(own, quarter):
        return (own, quarter + LANES)
    return (own + own // 2 * LANES // quarter, quarter)


def pack_kernel(w_ref, dw_ref, gain_ref, bias_ref, home_ref, near_ref, far_ref, turned, wide):
    own, hidden = w_ref.shape
    quarter = hidden // 4
    side = lax.axis_index("rep") % 2
    parity = (lax.axis_index("shard") // INNER) % 2
    turned[...] = jnp.zeros_like(turned)
    turned[TAPS : TAPS + 1, :own] = gain_ref[...].astype(F32)
    turned[TAPS + 1 : TAPS + 2, :own] = bias_ref[...].astype(F32)
    wide[...] = jnp.zeros_like(wide)
    wide[:, :TAPS] = dw_ref[...].astype(F32)
    extras = wide[...] + turned[...].T[:own]
    kinds = ((home_ref, side, parity), (near_ref, 1 - side, parity), (far_ref, 1 - side, 1 - parity))
    for ref, place, which in kinds:
        start = pl.multiple_of(place * (2 * quarter) + which * quarter, LANES)
        weights = w_ref[:, pl.ds(start, quarter)].astype(F32)
        ref[...] = with_small(weights, extras).astype(BF16)


def assemble_kernel(own, *refs):
    pieces, (weight_ref, extra_ref) = refs[:-2], refs[-2:]
    quarter = weight_ref.shape[1]
    parts = [without_small(piece[...].astype(F32), own, quarter) for piece in pieces]
    for line, (weights, _) in enumerate(parts):
        weight_ref[line * own : (line + 1) * own, :] = weights.astype(BF16)
    extras = jnp.concatenate([extra for _, extra in parts], axis=0)
    if extra_ref.shape[0] < extras.shape[0]:
        extras = fold(extras)
    extra_ref[...] = extras.astype(BF16)


def plane_sum_kernel(lines, *refs):
    pieces, small, outs = refs[:INNER], refs[INNER : 2 * INNER], refs[2 * INNER :]
    own = pieces[0].shape[0] // lines
    quarter = pieces[0].shape[1]
    extras = small[0][...]
    for part in small[1:]:
        extras = extras + part[...].astype(F32)
    if extras.shape[0] < pieces[0].shape[0]:
        extras = unfold(extras)
    for line, out in enumerate(outs):
        rows = slice(line * own, (line + 1) * own)
        total = pieces[0][rows, :]
        for part in pieces[1:]:
            total = total + part[rows, :].astype(F32)
        out[...] = with_small(total, extras[rows, :]).astype(out.dtype)


def line_sum_kernel(own, *refs):
    pieces, total_ref = refs[:-1], refs[-1]
    quarter = (total_ref.shape[1] - LANES) // 3
    near, far = None, None
    for line, piece in zip(range(len(pieces) - 1, 0, -1), pieces[1:]):
        came = piece[...].astype(F32)
        if line % 2:
            far = came if far is None else far + came
        else:
            near = came if near is None else near + came
    home, extras = without_small(pieces[0][...], own, quarter)
    total_ref[:, :quarter] = home
    for place, part in ((1, near), (2, far)):
        weights, more = without_small(part, own, quarter)
        total_ref[:, place * quarter : (place + 1) * quarter] = weights
        extras = extras + more
    total_ref[:, 3 * quarter :] = extras


def finish_kernel(factor, mine_ref, other_ref, up_ref, dw_ref, gain_ref, bias_ref):
    own, quarter = mine_ref.shape[0], (mine_ref.shape[1] - LANES) // 3
    side = lax.axis_index("rep") % 2
    parity = (lax.axis_index("shard") // INNER) % 2
    for place, home, came in ((side, mine_ref, other_ref), (1 - side, other_ref, mine_ref)):
        start = pl.multiple_of((2 * place + parity) * quarter, LANES)
        total = home[:, :quarter] + came[:, quarter : 2 * quarter]
        up_ref[:, pl.ds(start, quarter)] = total * factor
        start = pl.multiple_of((2 * place + 1 - parity) * quarter, LANES)
        up_ref[:, pl.ds(start, quarter)] = came[:, 2 * quarter : 3 * quarter] * factor
    low = 3 * quarter
    sums = (mine_ref[:, low:] + other_ref[:, low:]) * factor
    dw_ref[...] = sums[:, :TAPS]
    turned = sums.T
    gain_ref[...] = turned[TAPS : TAPS + 1, :]
    bias_ref[...] = turned[TAPS + 1 : TAPS + 2, :]


def fold(rows):
    half = rows.shape[0] // 2
    low = lax.broadcasted_iota(jnp.int32, (half, LANES), 1) < LANES // 2
    return jnp.where(low, rows[:half], pltpu.roll(rows[half:], LANES // 2, 1))


def unfold(rows):
    return jnp.concatenate([rows, pltpu.roll(rows, LANES // 2, 1)], axis=0)


def clear_borders(padded, breadth):
    shape = padded.shape[:-2] + (8, LANES)
    padded[..., :8, :] = jnp.zeros(shape, F32)
    padded[..., 8 + breadth :, :] = jnp.zeros(shape, F32)


def conv_norm_image(source, taps_ref, outs, padded, conv, height, breadth):
    normed_ref, white_ref, inv_ref = outs
    pixels, depth = normed_ref.shape
    tiles = depth // LANES
    clear_borders(padded, breadth)
    for tile in range(tiles):
        lanes = slice(tile * LANES, (tile + 1) * LANES)
        part = source[:pixels, lanes].astype(F32)
        padded[tile, :, 8 : 8 + breadth, :] = part.reshape(height, breadth, LANES)

    def one_tile(tile, carry):
        sums = correlate(
            padded,
            tile,
            lambda down, across: taps_ref[tile, pl.ds(down * KS + across, 1), :],
            height,
            breadth,
        )
        for line in range(height):
            conv[tile, line * breadth : (line + 1) * breadth, :] = sums[line]
        return carry

    lax.fori_loop(0, tiles, one_tile, 0)
    total = conv[0]
    for tile in range(1, tiles):
        total = total + conv[tile]
    average = jnp.sum(total, axis=-1, keepdims=True) / depth
    squares = None
    for tile in range(tiles):
        centered = conv[tile] - average
        squares = centered * centered if squares is None else squares + centered * centered
    variance = jnp.sum(squares, axis=-1, keepdims=True) / depth
    inv_std = lax.rsqrt(variance + NORM_EPS)
    inv_ref[...] = jnp.broadcast_to(inv_std, (pixels, LANES))
    for tile in range(tiles):
        lanes = slice(tile * LANES, (tile + 1) * LANES)
        whitened = (conv[tile] - average) * inv_std
        white_ref[:, lanes] = whitened
        gain = taps_ref[tile, TAPS : TAPS + 1, :]
        bias = taps_ref[tile, TAPS + 1 : TAPS + 2, :]
        normed_ref[:, lanes] = (whitened * gain + bias).astype(BF16)


def conv_norm_kernel(relative, own, height, breadth, *refs):
    small, x_ref = refs[:INNER], refs[INNER]
    *outs, taps_ref, gathered, unfolded, padded, conv = refs[INNER + 1 :]
    if relative:
        for group, piece in enumerate(small):
            unfolded[group * 2 * piece.shape[0] : (group + 1) * 2 * piece.shape[0], :] = unfold(
                piece[...].astype(F32)
            )
        count = unfolded.shape[0] // INNER
        small = [unfolded.at[pl.ds(group * count, count), :] for group in range(INNER)]
    place_rows(small, gathered, own, relative, F32)
    for tile in range(taps_ref.shape[0]):
        taps_ref[tile] = gathered[tile * LANES : (tile + 1) * LANES, :].T
    conv_norm_image(x_ref, taps_ref, outs, padded, conv, height, breadth)


def far_norm_kernel(height, breadth, taps_ref, far_ref, *refs):
    *outs, corner_ref, padded, conv = refs
    pixels, quarter = corner_ref.shape
    start = pl.multiple_of((1 - lax.axis_index("rep") % 2) * quarter, LANES)
    corner_ref[...] = far_ref[pixels:, pl.ds(start, quarter)]
    conv_norm_image(far_ref, taps_ref, outs, padded, conv, height, breadth)


def cot_pack_kernel(image_ref, cot_ref, across_ref, sibling_ref):
    pixels, half = sibling_ref.shape
    quarter = half // 2
    side = lax.axis_index("rep") % 2
    parity = (lax.axis_index("shard") // INNER) % 2
    for place in range(2):
        start = pl.multiple_of(place * half + (1 - parity) * quarter, LANES)
        lanes = slice(place * quarter, (place + 1) * quarter)
        across_ref[pixels:, lanes] = cot_ref[:, pl.ds(start, quarter)]
    across_ref[:pixels, :] = image_ref[...]
    sibling_ref[...] = cot_ref[:, pl.ds(pl.multiple_of((1 - side) * half, LANES), half)]


def join_kernel(own_ref, came_ref, out_ref):
    rows = own_ref.shape[0]
    out_ref[:rows, :] = own_ref[...]
    out_ref[rows:, :] = came_ref[...]


def order_kernel(relative, own, *refs):
    if not relative:
        place_rows(refs[:INNER], refs[INNER], own, relative)
        return
    home, first, second, out_ref = refs
    side = lax.axis_index("rep") % 2
    lines = home.shape[0] // own
    for line in range(lines):
        rows = slice(line * own, (line + 1) * own)
        below = slice((lines + line) * own, (lines + line + 1) * own)
        for ref, span, group in (
            (home, rows, 0),
            (first, rows, 1 + side),
            (second, rows, 2 - side),
            (second, below, INNER - 1),
        ):
            start = block_rows(True, group, line, own, lines)
            out_ref[pl.ds(start, own), :] = ref[span, :]


def project_kernel(relative, own, *refs):
    weight, *parts = refs[:5]
    cot_ref, sibling_ref, across_ref, corner_ref = refs[5:9]
    pieces = refs[9 : 9 + INNER]
    gp_ref, normed, cot, grad = refs[9 + INNER :]
    pixels, half = sibling_ref.shape
    quarter = half // 2
    side = lax.axis_index("rep") % 2
    parity = (lax.axis_index("shard") // INNER) % 2
    for place, part in enumerate(parts):
        normed[place * pixels : (place + 1) * pixels, :] = part[...]
    start = pl.multiple_of(side * half + parity * quarter, LANES)
    cot[:pixels, :] = cot_ref[:, pl.ds(start, quarter)]
    start = pl.multiple_of(side * quarter, LANES)
    cot[pixels : 2 * pixels, :] = across_ref[pixels:, pl.ds(start, quarter)]
    start = pl.multiple_of(parity * quarter, LANES)
    cot[2 * pixels : 3 * pixels, :] = sibling_ref[:, pl.ds(start, quarter)]
    cot[3 * pixels :, :] = corner_ref[...]
    for start in range(0, quarter, LANES):
        columns = slice(start, start + LANES)
        pre_act = jnp.dot(normed[...], weight[:, columns], preferred_element_type=F32)
        gp_ref[:, columns] = (cot[:, columns].astype(F32) * gelu_slope(pre_act)).astype(BF16)
    grad[...] = lax.dot_general(
        normed[...], gp_ref[...], (((0,), (0,)), ((), ())), preferred_element_type=F32
    )
    split_rows(grad, pieces, own, relative)


def back_project_kernel(weight, gp_ref, own_ref, other_ref):
    rows = own_ref.shape[0]
    grad_normed = lax.dot_general(
        gp_ref[...], weight[...], (((1,), (1,)), ((), ())), preferred_element_type=F32
    )
    own_ref[...] = grad_normed[:rows]
    other_ref[...] = grad_normed[rows:]


def norm_back_kernel(relative, own, height, breadth, *refs):
    gn_own, gn_other, *norms = refs[:6]
    taps_ref, x_ref, far_ref = refs[6:9]
    pieces = refs[9 : 9 + INNER]
    grad_ref, sent_ref, padded, grads_ref, rows, small, unfolded = refs[9 + INNER :]
    pixels, depth = x_ref.shape
    tiles = depth // LANES
    clear_borders(padded, breadth)
    rows[...] = jnp.zeros_like(rows)
    for image, source in enumerate((x_ref, far_ref)):
        span = slice(image * pixels, (image + 1) * pixels)
        white_ref, inv_ref = norms[2 * image : 2 * image + 2]
        first = None
        second = None
        for tile in range(tiles):
            lanes = slice(tile * LANES, (tile + 1) * LANES)
            part = source[:pixels, lanes].astype(F32)
            padded[image, tile, :, 8 : 8 + breadth, :] = part.reshape(height, breadth, LANES)
            grad_normed = gn_own[span, lanes] + gn_other[span, lanes]
            whitened = white_ref[:, lanes]
            product = grad_normed * whitened
            gain = taps_ref[tile, TAPS : TAPS + 1, :]
            rows[tile, TAPS : TAPS + 1, :] += jnp.sum(product, axis=0, keepdims=True)
            rows[tile, TAPS + 1 : TAPS + 2, :] += jnp.sum(grad_normed, axis=0, keepdims=True)
            one, two = grad_normed * gain, product * gain
            first = one if first is None else first + one
            second = two if second is None else second + two
        mean_first = jnp.sum(first, axis=-1, keepdims=True) / depth
        mean_second = jnp.sum(second, axis=-1, keepdims=True) / depth
        for tile in range(tiles):
            lanes = slice(tile * LANES, (tile + 1) * LANES)
            gain = taps_ref[tile, TAPS : TAPS + 1, :]
            grad_white = (gn_own[span, lanes] + gn_other[span, lanes]) * gain
            grad_conv = inv_ref[...] * (
                grad_white - mean_first - white_ref[:, lanes] * mean_second
            )
            grad_conv = grad_conv.reshape(height, breadth, LANES)
            grads_ref[image, tile] = grad_conv
            if image == 0:
                grad_ref[tile] = grad_conv
            else:
                sent_ref[tile] = grad_conv.astype(BF16)

    def one_tile(tile, carry):
        grads = [[grads_ref[image, tile, line] for line in range(height)] for image in range(2)]
        for across in range(KS):
            columns = slice(8 - MARGIN + across, 8 - MARGIN + across + breadth)
            shifted = [padded[image, tile, :, columns, :] for image in range(2)]
            for down in range(KS):
                total = None
                for image in range(2):
                    for line in range(height):
                        origin = line + down - MARGIN
                        if 0 <= origin < height:
                            term = grads[image][line] * shifted[image][origin]
                            total = term if total is None else total + term
                rows[tile, pl.ds(down * KS + across, 1), :] = jnp.sum(total, axis=0, keepdims=True)
        return carry

    lax.fori_loop(0, tiles, one_tile, 0)
    for tile in range(tiles):
        small[tile * LANES : (tile + 1) * LANES, :] = rows[tile].T
    if relative:
        whole = [unfolded.at[group] for group in range(INNER)]
        split_rows(small, whole, own, relative)
        for source, piece in zip(whole, pieces):
            piece[...] = fold(source[...]).astype(piece.dtype)
    else:
        split_rows(small, pieces, own, relative)


def conv_back_kernel(grad_ref, other_ref, taps_ref, out_ref, padded):
    tiles, height, breadth, _ = grad_ref.shape
    clear_borders(padded, breadth)
    padded[:, :, 8 : 8 + breadth, :] = grad_ref[...] + other_ref[...].astype(F32)

    def one_tile(tile, carry):
        sums = correlate(
            padded,
            tile,
            lambda down, across: taps_ref[tile, pl.ds(TAPS - 1 - down * KS - across, 1), :],
            height,
            breadth,
        )
        start = pl.multiple_of(tile * LANES, LANES)
        for line in range(height):
            out_ref[0, line, :, pl.ds(start, LANES)] = sums[line].astype(BF16)
        return carry

    lax.fori_loop(0, tiles, one_tile, 0)


def call(kernel, name, outs, scratch, micros, *args, mebibytes=48):
    flops = int(micros * 1.1e9)
    moved = sum(math.prod(a.shape) * a.dtype.itemsize for a in args)
    moved += sum(math.prod(o.shape) * o.dtype.itemsize for o in outs)
    return pl.pallas_call(
        kernel,
        out_shape=outs,
        in_specs=[VMEM] * len(args),
        out_specs=[VMEM] * len(outs),
        scratch_shapes=scratch,
        compiler_params=params(mebibytes),
        cost_estimate=pl.CostEstimate(flops=flops, bytes_accessed=moved, transcendentals=0),
        name=name,
    )(*args)


def body(images, cotangent, depthwise_weight, norm_gain, norm_bias, up_weight):
    shards, reps = lax.axis_size("shard"), lax.axis_size("rep")
    own, hidden = up_weight.shape
    depth = own * shards
    lines = shards // INNER
    half, quarter = hidden // 2, hidden // 4
    height, breadth = images.shape[1:3]
    pixels = height * breadth
    tiles = depth // LANES
    me = lax.axis_index("shard")
    side = lax.axis_index("rep") % 2
    parity = (me // INNER) % 2
    relative = own % 16 == 0

    def over_shard(array, flip):
        return lax.ppermute(array, "shard", [(i, i ^ flip) for i in range(shards)])

    def crossing(array, flip):
        pairs = [
            (i * reps + r, (i ^ flip) * reps + (r ^ 1)) for i in range(shards) for r in range(reps)
        ]
        return lax.ppermute(array, ("shard", "rep"), pairs)

    def hop(array, place):
        flips = [(1, 2), (2, 1)]
        pairs = [
            (i * reps + r, (i ^ flips[r % 2][place]) * reps + r)
            for i in range(shards)
            for r in range(reps)
        ]
        return lax.ppermute(array, ("shard", "rep"), pairs)

    def over_core(array):
        return lax.ppermute(array, "rep", [(i, i ^ 1) for i in range(reps)])

    def true_order(pieces):
        if relative:
            return pieces
        stacked = jnp.stack(pieces).reshape(shards, own, -1)
        flips = jnp.arange(shards) ^ me
        places = (flips % INNER) * lines + flips // INNER
        return list(jnp.take(stacked, places, axis=0).reshape(INNER, lines * own, -1))

    def relative_order(pieces):
        if relative:
            return pieces
        stacked = jnp.concatenate([p.astype(F32) for p in pieces]).reshape(shards, own, -1)
        flips = (jnp.arange(lines)[None, :] * INNER + jnp.arange(INNER)[:, None]).reshape(-1)
        moved = jnp.take(stacked, flips ^ me, axis=0).reshape(INNER, lines * own, -1)
        return [moved[0]] + [moved[i].astype(BF16) for i in range(1, INNER)]

    shape = jax.ShapeDtypeStruct
    home, near, far = call(
        pack_kernel,
        "pack",
        [shape(mixed_shape(own, quarter), BF16)] * 3,
        [
            pltpu.VMEM((LANES, LANES), F32),
            pltpu.VMEM((own, LANES), F32),
        ],
        0.5,
        up_weight,
        depthwise_weight,
        norm_gain[None, :],
        norm_bias[None, :],
        mebibytes=63,
    )
    image, cotangent = images.reshape(pixels, depth), cotangent.reshape(pixels, hidden)
    home, near, far, image, cotangent = lax.optimization_barrier(
        (home, near, far, image, cotangent)
    )
    gathered = [home] + [
        crossing(far if line % 2 else near, INNER * line) for line in range(1, lines)
    ]
    across, cot_sibling = call(
        cot_pack_kernel,
        "cot_pack",
        [shape((2 * pixels, half), BF16), shape((pixels, half), BF16)],
        [],
        0.4,
        image,
        cotangent,
    )
    across, cot_sibling = crossing(across, INNER), over_core(cot_sibling)

    rows = lines * own
    folded = rows // 2 if relative else rows
    weight_lines, extra_lines = call(
        functools.partial(assemble_kernel, own),
        "assemble",
        [shape((rows, quarter), BF16), shape((folded, LANES), BF16)],
        [],
        4.0,
        *gathered,
    )
    weight_lines, cot_sibling = lax.optimization_barrier((weight_lines, cot_sibling))
    first_lines = hop(weight_lines, 0)
    (joined,) = call(
        join_kernel,
        "join",
        [shape((2 * rows, quarter), BF16)],
        [],
        0.3,
        weight_lines,
        first_lines,
    )
    second_lines = hop(joined, 1)
    weights = [weight_lines, first_lines, second_lines]
    extras = [extra_lines] + [crossing(extra_lines, flip) for flip in range(1, INNER)]
    if not relative:
        extras = true_order(extras)
        x_lines = jnp.where(side == 0, first_lines, second_lines[:rows])
        y_lines = jnp.where(side == 0, second_lines[:rows], first_lines)
        weights = true_order([weight_lines, x_lines, y_lines, second_lines[rows:]])
    (weight,) = call(
        functools.partial(order_kernel, relative, own),
        "order",
        [shape((depth, quarter), BF16)],
        [],
        0.3,
        *weights,
    )

    padded = pltpu.VMEM((tiles, height, breadth + 16, LANES), F32)
    norm_shapes = [
        shape((pixels, depth), BF16),
        shape((pixels, depth), F32),
        shape((pixels, LANES), F32),
    ]
    conv = pltpu.VMEM((tiles, pixels, LANES), F32)
    normed, whitened, inv_std, taps = call(
        functools.partial(conv_norm_kernel, relative, own, height, breadth),
        "conv_norm",
        norm_shapes + [shape((tiles, LANES, LANES), F32)],
        [pltpu.VMEM((depth, LANES), F32), pltpu.VMEM((depth, LANES), F32), padded, conv],
        0.1,
        *extras,
        image,
    )
    normed_sibling = over_core(normed)
    far_normed, far_whitened, far_inv_std, corner = call(
        functools.partial(far_norm_kernel, height, breadth),
        "far_norm",
        norm_shapes + [shape((pixels, quarter), BF16)],
        [padded, conv],
        1.0,
        taps,
        across,
    )
    corner_normed, corner = over_core(far_normed), over_core(corner)

    *pieces, grad_pre = call(
        functools.partial(project_kernel, relative, own),
        "project",
        [shape((rows, quarter), F32)]
        + [shape((rows, quarter), BF16)] * (INNER - 1)
        + [shape((4 * pixels, quarter), BF16)],
        [
            pltpu.VMEM((4 * pixels, depth), BF16),
            pltpu.VMEM((4 * pixels, quarter), BF16),
            pltpu.VMEM((depth, quarter), F32),
        ],
        1.6,
        weight,
        normed,
        far_normed,
        normed_sibling,
        corner_normed,
        cotangent,
        cot_sibling,
        across,
        corner,
    )
    gn_kept, gn_sent = call(
        back_project_kernel,
        "back_project",
        [shape((2 * pixels, depth), F32)] * 2,
        [],
        0.7,
        weight,
        grad_pre,
    )
    pieces = relative_order(pieces)
    arrived = [over_shard(pieces[flip], flip) for flip in range(INNER - 1, 0, -1)]
    *small, grad_conv, grad_sent = call(
        functools.partial(norm_back_kernel, relative, own, height, breadth),
        "norm_back",
        [shape((folded, LANES), F32)]
        + [shape((folded, LANES), BF16)] * (INNER - 1)
        + [
            shape((tiles, height, breadth, LANES), F32),
            shape((tiles, height, breadth, LANES), BF16),
        ],
        [
            pltpu.VMEM((2, tiles, height, breadth + 16, LANES), F32),
            pltpu.VMEM((2, tiles, height, breadth, LANES), F32),
            pltpu.VMEM((tiles, LANES, LANES), F32),
            pltpu.VMEM((depth, LANES), F32),
            pltpu.VMEM((INNER, rows, LANES), F32),
        ],
        0.1,
        gn_kept,
        over_core(gn_sent),
        whitened,
        inv_std,
        far_whitened,
        far_inv_std,
        taps,
        image,
        across,
    )
    small = relative_order(small)
    small_arrived = [crossing(small[flip], flip) for flip in range(INNER - 1, 0, -1)]
    grad_other = crossing(grad_sent, INNER)
    (grad_images,) = call(
        conv_back_kernel,
        "conv_back",
        [shape(images.shape, BF16)],
        [padded],
        0.1,
        grad_conv,
        grad_other,
        taps,
    )

    home, *sent = call(
        functools.partial(plane_sum_kernel, lines),
        "plane_sum",
        [shape(mixed_shape(own, quarter), F32)]
        + [shape(mixed_shape(own, quarter), BF16)] * (lines - 1),
        [],
        2.0,
        pieces[0],
        *arrived,
        small[0],
        *small_arrived,
    )
    home, grad_images = lax.optimization_barrier((home, grad_images))
    came = [crossing(sent[line - 1], INNER * line) for line in range(lines - 1, 0, -1)]
    (total,) = call(
        functools.partial(line_sum_kernel, own),
        "line_sum",
        [shape((own, 3 * quarter + LANES), F32)],
        [],
        0.3,
        home,
        *came,
    )
    if reps > 2:
        groups = [[i for i in range(reps) if i % 2 == s] for s in range(2)]
        total = lax.psum(total, "rep", axis_index_groups=groups)
    other = over_core(total)
    factor = 1.0 / math.sqrt(images.shape[0] * pixels * shards * reps)
    grad_up, grad_depthwise, grad_gain, grad_bias = call(
        functools.partial(finish_kernel, factor),
        "finish",
        [
            shape((own, hidden), F32),
            shape((own, TAPS), F32),
            shape((1, own), F32),
            shape((1, own), F32),
        ],
        [],
        0.5,
        total,
        other,
    )
    return (grad_images, grad_up, grad_depthwise, grad_gain[0], grad_bias[0])


def solution(mesh):
    placed = (
        P(("shard", "rep"), None, None, None),
        P(("shard", "rep"), None, None, None),
        P("shard", None),
        P("shard"),
        P("shard"),
        P("shard", None),
    )
    return jax.shard_map(
        body,
        mesh=mesh,
        in_specs=placed,
        out_specs=(
            P(("shard", "rep"), None, None, None),
            P("shard", None),
            P("shard", None),
            P("shard"),
            P("shard"),
        ),
        check_vma=False,
    )
```

```python
import functools
import math

import jax
import jax.numpy as jnp
from jax import lax
from jax.experimental import pallas as pl
from jax.experimental.pallas import tpu as pltpu
from jax.sharding import PartitionSpec as P

KS = 7
TAPS = KS * KS
MARGIN = KS // 2
LANES = 128
INNER = 4
NORM_EPS = 1e-06
BF16 = jnp.bfloat16
F32 = jnp.float32
VMEM = pl.BlockSpec(memory_space=pltpu.VMEM)


def params(mebibytes):
    return pltpu.CompilerParams(vmem_limit_bytes=mebibytes * 1024 * 1024)


def gelu_slope(inputs):
    cumulative = 0.5 * (1.0 + lax.erf(inputs * 0.7071067811865476))
    return cumulative + inputs * jnp.exp(-0.5 * inputs * inputs) * 0.3989422804014327


def block_rows(relative, group, line, own, lines):
    if relative:
        place = lax.axis_index("shard") ^ (line * INNER + group)
        return pl.multiple_of(place * own, 16)
    return (group * lines + line) * own


def place_rows(pieces, target, own, relative, cast=None):
    for group, piece in enumerate(pieces):
        lines = piece.shape[0] // own
        if not relative:
            target[group * piece.shape[0] : (group + 1) * piece.shape[0], :] = (
                piece[...] if cast is None else piece[...].astype(cast)
            )
            continue
        for line in range(lines):
            rows = piece[line * own : (line + 1) * own, :]
            start = block_rows(True, group, line, own, lines)
            target[pl.ds(start, own), :] = rows if cast is None else rows.astype(cast)


def split_rows(source, pieces, own, relative):
    for group, piece in enumerate(pieces):
        lines = piece.shape[0] // own
        if not relative:
            piece[...] = source[group * piece.shape[0] : (group + 1) * piece.shape[0], :].astype(
                piece.dtype
            )
            continue
        for line in range(lines):
            start = block_rows(True, group, line, own, lines)
            piece[line * own : (line + 1) * own, :] = source[pl.ds(start, own), :].astype(
                piece.dtype
            )


def correlate(padded, tile, tap_row, height, breadth):
    sums = [None] * height
    for across in range(KS):
        shifted = padded[tile, :, 8 - MARGIN + across : 8 - MARGIN + across + breadth, :]
        for down in range(KS):
            row = tap_row(down, across)
            for line in range(height):
                origin = line + down - MARGIN
                if 0 <= origin < height:
                    term = shifted[origin] * row
                    sums[line] = term if sums[line] is None else sums[line] + term
    return sums


def tight(own, quarter):
    return own % (16 * (quarter // LANES)) == 0


def with_small(weights, extras):
    own, quarter = weights.shape
    if not tight(own, quarter):
        return jnp.concatenate([weights, extras], axis=1)
    folded = fold(extras)
    count = folded.shape[0] * LANES // quarter
    parts = [folded[at : at + count] for at in range(0, folded.shape[0], count)]
    return jnp.concatenate([weights, jnp.concatenate(parts, axis=1)], axis=0)


def without_small(mixed, own, quarter):
    if not tight(own, quarter):
        return mixed[:, :quarter], mixed[:, quarter:]
    parts = [mixed[own:, at : at + LANES] for at in range(0, quarter, LANES)]
    return mixed[:own], unfold(jnp.concatenate(parts, axis=0))


def mixed_shape(own, quarter):
    if not tight(own, quarter):
        return (own, quarter + LANES)
    return (own + own // 2 * LANES // quarter, quarter)


def pack_kernel(w_ref, dw_ref, gain_ref, bias_ref, home_ref, near_ref, far_ref, turned, wide):
    own, hidden = w_ref.shape
    quarter = hidden // 4
    side = lax.axis_index("rep") % 2
    parity = (lax.axis_index("shard") // INNER) % 2
    turned[...] = jnp.zeros_like(turned)
    turned[TAPS : TAPS + 1, :own] = gain_ref[...].astype(F32)
    turned[TAPS + 1 : TAPS + 2, :own] = bias_ref[...].astype(F32)
    wide[...] = jnp.zeros_like(wide)
    wide[:, :TAPS] = dw_ref[...].astype(F32)
    extras = wide[...] + turned[...].T[:own]
    kinds = ((home_ref, side, parity), (near_ref, 1 - side, parity), (far_ref, 1 - side, 1 - parity))
    for ref, place, which in kinds:
        start = pl.multiple_of(place * (2 * quarter) + which * quarter, LANES)
        weights = w_ref[:, pl.ds(start, quarter)].astype(F32)
        ref[...] = with_small(weights, extras).astype(BF16)


def assemble_kernel(own, *refs):
    pieces, (weight_ref, extra_ref) = refs[:-2], refs[-2:]
    quarter = weight_ref.shape[1]
    parts = [without_small(piece[...].astype(F32), own, quarter) for piece in pieces]
    for line, (weights, _) in enumerate(parts):
        weight_ref[line * own : (line + 1) * own, :] = weights.astype(BF16)
    extras = jnp.concatenate([extra for _, extra in parts], axis=0)
    if extra_ref.shape[0] < extras.shape[0]:
        extras = fold(extras)
    extra_ref[...] = extras.astype(BF16)


def plane_sum_kernel(lines, *refs):
    pieces, small, outs = refs[:INNER], refs[INNER : 2 * INNER], refs[2 * INNER :]
    own = pieces[0].shape[0] // lines
    quarter = pieces[0].shape[1]
    extras = small[0][...]
    for part in small[1:]:
        extras = extras + part[...].astype(F32)
    if extras.shape[0] < pieces[0].shape[0]:
        extras = unfold(extras)
    for line, out in enumerate(outs):
        rows = slice(line * own, (line + 1) * own)
        total = pieces[0][rows, :]
        for part in pieces[1:]:
            total = total + part[rows, :].astype(F32)
        out[...] = with_small(total, extras[rows, :]).astype(out.dtype)


def line_order(lines):
    return [*range(2, lines), 1]


def line_sum_kernel(own, *refs):
    pieces, total_ref = refs[:-1], refs[-1]
    quarter = (total_ref.shape[1] - LANES) // 3
    near, far = None, None
    for line, piece in zip(line_order(len(pieces)), pieces[1:]):
        came = piece[...].astype(F32)
        if line % 2:
            far = came if far is None else far + came
        else:
            near = came if near is None else near + came
    home, extras = without_small(pieces[0][...], own, quarter)
    total_ref[:, :quarter] = home
    for place, part in ((1, near), (2, far)):
        weights, more = without_small(part, own, quarter)
        total_ref[:, place * quarter : (place + 1) * quarter] = weights
        extras = extras + more
    total_ref[:, 3 * quarter :] = extras


def finish_kernel(factor, mine_ref, other_ref, up_ref, dw_ref, gain_ref, bias_ref):
    own, quarter = mine_ref.shape[0], (mine_ref.shape[1] - LANES) // 3
    side = lax.axis_index("rep") % 2
    parity = (lax.axis_index("shard") // INNER) % 2
    for place, home, came in ((side, mine_ref, other_ref), (1 - side, other_ref, mine_ref)):
        start = pl.multiple_of((2 * place + parity) * quarter, LANES)
        total = home[:, :quarter] + came[:, quarter : 2 * quarter]
        up_ref[:, pl.ds(start, quarter)] = total * factor
        start = pl.multiple_of((2 * place + 1 - parity) * quarter, LANES)
        up_ref[:, pl.ds(start, quarter)] = came[:, 2 * quarter : 3 * quarter] * factor
    low = 3 * quarter
    sums = (mine_ref[:, low:] + other_ref[:, low:]) * factor
    dw_ref[...] = sums[:, :TAPS]
    turned = sums.T
    gain_ref[...] = turned[TAPS : TAPS + 1, :]
    bias_ref[...] = turned[TAPS + 1 : TAPS + 2, :]


def fold(rows):
    half = rows.shape[0] // 2
    low = lax.broadcasted_iota(jnp.int32, (half, LANES), 1) < LANES // 2
    return jnp.where(low, rows[:half], pltpu.roll(rows[half:], LANES // 2, 1))


def unfold(rows):
    return jnp.concatenate([rows, pltpu.roll(rows, LANES // 2, 1)], axis=0)


def clear_borders(padded, breadth):
    shape = padded.shape[:-2] + (8, LANES)
    padded[..., :8, :] = jnp.zeros(shape, F32)
    padded[..., 8 + breadth :, :] = jnp.zeros(shape, F32)


def conv_norm_image(source, taps_ref, outs, padded, conv, height, breadth):
    normed_ref, white_ref, inv_ref = outs
    pixels, depth = normed_ref.shape
    tiles = depth // LANES
    clear_borders(padded, breadth)
    for tile in range(tiles):
        lanes = slice(tile * LANES, (tile + 1) * LANES)
        part = source[:pixels, lanes].astype(F32)
        padded[tile, :, 8 : 8 + breadth, :] = part.reshape(height, breadth, LANES)

    def one_tile(tile, carry):
        sums = correlate(
            padded,
            tile,
            lambda down, across: taps_ref[tile, pl.ds(down * KS + across, 1), :],
            height,
            breadth,
        )
        for line in range(height):
            conv[tile, line * breadth : (line + 1) * breadth, :] = sums[line]
        return carry

    lax.fori_loop(0, tiles, one_tile, 0)
    total = conv[0]
    for tile in range(1, tiles):
        total = total + conv[tile]
    average = jnp.sum(total, axis=-1, keepdims=True) / depth
    squares = None
    for tile in range(tiles):
        centered = conv[tile] - average
        squares = centered * centered if squares is None else squares + centered * centered
    variance = jnp.sum(squares, axis=-1, keepdims=True) / depth
    inv_std = lax.rsqrt(variance + NORM_EPS)
    inv_ref[...] = jnp.broadcast_to(inv_std, (pixels, LANES))
    for tile in range(tiles):
        lanes = slice(tile * LANES, (tile + 1) * LANES)
        whitened = (conv[tile] - average) * inv_std
        white_ref[:, lanes] = whitened
        gain = taps_ref[tile, TAPS : TAPS + 1, :]
        bias = taps_ref[tile, TAPS + 1 : TAPS + 2, :]
        normed_ref[:, lanes] = (whitened * gain + bias).astype(BF16)


def conv_norm_kernel(relative, own, height, breadth, *refs):
    small, x_ref = refs[:INNER], refs[INNER]
    *outs, taps_ref, gathered, unfolded, padded, conv = refs[INNER + 1 :]
    if relative:
        for group, piece in enumerate(small):
            unfolded[group * 2 * piece.shape[0] : (group + 1) * 2 * piece.shape[0], :] = unfold(
                piece[...].astype(F32)
            )
        count = unfolded.shape[0] // INNER
        small = [unfolded.at[pl.ds(group * count, count), :] for group in range(INNER)]
    place_rows(small, gathered, own, relative, F32)
    for tile in range(taps_ref.shape[0]):
        taps_ref[tile] = gathered[tile * LANES : (tile + 1) * LANES, :].T
    conv_norm_image(x_ref, taps_ref, outs, padded, conv, height, breadth)


def far_norm_kernel(height, breadth, taps_ref, far_ref, *refs):
    *outs, corner_ref, padded, conv = refs
    pixels, quarter = corner_ref.shape
    start = pl.multiple_of((1 - lax.axis_index("rep") % 2) * quarter, LANES)
    corner_ref[...] = far_ref[pixels:, pl.ds(start, quarter)]
    conv_norm_image(far_ref, taps_ref, outs, padded, conv, height, breadth)


def cot_pack_kernel(image_ref, cot_ref, across_ref, sibling_ref):
    pixels, half = sibling_ref.shape
    quarter = half // 2
    side = lax.axis_index("rep") % 2
    parity = (lax.axis_index("shard") // INNER) % 2
    for place in range(2):
        start = pl.multiple_of(place * half + (1 - parity) * quarter, LANES)
        lanes = slice(place * quarter, (place + 1) * quarter)
        across_ref[pixels:, lanes] = cot_ref[:, pl.ds(start, quarter)]
    across_ref[:pixels, :] = image_ref[...]
    sibling_ref[...] = cot_ref[:, pl.ds(pl.multiple_of((1 - side) * half, LANES), half)]


def join_kernel(own_ref, came_ref, out_ref):
    rows = own_ref.shape[0]
    out_ref[:rows, :] = own_ref[...]
    out_ref[rows:, :] = came_ref[...]


def order_kernel(relative, own, *refs):
    if not relative:
        place_rows(refs[:INNER], refs[INNER], own, relative)
        return
    home, first, second, out_ref = refs
    side = lax.axis_index("rep") % 2
    lines = home.shape[0] // own
    for line in range(lines):
        rows = slice(line * own, (line + 1) * own)
        below = slice((lines + line) * own, (lines + line + 1) * own)
        for ref, span, group in (
            (home, rows, 0),
            (first, rows, 1 + side),
            (second, rows, 2 - side),
            (second, below, INNER - 1),
        ):
            start = block_rows(True, group, line, own, lines)
            out_ref[pl.ds(start, own), :] = ref[span, :]


def project_kernel(relative, own, *refs):
    weight, *parts = refs[:5]
    cot_ref, sibling_ref, across_ref, corner_ref = refs[5:9]
    pieces = refs[9 : 9 + INNER]
    gp_ref, normed, cot, grad = refs[9 + INNER :]
    pixels, half = sibling_ref.shape
    quarter = half // 2
    side = lax.axis_index("rep") % 2
    parity = (lax.axis_index("shard") // INNER) % 2
    for place, part in enumerate(parts):
        normed[place * pixels : (place + 1) * pixels, :] = part[...]
    start = pl.multiple_of(side * half + parity * quarter, LANES)
    cot[:pixels, :] = cot_ref[:, pl.ds(start, quarter)]
    start = pl.multiple_of(side * quarter, LANES)
    cot[pixels : 2 * pixels, :] = across_ref[pixels:, pl.ds(start, quarter)]
    start = pl.multiple_of(parity * quarter, LANES)
    cot[2 * pixels : 3 * pixels, :] = sibling_ref[:, pl.ds(start, quarter)]
    cot[3 * pixels :, :] = corner_ref[...]
    for start in range(0, quarter, LANES):
        columns = slice(start, start + LANES)
        pre_act = jnp.dot(normed[...], weight[:, columns], preferred_element_type=F32)
        gp_ref[:, columns] = (cot[:, columns].astype(F32) * gelu_slope(pre_act)).astype(BF16)
    grad[...] = lax.dot_general(
        normed[...], gp_ref[...], (((0,), (0,)), ((), ())), preferred_element_type=F32
    )
    split_rows(grad, pieces, own, relative)


def back_project_kernel(weight, gp_ref, own_ref, other_ref):
    rows = own_ref.shape[0]
    grad_normed = lax.dot_general(
        gp_ref[...], weight[...], (((1,), (1,)), ((), ())), preferred_element_type=F32
    )
    own_ref[...] = grad_normed[:rows]
    other_ref[...] = grad_normed[rows:]


def norm_back_kernel(relative, own, height, breadth, *refs):
    gn_own, gn_other, *norms = refs[:6]
    taps_ref, x_ref, far_ref = refs[6:9]
    pieces = refs[9 : 9 + INNER]
    grad_ref, sent_ref, padded, grads_ref, rows, small, unfolded = refs[9 + INNER :]
    pixels, depth = x_ref.shape
    tiles = depth // LANES
    clear_borders(padded, breadth)
    rows[...] = jnp.zeros_like(rows)
    for image, source in enumerate((x_ref, far_ref)):
        span = slice(image * pixels, (image + 1) * pixels)
        white_ref, inv_ref = norms[2 * image : 2 * image + 2]
        first = None
        second = None
        for tile in range(tiles):
            lanes = slice(tile * LANES, (tile + 1) * LANES)
            part = source[:pixels, lanes].astype(F32)
            padded[image, tile, :, 8 : 8 + breadth, :] = part.reshape(height, breadth, LANES)
            grad_normed = gn_own[span, lanes] + gn_other[span, lanes]
            whitened = white_ref[:, lanes]
            product = grad_normed * whitened
            gain = taps_ref[tile, TAPS : TAPS + 1, :]
            rows[tile, TAPS : TAPS + 1, :] += jnp.sum(product, axis=0, keepdims=True)
            rows[tile, TAPS + 1 : TAPS + 2, :] += jnp.sum(grad_normed, axis=0, keepdims=True)
            one, two = grad_normed * gain, product * gain
            first = one if first is None else first + one
            second = two if second is None else second + two
        mean_first = jnp.sum(first, axis=-1, keepdims=True) / depth
        mean_second = jnp.sum(second, axis=-1, keepdims=True) / depth
        for tile in range(tiles):
            lanes = slice(tile * LANES, (tile + 1) * LANES)
            gain = taps_ref[tile, TAPS : TAPS + 1, :]
            grad_white = (gn_own[span, lanes] + gn_other[span, lanes]) * gain
            grad_conv = inv_ref[...] * (
                grad_white - mean_first - white_ref[:, lanes] * mean_second
            )
            grad_conv = grad_conv.reshape(height, breadth, LANES)
            grads_ref[image, tile] = grad_conv
            if image == 0:
                grad_ref[tile] = grad_conv
            else:
                sent_ref[tile] = grad_conv.astype(BF16)

    def one_tile(tile, carry):
        grads = [[grads_ref[image, tile, line] for line in range(height)] for image in range(2)]
        for across in range(KS):
            columns = slice(8 - MARGIN + across, 8 - MARGIN + across + breadth)
            shifted = [padded[image, tile, :, columns, :] for image in range(2)]
            for down in range(KS):
                total = None
                for image in range(2):
                    for line in range(height):
                        origin = line + down - MARGIN
                        if 0 <= origin < height:
                            term = grads[image][line] * shifted[image][origin]
                            total = term if total is None else total + term
                rows[tile, pl.ds(down * KS + across, 1), :] = jnp.sum(total, axis=0, keepdims=True)
        return carry

    lax.fori_loop(0, tiles, one_tile, 0)
    for tile in range(tiles):
        small[tile * LANES : (tile + 1) * LANES, :] = rows[tile].T
    if relative:
        whole = [unfolded.at[group] for group in range(INNER)]
        split_rows(small, whole, own, relative)
        for source, piece in zip(whole, pieces):
            piece[...] = fold(source[...]).astype(piece.dtype)
    else:
        split_rows(small, pieces, own, relative)


def conv_back_kernel(grad_ref, other_ref, taps_ref, out_ref, padded):
    tiles, height, breadth, _ = grad_ref.shape
    clear_borders(padded, breadth)
    padded[:, :, 8 : 8 + breadth, :] = grad_ref[...] + other_ref[...].astype(F32)

    def one_tile(tile, carry):
        sums = correlate(
            padded,
            tile,
            lambda down, across: taps_ref[tile, pl.ds(TAPS - 1 - down * KS - across, 1), :],
            height,
            breadth,
        )
        start = pl.multiple_of(tile * LANES, LANES)
        for line in range(height):
            out_ref[0, line, :, pl.ds(start, LANES)] = sums[line].astype(BF16)
        return carry

    lax.fori_loop(0, tiles, one_tile, 0)


def call(kernel, name, outs, scratch, micros, *args, mebibytes=48):
    flops = int(micros * 1.1e9)
    moved = sum(math.prod(a.shape) * a.dtype.itemsize for a in args)
    moved += sum(math.prod(o.shape) * o.dtype.itemsize for o in outs)
    return pl.pallas_call(
        kernel,
        out_shape=outs,
        in_specs=[VMEM] * len(args),
        out_specs=[VMEM] * len(outs),
        scratch_shapes=scratch,
        compiler_params=params(mebibytes),
        cost_estimate=pl.CostEstimate(flops=flops, bytes_accessed=moved, transcendentals=0),
        name=name,
    )(*args)


def body(images, cotangent, depthwise_weight, norm_gain, norm_bias, up_weight):
    shards, reps = lax.axis_size("shard"), lax.axis_size("rep")
    own, hidden = up_weight.shape
    depth = own * shards
    lines = shards // INNER
    half, quarter = hidden // 2, hidden // 4
    height, breadth = images.shape[1:3]
    pixels = height * breadth
    tiles = depth // LANES
    me = lax.axis_index("shard")
    side = lax.axis_index("rep") % 2
    parity = (me // INNER) % 2
    relative = own % 16 == 0

    def over_shard(array, flip):
        return lax.ppermute(array, "shard", [(i, i ^ flip) for i in range(shards)])

    def crossing(array, flip):
        pairs = [
            (i * reps + r, (i ^ flip) * reps + (r ^ 1)) for i in range(shards) for r in range(reps)
        ]
        return lax.ppermute(array, ("shard", "rep"), pairs)

    def hop(array, place):
        flips = [(1, 2), (2, 1)]
        pairs = [
            (i * reps + r, (i ^ flips[r % 2][place]) * reps + r)
            for i in range(shards)
            for r in range(reps)
        ]
        return lax.ppermute(array, ("shard", "rep"), pairs)

    def over_core(array):
        return lax.ppermute(array, "rep", [(i, i ^ 1) for i in range(reps)])

    def true_order(pieces):
        if relative:
            return pieces
        stacked = jnp.stack(pieces).reshape(shards, own, -1)
        flips = jnp.arange(shards) ^ me
        places = (flips % INNER) * lines + flips // INNER
        return list(jnp.take(stacked, places, axis=0).reshape(INNER, lines * own, -1))

    def relative_order(pieces):
        if relative:
            return pieces
        stacked = jnp.concatenate([p.astype(F32) for p in pieces]).reshape(shards, own, -1)
        flips = (jnp.arange(lines)[None, :] * INNER + jnp.arange(INNER)[:, None]).reshape(-1)
        moved = jnp.take(stacked, flips ^ me, axis=0).reshape(INNER, lines * own, -1)
        return [moved[0]] + [moved[i].astype(BF16) for i in range(1, INNER)]

    shape = jax.ShapeDtypeStruct
    home, near, far = call(
        pack_kernel,
        "pack",
        [shape(mixed_shape(own, quarter), BF16)] * 3,
        [
            pltpu.VMEM((LANES, LANES), F32),
            pltpu.VMEM((own, LANES), F32),
        ],
        0.5,
        up_weight,
        depthwise_weight,
        norm_gain[None, :],
        norm_bias[None, :],
        mebibytes=63,
    )
    image, cotangent = images.reshape(pixels, depth), cotangent.reshape(pixels, hidden)
    home, near, far, image, cotangent = lax.optimization_barrier(
        (home, near, far, image, cotangent)
    )
    gathered = [home] + [
        crossing(far if line % 2 else near, INNER * line) for line in range(1, lines)
    ]
    across, cot_sibling = call(
        cot_pack_kernel,
        "cot_pack",
        [shape((2 * pixels, half), BF16), shape((pixels, half), BF16)],
        [],
        0.4,
        image,
        cotangent,
    )
    across, cot_sibling = crossing(across, INNER), over_core(cot_sibling)

    rows = lines * own
    folded = rows // 2 if relative else rows
    weight_lines, extra_lines = call(
        functools.partial(assemble_kernel, own),
        "assemble",
        [shape((rows, quarter), BF16), shape((folded, LANES), BF16)],
        [],
        4.0,
        *gathered,
    )
    weight_lines, cot_sibling = lax.optimization_barrier((weight_lines, cot_sibling))
    first_lines = hop(weight_lines, 0)
    (joined,) = call(
        join_kernel,
        "join",
        [shape((2 * rows, quarter), BF16)],
        [],
        0.3,
        weight_lines,
        first_lines,
    )
    second_lines = hop(joined, 1)
    weights = [weight_lines, first_lines, second_lines]
    extras = [extra_lines] + [crossing(extra_lines, flip) for flip in range(1, INNER)]
    if not relative:
        extras = true_order(extras)
        x_lines = jnp.where(side == 0, first_lines, second_lines[:rows])
        y_lines = jnp.where(side == 0, second_lines[:rows], first_lines)
        weights = true_order([weight_lines, x_lines, y_lines, second_lines[rows:]])
    (weight,) = call(
        functools.partial(order_kernel, relative, own),
        "order",
        [shape((depth, quarter), BF16)],
        [],
        0.3,
        *weights,
    )

    padded = pltpu.VMEM((tiles, height, breadth + 16, LANES), F32)
    norm_shapes = [
        shape((pixels, depth), BF16),
        shape((pixels, depth), F32),
        shape((pixels, LANES), F32),
    ]
    conv = pltpu.VMEM((tiles, pixels, LANES), F32)
    normed, whitened, inv_std, taps = call(
        functools.partial(conv_norm_kernel, relative, own, height, breadth),
        "conv_norm",
        norm_shapes + [shape((tiles, LANES, LANES), F32)],
        [pltpu.VMEM((depth, LANES), F32), pltpu.VMEM((depth, LANES), F32), padded, conv],
        0.1,
        *extras,
        image,
    )
    normed_sibling = over_core(normed)
    far_normed, far_whitened, far_inv_std, corner = call(
        functools.partial(far_norm_kernel, height, breadth),
        "far_norm",
        norm_shapes + [shape((pixels, quarter), BF16)],
        [padded, conv],
        1.0,
        taps,
        across,
    )
    corner_normed, corner = over_core(far_normed), over_core(corner)

    *pieces, grad_pre = call(
        functools.partial(project_kernel, relative, own),
        "project",
        [shape((rows, quarter), F32)]
        + [shape((rows, quarter), BF16)] * (INNER - 1)
        + [shape((4 * pixels, quarter), BF16)],
        [
            pltpu.VMEM((4 * pixels, depth), BF16),
            pltpu.VMEM((4 * pixels, quarter), BF16),
            pltpu.VMEM((depth, quarter), F32),
        ],
        1.6,
        weight,
        normed,
        far_normed,
        normed_sibling,
        corner_normed,
        cotangent,
        cot_sibling,
        across,
        corner,
    )
    gn_kept, gn_sent = call(
        back_project_kernel,
        "back_project",
        [shape((2 * pixels, depth), F32)] * 2,
        [],
        0.7,
        weight,
        grad_pre,
    )
    pieces = relative_order(pieces)
    arrived = [over_shard(pieces[flip], flip) for flip in range(INNER - 1, 0, -1)]
    *small, grad_conv, grad_sent = call(
        functools.partial(norm_back_kernel, relative, own, height, breadth),
        "norm_back",
        [shape((folded, LANES), F32)]
        + [shape((folded, LANES), BF16)] * (INNER - 1)
        + [
            shape((tiles, height, breadth, LANES), F32),
            shape((tiles, height, breadth, LANES), BF16),
        ],
        [
            pltpu.VMEM((2, tiles, height, breadth + 16, LANES), F32),
            pltpu.VMEM((2, tiles, height, breadth, LANES), F32),
            pltpu.VMEM((tiles, LANES, LANES), F32),
            pltpu.VMEM((depth, LANES), F32),
            pltpu.VMEM((INNER, rows, LANES), F32),
        ],
        0.1,
        gn_kept,
        over_core(gn_sent),
        whitened,
        inv_std,
        far_whitened,
        far_inv_std,
        taps,
        image,
        across,
    )
    small = relative_order(small)
    small_arrived = [crossing(small[flip], flip) for flip in range(INNER - 1, 0, -1)]
    grad_other = crossing(grad_sent, INNER)
    (grad_images,) = call(
        conv_back_kernel,
        "conv_back",
        [shape(images.shape, BF16)],
        [padded],
        0.1,
        grad_conv,
        grad_other,
        taps,
    )

    home, *sent = call(
        functools.partial(plane_sum_kernel, lines),
        "plane_sum",
        [shape(mixed_shape(own, quarter), F32)]
        + [shape(mixed_shape(own, quarter), BF16)] * (lines - 1),
        [],
        2.0,
        pieces[0],
        *arrived,
        small[0],
        *small_arrived,
    )
    home, grad_images = lax.optimization_barrier((home, grad_images))
    came = [crossing(sent[line - 1], INNER * line) for line in line_order(lines)]
    (total,) = call(
        functools.partial(line_sum_kernel, own),
        "line_sum",
        [shape((own, 3 * quarter + LANES), F32)],
        [],
        0.3,
        home,
        *came,
    )
    if reps > 2:
        groups = [[i for i in range(reps) if i % 2 == s] for s in range(2)]
        total = lax.psum(total, "rep", axis_index_groups=groups)
    other = over_core(total)
    factor = 1.0 / math.sqrt(images.shape[0] * pixels * shards * reps)
    grad_up, grad_depthwise, grad_gain, grad_bias = call(
        functools.partial(finish_kernel, factor),
        "finish",
        [
            shape((own, hidden), F32),
            shape((own, TAPS), F32),
            shape((1, own), F32),
            shape((1, own), F32),
        ],
        [],
        0.5,
        total,
        other,
    )
    return (grad_images, grad_up, grad_depthwise, grad_gain[0], grad_bias[0])


def solution(mesh):
    placed = (
        P(("shard", "rep"), None, None, None),
        P(("shard", "rep"), None, None, None),
        P("shard", None),
        P("shard"),
        P("shard"),
        P("shard", None),
    )
    return jax.shard_map(
        body,
        mesh=mesh,
        in_specs=placed,
        out_specs=(
            P(("shard", "rep"), None, None, None),
            P("shard", None),
            P("shard", None),
            P("shard"),
            P("shard"),
        ),
        check_vma=False,
    )
```

```python
import functools
import math

import jax
import jax.numpy as jnp
from jax import lax
from jax.experimental import pallas as pl
from jax.experimental.pallas import tpu as pltpu
from jax.sharding import PartitionSpec as P

KS = 7
TAPS = KS * KS
MARGIN = KS // 2
LANES = 128
INNER = 4
NORM_EPS = 1e-06
BF16 = jnp.bfloat16
F32 = jnp.float32
VMEM = pl.BlockSpec(memory_space=pltpu.VMEM)


def params(mebibytes):
    return pltpu.CompilerParams(vmem_limit_bytes=mebibytes * 1024 * 1024)


def gelu_slope(inputs):
    cumulative = 0.5 * (1.0 + lax.erf(inputs * 0.7071067811865476))
    return cumulative + inputs * jnp.exp(-0.5 * inputs * inputs) * 0.3989422804014327


def block_rows(relative, group, line, own, lines):
    if relative:
        place = lax.axis_index("shard") ^ (line * INNER + group)
        return pl.multiple_of(place * own, 16)
    return (group * lines + line) * own


def place_rows(pieces, target, own, relative, cast=None):
    for group, piece in enumerate(pieces):
        lines = piece.shape[0] // own
        if not relative:
            target[group * piece.shape[0] : (group + 1) * piece.shape[0], :] = (
                piece[...] if cast is None else piece[...].astype(cast)
            )
            continue
        for line in range(lines):
            rows = piece[line * own : (line + 1) * own, :]
            start = block_rows(True, group, line, own, lines)
            target[pl.ds(start, own), :] = rows if cast is None else rows.astype(cast)


def split_rows(source, pieces, own, relative):
    for group, piece in enumerate(pieces):
        lines = piece.shape[0] // own
        if not relative:
            piece[...] = source[group * piece.shape[0] : (group + 1) * piece.shape[0], :].astype(
                piece.dtype
            )
            continue
        for line in range(lines):
            start = block_rows(True, group, line, own, lines)
            piece[line * own : (line + 1) * own, :] = source[pl.ds(start, own), :].astype(
                piece.dtype
            )


def correlate(padded, tile, tap_row, height, breadth):
    sums = [None] * height
    for across in range(KS):
        shifted = padded[tile, :, 8 - MARGIN + across : 8 - MARGIN + across + breadth, :]
        for down in range(KS):
            row = tap_row(down, across)
            for line in range(height):
                origin = line + down - MARGIN
                if 0 <= origin < height:
                    term = shifted[origin] * row
                    sums[line] = term if sums[line] is None else sums[line] + term
    return sums


def tight(own, quarter):
    return own % (16 * (quarter // LANES)) == 0


def with_small(weights, extras):
    own, quarter = weights.shape
    if not tight(own, quarter):
        return jnp.concatenate([weights, extras], axis=1)
    folded = fold(extras)
    count = folded.shape[0] * LANES // quarter
    parts = [folded[at : at + count] for at in range(0, folded.shape[0], count)]
    return jnp.concatenate([weights, jnp.concatenate(parts, axis=1)], axis=0)


def without_small(mixed, own, quarter):
    if not tight(own, quarter):
        return mixed[:, :quarter], mixed[:, quarter:]
    parts = [mixed[own:, at : at + LANES] for at in range(0, quarter, LANES)]
    return mixed[:own], unfold(jnp.concatenate(parts, axis=0))


def mixed_shape(own, quarter):
    if not tight(own, quarter):
        return (own, quarter + LANES)
    return (own + own // 2 * LANES // quarter, quarter)


def pack_kernel(w_ref, dw_ref, gain_ref, bias_ref, home_ref, near_ref, far_ref, turned, wide):
    own, hidden = w_ref.shape
    quarter = hidden // 4
    side = lax.axis_index("rep") % 2
    parity = (lax.axis_index("shard") // INNER) % 2
    turned[...] = jnp.zeros_like(turned)
    turned[TAPS : TAPS + 1, :own] = gain_ref[...].astype(F32)
    turned[TAPS + 1 : TAPS + 2, :own] = bias_ref[...].astype(F32)
    wide[...] = jnp.zeros_like(wide)
    wide[:, :TAPS] = dw_ref[...].astype(F32)
    extras = wide[...] + turned[...].T[:own]
    kinds = ((home_ref, side, parity), (near_ref, 1 - side, parity), (far_ref, 1 - side, 1 - parity))
    for ref, place, which in kinds:
        start = pl.multiple_of(place * (2 * quarter) + which * quarter, LANES)
        weights = w_ref[:, pl.ds(start, quarter)].astype(F32)
        ref[...] = with_small(weights, extras).astype(BF16)


def assemble_kernel(own, *refs):
    pieces, (weight_ref, extra_ref) = refs[:-2], refs[-2:]
    quarter = weight_ref.shape[1]
    parts = [without_small(piece[...].astype(F32), own, quarter) for piece in pieces]
    for line, (weights, _) in enumerate(parts):
        weight_ref[line * own : (line + 1) * own, :] = weights.astype(BF16)
    extras = jnp.concatenate([extra for _, extra in parts], axis=0)
    if extra_ref.shape[0] < extras.shape[0]:
        extras = fold(extras)
    extra_ref[...] = extras.astype(BF16)


def plane_sum_kernel(lines, *refs):
    pieces, small, outs = refs[:INNER], refs[INNER : 2 * INNER], refs[2 * INNER :]
    own = pieces[0].shape[0] // lines
    quarter = pieces[0].shape[1]
    extras = small[0][...]
    for part in small[1:]:
        extras = extras + part[...].astype(F32)
    if extras.shape[0] < pieces[0].shape[0]:
        extras = unfold(extras)
    for line, out in enumerate(outs):
        rows = slice(line * own, (line + 1) * own)
        total = pieces[0][rows, :]
        for part in pieces[1:]:
            total = total + part[rows, :].astype(F32)
        out[...] = with_small(total, extras[rows, :]).astype(out.dtype)


def line_order(lines):
    return [*range(2, lines), 1]


def line_sum_kernel(own, *refs):
    pieces, total_ref = refs[:-1], refs[-1]
    quarter = (total_ref.shape[1] - LANES) // 3
    near, far = None, None
    for line, piece in zip(line_order(len(pieces)), pieces[1:]):
        came = piece[...].astype(F32)
        if line % 2:
            far = came if far is None else far + came
        else:
            near = came if near is None else near + came
    home, extras = without_small(pieces[0][...], own, quarter)
    total_ref[:, :quarter] = home
    for place, part in ((1, near), (2, far)):
        weights, more = without_small(part, own, quarter)
        total_ref[:, place * quarter : (place + 1) * quarter] = weights
        extras = extras + more
    total_ref[:, 3 * quarter :] = extras


def finish_kernel(factor, mine_ref, other_ref, up_ref, dw_ref, gain_ref, bias_ref):
    own, quarter = mine_ref.shape[0], (mine_ref.shape[1] - LANES) // 3
    side = lax.axis_index("rep") % 2
    parity = (lax.axis_index("shard") // INNER) % 2
    for place, home, came in ((side, mine_ref, other_ref), (1 - side, other_ref, mine_ref)):
        start = pl.multiple_of((2 * place + parity) * quarter, LANES)
        total = home[:, :quarter] + came[:, quarter : 2 * quarter]
        up_ref[:, pl.ds(start, quarter)] = total * factor
        start = pl.multiple_of((2 * place + 1 - parity) * quarter, LANES)
        up_ref[:, pl.ds(start, quarter)] = came[:, 2 * quarter : 3 * quarter] * factor
    low = 3 * quarter
    sums = (mine_ref[:, low:] + other_ref[:, low:]) * factor
    dw_ref[...] = sums[:, :TAPS]
    turned = sums.T
    gain_ref[...] = turned[TAPS : TAPS + 1, :]
    bias_ref[...] = turned[TAPS + 1 : TAPS + 2, :]


def fold(rows):
    half = rows.shape[0] // 2
    low = lax.broadcasted_iota(jnp.int32, (half, LANES), 1) < LANES // 2
    return jnp.where(low, rows[:half], pltpu.roll(rows[half:], LANES // 2, 1))


def unfold(rows):
    return jnp.concatenate([rows, pltpu.roll(rows, LANES // 2, 1)], axis=0)


def clear_borders(padded, breadth):
    shape = padded.shape[:-2] + (8, LANES)
    padded[..., :8, :] = jnp.zeros(shape, F32)
    padded[..., 8 + breadth :, :] = jnp.zeros(shape, F32)


def conv_norm_image(source, taps_ref, outs, padded, conv, height, breadth):
    normed_ref, white_ref, inv_ref = outs
    pixels, depth = normed_ref.shape
    tiles = depth // LANES
    clear_borders(padded, breadth)
    for tile in range(tiles):
        lanes = slice(tile * LANES, (tile + 1) * LANES)
        part = source[:pixels, lanes].astype(F32)
        padded[tile, :, 8 : 8 + breadth, :] = part.reshape(height, breadth, LANES)

    def one_tile(tile, carry):
        sums = correlate(
            padded,
            tile,
            lambda down, across: taps_ref[tile, pl.ds(down * KS + across, 1), :],
            height,
            breadth,
        )
        for line in range(height):
            conv[tile, line * breadth : (line + 1) * breadth, :] = sums[line]
        return carry

    lax.fori_loop(0, tiles, one_tile, 0)
    total = conv[0]
    for tile in range(1, tiles):
        total = total + conv[tile]
    average = jnp.sum(total, axis=-1, keepdims=True) / depth
    squares = None
    for tile in range(tiles):
        centered = conv[tile] - average
        squares = centered * centered if squares is None else squares + centered * centered
    variance = jnp.sum(squares, axis=-1, keepdims=True) / depth
    inv_std = lax.rsqrt(variance + NORM_EPS)
    inv_ref[...] = jnp.broadcast_to(inv_std, (pixels, LANES))
    for tile in range(tiles):
        lanes = slice(tile * LANES, (tile + 1) * LANES)
        whitened = (conv[tile] - average) * inv_std
        white_ref[:, lanes] = whitened
        gain = taps_ref[tile, TAPS : TAPS + 1, :]
        bias = taps_ref[tile, TAPS + 1 : TAPS + 2, :]
        normed_ref[:, lanes] = (whitened * gain + bias).astype(BF16)


def conv_norm_kernel(relative, own, height, breadth, *refs):
    small, x_ref = refs[:INNER], refs[INNER]
    *outs, taps_ref, gathered, unfolded, padded, conv = refs[INNER + 1 :]
    if relative:
        for group, piece in enumerate(small):
            unfolded[group * 2 * piece.shape[0] : (group + 1) * 2 * piece.shape[0], :] = unfold(
                piece[...].astype(F32)
            )
        count = unfolded.shape[0] // INNER
        small = [unfolded.at[pl.ds(group * count, count), :] for group in range(INNER)]
    place_rows(small, gathered, own, relative, F32)
    for tile in range(taps_ref.shape[0]):
        taps_ref[tile] = gathered[tile * LANES : (tile + 1) * LANES, :].T
    conv_norm_image(x_ref, taps_ref, outs, padded, conv, height, breadth)


def far_norm_kernel(height, breadth, taps_ref, far_ref, *refs):
    *outs, corner_ref, padded, conv = refs
    pixels, quarter = corner_ref.shape
    start = pl.multiple_of((1 - lax.axis_index("rep") % 2) * quarter, LANES)
    corner_ref[...] = far_ref[pixels:, pl.ds(start, quarter)]
    conv_norm_image(far_ref, taps_ref, outs, padded, conv, height, breadth)


def cot_pack_kernel(image_ref, cot_ref, across_ref, sibling_ref):
    pixels, half = sibling_ref.shape
    quarter = half // 2
    side = lax.axis_index("rep") % 2
    parity = (lax.axis_index("shard") // INNER) % 2
    for place in range(2):
        start = pl.multiple_of(place * half + (1 - parity) * quarter, LANES)
        lanes = slice(place * quarter, (place + 1) * quarter)
        across_ref[pixels:, lanes] = cot_ref[:, pl.ds(start, quarter)]
    across_ref[:pixels, :] = image_ref[...]
    sibling_ref[...] = cot_ref[:, pl.ds(pl.multiple_of((1 - side) * half, LANES), half)]


def join_kernel(own_ref, came_ref, out_ref):
    rows = own_ref.shape[0]
    out_ref[:rows, :] = own_ref[...]
    out_ref[rows:, :] = came_ref[...]


def order_kernel(relative, own, *refs):
    if not relative:
        place_rows(refs[:INNER], refs[INNER], own, relative)
        return
    home, first, second, out_ref = refs
    side = lax.axis_index("rep") % 2
    lines = home.shape[0] // own
    for line in range(lines):
        rows = slice(line * own, (line + 1) * own)
        below = slice((lines + line) * own, (lines + line + 1) * own)
        for ref, span, group in (
            (home, rows, 0),
            (first, rows, 1 + side),
            (second, rows, 2 - side),
            (second, below, INNER - 1),
        ):
            start = block_rows(True, group, line, own, lines)
            out_ref[pl.ds(start, own), :] = ref[span, :]


def project_kernel(relative, own, *refs):
    weight, *parts = refs[:5]
    cot_ref, sibling_ref, across_ref, corner_ref = refs[5:9]
    pieces = refs[9 : 9 + INNER]
    gp_ref, normed, cot, grad = refs[9 + INNER :]
    pixels, half = sibling_ref.shape
    quarter = half // 2
    side = lax.axis_index("rep") % 2
    parity = (lax.axis_index("shard") // INNER) % 2
    for place, part in enumerate(parts):
        normed[place * pixels : (place + 1) * pixels, :] = part[...]
    start = pl.multiple_of(side * half + parity * quarter, LANES)
    cot[:pixels, :] = cot_ref[:, pl.ds(start, quarter)]
    start = pl.multiple_of(side * quarter, LANES)
    cot[pixels : 2 * pixels, :] = across_ref[pixels:, pl.ds(start, quarter)]
    start = pl.multiple_of(parity * quarter, LANES)
    cot[2 * pixels : 3 * pixels, :] = sibling_ref[:, pl.ds(start, quarter)]
    cot[3 * pixels :, :] = corner_ref[...]
    for start in range(0, quarter, LANES):
        columns = slice(start, start + LANES)
        pre_act = jnp.dot(normed[...], weight[:, columns], preferred_element_type=F32)
        gp_ref[:, columns] = (cot[:, columns].astype(F32) * gelu_slope(pre_act)).astype(BF16)
    grad[...] = lax.dot_general(
        normed[...], gp_ref[...], (((0,), (0,)), ((), ())), preferred_element_type=F32
    )
    split_rows(grad, pieces, own, relative)


def back_project_kernel(weight, gp_ref, own_ref, other_ref):
    rows = own_ref.shape[0]
    grad_normed = lax.dot_general(
        gp_ref[...], weight[...], (((1,), (1,)), ((), ())), preferred_element_type=F32
    )
    own_ref[...] = grad_normed[:rows]
    other_ref[...] = grad_normed[rows:]


def norm_back_kernel(relative, own, height, breadth, *refs):
    gn_own, gn_other, *norms = refs[:6]
    taps_ref, x_ref, far_ref = refs[6:9]
    pieces = refs[9 : 9 + INNER]
    grad_ref, sent_ref, padded, grads_ref, rows, small, unfolded = refs[9 + INNER :]
    pixels, depth = x_ref.shape
    tiles = depth // LANES
    clear_borders(padded, breadth)
    rows[...] = jnp.zeros_like(rows)
    for image, source in enumerate((x_ref, far_ref)):
        span = slice(image * pixels, (image + 1) * pixels)
        white_ref, inv_ref = norms[2 * image : 2 * image + 2]
        first = None
        second = None
        for tile in range(tiles):
            lanes = slice(tile * LANES, (tile + 1) * LANES)
            part = source[:pixels, lanes].astype(F32)
            padded[image, tile, :, 8 : 8 + breadth, :] = part.reshape(height, breadth, LANES)
            grad_normed = gn_own[span, lanes] + gn_other[span, lanes]
            whitened = white_ref[:, lanes]
            product = grad_normed * whitened
            gain = taps_ref[tile, TAPS : TAPS + 1, :]
            rows[tile, TAPS : TAPS + 1, :] += jnp.sum(product, axis=0, keepdims=True)
            rows[tile, TAPS + 1 : TAPS + 2, :] += jnp.sum(grad_normed, axis=0, keepdims=True)
            one, two = grad_normed * gain, product * gain
            first = one if first is None else first + one
            second = two if second is None else second + two
        mean_first = jnp.sum(first, axis=-1, keepdims=True) / depth
        mean_second = jnp.sum(second, axis=-1, keepdims=True) / depth
        for tile in range(tiles):
            lanes = slice(tile * LANES, (tile + 1) * LANES)
            gain = taps_ref[tile, TAPS : TAPS + 1, :]
            grad_white = (gn_own[span, lanes] + gn_other[span, lanes]) * gain
            grad_conv = inv_ref[...] * (
                grad_white - mean_first - white_ref[:, lanes] * mean_second
            )
            grad_conv = grad_conv.reshape(height, breadth, LANES)
            grads_ref[image, tile] = grad_conv
            if image == 0:
                grad_ref[tile] = grad_conv
            else:
                sent_ref[tile] = grad_conv.astype(BF16)

    def one_tile(tile, carry):
        grads = [[grads_ref[image, tile, line] for line in range(height)] for image in range(2)]
        for across in range(KS):
            columns = slice(8 - MARGIN + across, 8 - MARGIN + across + breadth)
            shifted = [padded[image, tile, :, columns, :] for image in range(2)]
            for down in range(KS):
                total = None
                for image in range(2):
                    for line in range(height):
                        origin = line + down - MARGIN
                        if 0 <= origin < height:
                            term = grads[image][line] * shifted[image][origin]
                            total = term if total is None else total + term
                rows[tile, pl.ds(down * KS + across, 1), :] = jnp.sum(total, axis=0, keepdims=True)
        return carry

    lax.fori_loop(0, tiles, one_tile, 0)
    for tile in range(tiles):
        small[tile * LANES : (tile + 1) * LANES, :] = rows[tile].T
    if relative:
        whole = [unfolded.at[group] for group in range(INNER)]
        split_rows(small, whole, own, relative)
        for source, piece in zip(whole, pieces):
            piece[...] = fold(source[...]).astype(piece.dtype)
    else:
        split_rows(small, pieces, own, relative)


def conv_back_kernel(grad_ref, other_ref, taps_ref, out_ref, padded):
    tiles, height, breadth, _ = grad_ref.shape
    clear_borders(padded, breadth)
    padded[:, :, 8 : 8 + breadth, :] = grad_ref[...] + other_ref[...].astype(F32)

    def one_tile(tile, carry):
        sums = correlate(
            padded,
            tile,
            lambda down, across: taps_ref[tile, pl.ds(TAPS - 1 - down * KS - across, 1), :],
            height,
            breadth,
        )
        start = pl.multiple_of(tile * LANES, LANES)
        for line in range(height):
            out_ref[0, line, :, pl.ds(start, LANES)] = sums[line].astype(BF16)
        return carry

    lax.fori_loop(0, tiles, one_tile, 0)


def call(kernel, name, outs, scratch, micros, *args, mebibytes=48):
    flops = int(micros * 1.1e9)
    moved = sum(math.prod(a.shape) * a.dtype.itemsize for a in args)
    moved += sum(math.prod(o.shape) * o.dtype.itemsize for o in outs)
    return pl.pallas_call(
        kernel,
        out_shape=outs,
        in_specs=[VMEM] * len(args),
        out_specs=[VMEM] * len(outs),
        scratch_shapes=scratch,
        compiler_params=params(mebibytes),
        cost_estimate=pl.CostEstimate(flops=flops, bytes_accessed=moved, transcendentals=0),
        name=name,
    )(*args)


def body(images, cotangent, depthwise_weight, norm_gain, norm_bias, up_weight):
    shards, reps = lax.axis_size("shard"), lax.axis_size("rep")
    own, hidden = up_weight.shape
    depth = own * shards
    lines = shards // INNER
    half, quarter = hidden // 2, hidden // 4
    height, breadth = images.shape[1:3]
    pixels = height * breadth
    tiles = depth // LANES
    me = lax.axis_index("shard")
    side = lax.axis_index("rep") % 2
    parity = (me // INNER) % 2
    relative = own % 16 == 0

    def over_shard(array, flip):
        return lax.ppermute(array, "shard", [(i, i ^ flip) for i in range(shards)])

    def crossing(array, flip):
        pairs = [
            (i * reps + r, (i ^ flip) * reps + (r ^ 1)) for i in range(shards) for r in range(reps)
        ]
        return lax.ppermute(array, ("shard", "rep"), pairs)

    def hop(array, place):
        flips = [(1, 2), (2, 1)]
        pairs = [
            (i * reps + r, (i ^ flips[r % 2][place]) * reps + r)
            for i in range(shards)
            for r in range(reps)
        ]
        return lax.ppermute(array, ("shard", "rep"), pairs)

    def over_core(array):
        return lax.ppermute(array, "rep", [(i, i ^ 1) for i in range(reps)])

    def true_order(pieces):
        if relative:
            return pieces
        stacked = jnp.stack(pieces).reshape(shards, own, -1)
        flips = jnp.arange(shards) ^ me
        places = (flips % INNER) * lines + flips // INNER
        return list(jnp.take(stacked, places, axis=0).reshape(INNER, lines * own, -1))

    def relative_order(pieces):
        if relative:
            return pieces
        stacked = jnp.concatenate([p.astype(F32) for p in pieces]).reshape(shards, own, -1)
        flips = (jnp.arange(lines)[None, :] * INNER + jnp.arange(INNER)[:, None]).reshape(-1)
        moved = jnp.take(stacked, flips ^ me, axis=0).reshape(INNER, lines * own, -1)
        return [moved[0]] + [moved[i].astype(BF16) for i in range(1, INNER)]

    shape = jax.ShapeDtypeStruct
    home, near, far = call(
        pack_kernel,
        "pack",
        [shape(mixed_shape(own, quarter), BF16)] * 3,
        [
            pltpu.VMEM((LANES, LANES), F32),
            pltpu.VMEM((own, LANES), F32),
        ],
        0.5,
        up_weight,
        depthwise_weight,
        norm_gain[None, :],
        norm_bias[None, :],
        mebibytes=63,
    )
    image, cotangent = images.reshape(pixels, depth), cotangent.reshape(pixels, hidden)
    home, near, far, image, cotangent = lax.optimization_barrier(
        (home, near, far, image, cotangent)
    )
    gathered = [home] + [
        crossing(far if line % 2 else near, INNER * line) for line in range(1, lines)
    ]
    across, cot_sibling = call(
        cot_pack_kernel,
        "cot_pack",
        [shape((2 * pixels, half), BF16), shape((pixels, half), BF16)],
        [],
        0.4,
        image,
        cotangent,
    )
    across, cot_sibling = crossing(across, INNER), over_core(cot_sibling)

    rows = lines * own
    folded = rows // 2 if relative else rows
    weight_lines, extra_lines = call(
        functools.partial(assemble_kernel, own),
        "assemble",
        [shape((rows, quarter), BF16), shape((folded, LANES), BF16)],
        [],
        4.0,
        *gathered,
    )
    weight_lines, cot_sibling = lax.optimization_barrier((weight_lines, cot_sibling))
    first_lines = hop(weight_lines, 0)
    (joined,) = call(
        join_kernel,
        "join",
        [shape((2 * rows, quarter), BF16)],
        [],
        0.3,
        weight_lines,
        first_lines,
    )
    second_lines = hop(joined, 1)
    weights = [weight_lines, first_lines, second_lines]
    extras = [extra_lines] + [crossing(extra_lines, flip) for flip in range(1, INNER)]
    if not relative:
        extras = true_order(extras)
        x_lines = jnp.where(side == 0, first_lines, second_lines[:rows])
        y_lines = jnp.where(side == 0, second_lines[:rows], first_lines)
        weights = true_order([weight_lines, x_lines, y_lines, second_lines[rows:]])
    (weight,) = call(
        functools.partial(order_kernel, relative, own),
        "order",
        [shape((depth, quarter), BF16)],
        [],
        0.3,
        *weights,
    )

    padded = pltpu.VMEM((tiles, height, breadth + 16, LANES), F32)
    norm_shapes = [
        shape((pixels, depth), BF16),
        shape((pixels, depth), F32),
        shape((pixels, LANES), F32),
    ]
    conv = pltpu.VMEM((tiles, pixels, LANES), F32)
    normed, whitened, inv_std, taps = call(
        functools.partial(conv_norm_kernel, relative, own, height, breadth),
        "conv_norm",
        norm_shapes + [shape((tiles, LANES, LANES), F32)],
        [pltpu.VMEM((depth, LANES), F32), pltpu.VMEM((depth, LANES), F32), padded, conv],
        0.1,
        *extras,
        image,
    )
    normed_sibling = over_core(normed)
    far_normed, far_whitened, far_inv_std, corner = call(
        functools.partial(far_norm_kernel, height, breadth),
        "far_norm",
        norm_shapes + [shape((pixels, quarter), BF16)],
        [padded, conv],
        1.0,
        taps,
        across,
    )
    corner_normed, corner = over_core(far_normed), over_core(corner)

    *pieces, grad_pre = call(
        functools.partial(project_kernel, relative, own),
        "project",
        [shape((rows, quarter), F32)]
        + [shape((rows, quarter), BF16)] * (INNER - 1)
        + [shape((4 * pixels, quarter), BF16)],
        [
            pltpu.VMEM((4 * pixels, depth), BF16),
            pltpu.VMEM((4 * pixels, quarter), BF16),
            pltpu.VMEM((depth, quarter), F32),
        ],
        1.6,
        weight,
        normed,
        far_normed,
        normed_sibling,
        corner_normed,
        cotangent,
        cot_sibling,
        across,
        corner,
    )
    gn_kept, gn_sent = call(
        back_project_kernel,
        "back_project",
        [shape((2 * pixels, depth), F32)] * 2,
        [],
        0.7,
        weight,
        grad_pre,
    )
    pieces = relative_order(pieces)
    arrived = [over_shard(pieces[flip], flip) for flip in range(1, INNER)]
    *small, grad_conv, grad_sent = call(
        functools.partial(norm_back_kernel, relative, own, height, breadth),
        "norm_back",
        [shape((folded, LANES), F32)]
        + [shape((folded, LANES), BF16)] * (INNER - 1)
        + [
            shape((tiles, height, breadth, LANES), F32),
            shape((tiles, height, breadth, LANES), BF16),
        ],
        [
            pltpu.VMEM((2, tiles, height, breadth + 16, LANES), F32),
            pltpu.VMEM((2, tiles, height, breadth, LANES), F32),
            pltpu.VMEM((tiles, LANES, LANES), F32),
            pltpu.VMEM((depth, LANES), F32),
            pltpu.VMEM((INNER, rows, LANES), F32),
        ],
        0.1,
        gn_kept,
        over_core(gn_sent),
        whitened,
        inv_std,
        far_whitened,
        far_inv_std,
        taps,
        image,
        across,
    )
    small = relative_order(small)
    small_arrived = [crossing(small[flip], flip) for flip in range(INNER - 1, 0, -1)]
    grad_other = crossing(grad_sent, INNER)
    (grad_images,) = call(
        conv_back_kernel,
        "conv_back",
        [shape(images.shape, BF16)],
        [padded],
        0.1,
        grad_conv,
        grad_other,
        taps,
    )

    home, *sent = call(
        functools.partial(plane_sum_kernel, lines),
        "plane_sum",
        [shape(mixed_shape(own, quarter), F32)]
        + [shape(mixed_shape(own, quarter), BF16)] * (lines - 1),
        [],
        2.0,
        pieces[0],
        *arrived,
        small[0],
        *small_arrived,
    )
    home, grad_images = lax.optimization_barrier((home, grad_images))
    came = [crossing(sent[line - 1], INNER * line) for line in line_order(lines)]
    (total,) = call(
        functools.partial(line_sum_kernel, own),
        "line_sum",
        [shape((own, 3 * quarter + LANES), F32)],
        [],
        0.3,
        home,
        *came,
    )
    if reps > 2:
        groups = [[i for i in range(reps) if i % 2 == s] for s in range(2)]
        total = lax.psum(total, "rep", axis_index_groups=groups)
    other = over_core(total)
    factor = 1.0 / math.sqrt(images.shape[0] * pixels * shards * reps)
    grad_up, grad_depthwise, grad_gain, grad_bias = call(
        functools.partial(finish_kernel, factor),
        "finish",
        [
            shape((own, hidden), F32),
            shape((own, TAPS), F32),
            shape((1, own), F32),
            shape((1, own), F32),
        ],
        [],
        0.5,
        total,
        other,
    )
    return (grad_images, grad_up, grad_depthwise, grad_gain[0], grad_bias[0])


def solution(mesh):
    placed = (
        P(("shard", "rep"), None, None, None),
        P(("shard", "rep"), None, None, None),
        P("shard", None),
        P("shard"),
        P("shard"),
        P("shard", None),
    )
    return jax.shard_map(
        body,
        mesh=mesh,
        in_specs=placed,
        out_specs=(
            P(("shard", "rep"), None, None, None),
            P("shard", None),
            P("shard", None),
            P("shard"),
            P("shard"),
        ),
        check_vma=False,
    )
```

```python
import functools
import math

import jax
import jax.numpy as jnp
from jax import lax
from jax.experimental import pallas as pl
from jax.experimental.pallas import tpu as pltpu
from jax.sharding import PartitionSpec as P

KS = 7
TAPS = KS * KS
MARGIN = KS // 2
LANES = 128
INNER = 4
NORM_EPS = 1e-06
BF16 = jnp.bfloat16
F32 = jnp.float32
VMEM = pl.BlockSpec(memory_space=pltpu.VMEM)


def params(mebibytes):
    return pltpu.CompilerParams(vmem_limit_bytes=mebibytes * 1024 * 1024)


def gelu_slope(inputs):
    cumulative = 0.5 * (1.0 + lax.erf(inputs * 0.7071067811865476))
    return cumulative + inputs * jnp.exp(-0.5 * inputs * inputs) * 0.3989422804014327


def block_rows(relative, group, line, own, lines):
    if relative:
        place = lax.axis_index("shard") ^ (line * INNER + group)
        return pl.multiple_of(place * own, 16)
    return (group * lines + line) * own


def place_rows(pieces, target, own, relative, cast=None):
    for group, piece in enumerate(pieces):
        lines = piece.shape[0] // own
        if not relative:
            target[group * piece.shape[0] : (group + 1) * piece.shape[0], :] = (
                piece[...] if cast is None else piece[...].astype(cast)
            )
            continue
        for line in range(lines):
            rows = piece[line * own : (line + 1) * own, :]
            start = block_rows(True, group, line, own, lines)
            target[pl.ds(start, own), :] = rows if cast is None else rows.astype(cast)


def split_rows(source, pieces, own, relative):
    for group, piece in enumerate(pieces):
        lines = piece.shape[0] // own
        if not relative:
            piece[...] = source[group * piece.shape[0] : (group + 1) * piece.shape[0], :].astype(
                piece.dtype
            )
            continue
        for line in range(lines):
            start = block_rows(True, group, line, own, lines)
            piece[line * own : (line + 1) * own, :] = source[pl.ds(start, own), :].astype(
                piece.dtype
            )


def correlate(padded, tile, tap_row, height, breadth):
    sums = [None] * height
    for across in range(KS):
        shifted = padded[tile, :, 8 - MARGIN + across : 8 - MARGIN + across + breadth, :]
        for down in range(KS):
            row = tap_row(down, across)
            for line in range(height):
                origin = line + down - MARGIN
                if 0 <= origin < height:
                    term = shifted[origin] * row
                    sums[line] = term if sums[line] is None else sums[line] + term
    return sums


def tight(own, quarter):
    return own % (16 * (quarter // LANES)) == 0


def with_small(weights, extras):
    own, quarter = weights.shape
    if not tight(own, quarter):
        return jnp.concatenate([weights, extras], axis=1)
    folded = fold(extras)
    count = folded.shape[0] * LANES // quarter
    parts = [folded[at : at + count] for at in range(0, folded.shape[0], count)]
    return jnp.concatenate([weights, jnp.concatenate(parts, axis=1)], axis=0)


def without_small(mixed, own, quarter):
    if not tight(own, quarter):
        return mixed[:, :quarter], mixed[:, quarter:]
    parts = [mixed[own:, at : at + LANES] for at in range(0, quarter, LANES)]
    return mixed[:own], unfold(jnp.concatenate(parts, axis=0))


def mixed_shape(own, quarter):
    if not tight(own, quarter):
        return (own, quarter + LANES)
    return (own + own // 2 * LANES // quarter, quarter)


def pack_kernel(w_ref, dw_ref, gain_ref, bias_ref, home_ref, near_ref, far_ref, turned, wide):
    own, hidden = w_ref.shape
    quarter = hidden // 4
    side = lax.axis_index("rep") % 2
    parity = (lax.axis_index("shard") // INNER) % 2
    turned[...] = jnp.zeros_like(turned)
    turned[TAPS : TAPS + 1, :own] = gain_ref[...].astype(F32)
    turned[TAPS + 1 : TAPS + 2, :own] = bias_ref[...].astype(F32)
    wide[...] = jnp.zeros_like(wide)
    wide[:, :TAPS] = dw_ref[...].astype(F32)
    extras = wide[...] + turned[...].T[:own]
    kinds = ((home_ref, side, parity), (near_ref, 1 - side, parity), (far_ref, 1 - side, 1 - parity))
    for ref, place, which in kinds:
        start = pl.multiple_of(place * (2 * quarter) + which * quarter, LANES)
        weights = w_ref[:, pl.ds(start, quarter)].astype(F32)
        ref[...] = with_small(weights, extras).astype(BF16)


def assemble_kernel(own, *refs):
    pieces, (weight_ref, extra_ref) = refs[:-2], refs[-2:]
    quarter = weight_ref.shape[1]
    parts = [without_small(piece[...].astype(F32), own, quarter) for piece in pieces]
    for line, (weights, _) in enumerate(parts):
        weight_ref[line * own : (line + 1) * own, :] = weights.astype(BF16)
    extras = jnp.concatenate([extra for _, extra in parts], axis=0)
    if extra_ref.shape[0] < extras.shape[0]:
        extras = fold(extras)
    extra_ref[...] = extras.astype(BF16)


def plane_sum_kernel(lines, *refs):
    pieces, small, outs = refs[:INNER], refs[INNER : 2 * INNER], refs[2 * INNER :]
    own = pieces[0].shape[0] // lines
    quarter = pieces[0].shape[1]
    extras = small[0][...]
    for part in small[1:]:
        extras = extras + part[...].astype(F32)
    if extras.shape[0] < pieces[0].shape[0]:
        extras = unfold(extras)
    for line, out in enumerate(outs):
        rows = slice(line * own, (line + 1) * own)
        total = pieces[0][rows, :]
        for part in pieces[1:]:
            total = total + part[rows, :].astype(F32)
        out[...] = with_small(total, extras[rows, :]).astype(out.dtype)


def line_order(lines):
    return [*range(2, lines), 1]


def line_sum_kernel(own, *refs):
    pieces, total_ref = refs[:-1], refs[-1]
    quarter = (total_ref.shape[1] - LANES) // 3
    near, far = None, None
    for line, piece in zip(line_order(len(pieces)), pieces[1:]):
        came = piece[...].astype(F32)
        if line % 2:
            far = came if far is None else far + came
        else:
            near = came if near is None else near + came
    home, extras = without_small(pieces[0][...], own, quarter)
    total_ref[:, :quarter] = home
    for place, part in ((1, near), (2, far)):
        weights, more = without_small(part, own, quarter)
        total_ref[:, place * quarter : (place + 1) * quarter] = weights
        extras = extras + more
    total_ref[:, 3 * quarter :] = extras


def finish_kernel(factor, mine_ref, other_ref, up_ref, dw_ref, gain_ref, bias_ref):
    own, quarter = mine_ref.shape[0], (mine_ref.shape[1] - LANES) // 3
    side = lax.axis_index("rep") % 2
    parity = (lax.axis_index("shard") // INNER) % 2
    for place, home, came in ((side, mine_ref, other_ref), (1 - side, other_ref, mine_ref)):
        start = pl.multiple_of((2 * place + parity) * quarter, LANES)
        total = home[:, :quarter] + came[:, quarter : 2 * quarter]
        up_ref[:, pl.ds(start, quarter)] = total * factor
        start = pl.multiple_of((2 * place + 1 - parity) * quarter, LANES)
        up_ref[:, pl.ds(start, quarter)] = came[:, 2 * quarter : 3 * quarter] * factor
    low = 3 * quarter
    sums = (mine_ref[:, low:] + other_ref[:, low:]) * factor
    dw_ref[...] = sums[:, :TAPS]
    turned = sums.T
    gain_ref[...] = turned[TAPS : TAPS + 1, :]
    bias_ref[...] = turned[TAPS + 1 : TAPS + 2, :]


def fold(rows):
    half = rows.shape[0] // 2
    low = lax.broadcasted_iota(jnp.int32, (half, LANES), 1) < LANES // 2
    return jnp.where(low, rows[:half], pltpu.roll(rows[half:], LANES // 2, 1))


def unfold(rows):
    return jnp.concatenate([rows, pltpu.roll(rows, LANES // 2, 1)], axis=0)


def clear_borders(padded, breadth):
    shape = padded.shape[:-2] + (8, LANES)
    padded[..., :8, :] = jnp.zeros(shape, F32)
    padded[..., 8 + breadth :, :] = jnp.zeros(shape, F32)


def conv_norm_image(source, taps_ref, outs, padded, conv, height, breadth):
    normed_ref, white_ref, inv_ref = outs
    pixels, depth = normed_ref.shape
    tiles = depth // LANES
    clear_borders(padded, breadth)
    for tile in range(tiles):
        lanes = slice(tile * LANES, (tile + 1) * LANES)
        part = source[:pixels, lanes].astype(F32)
        padded[tile, :, 8 : 8 + breadth, :] = part.reshape(height, breadth, LANES)

    def one_tile(tile, carry):
        sums = correlate(
            padded,
            tile,
            lambda down, across: taps_ref[tile, pl.ds(down * KS + across, 1), :],
            height,
            breadth,
        )
        for line in range(height):
            conv[tile, line * breadth : (line + 1) * breadth, :] = sums[line]
        return carry

    lax.fori_loop(0, tiles, one_tile, 0)
    total = conv[0]
    for tile in range(1, tiles):
        total = total + conv[tile]
    average = jnp.sum(total, axis=-1, keepdims=True) / depth
    squares = None
    for tile in range(tiles):
        centered = conv[tile] - average
        squares = centered * centered if squares is None else squares + centered * centered
    variance = jnp.sum(squares, axis=-1, keepdims=True) / depth
    inv_std = lax.rsqrt(variance + NORM_EPS)
    inv_ref[...] = jnp.broadcast_to(inv_std, (pixels, LANES))
    for tile in range(tiles):
        lanes = slice(tile * LANES, (tile + 1) * LANES)
        whitened = (conv[tile] - average) * inv_std
        white_ref[:, lanes] = whitened
        gain = taps_ref[tile, TAPS : TAPS + 1, :]
        bias = taps_ref[tile, TAPS + 1 : TAPS + 2, :]
        normed_ref[:, lanes] = (whitened * gain + bias).astype(BF16)


def conv_norm_kernel(relative, own, height, breadth, *refs):
    small, x_ref = refs[:INNER], refs[INNER]
    *outs, taps_ref, gathered, unfolded, padded, conv = refs[INNER + 1 :]
    if relative:
        for group, piece in enumerate(small):
            unfolded[group * 2 * piece.shape[0] : (group + 1) * 2 * piece.shape[0], :] = unfold(
                piece[...].astype(F32)
            )
        count = unfolded.shape[0] // INNER
        small = [unfolded.at[pl.ds(group * count, count), :] for group in range(INNER)]
    place_rows(small, gathered, own, relative, F32)
    for tile in range(taps_ref.shape[0]):
        taps_ref[tile] = gathered[tile * LANES : (tile + 1) * LANES, :].T
    conv_norm_image(x_ref, taps_ref, outs, padded, conv, height, breadth)


def far_norm_kernel(height, breadth, taps_ref, far_ref, *refs):
    *outs, corner_ref, padded, conv = refs
    pixels, quarter = corner_ref.shape
    start = pl.multiple_of((1 - lax.axis_index("rep") % 2) * quarter, LANES)
    corner_ref[...] = far_ref[pixels:, pl.ds(start, quarter)]
    conv_norm_image(far_ref, taps_ref, outs, padded, conv, height, breadth)


def cot_pack_kernel(image_ref, cot_ref, across_ref, sibling_ref):
    pixels, half = sibling_ref.shape
    quarter = half // 2
    side = lax.axis_index("rep") % 2
    parity = (lax.axis_index("shard") // INNER) % 2
    for place in range(2):
        start = pl.multiple_of(place * half + (1 - parity) * quarter, LANES)
        lanes = slice(place * quarter, (place + 1) * quarter)
        across_ref[pixels:, lanes] = cot_ref[:, pl.ds(start, quarter)]
    across_ref[:pixels, :] = image_ref[...]
    sibling_ref[...] = cot_ref[:, pl.ds(pl.multiple_of((1 - side) * half, LANES), half)]


def join_kernel(own_ref, came_ref, out_ref):
    rows = own_ref.shape[0]
    out_ref[:rows, :] = own_ref[...]
    out_ref[rows:, :] = came_ref[...]


def order_kernel(relative, own, *refs):
    if not relative:
        place_rows(refs[:INNER], refs[INNER], own, relative)
        return
    home, first, second, out_ref = refs
    side = lax.axis_index("rep") % 2
    lines = home.shape[0] // own
    for line in range(lines):
        rows = slice(line * own, (line + 1) * own)
        below = slice((lines + line) * own, (lines + line + 1) * own)
        for ref, span, group in (
            (home, rows, 0),
            (first, rows, 1 + side),
            (second, rows, 2 - side),
            (second, below, INNER - 1),
        ):
            start = block_rows(True, group, line, own, lines)
            out_ref[pl.ds(start, own), :] = ref[span, :]


def project_kernel(relative, own, *refs):
    weight, *parts = refs[:5]
    cot_ref, sibling_ref, across_ref, corner_ref = refs[5:9]
    pieces = refs[9 : 9 + INNER]
    gp_ref, normed, cot, grad = refs[9 + INNER :]
    pixels, half = sibling_ref.shape
    quarter = half // 2
    side = lax.axis_index("rep") % 2
    parity = (lax.axis_index("shard") // INNER) % 2
    for place, part in enumerate(parts):
        normed[place * pixels : (place + 1) * pixels, :] = part[...]
    start = pl.multiple_of(side * half + parity * quarter, LANES)
    cot[:pixels, :] = cot_ref[:, pl.ds(start, quarter)]
    start = pl.multiple_of(side * quarter, LANES)
    cot[pixels : 2 * pixels, :] = across_ref[pixels:, pl.ds(start, quarter)]
    start = pl.multiple_of(parity * quarter, LANES)
    cot[2 * pixels : 3 * pixels, :] = sibling_ref[:, pl.ds(start, quarter)]
    cot[3 * pixels :, :] = corner_ref[...]
    for start in range(0, quarter, LANES):
        columns = slice(start, start + LANES)
        pre_act = jnp.dot(normed[...], weight[:, columns], preferred_element_type=F32)
        gp_ref[:, columns] = (cot[:, columns].astype(F32) * gelu_slope(pre_act)).astype(BF16)
    grad[...] = lax.dot_general(
        normed[...], gp_ref[...], (((0,), (0,)), ((), ())), preferred_element_type=F32
    )
    split_rows(grad, pieces, own, relative)


def back_project_kernel(weight, gp_ref, own_ref, other_ref):
    rows = own_ref.shape[0]
    grad_normed = lax.dot_general(
        gp_ref[...], weight[...], (((1,), (1,)), ((), ())), preferred_element_type=F32
    )
    own_ref[...] = grad_normed[:rows]
    other_ref[...] = grad_normed[rows:].astype(BF16)


def norm_back_kernel(relative, own, height, breadth, *refs):
    gn_own, gn_other, *norms = refs[:6]
    taps_ref, x_ref, far_ref = refs[6:9]
    pieces = refs[9 : 9 + INNER]
    grad_ref, sent_ref, padded, grads_ref, rows, small, unfolded = refs[9 + INNER :]
    pixels, depth = x_ref.shape
    tiles = depth // LANES
    clear_borders(padded, breadth)
    rows[...] = jnp.zeros_like(rows)
    for image, source in enumerate((x_ref, far_ref)):
        span = slice(image * pixels, (image + 1) * pixels)
        white_ref, inv_ref = norms[2 * image : 2 * image + 2]
        first = None
        second = None
        for tile in range(tiles):
            lanes = slice(tile * LANES, (tile + 1) * LANES)
            part = source[:pixels, lanes].astype(F32)
            padded[image, tile, :, 8 : 8 + breadth, :] = part.reshape(height, breadth, LANES)
            grad_normed = gn_own[span, lanes] + gn_other[span, lanes].astype(F32)
            whitened = white_ref[:, lanes]
            product = grad_normed * whitened
            gain = taps_ref[tile, TAPS : TAPS + 1, :]
            rows[tile, TAPS : TAPS + 1, :] += jnp.sum(product, axis=0, keepdims=True)
            rows[tile, TAPS + 1 : TAPS + 2, :] += jnp.sum(grad_normed, axis=0, keepdims=True)
            one, two = grad_normed * gain, product * gain
            first = one if first is None else first + one
            second = two if second is None else second + two
        mean_first = jnp.sum(first, axis=-1, keepdims=True) / depth
        mean_second = jnp.sum(second, axis=-1, keepdims=True) / depth
        for tile in range(tiles):
            lanes = slice(tile * LANES, (tile + 1) * LANES)
            gain = taps_ref[tile, TAPS : TAPS + 1, :]
            grad_white = (gn_own[span, lanes] + gn_other[span, lanes].astype(F32)) * gain
            grad_conv = inv_ref[...] * (
                grad_white - mean_first - white_ref[:, lanes] * mean_second
            )
            grad_conv = grad_conv.reshape(height, breadth, LANES)
            grads_ref[image, tile] = grad_conv
            if image == 0:
                grad_ref[tile] = grad_conv
            else:
                sent_ref[tile] = grad_conv.astype(BF16)

    def one_tile(tile, carry):
        grads = [[grads_ref[image, tile, line] for line in range(height)] for image in range(2)]
        for across in range(KS):
            columns = slice(8 - MARGIN + across, 8 - MARGIN + across + breadth)
            shifted = [padded[image, tile, :, columns, :] for image in range(2)]
            for down in range(KS):
                total = None
                for image in range(2):
                    for line in range(height):
                        origin = line + down - MARGIN
                        if 0 <= origin < height:
                            term = grads[image][line] * shifted[image][origin]
                            total = term if total is None else total + term
                rows[tile, pl.ds(down * KS + across, 1), :] = jnp.sum(total, axis=0, keepdims=True)
        return carry

    lax.fori_loop(0, tiles, one_tile, 0)
    for tile in range(tiles):
        small[tile * LANES : (tile + 1) * LANES, :] = rows[tile].T
    if relative:
        whole = [unfolded.at[group] for group in range(INNER)]
        split_rows(small, whole, own, relative)
        for source, piece in zip(whole, pieces):
            piece[...] = fold(source[...]).astype(piece.dtype)
    else:
        split_rows(small, pieces, own, relative)


def conv_back_kernel(grad_ref, other_ref, taps_ref, out_ref, padded):
    tiles, height, breadth, _ = grad_ref.shape
    clear_borders(padded, breadth)
    padded[:, :, 8 : 8 + breadth, :] = grad_ref[...] + other_ref[...].astype(F32)

    def one_tile(tile, carry):
        sums = correlate(
            padded,
            tile,
            lambda down, across: taps_ref[tile, pl.ds(TAPS - 1 - down * KS - across, 1), :],
            height,
            breadth,
        )
        start = pl.multiple_of(tile * LANES, LANES)
        for line in range(height):
            out_ref[0, line, :, pl.ds(start, LANES)] = sums[line].astype(BF16)
        return carry

    lax.fori_loop(0, tiles, one_tile, 0)


def call(kernel, name, outs, scratch, micros, *args, mebibytes=48):
    flops = int(micros * 1.1e9)
    moved = sum(math.prod(a.shape) * a.dtype.itemsize for a in args)
    moved += sum(math.prod(o.shape) * o.dtype.itemsize for o in outs)
    return pl.pallas_call(
        kernel,
        out_shape=outs,
        in_specs=[VMEM] * len(args),
        out_specs=[VMEM] * len(outs),
        scratch_shapes=scratch,
        compiler_params=params(mebibytes),
        cost_estimate=pl.CostEstimate(flops=flops, bytes_accessed=moved, transcendentals=0),
        name=name,
    )(*args)


def body(images, cotangent, depthwise_weight, norm_gain, norm_bias, up_weight):
    shards, reps = lax.axis_size("shard"), lax.axis_size("rep")
    own, hidden = up_weight.shape
    depth = own * shards
    lines = shards // INNER
    half, quarter = hidden // 2, hidden // 4
    height, breadth = images.shape[1:3]
    pixels = height * breadth
    tiles = depth // LANES
    me = lax.axis_index("shard")
    side = lax.axis_index("rep") % 2
    parity = (me // INNER) % 2
    relative = own % 16 == 0

    def over_shard(array, flip):
        return lax.ppermute(array, "shard", [(i, i ^ flip) for i in range(shards)])

    def crossing(array, flip):
        pairs = [
            (i * reps + r, (i ^ flip) * reps + (r ^ 1)) for i in range(shards) for r in range(reps)
        ]
        return lax.ppermute(array, ("shard", "rep"), pairs)

    def hop(array, place):
        flips = [(1, 2), (2, 1)]
        pairs = [
            (i * reps + r, (i ^ flips[r % 2][place]) * reps + r)
            for i in range(shards)
            for r in range(reps)
        ]
        return lax.ppermute(array, ("shard", "rep"), pairs)

    def over_core(array):
        return lax.ppermute(array, "rep", [(i, i ^ 1) for i in range(reps)])

    def true_order(pieces):
        if relative:
            return pieces
        stacked = jnp.stack(pieces).reshape(shards, own, -1)
        flips = jnp.arange(shards) ^ me
        places = (flips % INNER) * lines + flips // INNER
        return list(jnp.take(stacked, places, axis=0).reshape(INNER, lines * own, -1))

    def relative_order(pieces):
        if relative:
            return pieces
        stacked = jnp.concatenate([p.astype(F32) for p in pieces]).reshape(shards, own, -1)
        flips = (jnp.arange(lines)[None, :] * INNER + jnp.arange(INNER)[:, None]).reshape(-1)
        moved = jnp.take(stacked, flips ^ me, axis=0).reshape(INNER, lines * own, -1)
        return [moved[0]] + [moved[i].astype(BF16) for i in range(1, INNER)]

    shape = jax.ShapeDtypeStruct
    home, near, far = call(
        pack_kernel,
        "pack",
        [shape(mixed_shape(own, quarter), BF16)] * 3,
        [
            pltpu.VMEM((LANES, LANES), F32),
            pltpu.VMEM((own, LANES), F32),
        ],
        0.5,
        up_weight,
        depthwise_weight,
        norm_gain[None, :],
        norm_bias[None, :],
        mebibytes=63,
    )
    image, cotangent = images.reshape(pixels, depth), cotangent.reshape(pixels, hidden)
    home, near, far, image, cotangent = lax.optimization_barrier(
        (home, near, far, image, cotangent)
    )
    gathered = [home] + [
        crossing(far if line % 2 else near, INNER * line) for line in range(1, lines)
    ]
    across, cot_sibling = call(
        cot_pack_kernel,
        "cot_pack",
        [shape((2 * pixels, half), BF16), shape((pixels, half), BF16)],
        [],
        0.4,
        image,
        cotangent,
    )
    across, cot_sibling = crossing(across, INNER), over_core(cot_sibling)

    rows = lines * own
    folded = rows // 2 if relative else rows
    weight_lines, extra_lines = call(
        functools.partial(assemble_kernel, own),
        "assemble",
        [shape((rows, quarter), BF16), shape((folded, LANES), BF16)],
        [],
        4.0,
        *gathered,
    )
    weight_lines, cot_sibling = lax.optimization_barrier((weight_lines, cot_sibling))
    first_lines = hop(weight_lines, 0)
    (joined,) = call(
        join_kernel,
        "join",
        [shape((2 * rows, quarter), BF16)],
        [],
        0.3,
        weight_lines,
        first_lines,
    )
    second_lines = hop(joined, 1)
    weights = [weight_lines, first_lines, second_lines]
    extras = [extra_lines] + [crossing(extra_lines, flip) for flip in range(1, INNER)]
    if not relative:
        extras = true_order(extras)
        x_lines = jnp.where(side == 0, first_lines, second_lines[:rows])
        y_lines = jnp.where(side == 0, second_lines[:rows], first_lines)
        weights = true_order([weight_lines, x_lines, y_lines, second_lines[rows:]])
    (weight,) = call(
        functools.partial(order_kernel, relative, own),
        "order",
        [shape((depth, quarter), BF16)],
        [],
        0.3,
        *weights,
    )

    padded = pltpu.VMEM((tiles, height, breadth + 16, LANES), F32)
    norm_shapes = [
        shape((pixels, depth), BF16),
        shape((pixels, depth), F32),
        shape((pixels, LANES), F32),
    ]
    conv = pltpu.VMEM((tiles, pixels, LANES), F32)
    normed, whitened, inv_std, taps = call(
        functools.partial(conv_norm_kernel, relative, own, height, breadth),
        "conv_norm",
        norm_shapes + [shape((tiles, LANES, LANES), F32)],
        [pltpu.VMEM((depth, LANES), F32), pltpu.VMEM((depth, LANES), F32), padded, conv],
        0.1,
        *extras,
        image,
    )
    normed_sibling = over_core(normed)
    far_normed, far_whitened, far_inv_std, corner = call(
        functools.partial(far_norm_kernel, height, breadth),
        "far_norm",
        norm_shapes + [shape((pixels, quarter), BF16)],
        [padded, conv],
        1.0,
        taps,
        across,
    )
    corner_normed, corner = over_core(far_normed), over_core(corner)

    *pieces, grad_pre = call(
        functools.partial(project_kernel, relative, own),
        "project",
        [shape((rows, quarter), F32)]
        + [shape((rows, quarter), BF16)] * (INNER - 1)
        + [shape((4 * pixels, quarter), BF16)],
        [
            pltpu.VMEM((4 * pixels, depth), BF16),
            pltpu.VMEM((4 * pixels, quarter), BF16),
            pltpu.VMEM((depth, quarter), F32),
        ],
        1.6,
        weight,
        normed,
        far_normed,
        normed_sibling,
        corner_normed,
        cotangent,
        cot_sibling,
        across,
        corner,
    )
    gn_kept, gn_sent = call(
        back_project_kernel,
        "back_project",
        [shape((2 * pixels, depth), F32), shape((2 * pixels, depth), BF16)],
        [],
        0.7,
        weight,
        grad_pre,
    )
    pieces = relative_order(pieces)
    arrived = [over_shard(pieces[flip], flip) for flip in range(1, INNER)]
    *small, grad_conv, grad_sent = call(
        functools.partial(norm_back_kernel, relative, own, height, breadth),
        "norm_back",
        [shape((folded, LANES), F32)]
        + [shape((folded, LANES), BF16)] * (INNER - 1)
        + [
            shape((tiles, height, breadth, LANES), F32),
            shape((tiles, height, breadth, LANES), BF16),
        ],
        [
            pltpu.VMEM((2, tiles, height, breadth + 16, LANES), F32),
            pltpu.VMEM((2, tiles, height, breadth, LANES), F32),
            pltpu.VMEM((tiles, LANES, LANES), F32),
            pltpu.VMEM((depth, LANES), F32),
            pltpu.VMEM((INNER, rows, LANES), F32),
        ],
        0.1,
        gn_kept,
        over_core(gn_sent),
        whitened,
        inv_std,
        far_whitened,
        far_inv_std,
        taps,
        image,
        across,
    )
    small = relative_order(small)
    small_arrived = [crossing(small[flip], flip) for flip in range(INNER - 1, 0, -1)]
    grad_other = crossing(grad_sent, INNER)
    (grad_images,) = call(
        conv_back_kernel,
        "conv_back",
        [shape(images.shape, BF16)],
        [padded],
        0.1,
        grad_conv,
        grad_other,
        taps,
    )

    home, *sent = call(
        functools.partial(plane_sum_kernel, lines),
        "plane_sum",
        [shape(mixed_shape(own, quarter), F32)]
        + [shape(mixed_shape(own, quarter), BF16)] * (lines - 1),
        [],
        2.0,
        pieces[0],
        *arrived,
        small[0],
        *small_arrived,
    )
    home, grad_images = lax.optimization_barrier((home, grad_images))
    came = [crossing(sent[line - 1], INNER * line) for line in line_order(lines)]
    (total,) = call(
        functools.partial(line_sum_kernel, own),
        "line_sum",
        [shape((own, 3 * quarter + LANES), F32)],
        [],
        0.3,
        home,
        *came,
    )
    if reps > 2:
        groups = [[i for i in range(reps) if i % 2 == s] for s in range(2)]
        total = lax.psum(total, "rep", axis_index_groups=groups)
    other = over_core(total)
    factor = 1.0 / math.sqrt(images.shape[0] * pixels * shards * reps)
    grad_up, grad_depthwise, grad_gain, grad_bias = call(
        functools.partial(finish_kernel, factor),
        "finish",
        [
            shape((own, hidden), F32),
            shape((own, TAPS), F32),
            shape((1, own), F32),
            shape((1, own), F32),
        ],
        [],
        0.5,
        total,
        other,
    )
    return (grad_images, grad_up, grad_depthwise, grad_gain[0], grad_bias[0])


def solution(mesh):
    placed = (
        P(("shard", "rep"), None, None, None),
        P(("shard", "rep"), None, None, None),
        P("shard", None),
        P("shard"),
        P("shard"),
        P("shard", None),
    )
    return jax.shard_map(
        body,
        mesh=mesh,
        in_specs=placed,
        out_specs=(
            P(("shard", "rep"), None, None, None),
            P("shard", None),
            P("shard", None),
            P("shard"),
            P("shard"),
        ),
        check_vma=False,
    )
```
